32 devices in a mesh: lat: 4 (over z), lon: 8 (over y, x, core).
Axes of the slice: x: 2, y: 2, z: 4, core: 2. Of those that a mesh axis runs over, the one named last changes fastest.
Arguments:
- tokens: bfloat16 [2, 64, 192, 1024], P(None, 'lat', 'lon'), may hold values from -6 to 6
- qkv_weight: bfloat16 [1024, 3072], replicated, may hold values from -0.1875 to 0.1875
- out_weight: bfloat16 [1024, 1024], replicated, may hold values from -0.1875 to 0.1875
- merge_weight: bfloat16 [4096, 1024], replicated, may hold values from -0.09375 to 0.09375
- merged_grad: bfloat16 [2, 32, 96, 1024], P(None, 'lat', 'lon'), may hold values from -6 to 6
Outputs:
- merged: bfloat16 [2, 32, 96, 1024], P(None, 'lat', 'lon')
- tokens_grad: bfloat16 [2, 64, 192, 1024], P(None, 'lat', 'lon')
- qkv_weight_grad: float32 [1024, 3072], P(('lat', 'lon'))
- out_weight_grad: float32 [1024, 1024], P(('lat', 'lon'))
The draws below stay inside these ranges and needn't reach their ends.
All inputs are finite; a program needn't handle non-finite values.
Results may differ from the reference program's by a relative error of at most 0.02.
Values may be sent and summed in bfloat16 or wider, within the bound.
No kernel may reach another device: no remote copies, remote signals or barrier semaphores. Data moves between devices by JAX's collectives and lax.ppermute only.
A program may use at most 192 MiB of HBM per device.

```python
import jax
import jax.numpy as jnp
from jax import lax

C = 1024
HEADS = 32
MERGED = 1024
LEV = 2
WIN = 8
SHIFT = 4
GRID_LAT = 64
GRID_LON = 192


def steps_of(own_key, dims, shards, least, largest):
    factor_of, own = 1.0, jax.random.fold_in(own_key, 6)
    for position, blocks in shards:
        draws = jnp.exp(jax.random.uniform(jax.random.fold_in(own, position), (blocks,), jnp.float32, least / len(shards), largest / len(shards)))
        factor_of = factor_of * jnp.repeat(draws, dims[position] // blocks).reshape([-1 if axis == position else 1 for axis in range(len(dims))])
    return factor_of


def normal_values(own_key, extent, scale, most, cuts=(), dtype=jnp.bfloat16):
    drawn = scale * jax.random.normal(own_key, extent, jnp.float32)
    if cuts:
        drawn = drawn * steps_of(own_key, extent, cuts, -0.22, 0.18)
    return jnp.clip(drawn, -most, most).astype(dtype)


def setup_inputs(seed: int = 0) -> dict:
    seeds = jax.random.split(jax.random.key(seed), 6)
    tokens = normal_values(seeds[0], (LEV, GRID_LAT, GRID_LON, C), 1.0, 6.0, ((1, 4), (2, 8)))
    qkv_weight = normal_values(seeds[1], (C, 3 * C), C ** -0.5, 0.1875)
    out_weight = normal_values(seeds[2], (C, C), C ** -0.5, 0.1875)
    merge_weight = normal_values(seeds[3], (4 * C, MERGED), (4 * C) ** -0.5, 0.09375)
    merged_grad = normal_values(seeds[4], (LEV, GRID_LAT // 2, GRID_LON // 2, MERGED), 1.0, 6.0, ((1, 4), (2, 8)))
    return dict(tokens=tokens, qkv_weight=qkv_weight, out_weight=out_weight, merge_weight=merge_weight, merged_grad=merged_grad)


epsilon = 1e-05

def normalize(grid_field):
    values = grid_field.astype(jnp.float32)
    center = lax.optimization_barrier(jnp.mean(values, axis=-1, keepdims=True))
    spread = lax.optimization_barrier(jnp.mean(jnp.square(values - center), axis=-1, keepdims=True))
    return ((values - center) * lax.rsqrt(spread + epsilon)).astype(jnp.bfloat16)

def window_attention(window_values, region_marks):
    windows = window_values.shape[0]
    places = window_values.shape[1]
    channels = window_values.shape[2] // 3
    head_dim = channels // HEADS
    pieces = window_values.reshape(windows, places, 3, HEADS, head_dim)
    queries = pieces[:, :, 0].astype(jnp.float32)
    keys_part = pieces[:, :, 1].astype(jnp.float32)
    values_part = pieces[:, :, 2].astype(jnp.float32)
    scores = jnp.einsum('bqhd,bkhd->bhqk', queries, keys_part) * head_dim ** (-0.5)
    same_region = region_marks[:, None, :, None] == region_marks[:, None, None, :]
    weights = jnp.where(same_region, jnp.exp(scores), 0.0)
    attention = (weights / lax.optimization_barrier(jnp.sum(weights, axis=-1, keepdims=True))).astype(jnp.bfloat16)
    mixture = jnp.einsum('bhqk,bkhd->bqhd', attention.astype(jnp.float32), values_part)
    return mixture.astype(jnp.bfloat16).reshape(windows, places, channels)

def to_windows(grid_field):
    lev_count, lat_rows, lon_cols, channels = grid_field.shape
    blocks = grid_field.reshape(lev_count, lat_rows // WIN, WIN, lon_cols // WIN, WIN, channels)
    blocks = blocks.transpose(1, 3, 0, 2, 4, 5)
    return blocks.reshape(lat_rows // WIN, lon_cols // WIN, lev_count * WIN * WIN, channels)

def from_windows(blocks, lev_count, lat_rows, lon_cols):
    channels = blocks.shape[-1]
    grid_field = blocks.reshape(lat_rows // WIN, lon_cols // WIN, lev_count, WIN, WIN, channels)
    return grid_field.transpose(2, 0, 3, 1, 4, 5).reshape(lev_count, lat_rows, lon_cols, channels)

def attend_all(projected, region):
    blocks = to_windows(projected)
    region_blocks = to_windows(region[..., None])[..., 0]
    window_step = jax.checkpoint(lambda window_pair: window_attention(window_pair[0], window_pair[1]))
    mixture = lax.map(window_step, (blocks, region_blocks))
    return from_windows(mixture, LEV, GRID_LAT, GRID_LON)

def merge(grid_field, merge_weight):
    lev_count, lat_rows, lon_cols, channels = grid_field.shape
    groups = grid_field.reshape(lev_count, lat_rows // 2, 2, lon_cols // 2, 2, channels)
    groups = groups.transpose(0, 1, 3, 4, 2, 5).reshape(lev_count, lat_rows // 2, lon_cols // 2, 4 * channels)
    normed = normalize(groups)
    result = jnp.dot(normed.reshape(-1, 4 * channels), merge_weight, preferred_element_type=jnp.float32)
    return result.astype(jnp.bfloat16).reshape(lev_count, lat_rows // 2, lon_cols // 2, merge_weight.shape[1])

def reference(tokens, qkv_weight, out_weight, merge_weight, merged_grad):
    channels = tokens.shape[-1]
    rolled = jnp.roll(tokens, (-SHIFT, -SHIFT), axis=(1, 2))
    normed, norm_back = jax.vjp(normalize, rolled)
    flat_norm = normed.reshape(-1, channels)
    projected = jnp.dot(flat_norm, qkv_weight, preferred_element_type=jnp.float32).astype(jnp.bfloat16)
    projected = projected.reshape(LEV, GRID_LAT, GRID_LON, 3 * channels)
    region_rows = (jnp.arange(GRID_LAT) >= GRID_LAT - SHIFT).astype(jnp.int32)
    region = jnp.broadcast_to(region_rows[None, :, None], (LEV, GRID_LAT, GRID_LON))
    mixture, attend_back = jax.vjp(lambda grid_values: attend_all(grid_values, region), projected)
    mixture_flat = mixture.reshape(-1, channels)
    branch = jnp.dot(mixture_flat, out_weight, preferred_element_type=jnp.float32)
    shifted_out = (rolled.reshape(-1, channels).astype(jnp.float32) + branch).astype(jnp.bfloat16)
    block_out = jnp.roll(shifted_out.reshape(rolled.shape), (SHIFT, SHIFT), axis=(1, 2))
    merged, merge_back = jax.vjp(lambda grid_values: merge(grid_values, merge_weight), block_out)
    block_grad = merge_back(merged_grad)[0]
    grad_rolled = jnp.roll(block_grad, (-SHIFT, -SHIFT), axis=(1, 2)).reshape(-1, channels)
    mixture_grad = lax.dot_general(grad_rolled, out_weight, (((1,), (1,)), ((), ())), preferred_element_type=jnp.float32).astype(jnp.bfloat16)
    out_weight_grad = lax.dot_general(mixture_flat, grad_rolled, (((0,), (0,)), ((), ())), preferred_element_type=jnp.float32)
    projected_grad = attend_back(mixture_grad.reshape(mixture.shape))[0].reshape(-1, 3 * channels)
    qkv_weight_grad = lax.dot_general(flat_norm, projected_grad, (((0,), (0,)), ((), ())), preferred_element_type=jnp.float32)
    normed_grad = lax.dot_general(projected_grad, qkv_weight, (((1,), (1,)), ((), ())), preferred_element_type=jnp.float32).astype(jnp.bfloat16)
    input_part = norm_back(normed_grad.reshape(normed.shape))[0].reshape(-1, channels)
    rolled_grad = (grad_rolled.astype(jnp.float32) + input_part.astype(jnp.float32)).astype(jnp.bfloat16)
    tokens_grad = jnp.roll(rolled_grad.reshape(rolled.shape), (SHIFT, SHIFT), axis=(1, 2))
    return (merged, tokens_grad, qkv_weight_grad, out_weight_grad)
```

```python
import functools

import jax
import jax.numpy as jnp
import numpy as np
from jax import lax
from jax.experimental import pallas as pl
from jax.experimental.pallas import tpu as pltpu
from jax.sharding import PartitionSpec as P

HEADS = 32
WIN = 8
SHIFT = 4
LANES = 128
HALF = SHIFT // 2
EPSILON = 1e-05
MIB = 1 << 20

NN = (((1,), (0,)), ((), ()))
NT = (((1,), (1,)), ((), ()))
TN = (((0,), (0,)), ((), ()))
BF16 = jnp.bfloat16
F32 = jnp.float32


def dot(a, b, dims=NN):
    return lax.dot_general(a, b, dims, preferred_element_type=F32)


def window_order(levels, columns):
    windows, half = columns // WIN, WIN // 2
    order = []
    for window in range(windows):
        for sub in range(4):
            for level in range(levels):
                for row in range(half):
                    for column in range(half):
                        order.append(
                            (level * WIN + 2 * row + sub % 2) * columns
                            + window * WIN + 2 * column + sub // 2
                        )
    return np.eye(len(order), dtype=np.float32)[np.array(order)]


def group_order(levels, rows, columns):
    half = WIN // 2
    order = []
    for window_row in range(rows // half):
        for window in range(columns // half):
            for level in range(levels):
                for row in range(half):
                    for column in range(half):
                        order.append(
                            (level * rows + window_row * half + row) * columns
                            + window * half + column
                        )
    return np.eye(len(order), dtype=np.float32)[np.array(order)]


def head_masks():
    head = lax.broadcasted_iota(jnp.int32, (LANES, LANES), 1) // (LANES // 4)
    return [jnp.where(head == h, 1.0, 0.0).astype(BF16) for h in range(4)]


def region_bias(places, active):
    step = 2 * (WIN // 2)
    one = (lax.broadcasted_iota(jnp.int32, (places, places), 0) // step) % 2
    other = (lax.broadcasted_iota(jnp.int32, (places, places), 1) // step) % 2
    return jnp.where((one != other) & active, -1e30, 0.0)


def score_scale(channels):
    return float((channels // HEADS) ** -0.5 * np.log2(np.e))


def forward_kernel(
    edge, framed, merged_grad, order, group, rowmap, wqkv_h, wout_h, wm_h,
    normed_h, normt_h, proj_h, dmr_h, dmm_h, grad_h, rstd, merged, out_mine, out_theirs,
    wqkv, wout, wm, xw, normed, normt, proj, mixture, inverse, subs, dsubs, grad, dmr, dmm,
    in_sem, out_sem,
):
    tokens, channels = xw.shape
    places = 2 * WIN * WIN
    windows = tokens // places
    per_row = order.shape[0] // places
    quarter = places // 4
    groups = tokens // 4
    tile = 256

    loads = [
        pltpu.make_async_copy(src, dst, in_sem.at[i])
        for i, (src, dst) in enumerate([(wqkv_h, wqkv), (wout_h, wout), (wm_h, wm)])
    ]
    for load in loads:
        load.start()
    stores = [
        pltpu.make_async_copy(src, dst, out_sem.at[i])
        for i, (src, dst) in enumerate(
            [(normed, normed_h), (proj, proj_h), (normt, normt_h),
             (grad, grad_h), (dmr, dmr_h), (dmm, dmm_h)]
        )
    ]

    span = order.shape[0] // 2

    @pl.loop(0, windows)
    def _(w):
        wi, wj = w // per_row, w % per_row
        first = framed[pl.ds(pl.multiple_of(wi * span, 64), span)]
        second = framed[pl.ds(pl.multiple_of(tokens // 2 + wi * span, 64), span)]
        source = jnp.concatenate([first, second], axis=0)
        x = dot(order[pl.ds(pl.multiple_of(wj * places, places), places)], source)
        rows = pl.ds(pl.multiple_of(w * places, places), places)
        xw[rows] = x.astype(BF16)
        center = jnp.mean(x, axis=1, keepdims=True)
        moved = x - center
        scale = lax.rsqrt(jnp.mean(moved * moved, axis=1, keepdims=True) + EPSILON)
        rstd[rows] = jnp.broadcast_to(scale, (places, LANES))
        normed[rows] = (moved * scale).astype(BF16)

    stores[0].start()
    loads[0].wait()

    @pl.loop(0, wqkv.shape[1] // tile)
    def _(n):
        columns = pl.ds(pl.multiple_of(n * tile, tile), tile)
        proj[:, columns] = dot(normed[...], wqkv[:, columns]).astype(BF16)

    stores[1].start()

    masks = head_masks()
    factor = score_scale(channels)

    @pl.loop(0, windows)
    def _(w):
        rows = pl.ds(pl.multiple_of(w * places, places), places)
        bias = region_bias(places, (edge[0] == 1) & (w < per_row))
        for g in range(channels // LANES):
            lanes = pl.ds(g * LANES, LANES)
            q = proj[rows, lanes]
            k = proj[rows, pl.ds(channels + g * LANES, LANES)]
            v = proj[rows, pl.ds(2 * channels + g * LANES, LANES)]
            scores = dot(q, jnp.concatenate([k * m for m in masks], axis=0), NT)
            parts = []
            for h in range(4):
                part = scores[:, h * places:(h + 1) * places] * factor + bias
                part = part - jnp.max(part, axis=1, keepdims=True)
                parts.append(jnp.exp2(part).astype(BF16))
            values = jnp.concatenate(
                [jnp.concatenate([v * m, m], axis=1) for m in masks], axis=0
            )
            summed = dot(jnp.concatenate(parts, axis=1), values)
            inv = 1.0 / summed[:, LANES:]
            inverse[rows, lanes] = inv
            mixture[rows, lanes] = (summed[:, :LANES] * inv).astype(BF16)

    loads[1].wait()

    @pl.loop(0, channels // tile)
    def _(n):
        columns = pl.ds(pl.multiple_of(n * tile, tile), tile)
        out = dot(mixture[...], wout[:, columns]) + xw[:, columns].astype(F32)
        out = out.astype(BF16)
        for w in range(windows):
            for s in range(4):
                at = w * places + s * quarter
                subs[s, w * quarter:(w + 1) * quarter, columns] = out[at:at + quarter]

    total = jnp.zeros((groups, 1), F32)
    for s in range(4):
        total += jnp.sum(subs[s].astype(F32), axis=1, keepdims=True)
    center = total / (4 * channels)
    total = jnp.zeros((groups, 1), F32)
    for s in range(4):
        moved = subs[s].astype(F32) - center
        total += jnp.sum(moved * moved, axis=1, keepdims=True)
    scale = lax.rsqrt(total / (4 * channels) + EPSILON)
    loads[2].wait()
    result = jnp.zeros((groups, wm.shape[1]), F32)
    for s in range(4):
        unit = ((subs[s].astype(F32) - center) * scale).astype(BF16)
        result += dot(unit, wm[s * channels:(s + 1) * channels])
    merged[...] = dot(group[...], result.astype(BF16), TN).astype(BF16)

    cotangent = dot(group[...], merged_grad[...]).astype(BF16)
    mean_g = jnp.zeros((groups, 1), F32)
    mean_gx = jnp.zeros((groups, 1), F32)
    for s in range(4):
        d = dot(cotangent, wm[s * channels:(s + 1) * channels], NT).astype(BF16)
        dsubs[s] = d
        d = d.astype(F32)
        mean_g += jnp.sum(d, axis=1, keepdims=True)
        mean_gx += jnp.sum(d * ((subs[s].astype(F32) - center) * scale), axis=1, keepdims=True)
    mean_g = mean_g / (4 * channels)
    mean_gx = mean_gx / (4 * channels)
    for s in range(4):
        unit = (subs[s].astype(F32) - center) * scale
        d = (scale * (dsubs[s].astype(F32) - mean_g - unit * mean_gx)).astype(BF16)
        for w in range(windows):
            at = w * places + s * quarter
            grad[at:at + quarter] = d[w * quarter:(w + 1) * quarter]
    stores[3].start()

    @pl.loop(0, channels // tile)
    def _(n):
        columns = pl.ds(pl.multiple_of(n * tile, tile), tile)
        d = dot(grad[...], wout[columns], NT).astype(BF16).astype(F32)
        d = d * inverse[:, columns]
        dmr[:, columns] = d.astype(BF16)
        dmm[:, columns] = (-d * mixture[:, columns].astype(F32)).astype(BF16)

    stores[4].start()
    stores[5].start()

    @pl.loop(0, channels // tile)
    def _(n):
        rows = pl.ds(pl.multiple_of(n * tile, tile), tile)
        spot = lax.broadcasted_iota(jnp.int32, (tile, channels), 1)
        pick = jnp.where(spot == rowmap[rows], 1.0, 0.0).astype(BF16)
        normt[rows] = dot(pick, normed[...], NT).astype(BF16)
        turned = dot(pick, mixture[...], NT).astype(BF16)
        part = dot(turned, grad[...]).astype(BF16)

        @pl.when(n < channels // tile // 2)
        def _():
            out_mine[rows] = part

        @pl.when(n >= channels // tile // 2)
        def _():
            out_theirs[pl.ds(pl.multiple_of(n * tile - channels // 2, tile), tile)] = part

    stores[2].start()
    for store in stores:
        store.wait()


def backward_kernel(
    edge, q_ref, k_ref, v_ref, dmr, dmm, normt, pgrad, mine, theirs
):
    tokens, width = q_ref.shape
    channels = normt.shape[0]
    places = 2 * WIN * WIN
    windows = tokens // places
    per_row = windows // 2
    masks = head_masks()
    factor = score_scale(channels)
    plain = (channels // HEADS) ** -0.5

    @pl.loop(0, windows)
    def _(w):
        rows = pl.ds(pl.multiple_of(w * places, places), places)
        bias = region_bias(places, (edge[0] == 1) & (w < per_row))
        for g in range(width // LANES):
            lanes = pl.ds(g * LANES, LANES)
            q, k, v = q_ref[rows, lanes], k_ref[rows, lanes], v_ref[rows, lanes]
            dm, dd = dmr[rows, lanes], dmm[rows, lanes]
            keys = jnp.concatenate([k * m for m in masks], axis=0)
            scores = dot(keys, q, NT)
            values = jnp.concatenate(
                [jnp.concatenate([v * m, m], axis=1) for m in masks], axis=0
            )
            slope = dot(values, jnp.concatenate([dm, dd], axis=1), NT)
            weights, slopes = [], []
            for h in range(4):
                block = slice(h * places, (h + 1) * places)
                part = scores[block] * factor + bias
                part = jnp.exp2(part - jnp.max(part, axis=0, keepdims=True))
                weights.append(part.astype(BF16))
                slopes.append((part * slope[block]).astype(BF16))
            dv = dot(
                jnp.concatenate(weights, axis=1),
                jnp.concatenate([dm * m for m in masks], axis=0),
            )
            dk = dot(
                jnp.concatenate(slopes, axis=1),
                jnp.concatenate([q * m for m in masks], axis=0),
            )
            dq = dot(jnp.concatenate(slopes, axis=0), keys, TN)
            pgrad[rows, lanes] = (dq * plain).astype(BF16)
            pgrad[rows, pl.ds(width + g * LANES, LANES)] = (dk * plain).astype(BF16)
            pgrad[rows, pl.ds(2 * width + g * LANES, LANES)] = dv.astype(BF16)

    tile = 256

    @pl.loop(0, 3 * width // tile)
    def _(n):
        columns = pl.ds(pl.multiple_of(n * tile, tile), tile)
        half = channels // 2
        mine[:, columns] = dot(normt[:half], pgrad[:, columns]).astype(BF16)
        theirs[:, columns] = dot(normt[half:], pgrad[:, columns]).astype(BF16)


def input_kernel(chunks, *refs):
    pgrads = refs[:chunks]
    wqkv, normed, rstd, grad, order, out, ngrad, full = refs[chunks:]
    tokens, channels = normed.shape
    places = 2 * WIN * WIN
    windows = tokens // places
    width = channels // chunks
    tile = 256

    @pl.loop(0, channels // tile)
    def _(n):
        rows = pl.ds(pl.multiple_of(n * tile, tile), tile)
        total = jnp.zeros((tokens, tile), F32)
        for c in range(chunks):
            for part in range(3):
                total += dot(
                    pgrads[c][:, part * width:(part + 1) * width],
                    wqkv[rows, pl.ds(part * channels + c * width, width)],
                    NT,
                )
        ngrad[:, rows] = total.astype(BF16)

    @pl.loop(0, windows)
    def _(w):
        rows = pl.ds(pl.multiple_of(w * places, places), places)
        d = ngrad[rows].astype(F32)
        unit = normed[rows].astype(F32)
        mean_d = jnp.mean(d, axis=1, keepdims=True)
        mean_dx = jnp.mean(d * unit, axis=1, keepdims=True)
        part = rstd[rows, :1] * (d - mean_d - unit * mean_dx)
        full[rows] = (part.astype(BF16).astype(F32) + grad[rows].astype(F32)).astype(BF16)

    count = order.shape[0]
    for wi in range(tokens // count):
        moved = dot(order[...], full[wi * count:(wi + 1) * count], TN).astype(BF16)
        for level in range(2):
            at = level * (tokens // 2) + wi * (count // 2)
            out[at:at + count // 2] = moved[level * (count // 2):(level + 1) * (count // 2)]


def linear_route(sizes, lat_step, lon_step):
    n_lat, n_lon = sizes
    return [
        (a * n_lon + b, (a + lat_step) % n_lat * n_lon + (b + lon_step) % n_lon)
        for a in range(n_lat) for b in range(n_lon)
    ]


def sent(block, sizes, lat_step, lon_step):
    return lax.ppermute(block, ("lat", "lon"), linear_route(sizes, lat_step, lon_step))


def forward_move(field, width, sizes):
    kept_rows = field[:, :-width]
    last_rows = field[:, -width:]
    side = sent(kept_rows[:, :, -width:], sizes, 0, 1)
    above = sent(last_rows[:, :, :-width], sizes, 1, 0)
    corner = sent(last_rows[:, :, -width:], sizes, 1, 1)
    top = jnp.concatenate([corner, above], axis=2)
    rest = jnp.concatenate([side, kept_rows[:, :, :-width]], axis=2)
    return jnp.concatenate([top, rest], axis=1)


def backward_move(field, width, sizes):
    first_rows = field[:, :width]
    kept_rows = field[:, width:]
    side = sent(kept_rows[:, :, :width], sizes, 0, -1)
    below = sent(first_rows[:, :, width:], sizes, -1, 0)
    corner = sent(first_rows[:, :, :width], sizes, -1, -1)
    rest = jnp.concatenate([kept_rows[:, :, width:], side], axis=2)
    bottom = jnp.concatenate([below, corner], axis=2)
    return jnp.concatenate([rest, bottom], axis=1)


def bit_list(count):
    return [1 << i for i in range(count.bit_length() - 1)]


def device_rows(channels, sizes):
    n_lat, n_lon = sizes
    devices = n_lat * n_lon
    bits = bit_list(devices)
    rows = channels // devices
    place = np.arange(channels) // rows
    partner = np.zeros_like(place)
    for i, bit in enumerate(bits):
        partner |= np.where(place & (devices >> (i + 1)), bit, 0)
    me = lax.axis_index("lat") * n_lon + lax.axis_index("lon")
    owner = jnp.bitwise_xor(jnp.asarray(partner, jnp.int32), me.astype(jnp.int32))
    return (owner * rows + jnp.asarray(np.arange(channels) % rows, jnp.int32))[:, None]


def exchange(block, sizes, bit):
    devices = sizes[0] * sizes[1]
    return lax.ppermute(block, ("lat", "lon"), [(i, i ^ bit) for i in range(devices)])


def added(a, b, dtype=BF16):
    return (a.astype(F32) + b.astype(F32)).astype(dtype)


def halved(block, bits, bit, sizes, dtype=BF16):
    axis = bits.index(bit)
    kept = lax.index_in_dim(block, 0, axis, keepdims=False)
    given = lax.index_in_dim(block, 1, axis, keepdims=False)
    return added(kept, exchange(given, sizes, bit), dtype), [b for b in bits if b != bit]


def scattered_sum(mine, theirs, sizes):
    n_lat, n_lon = sizes
    lon_bits = bit_list(n_lon)
    lat_bits = [n_lon * b for b in bit_list(n_lat)]
    columns = mine.shape[1]
    rows = 2 * mine.shape[0] // (n_lat * n_lon)
    half = added(mine, exchange(theirs, sizes, lon_bits[0]))
    left = lon_bits[1:] + lat_bits
    parts = []
    for i, turn in enumerate((lon_bits[1:], lon_bits[:0:-1])):
        part = half[:, i * (columns // 2):(i + 1) * (columns // 2)]
        part = part.reshape([2] * len(left) + [rows, columns // 2])
        bits = left
        for bit in turn:
            part, bits = halved(part, bits, bit, sizes)
        parts.append(part)
    part = jnp.concatenate(parts, axis=-1)
    for bit in lat_bits:
        part, bits = halved(part, bits, bit, sizes, F32 if bit == lat_bits[-1] else BF16)
    return part


def shards(sizes, tokens, qkv_weight, out_weight, merge_weight, merged_grad):
    levels, lat_rows, lon_cols, channels = tokens.shape
    merged_width = merge_weight.shape[1]
    count = levels * lat_rows * lon_cols
    groups = count // 4
    half = channels // 2
    vmem = pl.BlockSpec(memory_space=pltpu.VMEM)
    smem = pl.BlockSpec(memory_space=pltpu.SMEM)
    hbm = pl.BlockSpec(memory_space=pl.ANY)

    order = jnp.asarray(window_order(levels, lon_cols), BF16)
    group = jnp.asarray(group_order(levels, lat_rows // 2, lon_cols // 2), BF16)
    edge = (lax.axis_index("lat") == 0).astype(jnp.int32).reshape(1)
    rowmap = device_rows(channels, sizes)

    framed = forward_move(tokens, SHIFT, sizes).reshape(count, channels)
    framed_grad = forward_move(merged_grad, HALF, sizes).reshape(groups, merged_width)

    wide = jax.ShapeDtypeStruct((count, channels), BF16)
    normed, normt, proj, dmr, dmm, grad, rstd, merged, out_mine, out_theirs = pl.pallas_call(
        forward_kernel,
        out_shape=[
            wide,
            jax.ShapeDtypeStruct((channels, count), BF16),
            jax.ShapeDtypeStruct((count, 3 * channels), BF16),
            wide, wide, wide,
            jax.ShapeDtypeStruct((count, LANES), F32),
            jax.ShapeDtypeStruct((groups, merged_width), BF16),
            jax.ShapeDtypeStruct((half, channels), BF16),
            jax.ShapeDtypeStruct((half, channels), BF16),
        ],
        in_specs=[smem] + [vmem] * 5 + [hbm] * 3,
        out_specs=[hbm] * 6 + [vmem] * 4,
        scratch_shapes=[
            pltpu.VMEM(qkv_weight.shape, BF16),
            pltpu.VMEM(out_weight.shape, BF16),
            pltpu.VMEM(merge_weight.shape, BF16),
            pltpu.VMEM((count, channels), BF16),
            pltpu.VMEM((count, channels), BF16),
            pltpu.VMEM((channels, count), BF16),
            pltpu.VMEM((count, 3 * channels), BF16),
            pltpu.VMEM((count, channels), BF16),
            pltpu.VMEM((count, channels), F32),
            pltpu.VMEM((4, groups, channels), BF16),
            pltpu.VMEM((4, groups, channels), BF16),
            pltpu.VMEM((count, channels), BF16),
            pltpu.VMEM((count, channels), BF16),
            pltpu.VMEM((count, channels), BF16),
            pltpu.SemaphoreType.DMA((3,)),
            pltpu.SemaphoreType.DMA((6,)),
        ],
        compiler_params=pltpu.CompilerParams(vmem_limit_bytes=58 * MIB),
        cost_estimate=pl.CostEstimate(
            flops=24 * count * channels * channels, bytes_accessed=34 * MIB, transcendentals=0
        ),
        name="block_forward",
    )(edge, framed, framed_grad, order, group, rowmap, qkv_weight, out_weight, merge_weight)

    merged = backward_move(
        merged.reshape(levels, lat_rows // 2, lon_cols // 2, merged_width), HALF, sizes
    )
    out_weight_grad = scattered_sum(out_mine, out_theirs, sizes)

    chunks = 2
    width = channels // chunks
    pgrads, qkv_parts = [], []
    for c in range(chunks):
        def columns(part, c=c):
            return pl.BlockSpec((count, width), lambda i: (0, part * chunks + c))

        pgrad, mine, theirs = pl.pallas_call(
            backward_kernel,
            grid=(1,),
            out_shape=[
                jax.ShapeDtypeStruct((count, 3 * width), BF16),
                jax.ShapeDtypeStruct((half, 3 * width), BF16),
                jax.ShapeDtypeStruct((half, 3 * width), BF16),
            ],
            in_specs=[smem, columns(0), columns(1), columns(2), columns(0), columns(0),
                      pl.BlockSpec((channels, count), lambda i: (0, 0))],
            out_specs=[
                pl.BlockSpec((count, 3 * width), lambda i: (0, 0)),
                pl.BlockSpec((half, 3 * width), lambda i: (0, 0)),
                pl.BlockSpec((half, 3 * width), lambda i: (0, 0)),
            ],
            compiler_params=pltpu.CompilerParams(vmem_limit_bytes=48 * MIB),
            cost_estimate=pl.CostEstimate(
                flops=8 * count * channels * channels, bytes_accessed=12 * MIB, transcendentals=0
            ),
            name="attention_backward",
        )(edge, proj, proj, proj, dmr, dmm, normt)
        pgrads.append(pgrad)
        qkv_parts.append(scattered_sum(mine, theirs, sizes))

    framed_out = pl.pallas_call(
        functools.partial(input_kernel, chunks),
        out_shape=wide,
        in_specs=[vmem] * (chunks + 5),
        out_specs=vmem,
        scratch_shapes=[pltpu.VMEM((count, channels), BF16)] * 2,
        compiler_params=pltpu.CompilerParams(vmem_limit_bytes=48 * MIB),
        cost_estimate=pl.CostEstimate(
            flops=7 * count * channels * channels, bytes_accessed=18 * MIB, transcendentals=0
        ),
        name="input_backward",
    )(*pgrads, qkv_weight, normed, rstd, grad, order)
    tokens_grad = backward_move(framed_out.reshape(tokens.shape), SHIFT, sizes)

    qkv_weight_grad = jnp.concatenate(
        [part[:, i * width:(i + 1) * width] for i in range(3) for part in qkv_parts], axis=1
    )
    return merged, tokens_grad, qkv_weight_grad, out_weight_grad


def solution(mesh):
    sizes = (mesh.shape["lat"], mesh.shape["lon"])
    in_specs = (P(None, "lat", "lon", None), P(), P(), P(), P(None, "lat", "lon", None))
    out_specs = (
        P(None, "lat", "lon", None),
        P(None, "lat", "lon", None),
        P(("lat", "lon"), None),
        P(("lat", "lon"), None),
    )
    return jax.shard_map(
        functools.partial(shards, sizes),
        mesh=mesh, in_specs=in_specs, out_specs=out_specs, check_vma=False,
    )
```

```python
import functools

import jax
import jax.numpy as jnp
import numpy as np
from jax import lax
from jax.experimental import pallas as pl
from jax.experimental.pallas import tpu as pltpu
from jax.sharding import PartitionSpec as P

HEADS = 32
WIN = 8
SHIFT = 4
LANES = 128
HALF = SHIFT // 2
TILE = 256
EPSILON = 1e-05
MIB = 1 << 20
PARTS = 4

NN = (((1,), (0,)), ((), ()))
NT = (((1,), (1,)), ((), ()))
TN = (((0,), (0,)), ((), ()))
BF16 = jnp.bfloat16
F32 = jnp.float32


def dot(a, b, dims=NN):
    return lax.dot_general(a, b, dims, preferred_element_type=F32)


def window_cells(levels, rows, columns):
    half = WIN // 2
    return [
        (level, wi * WIN + 2 * row + sub % 2, wj * WIN + 2 * column + sub // 2)
        for wi in range(rows // WIN) for wj in range(columns // WIN) for sub in range(4)
        for level in range(levels) for row in range(half) for column in range(half)
    ]


def window_groups(levels, rows, columns):
    half = WIN // 2
    return [
        (level, wi * half + row, wj * half + column)
        for wi in range(rows // half) for wj in range(columns // half)
        for level in range(levels) for row in range(half) for column in range(half)
    ]


def box(levels, rows, columns):
    return [(l, r, c) for l in range(levels) for r in rows for c in columns]


def turned_box(levels, rows, columns):
    return [(l, r, c) for l in range(levels) for c in columns for r in rows]


def padded(cells, step=16):
    return cells + [None] * (-len(cells) % step)


def picks(wanted, held):
    spot = {cell: i for i, cell in enumerate(held) if cell is not None}
    table = np.zeros((len(wanted), len(held)), np.float32)
    for i, cell in enumerate(wanted):
        if cell is not None:
            table[i, spot[cell]] = 1.0
    return jnp.asarray(table, BF16)


class Strips:
    def __init__(self, levels, rows, columns, width, cut):
        self.side = (box(levels, range(width, 2 * width), range(width))
                     + box(levels, range(2 * width, rows), range(width)))
        self.above = box(levels, range(width), range(width, columns))
        self.corner = box(levels, range(width), range(width))
        if not cut:
            self.side = box(levels, range(width, rows), range(width))

    @staticmethod
    def sent(cells, down, across):
        return [None if c is None else (c[0], c[1] + down, c[2] + across) for c in cells]


def head_masks():
    head = lax.broadcasted_iota(jnp.int32, (LANES, LANES), 1) // (LANES // 4)
    return [jnp.where(head == h, 1.0, 0.0).astype(BF16) for h in range(4)]


def region_bias(places, active):
    step = 2 * (WIN // 2)
    one = (lax.broadcasted_iota(jnp.int32, (places, places), 0) // step) % 2
    other = (lax.broadcasted_iota(jnp.int32, (places, places), 1) // step) % 2
    return jnp.where((one != other) & active, -1e30, 0.0)


def score_scale(channels):
    return float((channels // HEADS) ** -0.5 * np.log2(np.e))


def aligned(start, size, step=None):
    return pl.ds(pl.multiple_of(start, step or size), size)


def pack_kernel(tokens, merged_grad, pick_cells, pick_groups, side, above, corner):
    cells = dot(pick_cells[...], tokens[...]).astype(BF16)
    groups = dot(pick_groups[...], merged_grad[...]).astype(BF16)
    at, at_group = 0, 0
    for out, (count, extra) in zip((side, above, corner), strip_rows(pick_cells, pick_groups)):
        out[:count] = cells[at:at + count]
        out[count:] = groups[at_group:at_group + extra]
        at, at_group = at + count, at_group + extra


def strip_rows(pick_cells, pick_groups):
    levels = 2
    rows, columns = strip_rows.extent
    cells = [levels * (rows - SHIFT) * SHIFT, levels * SHIFT * (columns - SHIFT), levels * SHIFT * SHIFT]
    groups = [n // 4 + (-(n // 4)) % 16 for n in cells]
    return list(zip(cells, groups))


def forward_kernel(
    edge, owner, tokens, merged_grad, side, above, corner, order, group, rowmap,
    wqkv_h, wout_h, wm_h,
    normed_h, normt_h, proj_h, dmr_h, dmm_h, grad_h, rstd, merged, out_mine, out_theirs,
    wqkv, wout, wm, source, xw, normed, normt, proj, mixture, inverse, subs, dsubs, grad,
    dmr, dmm, turned, in_sem, out_sem,
):
    count, channels = xw.shape
    places = 2 * WIN * WIN
    windows = count // places
    per_row = windows // 2
    quarter = places // 4
    groups = count // 4
    devices = owner.shape[0]
    block = channels // devices

    loads = [
        pltpu.make_async_copy(src, dst, in_sem.at[i])
        for i, (src, dst) in enumerate([(wqkv_h, wqkv), (wout_h, wout), (wm_h, wm)])
    ]
    for load in loads:
        load.start()
    stores = [
        pltpu.make_async_copy(src, dst, out_sem.at[i])
        for i, (src, dst) in enumerate(
            [(normed, normed_h), (proj, proj_h), (normt, normt_h),
             (grad, grad_h), (dmr, dmr_h), (dmm, dmm_h)]
        )
    ]

    (n_side, g_side), (n_above, g_above), (n_corner, g_corner) = strip_rows(None, None)
    half = count // 2
    line = half // (2 * WIN)
    cut = SHIFT * line
    side_cut = 2 * SHIFT * SHIFT
    blocks = [
        [tokens[:cut], tokens[half:half + cut], side[:side_cut], above[:n_above], corner[:n_corner]],
        [tokens[cut:cut + WIN * line], tokens[half + cut:half + cut + WIN * line], side[side_cut:n_side]],
    ]
    for wi in range(2):
        at = 0
        for piece in blocks[wi]:
            source[wi, at:at + piece.shape[0]] = piece
            at += piece.shape[0]
        if at < source.shape[1]:
            source[wi, at:] = jnp.zeros((source.shape[1] - at, channels), BF16)

    @pl.loop(0, windows)
    def _(w):
        rows = aligned(w * places, places)
        x = dot(order[rows], source[w // per_row])
        xw[rows] = x.astype(BF16)
        center = jnp.mean(x, axis=1, keepdims=True)
        moved = x - center
        scale = lax.rsqrt(jnp.mean(moved * moved, axis=1, keepdims=True) + EPSILON)
        rstd[rows] = jnp.broadcast_to(scale, (places, LANES))
        normed[rows] = (moved * scale).astype(BF16)

    stores[0].start()
    loads[0].wait()

    @pl.loop(0, wqkv.shape[1] // TILE)
    def _(n):
        columns = aligned(n * TILE, TILE)
        proj[:, columns] = dot(normed[...], wqkv[:, columns]).astype(BF16)

    stores[1].start()

    masks = head_masks()
    factor = score_scale(channels)

    @pl.loop(0, windows)
    def _(w):
        rows = aligned(w * places, places)
        bias = region_bias(places, (edge[0] == 1) & (w < per_row))
        for g in range(channels // LANES):
            lanes = pl.ds(g * LANES, LANES)
            q = proj[rows, lanes]
            k = proj[rows, pl.ds(channels + g * LANES, LANES)]
            v = proj[rows, pl.ds(2 * channels + g * LANES, LANES)]
            scores = dot(q, jnp.concatenate([k * m for m in masks], axis=0), NT)
            parts = []
            for h in range(4):
                part = scores[:, h * places:(h + 1) * places] * factor + bias
                part = part - jnp.max(part, axis=1, keepdims=True)
                parts.append(jnp.exp2(part).astype(BF16))
            values = jnp.concatenate(
                [jnp.concatenate([v * m, m], axis=1) for m in masks], axis=0
            )
            summed = dot(jnp.concatenate(parts, axis=1), values)
            inv = 1.0 / summed[:, LANES:]
            inverse[rows, lanes] = inv
            mixture[rows, lanes] = (summed[:, :LANES] * inv).astype(BF16)

    loads[1].wait()

    @pl.loop(0, channels // TILE)
    def _(n):
        columns = aligned(n * TILE, TILE)
        out = dot(mixture[...], wout[:, columns]) + xw[:, columns].astype(F32)
        out = out.astype(BF16)
        for w in range(windows):
            for s in range(4):
                at = w * places + s * quarter
                subs[s, w * quarter:(w + 1) * quarter, columns] = out[at:at + quarter]

    total = jnp.zeros((groups, 1), F32)
    for s in range(4):
        total += jnp.sum(subs[s].astype(F32), axis=1, keepdims=True)
    center = total / (4 * channels)
    total = jnp.zeros((groups, 1), F32)
    for s in range(4):
        moved = subs[s].astype(F32) - center
        total += jnp.sum(moved * moved, axis=1, keepdims=True)
    scale = lax.rsqrt(total / (4 * channels) + EPSILON)
    loads[2].wait()
    result = jnp.zeros((groups, wm.shape[1]), F32)
    for s in range(4):
        unit = ((subs[s].astype(F32) - center) * scale).astype(BF16)
        result += dot(unit, wm[s * channels:(s + 1) * channels])
    merged[...] = result.astype(BF16)

    held = jnp.concatenate(
        [merged_grad[...], side[n_side:], above[n_above:], corner[n_corner:]], axis=0
    )
    cotangent = dot(group[...], held).astype(BF16)
    mean_g = jnp.zeros((groups, 1), F32)
    mean_gx = jnp.zeros((groups, 1), F32)
    for s in range(4):
        d = dot(cotangent, wm[s * channels:(s + 1) * channels], NT).astype(BF16)
        dsubs[s] = d
        d = d.astype(F32)
        mean_g += jnp.sum(d, axis=1, keepdims=True)
        mean_gx += jnp.sum(d * ((subs[s].astype(F32) - center) * scale), axis=1, keepdims=True)
    mean_g = mean_g / (4 * channels)
    mean_gx = mean_gx / (4 * channels)
    for s in range(4):
        unit = (subs[s].astype(F32) - center) * scale
        d = (scale * (dsubs[s].astype(F32) - mean_g - unit * mean_gx)).astype(BF16)
        for w in range(windows):
            at = w * places + s * quarter
            grad[at:at + quarter] = d[w * quarter:(w + 1) * quarter]
    stores[3].start()

    @pl.loop(0, channels // TILE)
    def _(n):
        columns = aligned(n * TILE, TILE)
        d = dot(grad[...], wout[columns], NT).astype(BF16).astype(F32)
        d = d * inverse[:, columns]
        dmr[:, columns] = d.astype(BF16)
        dmm[:, columns] = (-d * mixture[:, columns].astype(F32)).astype(BF16)

    stores[4].start()
    stores[5].start()

    def turn(field, out):
        if block % 16:
            @pl.loop(0, channels // TILE)
            def _(n):
                rows = aligned(n * TILE, TILE)
                spot = lax.broadcasted_iota(jnp.int32, (TILE, channels), 1)
                pick = jnp.where(spot == rowmap[rows], 1.0, 0.0).astype(BF16)
                out[rows] = dot(pick, field[...], NT).astype(BF16)
        else:
            @pl.loop(0, channels // TILE)
            def _(n):
                rows = aligned(n * TILE, TILE)
                turned[rows] = field[:, rows].T

            for d in range(devices):
                out[d * block:(d + 1) * block] = turned[aligned(owner[d] * block, block)]

    turn(normed, normt)
    stores[2].start()
    mixt = wqkv.at[:, :count]
    turn(mixture, mixt)
    part = channels // 2

    @pl.loop(0, channels // TILE)
    def _(n):
        columns = aligned(n * TILE, TILE)
        out_mine[:, columns] = dot(mixt[:part], grad[:, columns]).astype(BF16)
        out_theirs[:, columns] = dot(mixt[part:], grad[:, columns]).astype(BF16)

    for store in stores:
        store.wait()


def backward_kernel(index, waits, summing, *refs):
    refs = refs[waits:]
    edge, proj_h, dmr_h, dmm_h, normt_h = refs[:5]
    if summing:
        before_h, pgrad_h, mine_h, theirs_h, held, pgrad, normt, mine, theirs = refs[5:14]
        in_sem, sem, out_sem = refs[14:]
    else:
        pgrad_h, held, pgrad, in_sem, sem, out_sem = refs[5:]
    _, count, width = held.shape
    channels = dmr_h.shape[1]
    places = 2 * WIN * WIN
    windows = count // places
    per_row = windows // 2
    masks = head_masks()
    factor = score_scale(channels)
    plain = (channels // HEADS) ** -0.5
    first = 3 * width if summing else 0

    def loads(w):
        rows = aligned(w * places, places)
        for i in range(5):
            field, start = (proj_h, i * channels) if i < 3 else ((dmr_h, dmm_h)[i - 3], 0)
            columns = pl.ds(start + index * width, width)
            yield pltpu.make_async_copy(field.at[rows, columns], held.at[i, rows], in_sem.at[w, i])

    for w in range(windows):
        for load in loads(w):
            load.start()
    if summing:
        extra = [
            pltpu.make_async_copy(normt_h, normt, sem.at[0]),
            pltpu.make_async_copy(before_h, pgrad.at[:, pl.ds(0, first)], sem.at[1]),
        ]
        for load in extra:
            load.start()

    @pl.loop(0, windows)
    def _(w):
        for load in loads(w):
            load.wait()
        rows = aligned(w * places, places)
        bias = region_bias(places, (edge[0] == 1) & (w < per_row))
        for g in range(width // LANES):
            lanes = pl.ds(g * LANES, LANES)
            q, k, v, dm, dd = (held[i, rows, lanes] for i in range(5))
            keys = jnp.concatenate([k * m for m in masks], axis=0)
            scores = dot(keys, q, NT)
            values = jnp.concatenate(
                [jnp.concatenate([v * m, m], axis=1) for m in masks], axis=0
            )
            slope = dot(values, jnp.concatenate([dm, dd], axis=1), NT)
            weights, slopes = [], []
            for h in range(4):
                block = slice(h * places, (h + 1) * places)
                part = scores[block] * factor + bias
                part = jnp.exp2(part - jnp.max(part, axis=0, keepdims=True))
                weights.append(part.astype(BF16))
                slopes.append((part * slope[block]).astype(BF16))
            dv = dot(
                jnp.concatenate(weights, axis=1),
                jnp.concatenate([dm * m for m in masks], axis=0),
            )
            dk = dot(
                jnp.concatenate(slopes, axis=1),
                jnp.concatenate([q * m for m in masks], axis=0),
            )
            dq = dot(jnp.concatenate(slopes, axis=0), keys, TN)
            at = first + g * LANES
            pgrad[rows, pl.ds(at, LANES)] = (dq * plain).astype(BF16)
            pgrad[rows, pl.ds(at + width, LANES)] = (dk * plain).astype(BF16)
            pgrad[rows, pl.ds(at + 2 * width, LANES)] = dv.astype(BF16)

    stores = [pltpu.make_async_copy(pgrad.at[:, pl.ds(first, 3 * width)], pgrad_h, out_sem.at[0])]
    stores[0].start()
    if summing:
        for load in extra:
            load.wait()
        half = channels // 2
        for n in range(2 * first // TILE):
            columns = pl.ds(n * TILE, TILE)
            right = pgrad[:, columns]
            mine[:, columns] = dot(normt[:half], right).astype(BF16)
            theirs[:, columns] = dot(normt[half:], right).astype(BF16)
        stores += [
            pltpu.make_async_copy(mine, mine_h, out_sem.at[1]),
            pltpu.make_async_copy(theirs, theirs_h, out_sem.at[2]),
        ]
        stores[1].start()
        stores[2].start()
    for store in stores:
        store.wait()


def projection_back(pgrads, wqkv_h, pgrad, wqkv, sem, start):
    width = pgrads[0].shape[1] // 3
    channels = wqkv_h.shape[1] // 3
    rows = pl.ds(start, wqkv.shape[0])
    loads = []
    for c, field in enumerate(pgrads):
        at = 3 * width * c
        loads.append(pltpu.make_async_copy(field, pgrad.at[:, pl.ds(at, 3 * width)], sem.at[c, 3]))
        for i in range(3):
            loads.append(pltpu.make_async_copy(
                wqkv_h.at[rows, pl.ds(i * channels + c * width, width)],
                wqkv.at[:, pl.ds(at + i * width, width)], sem.at[c, i],
            ))
    for load in loads:
        load.start()
    return loads


def input_first_kernel(waits, *refs):
    pgrads = refs[waits:waits + PARTS]
    wqkv_h, ngrad, pgrad, wqkv, sem = refs[waits + PARTS:]
    for load in projection_back(pgrads, wqkv_h, pgrad, wqkv, sem, 0):
        load.wait()
    for n in range(wqkv.shape[0] // TILE):
        rows = slice(n * TILE, (n + 1) * TILE)
        ngrad[:, rows] = dot(pgrad[...], wqkv[rows], NT).astype(BF16)


def input_last_kernel(waits, *refs):
    pgrads = refs[waits:waits + PARTS]
    (wqkv_h, nfirst_h, normed_h, rstd_h, grad_h, merged, pick_first, pick_last, pick_groups,
     full, side, below, corner,
     pgrad, wqkv, ngrad, normed, rstd, grad, sem, more_sem) = refs[waits + PARTS:]
    count, channels = ngrad.shape
    half = channels // 2
    loads = projection_back(pgrads, wqkv_h, pgrad, wqkv, sem, half)
    more = [
        pltpu.make_async_copy(src, dst, more_sem.at[i])
        for i, (src, dst) in enumerate(
            [(nfirst_h, ngrad.at[:, pl.ds(0, half)]), (normed_h, normed), (rstd_h, rstd), (grad_h, grad)]
        )
    ]
    for load in more:
        load.start()
    for load in loads:
        load.wait()
    for n in range(half // TILE):
        rows = slice(n * TILE, (n + 1) * TILE)
        ngrad[:, half + n * TILE:half + (n + 1) * TILE] = dot(
            pgrad[...], wqkv[rows], NT
        ).astype(BF16)
    for load in more:
        load.wait()
    places = 2 * WIN * WIN

    @pl.loop(0, count // places)
    def _(w):
        rows = aligned(w * places, places)
        d = ngrad[rows].astype(F32)
        unit = normed[rows].astype(F32)
        mean_d = jnp.mean(d, axis=1, keepdims=True)
        mean_dx = jnp.mean(d * unit, axis=1, keepdims=True)
        part = rstd[rows, :1] * (d - mean_d - unit * mean_dx)
        full[rows] = (part.astype(BF16).astype(F32) + grad[rows].astype(F32)).astype(BF16)

    (n_side, g_side), (n_above, g_above), (n_corner, g_corner) = strip_rows(None, None)
    side_cut = 2 * SHIFT * SHIFT
    first = dot(pick_first[...], full[:count // 2]).astype(BF16)
    last = dot(pick_last[...], full[count // 2:]).astype(BF16)
    groups = dot(pick_groups[...], merged[...]).astype(BF16)
    side[:side_cut] = first[:side_cut]
    side[side_cut:n_side] = last
    below[:n_above] = first[side_cut:side_cut + n_above]
    corner[:n_corner] = first[side_cut + n_above:]
    side[n_side:] = groups[:g_side]
    below[n_above:] = groups[g_side:g_side + g_above]
    corner[n_corner:] = groups[g_side + g_above:]


def unpack_kernel(full, merged, side, below, corner, pick_top, pick_middle, pick_bottom,
                  pick_groups, tokens_out, merged_out):
    count = full.shape[0]
    half = count // 2
    (n_side, _), (n_above, _), (n_corner, _) = strip_rows(None, None)
    side_cut = 2 * SHIFT * SHIFT
    line = half // (2 * WIN)
    pieces = [
        (pick_top, [full[:half], side[:side_cut]]),
        (pick_middle, [full[half:], side[side_cut:n_side]]),
        (pick_bottom, [below[:n_above], corner[:n_corner]]),
    ]
    at = 0
    for pick, held in pieces:
        rows = pick.shape[0] // 2
        out = dot(pick[...], jnp.concatenate(held, axis=0)).astype(BF16)
        for level in range(2):
            start = level * half + at
            tokens_out[start:start + rows] = out[level * rows:(level + 1) * rows]
        at += rows
    held = [merged[...], side[n_side:], below[n_above:], corner[n_corner:]]
    merged_out[...] = dot(pick_groups[...], jnp.concatenate(held, axis=0)).astype(BF16)


def sent(block, sizes, lat_step, lon_step):
    n_lat, n_lon = sizes
    route = [
        (a * n_lon + b, (a + lat_step) % n_lat * n_lon + (b + lon_step) % n_lon)
        for a in range(n_lat) for b in range(n_lon)
    ]
    return lax.ppermute(block, ("lat", "lon"), route)


def sent_strips(strips, sizes, step):
    side, lines, corner = strips
    return [sent(side, sizes, 0, step), sent(lines, sizes, step, 0), sent(corner, sizes, step, step)]


def device_rows(channels, sizes):
    n_lat, n_lon = sizes
    devices = n_lat * n_lon
    rows = channels // devices
    place = np.arange(devices)
    lon = 2 * (place // n_lat % (n_lon // 2)) + place // (devices // 2)
    lat = place % n_lat
    owner = (
        jnp.bitwise_xor(lax.axis_index("lat").astype(jnp.int32), jnp.asarray(lat, jnp.int32)) * n_lon
        + jnp.bitwise_xor(lax.axis_index("lon").astype(jnp.int32), jnp.asarray(lon, jnp.int32))
    )
    rowmap = owner[:, None] * rows + jnp.arange(rows, dtype=jnp.int32)[None, :]
    return owner, rowmap.reshape(channels, 1)


def exchange(block, sizes, lat_bits, lon_bits):
    n_lat, n_lon = sizes
    route = [
        (a * n_lon + b, (a ^ lat_bits) * n_lon + (b ^ lon_bits))
        for a in range(n_lat) for b in range(n_lon)
    ]
    return lax.ppermute(block, ("lat", "lon"), route)


def core_step(theirs, sizes):
    return exchange(theirs, sizes, 0, 1)


def layer_blocks(mine, arrived, sizes):
    blocks = sizes[1] // 2
    rows = mine.shape[0] // blocks
    total = [
        (mine[i * rows:(i + 1) * rows].astype(F32) + arrived[i * rows:(i + 1) * rows].astype(F32))
        for i in range(blocks)
    ]
    return [total[0]] + [t.astype(BF16) for t in total[1:]]


def layer_step(blocks, sizes):
    return [exchange(b, sizes, 0, 2 * i) for i, b in enumerate(blocks) if i]


def column_blocks(kept, arrived, sizes):
    total = kept
    for block in arrived:
        total = total + block.astype(F32)
    rows = total.shape[0] // sizes[0]
    blocks = [total[i * rows:(i + 1) * rows] for i in range(sizes[0])]
    return [blocks[0]] + [b.astype(BF16) for b in blocks[1:]]


def column_step(blocks, sizes):
    return [exchange(b, sizes, i, 0) for i, b in enumerate(blocks) if i]


def finished(kept, arrived):
    for block in arrived:
        kept = kept + block.astype(F32)
    return kept


def shards(sizes, tokens, qkv_weight, out_weight, merge_weight, merged_grad):
    levels, lat_rows, lon_cols, channels = tokens.shape
    merged_width = merge_weight.shape[1]
    count = levels * lat_rows * lon_cols
    groups = count // 4
    half = channels // 2
    strip_rows.extent = (lat_rows, lon_cols)
    vmem = pl.BlockSpec(memory_space=pltpu.VMEM)
    smem = pl.BlockSpec(memory_space=pltpu.SMEM)
    hbm = pl.BlockSpec(memory_space=pl.ANY)

    def shape(*extent, dtype=BF16):
        return jax.ShapeDtypeStruct(extent, dtype)

    def settings(limit, flops, moved):
        return dict(
            compiler_params=pltpu.CompilerParams(vmem_limit_bytes=limit * MIB),
            cost_estimate=pl.CostEstimate(
                flops=int(flops * count * channels * channels), bytes_accessed=int(moved * MIB),
                transcendentals=0,
            ),
        )

    g_rows, g_cols = lat_rows // 2, lon_cols // 2
    cells = window_cells(levels, lat_rows, lon_cols)
    grps = window_groups(levels, g_rows, g_cols)
    cs = Strips(levels, lat_rows, lon_cols, SHIFT, True)
    gs = Strips(levels, g_rows, g_cols, HALF, False)
    g_strips = [padded(gs.side), padded(gs.above), padded(gs.corner)]
    to = ((0, lon_cols), (lat_rows, 0), (lat_rows, lon_cols))
    g_to = ((0, g_cols), (g_rows, 0), (g_rows, g_cols))
    own_rows = range(SHIFT, SHIFT + lat_rows)
    own_cols = range(SHIFT, SHIFT + lon_cols)
    own = box(levels, own_rows, own_cols)
    g_own = turned_box(levels, range(HALF, HALF + g_rows), range(HALF, HALF + g_cols))
    half_cells = count // 2
    side_cut = levels * SHIFT * SHIFT
    sent_cells = sum((Strips.sent(s, *t) for s, t in zip((cs.side, cs.above, cs.corner), to)), [])
    sent_groups = sum((Strips.sent(s, *t) for s, t in zip(g_strips, g_to)), [])
    held_top = box(levels, range(SHIFT, 2 * SHIFT), own_cols) + cs.side[:side_cut] + cs.above + cs.corner
    held_low = box(levels, range(2 * SHIFT, lat_rows), own_cols) + cs.side[side_cut:]
    depth = max(len(held_top), len(held_low))
    depth += -depth % 16
    held_top += [None] * (depth - len(held_top))
    held_low += [None] * (depth - len(held_low))

    tokens_flat = tokens.reshape(count, channels)
    merged_grad_flat = merged_grad.transpose(0, 2, 1, 3).reshape(groups, merged_width)
    extents = [(n + g, channels) for n, g in strip_rows(None, None)]
    strips = pl.pallas_call(
        pack_kernel,
        out_shape=[shape(*e) for e in extents],
        in_specs=[vmem] * 4, out_specs=[vmem] * 3,
        name="pack_strips", **settings(24, 1, 3),
    )(tokens_flat, merged_grad_flat, picks(sent_cells, own), picks(sent_groups, g_own))
    strips = sent_strips(strips, sizes, 1)

    order = jnp.concatenate([picks(cells[:half_cells], held_top), picks(cells[half_cells:], held_low)])
    group = picks(grps, g_own + sum(g_strips, []))
    edge = (lax.axis_index("lat") == 0).astype(jnp.int32).reshape(1)
    owner, rowmap = device_rows(channels, sizes)

    wide = shape(count, channels)
    normed, normt, proj, dmr, dmm, grad, rstd, merged, out_mine, out_theirs = pl.pallas_call(
        forward_kernel,
        out_shape=[
            wide, shape(channels, count), shape(count, 3 * channels), wide, wide, wide,
            shape(count, LANES, dtype=F32), shape(groups, merged_width),
            shape(half, channels), shape(half, channels),
        ],
        in_specs=[smem, smem] + [vmem] * 8 + [hbm] * 3,
        out_specs=[hbm] * 6 + [vmem] * 4,
        scratch_shapes=[
            pltpu.VMEM(qkv_weight.shape, BF16),
            pltpu.VMEM(out_weight.shape, BF16),
            pltpu.VMEM(merge_weight.shape, BF16),
            pltpu.VMEM((2, depth, channels), BF16),
            pltpu.VMEM((count, channels), BF16),
            pltpu.VMEM((count, channels), BF16),
            pltpu.VMEM((channels, count), BF16),
            pltpu.VMEM((count, 3 * channels), BF16),
            pltpu.VMEM((count, channels), BF16),
            pltpu.VMEM((count, channels), F32),
            pltpu.VMEM((4, groups, channels), BF16),
            pltpu.VMEM((4, groups, channels), BF16),
            pltpu.VMEM((count, channels), BF16),
            pltpu.VMEM((count, channels), BF16),
            pltpu.VMEM((count, channels), BF16),
            pltpu.VMEM((channels, count), BF16),
            pltpu.SemaphoreType.DMA((3,)),
            pltpu.SemaphoreType.DMA((6,)),
        ],
        name="block_forward", **settings(58, 24, 34),
    )(edge, owner, tokens_flat, merged_grad_flat, *strips, order, group, rowmap,
      qkv_weight, out_weight, merge_weight)

    width = channels // PARTS

    def backward(index, before, after):
        summing = before is not None
        outs = [shape(count, 3 * width)]
        scratch = [
            pltpu.VMEM((5, count, width), BF16),
            pltpu.VMEM((count, (6 if summing else 3) * width), BF16),
        ]
        if summing:
            outs += [shape(half, 6 * width)] * 2
            scratch += [
                pltpu.VMEM((channels, count), BF16),
                pltpu.VMEM((half, 6 * width), BF16),
                pltpu.VMEM((half, 6 * width), BF16),
            ]
        scratch += [
            pltpu.SemaphoreType.DMA((count // (2 * WIN * WIN), 5)),
            pltpu.SemaphoreType.DMA((2,)),
            pltpu.SemaphoreType.DMA((3,)),
        ]
        operands = [edge, proj, dmr, dmm, normt] + ([before] if summing else [])
        return pl.pallas_call(
            functools.partial(backward_kernel, index, len(after), summing),
            out_shape=outs,
            in_specs=[hbm] * len(after) + [smem] + [hbm] * (len(operands) - 1),
            out_specs=[hbm] * len(outs),
            scratch_shapes=scratch,
            name="attention_backward", **settings(40, 6 if summing else 3, 6),
        )(*after, *operands)

    arrived = core_step(out_theirs, sizes)
    (pg0,) = backward(0, None, [])
    out_layer = layer_blocks(out_mine, arrived, sizes)
    arrived = layer_step(out_layer, sizes)
    pg1, mine1, theirs1 = backward(1, pg0, out_layer[1:])
    out_column = column_blocks(out_layer[0], arrived, sizes)
    out_arrived = column_step(out_column, sizes)
    arrived = core_step(theirs1, sizes)
    (pg2,) = backward(2, None, out_column[1:])
    layer1 = layer_blocks(mine1, arrived, sizes)
    arrived1 = layer_step(layer1, sizes)
    pg3, mine2, theirs2 = backward(3, pg2, layer1[1:])
    arrived2 = core_step(theirs2, sizes)
    pgrads = [pg0, pg1, pg2, pg3]

    in_scratch = [
        pltpu.VMEM((count, 3 * channels), BF16),
        pltpu.VMEM((half, 3 * channels), BF16),
    ]
    in_sems = pltpu.SemaphoreType.DMA((PARTS, 4))
    nfirst = pl.pallas_call(
        functools.partial(input_first_kernel, 0),
        out_shape=shape(count, half),
        in_specs=[hbm] * (PARTS + 1), out_specs=vmem,
        scratch_shapes=in_scratch + [in_sems],
        name="input_first", **settings(40, 3, 8),
    )(*pgrads, qkv_weight)
    column1 = column_blocks(layer1[0], arrived1, sizes)
    column_arrived1 = column_step(column1, sizes)
    layer2 = layer_blocks(mine2, arrived2, sizes)
    arrived2 = layer_step(layer2, sizes)
    after = layer2[1:] + column1[1:]

    first_picks = picks(cs.side[:side_cut] + cs.above + cs.corner, cells[:half_cells])
    last_picks = picks(cs.side[side_cut:], cells[half_cells:])
    full, *strips = pl.pallas_call(
        functools.partial(input_last_kernel, len(after)),
        out_shape=[wide] + [shape(*e) for e in extents],
        in_specs=[hbm] * (len(after) + PARTS + 5) + [vmem] * 4, out_specs=[vmem] * 4,
        scratch_shapes=in_scratch + [
            pltpu.VMEM((count, channels), BF16),
            pltpu.VMEM((count, channels), BF16),
            pltpu.VMEM((count, LANES), F32),
            pltpu.VMEM((count, channels), BF16),
            in_sems,
            pltpu.SemaphoreType.DMA((4,)),
        ],
        name="input_last", **settings(48, 4, 12),
    )(*after, *pgrads, qkv_weight, nfirst, normed, rstd, grad, merged,
      first_picks, last_picks, picks(sum(g_strips, []), grps))
    strips = sent_strips(strips, sizes, -1)

    column2 = column_blocks(layer2[0], arrived2, sizes)
    column_arrived2 = column_step(column2, sizes)

    got = [Strips.sent(s, *t) for s, t in zip((cs.side, cs.above, cs.corner), to)]
    g_got = sum((Strips.sent(s, *t) for s, t in zip(g_strips, g_to)), [])
    tokens_grad, merged = pl.pallas_call(
        unpack_kernel,
        out_shape=[wide, shape(groups, merged_width)],
        in_specs=[vmem] * 9, out_specs=[vmem] * 2,
        name="unpack_strips", **settings(24, 1, 5),
    )(
        full, merged, *strips,
        picks(box(levels, range(SHIFT, 2 * SHIFT), own_cols), cells[:half_cells] + got[0][:side_cut]),
        picks(box(levels, range(2 * SHIFT, lat_rows), own_cols), cells[half_cells:] + got[0][side_cut:]),
        picks(box(levels, range(lat_rows, lat_rows + SHIFT), own_cols), got[1] + got[2]),
        picks(g_own, grps + g_got),
    )
    merged = merged.reshape(levels, g_cols, g_rows, merged_width).transpose(0, 2, 1, 3)

    out_weight_grad = finished(out_column[0], out_arrived)
    parts = [finished(column1[0], column_arrived1), finished(column2[0], column_arrived2)]
    pieces = [
        part[:, (3 * i + kind) * width:(3 * i + kind + 1) * width]
        for kind in range(3) for part in parts for i in range(2)
    ]
    qkv_weight_grad = jnp.concatenate(pieces, axis=1)
    return merged, tokens_grad.reshape(tokens.shape), qkv_weight_grad, out_weight_grad


def solution(mesh):
    sizes = (mesh.shape["lat"], mesh.shape["lon"])
    in_specs = (P(None, "lat", "lon", None), P(), P(), P(), P(None, "lat", "lon", None))
    out_specs = (
        P(None, "lat", "lon", None),
        P(None, "lat", "lon", None),
        P(("lat", "lon"), None),
        P(("lat", "lon"), None),
    )
    return jax.shard_map(
        functools.partial(shards, sizes),
        mesh=mesh, in_specs=in_specs, out_specs=out_specs, check_vma=False,
    )
```

```python
import functools

import jax
import jax.numpy as jnp
import numpy as np
from jax import lax
from jax.experimental import pallas as pl
from jax.experimental.pallas import tpu as pltpu
from jax.sharding import PartitionSpec as P

HEADS = 32
WIN = 8
SHIFT = 4
LANES = 128
HALF = SHIFT // 2
TILE = 256
EPSILON = 1e-05
MIB = 1 << 20
PARTS = 4

NN = (((1,), (0,)), ((), ()))
NT = (((1,), (1,)), ((), ()))
TN = (((0,), (0,)), ((), ()))
BF16 = jnp.bfloat16
F32 = jnp.float32


def dot(a, b, dims=NN):
    return lax.dot_general(a, b, dims, preferred_element_type=F32)


def window_cells(levels, rows, columns):
    half = WIN // 2
    return [
        (level, wi * WIN + 2 * row + sub % 2, wj * WIN + 2 * column + sub // 2)
        for wi in range(rows // WIN) for wj in range(columns // WIN) for sub in range(4)
        for level in range(levels) for row in range(half) for column in range(half)
    ]


def window_groups(levels, rows, columns):
    half = WIN // 2
    return [
        (level, wi * half + row, wj * half + column)
        for wi in range(rows // half) for wj in range(columns // half)
        for level in range(levels) for row in range(half) for column in range(half)
    ]


def box(levels, rows, columns):
    return [(l, r, c) for l in range(levels) for r in rows for c in columns]


def turned_box(levels, rows, columns):
    return [(l, r, c) for l in range(levels) for c in columns for r in rows]


def padded(cells, step=16):
    return cells + [None] * (-len(cells) % step)


def picks(wanted, held):
    spot = {cell: i for i, cell in enumerate(held) if cell is not None}
    table = np.zeros((len(wanted), len(held)), np.float32)
    for i, cell in enumerate(wanted):
        if cell is not None:
            table[i, spot[cell]] = 1.0
    return jnp.asarray(table, BF16)


class Strips:
    def __init__(self, levels, rows, columns, width, cut):
        self.side = (box(levels, range(width, 2 * width), range(width))
                     + box(levels, range(2 * width, rows), range(width)))
        self.above = box(levels, range(width), range(width, columns))
        self.corner = box(levels, range(width), range(width))
        if not cut:
            self.side = box(levels, range(width, rows), range(width))

    @staticmethod
    def sent(cells, down, across):
        return [None if c is None else (c[0], c[1] + down, c[2] + across) for c in cells]


def head_masks():
    head = lax.broadcasted_iota(jnp.int32, (LANES, LANES), 1) // (LANES // 4)
    return [jnp.where(head == h, 1.0, 0.0).astype(BF16) for h in range(4)]


def region_bias(places, active):
    step = 2 * (WIN // 2)
    one = (lax.broadcasted_iota(jnp.int32, (places, places), 0) // step) % 2
    other = (lax.broadcasted_iota(jnp.int32, (places, places), 1) // step) % 2
    return jnp.where((one != other) & active, -1e30, 0.0)


def score_scale(channels):
    return float((channels // HEADS) ** -0.5 * np.log2(np.e))


def aligned(start, size, step=None):
    return pl.ds(pl.multiple_of(start, step or size), size)


def pack_kernel(tokens, merged_grad, pick_cells, pick_groups, side, above, corner):
    cells = dot(pick_cells[...], tokens[...]).astype(BF16)
    groups = dot(pick_groups[...], merged_grad[...]).astype(BF16)
    at, at_group = 0, 0
    for out, (count, extra) in zip((side, above, corner), strip_rows(pick_cells, pick_groups)):
        out[:count] = cells[at:at + count]
        out[count:] = groups[at_group:at_group + extra]
        at, at_group = at + count, at_group + extra


def strip_rows(pick_cells, pick_groups):
    levels = 2
    rows, columns = strip_rows.extent
    cells = [levels * (rows - SHIFT) * SHIFT, levels * SHIFT * (columns - SHIFT), levels * SHIFT * SHIFT]
    groups = [n // 4 + (-(n // 4)) % 16 for n in cells]
    return list(zip(cells, groups))


def forward_kernel(
    edge, owner, tokens, merged_grad, side, above, corner, order, group, rowmap,
    wqkv_h, wout_h, wm_h,
    normed_h, normt_h, proj_h, dmr_h, dmm_h, grad_h, rstd, merged, out_mine, out_theirs,
    wqkv, wout, wm, source, xw, normed, normt, proj, mixture, inverse, subs, dsubs, cotangent,
    grad, dmr, dmm, turned, in_sem, out_sem,
):
    count, channels = xw.shape
    places = 2 * WIN * WIN
    windows = count // places
    per_row = windows // 2
    quarter = places // 4
    groups = count // 4
    devices = owner.shape[0]
    block = channels // devices

    loads = [
        pltpu.make_async_copy(src, dst, in_sem.at[i])
        for i, (src, dst) in enumerate([(wqkv_h, wqkv), (wout_h, wout), (wm_h, wm)])
    ]
    for load in loads:
        load.start()
    stores = [
        pltpu.make_async_copy(src, dst, out_sem.at[i])
        for i, (src, dst) in enumerate(
            [(normed, normed_h), (proj, proj_h), (normt, normt_h),
             (grad, grad_h), (dmr, dmr_h), (dmm, dmm_h)]
        )
    ]

    (n_side, g_side), (n_above, g_above), (n_corner, g_corner) = strip_rows(None, None)
    half = count // 2
    line = half // (2 * WIN)
    cut = SHIFT * line
    side_cut = 2 * SHIFT * SHIFT
    blocks = [
        [tokens[:cut], tokens[half:half + cut], side[:side_cut], above[:n_above], corner[:n_corner]],
        [tokens[cut:cut + WIN * line], tokens[half + cut:half + cut + WIN * line], side[side_cut:n_side]],
    ]
    for wi in range(2):
        at = 0
        for piece in blocks[wi]:
            source[wi, at:at + piece.shape[0]] = piece
            at += piece.shape[0]
        if at < source.shape[1]:
            source[wi, at:] = jnp.zeros((source.shape[1] - at, channels), BF16)

    @pl.loop(0, windows)
    def _(w):
        rows = aligned(w * places, places)
        x = dot(order[rows], source[w // per_row])
        xw[rows] = x.astype(BF16)
        center = jnp.mean(x, axis=1, keepdims=True)
        moved = x - center
        scale = lax.rsqrt(jnp.mean(moved * moved, axis=1, keepdims=True) + EPSILON)
        rstd[rows] = jnp.broadcast_to(scale, (places, LANES))
        normed[rows] = (moved * scale).astype(BF16)

    stores[0].start()
    loads[0].wait()

    @pl.loop(0, wqkv.shape[1] // TILE)
    def _(n):
        columns = aligned(n * TILE, TILE)
        proj[:, columns] = dot(normed[...], wqkv[:, columns]).astype(BF16)

    stores[1].start()

    masks = head_masks()
    factor = score_scale(channels)

    edge_bias = region_bias(places, edge[0] == 1)
    held = jnp.concatenate(
        [merged_grad[...], side[n_side:], above[n_above:], corner[n_corner:]], axis=0
    )
    cotangent[...] = dot(group[...], held).astype(BF16)
    loads[2].wait()
    steps = channels // LANES
    per_step = 4 * channels // TILE // steps

    @pl.loop(0, steps)
    def _(g):
        lanes = aligned(g * LANES, LANES)
        key_lanes = aligned(channels + g * LANES, LANES)
        value_lanes = aligned(2 * channels + g * LANES, LANES)
        for w in range(windows):
            rows = slice(w * places, (w + 1) * places)
            q, k, v = proj[rows, lanes], proj[rows, key_lanes], proj[rows, value_lanes]
            scores = dot(q, jnp.concatenate([k * m for m in masks], axis=0), NT)
            parts = []
            for h in range(4):
                part = scores[:, h * places:(h + 1) * places] * factor
                if w < per_row:
                    part = part + edge_bias
                part = part - jnp.max(part, axis=1, keepdims=True)
                parts.append(jnp.exp2(part).astype(BF16))
            values = jnp.concatenate(
                [jnp.concatenate([v * m, m], axis=1) for m in masks], axis=0
            )
            summed = dot(jnp.concatenate(parts, axis=1), values)
            inv = 1.0 / summed[:, LANES:]
            inverse[rows, lanes] = inv
            mixture[rows, lanes] = (summed[:, :LANES] * inv).astype(BF16)
        for i in range(per_step):
            at = aligned((g * per_step + i) * TILE, TILE)
            dsubs[:, at] = dot(cotangent[...], wm[at], NT).astype(BF16)

    loads[1].wait()

    @pl.loop(0, channels // TILE)
    def _(n):
        columns = aligned(n * TILE, TILE)
        out = dot(mixture[...], wout[:, columns]) + xw[:, columns].astype(F32)
        out = out.astype(BF16)
        for w in range(windows):
            for s in range(4):
                at = w * places + s * quarter
                subs[s, w * quarter:(w + 1) * quarter, columns] = out[at:at + quarter]

    total = jnp.zeros((groups, 1), F32)
    for s in range(4):
        total += jnp.sum(subs[s].astype(F32), axis=1, keepdims=True)
    center = total / (4 * channels)
    total = jnp.zeros((groups, 1), F32)
    for s in range(4):
        moved = subs[s].astype(F32) - center
        total += jnp.sum(moved * moved, axis=1, keepdims=True)
    scale = lax.rsqrt(total / (4 * channels) + EPSILON)
    result = jnp.zeros((groups, wm.shape[1]), F32)
    for s in range(4):
        unit = ((subs[s].astype(F32) - center) * scale).astype(BF16)
        result += dot(unit, wm[s * channels:(s + 1) * channels])
    merged[...] = result.astype(BF16)

    mean_g = jnp.zeros((groups, 1), F32)
    mean_gx = jnp.zeros((groups, 1), F32)
    for s in range(4):
        d = dsubs[:, s * channels:(s + 1) * channels].astype(F32)
        mean_g += jnp.sum(d, axis=1, keepdims=True)
        mean_gx += jnp.sum(d * ((subs[s].astype(F32) - center) * scale), axis=1, keepdims=True)
    mean_g = mean_g / (4 * channels)
    mean_gx = mean_gx / (4 * channels)
    for s in range(4):
        unit = (subs[s].astype(F32) - center) * scale
        d = dsubs[:, s * channels:(s + 1) * channels].astype(F32)
        d = (scale * (d - mean_g - unit * mean_gx)).astype(BF16)
        for w in range(windows):
            at = w * places + s * quarter
            grad[at:at + quarter] = d[w * quarter:(w + 1) * quarter]
    stores[3].start()

    @pl.loop(0, channels // TILE)
    def _(n):
        columns = aligned(n * TILE, TILE)
        d = dot(grad[...], wout[columns], NT).astype(BF16).astype(F32)
        d = d * inverse[:, columns]
        dmr[:, columns] = d.astype(BF16)
        dmm[:, columns] = (-d * mixture[:, columns].astype(F32)).astype(BF16)

    stores[4].start()
    stores[5].start()

    def turn(field, out):
        if block % 16:
            @pl.loop(0, channels // TILE)
            def _(n):
                rows = aligned(n * TILE, TILE)
                spot = lax.broadcasted_iota(jnp.int32, (TILE, channels), 1)
                pick = jnp.where(spot == rowmap[rows], 1.0, 0.0).astype(BF16)
                out[rows] = dot(pick, field[...], NT).astype(BF16)
        else:
            @pl.loop(0, channels // TILE)
            def _(n):
                rows = aligned(n * TILE, TILE)
                turned[rows] = field[:, rows].T

            for d in range(devices):
                out[d * block:(d + 1) * block] = turned[aligned(owner[d] * block, block)]

    turn(normed, normt)
    stores[2].start()
    mixt = wqkv.at[:, :count]
    turn(mixture, mixt)
    part = channels // 2

    @pl.loop(0, channels // TILE)
    def _(n):
        columns = aligned(n * TILE, TILE)
        out_mine[:, columns] = dot(mixt[:part], grad[:, columns]).astype(BF16)
        out_theirs[:, columns] = dot(mixt[part:], grad[:, columns]).astype(BF16)

    for store in stores:
        store.wait()


def backward_kernel(index, waits, summing, *refs):
    refs = refs[waits:]
    edge, proj_h, dmr_h, dmm_h, normt_h = refs[:5]
    if summing:
        before_h, pgrad_h, mine_h, theirs_h, held, pgrad, normt, mine, theirs = refs[5:14]
        in_sem, sem, out_sem = refs[14:]
    else:
        pgrad_h, held, pgrad, in_sem, sem, out_sem = refs[5:]
    _, count, width = held.shape
    channels = dmr_h.shape[1]
    places = 2 * WIN * WIN
    windows = count // places
    per_row = windows // 2
    masks = head_masks()
    factor = score_scale(channels)
    plain = (channels // HEADS) ** -0.5
    first = 3 * width if summing else 0

    def loads(w):
        rows = aligned(w * places, places)
        for i in range(5):
            field, start = (proj_h, i * channels) if i < 3 else ((dmr_h, dmm_h)[i - 3], 0)
            columns = pl.ds(start + index * width, width)
            yield pltpu.make_async_copy(field.at[rows, columns], held.at[i, rows], in_sem.at[w, i])

    for w in range(windows):
        for load in loads(w):
            load.start()
    if summing:
        extra = [
            pltpu.make_async_copy(normt_h, normt, sem.at[0]),
            pltpu.make_async_copy(before_h, pgrad.at[:, pl.ds(0, first)], sem.at[1]),
        ]
        for load in extra:
            load.start()

    @pl.loop(0, windows)
    def _(w):
        for load in loads(w):
            load.wait()
        rows = aligned(w * places, places)
        bias = region_bias(places, (edge[0] == 1) & (w < per_row))
        for g in range(width // LANES):
            lanes = pl.ds(g * LANES, LANES)
            q, k, v, dm, dd = (held[i, rows, lanes] for i in range(5))
            keys = jnp.concatenate([k * m for m in masks], axis=0)
            scores = dot(keys, q, NT)
            values = jnp.concatenate(
                [jnp.concatenate([v * m, m], axis=1) for m in masks], axis=0
            )
            slope = dot(values, jnp.concatenate([dm, dd], axis=1), NT)
            weights, slopes = [], []
            for h in range(4):
                block = slice(h * places, (h + 1) * places)
                part = scores[block] * factor + bias
                part = jnp.exp2(part - jnp.max(part, axis=0, keepdims=True))
                weights.append(part.astype(BF16))
                slopes.append((part * slope[block]).astype(BF16))
            dv = dot(
                jnp.concatenate(weights, axis=1),
                jnp.concatenate([dm * m for m in masks], axis=0),
            )
            dk = dot(
                jnp.concatenate(slopes, axis=1),
                jnp.concatenate([q * m for m in masks], axis=0),
            )
            dq = dot(jnp.concatenate(slopes, axis=0), keys, TN)
            at = first + g * LANES
            pgrad[rows, pl.ds(at, LANES)] = (dq * plain).astype(BF16)
            pgrad[rows, pl.ds(at + width, LANES)] = (dk * plain).astype(BF16)
            pgrad[rows, pl.ds(at + 2 * width, LANES)] = dv.astype(BF16)

    stores = [pltpu.make_async_copy(pgrad.at[:, pl.ds(first, 3 * width)], pgrad_h, out_sem.at[0])]
    stores[0].start()
    if summing:
        for load in extra:
            load.wait()
        half = channels // 2
        for n in range(2 * first // TILE):
            columns = pl.ds(n * TILE, TILE)
            right = pgrad[:, columns]
            mine[:, columns] = dot(normt[:half], right).astype(BF16)
            theirs[:, columns] = dot(normt[half:], right).astype(BF16)
        stores += [
            pltpu.make_async_copy(mine, mine_h, out_sem.at[1]),
            pltpu.make_async_copy(theirs, theirs_h, out_sem.at[2]),
        ]
        stores[1].start()
        stores[2].start()
    for store in stores:
        store.wait()


def projection_back(pgrads, wqkv_h, pgrad, wqkv, sem, start):
    width = pgrads[0].shape[1] // 3
    channels = wqkv_h.shape[1] // 3
    rows = pl.ds(start, wqkv.shape[0])
    loads = []
    for c, field in enumerate(pgrads):
        at = 3 * width * c
        loads.append(pltpu.make_async_copy(field, pgrad.at[:, pl.ds(at, 3 * width)], sem.at[c, 3]))
        for i in range(3):
            loads.append(pltpu.make_async_copy(
                wqkv_h.at[rows, pl.ds(i * channels + c * width, width)],
                wqkv.at[:, pl.ds(at + i * width, width)], sem.at[c, i],
            ))
    for load in loads:
        load.start()
    return loads


def input_first_kernel(waits, *refs):
    pgrads = refs[waits:waits + PARTS]
    wqkv_h, ngrad, pgrad, wqkv, sem = refs[waits + PARTS:]
    for load in projection_back(pgrads, wqkv_h, pgrad, wqkv, sem, 0):
        load.wait()
    for n in range(wqkv.shape[0] // TILE):
        rows = slice(n * TILE, (n + 1) * TILE)
        ngrad[:, rows] = dot(pgrad[...], wqkv[rows], NT).astype(BF16)


def input_last_kernel(waits, *refs):
    pgrads = refs[waits:waits + PARTS]
    (wqkv_h, nfirst_h, normed_h, rstd_h, grad_h, merged, pick_first, pick_last, pick_groups,
     full, side, below, corner,
     pgrad, wqkv, ngrad, normed, rstd, grad, sem, more_sem) = refs[waits + PARTS:]
    count, channels = ngrad.shape
    half = channels // 2
    loads = projection_back(pgrads, wqkv_h, pgrad, wqkv, sem, half)
    more = [
        pltpu.make_async_copy(src, dst, more_sem.at[i])
        for i, (src, dst) in enumerate(
            [(nfirst_h, ngrad.at[:, pl.ds(0, half)]), (normed_h, normed), (rstd_h, rstd), (grad_h, grad)]
        )
    ]
    for load in more:
        load.start()
    for load in loads:
        load.wait()
    for n in range(half // TILE):
        rows = slice(n * TILE, (n + 1) * TILE)
        ngrad[:, half + n * TILE:half + (n + 1) * TILE] = dot(
            pgrad[...], wqkv[rows], NT
        ).astype(BF16)
    for load in more:
        load.wait()
    places = 2 * WIN * WIN

    @pl.loop(0, count // places)
    def _(w):
        rows = aligned(w * places, places)
        d = ngrad[rows].astype(F32)
        unit = normed[rows].astype(F32)
        mean_d = jnp.mean(d, axis=1, keepdims=True)
        mean_dx = jnp.mean(d * unit, axis=1, keepdims=True)
        part = rstd[rows, :1] * (d - mean_d - unit * mean_dx)
        full[rows] = (part.astype(BF16).astype(F32) + grad[rows].astype(F32)).astype(BF16)

    (n_side, g_side), (n_above, g_above), (n_corner, g_corner) = strip_rows(None, None)
    side_cut = 2 * SHIFT * SHIFT
    first = dot(pick_first[...], full[:count // 2]).astype(BF16)
    last = dot(pick_last[...], full[count // 2:]).astype(BF16)
    groups = dot(pick_groups[...], merged[...]).astype(BF16)
    side[:side_cut] = first[:side_cut]
    side[side_cut:n_side] = last
    below[:n_above] = first[side_cut:side_cut + n_above]
    corner[:n_corner] = first[side_cut + n_above:]
    side[n_side:] = groups[:g_side]
    below[n_above:] = groups[g_side:g_side + g_above]
    corner[n_corner:] = groups[g_side + g_above:]


def unpack_kernel(full, merged, side, below, corner, pick_top, pick_middle, pick_bottom,
                  pick_groups, tokens_out, merged_out):
    count = full.shape[0]
    half = count // 2
    (n_side, _), (n_above, _), (n_corner, _) = strip_rows(None, None)
    side_cut = 2 * SHIFT * SHIFT
    line = half // (2 * WIN)
    pieces = [
        (pick_top, [full[:half], side[:side_cut]]),
        (pick_middle, [full[half:], side[side_cut:n_side]]),
        (pick_bottom, [below[:n_above], corner[:n_corner]]),
    ]
    at = 0
    for pick, held in pieces:
        rows = pick.shape[0] // 2
        out = dot(pick[...], jnp.concatenate(held, axis=0)).astype(BF16)
        for level in range(2):
            start = level * half + at
            tokens_out[start:start + rows] = out[level * rows:(level + 1) * rows]
        at += rows
    held = [merged[...], side[n_side:], below[n_above:], corner[n_corner:]]
    merged_out[...] = dot(pick_groups[...], jnp.concatenate(held, axis=0)).astype(BF16)


def sent(block, sizes, lat_step, lon_step):
    n_lat, n_lon = sizes
    route = [
        (a * n_lon + b, (a + lat_step) % n_lat * n_lon + (b + lon_step) % n_lon)
        for a in range(n_lat) for b in range(n_lon)
    ]
    return lax.ppermute(block, ("lat", "lon"), route)


def sent_strips(strips, sizes, step):
    side, lines, corner = strips
    return [sent(side, sizes, 0, step), sent(lines, sizes, step, 0), sent(corner, sizes, step, step)]


def device_rows(channels, sizes):
    n_lat, n_lon = sizes
    devices = n_lat * n_lon
    rows = channels // devices
    place = np.arange(devices)
    lon = 2 * (place // n_lat % (n_lon // 2)) + place // (devices // 2)
    lat = place % n_lat
    owner = (
        jnp.bitwise_xor(lax.axis_index("lat").astype(jnp.int32), jnp.asarray(lat, jnp.int32)) * n_lon
        + jnp.bitwise_xor(lax.axis_index("lon").astype(jnp.int32), jnp.asarray(lon, jnp.int32))
    )
    rowmap = owner[:, None] * rows + jnp.arange(rows, dtype=jnp.int32)[None, :]
    return owner, rowmap.reshape(channels, 1)


def exchange(block, sizes, lat_bits, lon_bits):
    n_lat, n_lon = sizes
    route = [
        (a * n_lon + b, (a ^ lat_bits) * n_lon + (b ^ lon_bits))
        for a in range(n_lat) for b in range(n_lon)
    ]
    return lax.ppermute(block, ("lat", "lon"), route)


def core_step(theirs, sizes):
    return exchange(theirs, sizes, 0, 1)


def layer_blocks(mine, arrived, sizes):
    blocks = sizes[1] // 2
    rows = mine.shape[0] // blocks
    total = [
        (mine[i * rows:(i + 1) * rows].astype(F32) + arrived[i * rows:(i + 1) * rows].astype(F32))
        for i in range(blocks)
    ]
    return [total[0]] + [t.astype(BF16) for t in total[1:]]


def layer_step(blocks, sizes):
    return [exchange(b, sizes, 0, 2 * i) for i, b in enumerate(blocks) if i]


def column_blocks(kept, arrived, sizes):
    total = kept
    for block in arrived:
        total = total + block.astype(F32)
    rows = total.shape[0] // sizes[0]
    blocks = [total[i * rows:(i + 1) * rows] for i in range(sizes[0])]
    return [blocks[0]] + [b.astype(BF16) for b in blocks[1:]]


def column_step(blocks, sizes):
    return [exchange(b, sizes, i, 0) for i, b in enumerate(blocks) if i]


def finished(kept, arrived):
    for block in arrived:
        kept = kept + block.astype(F32)
    return kept


def shards(sizes, tokens, qkv_weight, out_weight, merge_weight, merged_grad):
    levels, lat_rows, lon_cols, channels = tokens.shape
    merged_width = merge_weight.shape[1]
    count = levels * lat_rows * lon_cols
    groups = count // 4
    half = channels // 2
    strip_rows.extent = (lat_rows, lon_cols)
    vmem = pl.BlockSpec(memory_space=pltpu.VMEM)
    smem = pl.BlockSpec(memory_space=pltpu.SMEM)
    hbm = pl.BlockSpec(memory_space=pl.ANY)

    def shape(*extent, dtype=BF16):
        return jax.ShapeDtypeStruct(extent, dtype)

    def settings(weight):
        return dict(
            compiler_params=pltpu.CompilerParams(vmem_limit_bytes=60 * MIB),
            cost_estimate=pl.CostEstimate(
                flops=int(weight * 1e10), bytes_accessed=16 * MIB, transcendentals=0
            ),
        )

    g_rows, g_cols = lat_rows // 2, lon_cols // 2
    cells = window_cells(levels, lat_rows, lon_cols)
    grps = window_groups(levels, g_rows, g_cols)
    cs = Strips(levels, lat_rows, lon_cols, SHIFT, True)
    gs = Strips(levels, g_rows, g_cols, HALF, False)
    g_strips = [padded(gs.side), padded(gs.above), padded(gs.corner)]
    to = ((0, lon_cols), (lat_rows, 0), (lat_rows, lon_cols))
    g_to = ((0, g_cols), (g_rows, 0), (g_rows, g_cols))
    own_rows = range(SHIFT, SHIFT + lat_rows)
    own_cols = range(SHIFT, SHIFT + lon_cols)
    own = box(levels, own_rows, own_cols)
    g_own = turned_box(levels, range(HALF, HALF + g_rows), range(HALF, HALF + g_cols))
    half_cells = count // 2
    side_cut = levels * SHIFT * SHIFT
    sent_cells = sum((Strips.sent(s, *t) for s, t in zip((cs.side, cs.above, cs.corner), to)), [])
    sent_groups = sum((Strips.sent(s, *t) for s, t in zip(g_strips, g_to)), [])
    held_top = box(levels, range(SHIFT, 2 * SHIFT), own_cols) + cs.side[:side_cut] + cs.above + cs.corner
    held_low = box(levels, range(2 * SHIFT, lat_rows), own_cols) + cs.side[side_cut:]
    depth = max(len(held_top), len(held_low))
    depth += -depth % 16
    held_top += [None] * (depth - len(held_top))
    held_low += [None] * (depth - len(held_low))

    tokens_flat = tokens.reshape(count, channels)
    merged_grad_flat = merged_grad.transpose(0, 2, 1, 3).reshape(groups, merged_width)
    extents = [(n + g, channels) for n, g in strip_rows(None, None)]
    strips = pl.pallas_call(
        pack_kernel,
        out_shape=[shape(*e) for e in extents],
        in_specs=[vmem] * 4, out_specs=[vmem] * 3,
        name="pack_strips", **settings(1),
    )(tokens_flat, merged_grad_flat, picks(sent_cells, own), picks(sent_groups, g_own))
    strips = sent_strips(strips, sizes, 1)

    order = jnp.concatenate([picks(cells[:half_cells], held_top), picks(cells[half_cells:], held_low)])
    group = picks(grps, g_own + sum(g_strips, []))
    edge = (lax.axis_index("lat") == 0).astype(jnp.int32).reshape(1)
    owner, rowmap = device_rows(channels, sizes)

    wide = shape(count, channels)
    normed, normt, proj, dmr, dmm, grad, rstd, merged, out_mine, out_theirs = pl.pallas_call(
        forward_kernel,
        out_shape=[
            wide, shape(channels, count), shape(count, 3 * channels), wide, wide, wide,
            shape(count, LANES, dtype=F32), shape(groups, merged_width),
            shape(half, channels), shape(half, channels),
        ],
        in_specs=[smem, smem] + [vmem] * 8 + [hbm] * 3,
        out_specs=[hbm] * 6 + [vmem] * 4,
        scratch_shapes=[
            pltpu.VMEM(qkv_weight.shape, BF16),
            pltpu.VMEM(out_weight.shape, BF16),
            pltpu.VMEM(merge_weight.shape, BF16),
            pltpu.VMEM((2, depth, channels), BF16),
            pltpu.VMEM((count, channels), BF16),
            pltpu.VMEM((count, channels), BF16),
            pltpu.VMEM((channels, count), BF16),
            pltpu.VMEM((count, 3 * channels), BF16),
            pltpu.VMEM((count, channels), BF16),
            pltpu.VMEM((count, channels), F32),
            pltpu.VMEM((4, groups, channels), BF16),
            pltpu.VMEM((groups, 4 * channels), BF16),
            pltpu.VMEM((groups, merged_width), BF16),
            pltpu.VMEM((count, channels), BF16),
            pltpu.VMEM((count, channels), BF16),
            pltpu.VMEM((count, channels), BF16),
            pltpu.VMEM((channels, count), BF16),
            pltpu.SemaphoreType.DMA((3,)),
            pltpu.SemaphoreType.DMA((6,)),
        ],
        name="block_forward", **settings(30),
    )(edge, owner, tokens_flat, merged_grad_flat, *strips, order, group, rowmap,
      qkv_weight, out_weight, merge_weight)

    width = channels // PARTS

    def backward(index, before, after):
        summing = before is not None
        outs = [shape(count, 3 * width)]
        scratch = [
            pltpu.VMEM((5, count, width), BF16),
            pltpu.VMEM((count, (6 if summing else 3) * width), BF16),
        ]
        if summing:
            outs += [shape(half, 6 * width)] * 2
            scratch += [
                pltpu.VMEM((channels, count), BF16),
                pltpu.VMEM((half, 6 * width), BF16),
                pltpu.VMEM((half, 6 * width), BF16),
            ]
        scratch += [
            pltpu.SemaphoreType.DMA((count // (2 * WIN * WIN), 5)),
            pltpu.SemaphoreType.DMA((2,)),
            pltpu.SemaphoreType.DMA((3,)),
        ]
        operands = [edge, proj, dmr, dmm, normt] + ([before] if summing else [])
        return pl.pallas_call(
            functools.partial(backward_kernel, index, len(after), summing),
            out_shape=outs,
            in_specs=[hbm] * len(after) + [smem] + [hbm] * (len(operands) - 1),
            out_specs=[hbm] * len(outs),
            scratch_shapes=scratch,
            name="attention_backward", **settings(10 if summing else 6),
        )(*after, *operands)

    arrived = core_step(out_theirs, sizes)
    (pg0,) = backward(0, None, [])
    out_layer = layer_blocks(out_mine, arrived, sizes)
    arrived = layer_step(out_layer, sizes)
    pg1, mine1, theirs1 = backward(1, pg0, out_layer[1:])
    out_column = column_blocks(out_layer[0], arrived, sizes)
    out_arrived = column_step(out_column, sizes)
    arrived = core_step(theirs1, sizes)
    (pg2,) = backward(2, None, out_column[1:])
    layer1 = layer_blocks(mine1, arrived, sizes)
    arrived1 = layer_step(layer1, sizes)
    pg3, mine2, theirs2 = backward(3, pg2, layer1[1:])
    arrived2 = core_step(theirs2, sizes)
    pgrads = [pg0, pg1, pg2, pg3]

    in_scratch = [
        pltpu.VMEM((count, 3 * channels), BF16),
        pltpu.VMEM((half, 3 * channels), BF16),
    ]
    in_sems = pltpu.SemaphoreType.DMA((PARTS, 4))
    nfirst = pl.pallas_call(
        functools.partial(input_first_kernel, 0),
        out_shape=shape(count, half),
        in_specs=[hbm] * (PARTS + 1), out_specs=vmem,
        scratch_shapes=in_scratch + [in_sems],
        name="input_first", **settings(5),
    )(*pgrads, qkv_weight)
    column1 = column_blocks(layer1[0], arrived1, sizes)
    column_arrived1 = column_step(column1, sizes)
    layer2 = layer_blocks(mine2, arrived2, sizes)
    arrived2 = layer_step(layer2, sizes)
    after = layer2[1:] + column1[1:]

    first_picks = picks(cs.side[:side_cut] + cs.above + cs.corner, cells[:half_cells])
    last_picks = picks(cs.side[side_cut:], cells[half_cells:])
    full, *strips = pl.pallas_call(
        functools.partial(input_last_kernel, len(after)),
        out_shape=[wide] + [shape(*e) for e in extents],
        in_specs=[hbm] * (len(after) + PARTS + 5) + [vmem] * 4, out_specs=[vmem] * 4,
        scratch_shapes=in_scratch + [
            pltpu.VMEM((count, channels), BF16),
            pltpu.VMEM((count, channels), BF16),
            pltpu.VMEM((count, LANES), F32),
            pltpu.VMEM((count, channels), BF16),
            in_sems,
            pltpu.SemaphoreType.DMA((4,)),
        ],
        name="input_last", **settings(9),
    )(*after, *pgrads, qkv_weight, nfirst, normed, rstd, grad, merged,
      first_picks, last_picks, picks(sum(g_strips, []), grps))
    strips = sent_strips(strips, sizes, -1)

    column2 = column_blocks(layer2[0], arrived2, sizes)
    column_arrived2 = column_step(column2, sizes)

    got = [Strips.sent(s, *t) for s, t in zip((cs.side, cs.above, cs.corner), to)]
    g_got = sum((Strips.sent(s, *t) for s, t in zip(g_strips, g_to)), [])
    tokens_grad, merged = pl.pallas_call(
        unpack_kernel,
        out_shape=[wide, shape(groups, merged_width)],
        in_specs=[vmem] * 9, out_specs=[vmem] * 2,
        name="unpack_strips", **settings(2),
    )(
        full, merged, *strips,
        picks(box(levels, range(SHIFT, 2 * SHIFT), own_cols), cells[:half_cells] + got[0][:side_cut]),
        picks(box(levels, range(2 * SHIFT, lat_rows), own_cols), cells[half_cells:] + got[0][side_cut:]),
        picks(box(levels, range(lat_rows, lat_rows + SHIFT), own_cols), got[1] + got[2]),
        picks(g_own, grps + g_got),
    )
    merged = merged.reshape(levels, g_cols, g_rows, merged_width).transpose(0, 2, 1, 3)

    out_weight_grad = finished(out_column[0], out_arrived)
    parts = [finished(column1[0], column_arrived1), finished(column2[0], column_arrived2)]
    pieces = [
        part[:, (3 * i + kind) * width:(3 * i + kind + 1) * width]
        for kind in range(3) for part in parts for i in range(2)
    ]
    qkv_weight_grad = jnp.concatenate(pieces, axis=1)
    return merged, tokens_grad.reshape(tokens.shape), qkv_weight_grad, out_weight_grad


def solution(mesh):
    sizes = (mesh.shape["lat"], mesh.shape["lon"])
    in_specs = (P(None, "lat", "lon", None), P(), P(), P(), P(None, "lat", "lon", None))
    out_specs = (
        P(None, "lat", "lon", None),
        P(None, "lat", "lon", None),
        P(("lat", "lon"), None),
        P(("lat", "lon"), None),
    )
    return jax.shard_map(
        functools.partial(shards, sizes),
        mesh=mesh, in_specs=in_specs, out_specs=out_specs, check_vma=False,
    )
```

```python
import functools

import jax
import jax.numpy as jnp
import numpy as np
from jax import lax
from jax.experimental import pallas as pl
from jax.experimental.pallas import tpu as pltpu
from jax.sharding import PartitionSpec as P

HEADS = 32
WIN = 8
SHIFT = 4
LANES = 128
HALF = SHIFT // 2
TILE = 256
EPSILON = 1e-05
MIB = 1 << 20

NN = (((1,), (0,)), ((), ()))
NT = (((1,), (1,)), ((), ()))
TN = (((0,), (0,)), ((), ()))
BF16 = jnp.bfloat16
F32 = jnp.float32


def dot(a, b, dims=NN):
    return lax.dot_general(a, b, dims, preferred_element_type=F32)


def window_cells(levels, rows, columns):
    half = WIN // 2
    return [
        (level, wi * WIN + 2 * row + sub % 2, wj * WIN + 2 * column + sub // 2)
        for wi in range(rows // WIN) for wj in range(columns // WIN) for sub in range(4)
        for level in range(levels) for row in range(half) for column in range(half)
    ]


def window_groups(levels, rows, columns):
    half = WIN // 2
    return [
        (level, wi * half + row, wj * half + column)
        for wi in range(rows // half) for wj in range(columns // half)
        for level in range(levels) for row in range(half) for column in range(half)
    ]


def box(levels, rows, columns):
    return [(l, r, c) for l in range(levels) for r in rows for c in columns]


def turned_box(levels, rows, columns):
    return [(l, r, c) for l in range(levels) for c in columns for r in rows]


def padded(cells, step=16):
    return cells + [None] * (-len(cells) % step)


def picks(wanted, held):
    spot = {cell: i for i, cell in enumerate(held) if cell is not None}
    table = np.zeros((len(wanted), len(held)), np.float32)
    for i, cell in enumerate(wanted):
        if cell is not None:
            table[i, spot[cell]] = 1.0
    return jnp.asarray(table, BF16)


class Strips:
    def __init__(self, levels, rows, columns, width, cut):
        self.side = (box(levels, range(width, 2 * width), range(width))
                     + box(levels, range(2 * width, rows), range(width)))
        self.above = box(levels, range(width), range(width, columns))
        self.corner = box(levels, range(width), range(width))
        if not cut:
            self.side = box(levels, range(width, rows), range(width))

    @staticmethod
    def sent(cells, down, across):
        return [None if c is None else (c[0], c[1] + down, c[2] + across) for c in cells]


def head_masks():
    head = lax.broadcasted_iota(jnp.int32, (LANES, LANES), 1) // (LANES // 4)
    return [jnp.where(head == h, 1.0, 0.0).astype(BF16) for h in range(4)]


def region_bias(places, active):
    step = 2 * (WIN // 2)
    one = (lax.broadcasted_iota(jnp.int32, (places, places), 0) // step) % 2
    other = (lax.broadcasted_iota(jnp.int32, (places, places), 1) // step) % 2
    return jnp.where((one != other) & active, -1e30, 0.0)


def score_scale(channels):
    return float((channels // HEADS) ** -0.5 * np.log2(np.e))


def aligned(start, size, step=None):
    return pl.ds(pl.multiple_of(start, step or size), size)


def pack_kernel(tokens, merged_grad, pick_cells, pick_groups, side, above, corner):
    cells = dot(pick_cells[...], tokens[...]).astype(BF16)
    groups = dot(pick_groups[...], merged_grad[...]).astype(BF16)
    at, at_group = 0, 0
    for out, (count, extra) in zip((side, above, corner), strip_rows(pick_cells, pick_groups)):
        out[:count] = cells[at:at + count]
        out[count:] = groups[at_group:at_group + extra]
        at, at_group = at + count, at_group + extra


def strip_rows(pick_cells, pick_groups):
    levels = 2
    rows, columns = strip_rows.extent
    cells = [levels * (rows - SHIFT) * SHIFT, levels * SHIFT * (columns - SHIFT), levels * SHIFT * SHIFT]
    groups = [n // 4 + (-(n // 4)) % 16 for n in cells]
    return list(zip(cells, groups))


def forward_kernel(
    owner, edge, tokens, merged_grad, side, above, corner, order, group,
    wqkv_h, wout_h, wm_h,
    normed_h, normt_h, proj_h, dmr_h, dmm_h, grad_h, rstd, merged, out_terms,
    wqkv, wout, wm, source, xw, normed, normt, proj, mixture, inverse, subs, dsubs, cotangent,
    grad, dmr, dmm, turned, in_sem, out_sem,
):
    count, channels = xw.shape
    places = 2 * WIN * WIN
    windows = count // places
    per_row = windows // 2
    quarter = places // 4
    groups = count // 4
    devices = len(owner)
    block = channels // devices

    loads = [
        pltpu.make_async_copy(src, dst, in_sem.at[i])
        for i, (src, dst) in enumerate([(wqkv_h, wqkv), (wout_h, wout), (wm_h, wm)])
    ]
    for load in loads:
        load.start()
    stores = [
        pltpu.make_async_copy(src, dst, out_sem.at[i])
        for i, (src, dst) in enumerate(
            [(normed, normed_h), (proj, proj_h), (normt, normt_h),
             (grad, grad_h), (dmr, dmr_h), (dmm, dmm_h)]
        )
    ]

    (n_side, g_side), (n_above, g_above), (n_corner, g_corner) = strip_rows(None, None)
    half = count // 2
    line = half // (2 * WIN)
    cut = SHIFT * line
    side_cut = 2 * SHIFT * SHIFT
    blocks = [
        [tokens[:cut], tokens[half:half + cut], side[:side_cut], above[:n_above], corner[:n_corner]],
        [tokens[cut:cut + WIN * line], tokens[half + cut:half + cut + WIN * line], side[side_cut:n_side]],
    ]
    for wi in range(2):
        at = 0
        for piece in blocks[wi]:
            source[wi, at:at + piece.shape[0]] = piece
            at += piece.shape[0]
        if at < source.shape[1]:
            source[wi, at:] = jnp.zeros((source.shape[1] - at, channels), BF16)

    @pl.loop(0, windows)
    def _(w):
        rows = aligned(w * places, places)
        x = dot(order[rows], source[w // per_row])
        xw[rows] = x.astype(BF16)
        center = jnp.mean(x, axis=1, keepdims=True)
        moved = x - center
        scale = lax.rsqrt(jnp.mean(moved * moved, axis=1, keepdims=True) + EPSILON)
        rstd[rows] = jnp.broadcast_to(scale, (places, LANES))
        normed[rows] = (moved * scale).astype(BF16)

    stores[0].start()
    loads[0].wait()

    @pl.loop(0, wqkv.shape[1] // TILE)
    def _(n):
        columns = aligned(n * TILE, TILE)
        proj[:, columns] = dot(normed[...], wqkv[:, columns]).astype(BF16)

    stores[1].start()

    masks = head_masks()
    factor = score_scale(channels)

    edge_bias = region_bias(places, edge[0] == 1)
    held = jnp.concatenate(
        [merged_grad[...], side[n_side:], above[n_above:], corner[n_corner:]], axis=0
    )
    cotangent[...] = dot(group[...], held).astype(BF16)
    loads[2].wait()
    steps = channels // LANES
    per_step = 4 * channels // TILE // steps

    @pl.loop(0, steps)
    def _(g):
        lanes = aligned(g * LANES, LANES)
        key_lanes = aligned(channels + g * LANES, LANES)
        value_lanes = aligned(2 * channels + g * LANES, LANES)
        for w in range(windows):
            rows = slice(w * places, (w + 1) * places)
            q, k, v = proj[rows, lanes], proj[rows, key_lanes], proj[rows, value_lanes]
            scores = dot(q, jnp.concatenate([k * m for m in masks], axis=0), NT)
            parts = []
            for h in range(4):
                part = scores[:, h * places:(h + 1) * places] * factor
                if w < per_row:
                    part = part + edge_bias
                part = part - jnp.max(part, axis=1, keepdims=True)
                parts.append(jnp.exp2(part).astype(BF16))
            values = jnp.concatenate(
                [jnp.concatenate([v * m, m], axis=1) for m in masks], axis=0
            )
            summed = dot(jnp.concatenate(parts, axis=1), values)
            inv = 1.0 / summed[:, LANES:]
            inverse[rows, lanes] = inv
            mixture[rows, lanes] = (summed[:, :LANES] * inv).astype(BF16)
        for i in range(per_step):
            at = aligned((g * per_step + i) * TILE, TILE)
            dsubs[:, at] = dot(cotangent[...], wm[at], NT).astype(BF16)

    loads[1].wait()

    @pl.loop(0, channels // TILE)
    def _(n):
        columns = aligned(n * TILE, TILE)
        out = dot(mixture[...], wout[:, columns]) + xw[:, columns].astype(F32)
        out = out.astype(BF16)
        for w in range(windows):
            for s in range(4):
                at = w * places + s * quarter
                subs[s, w * quarter:(w + 1) * quarter, columns] = out[at:at + quarter]

    total = jnp.zeros((groups, 1), F32)
    for s in range(4):
        total += jnp.sum(subs[s].astype(F32), axis=1, keepdims=True)
    center = total / (4 * channels)
    total = jnp.zeros((groups, 1), F32)
    for s in range(4):
        moved = subs[s].astype(F32) - center
        total += jnp.sum(moved * moved, axis=1, keepdims=True)
    scale = lax.rsqrt(total / (4 * channels) + EPSILON)
    result = jnp.zeros((groups, wm.shape[1]), F32)
    for s in range(4):
        unit = ((subs[s].astype(F32) - center) * scale).astype(BF16)
        result += dot(unit, wm[s * channels:(s + 1) * channels])
    merged[...] = result.astype(BF16)

    mean_g = jnp.zeros((groups, 1), F32)
    mean_gx = jnp.zeros((groups, 1), F32)
    for s in range(4):
        d = dsubs[:, s * channels:(s + 1) * channels].astype(F32)
        mean_g += jnp.sum(d, axis=1, keepdims=True)
        mean_gx += jnp.sum(d * ((subs[s].astype(F32) - center) * scale), axis=1, keepdims=True)
    mean_g = mean_g / (4 * channels)
    mean_gx = mean_gx / (4 * channels)
    for s in range(4):
        unit = (subs[s].astype(F32) - center) * scale
        d = dsubs[:, s * channels:(s + 1) * channels].astype(F32)
        d = (scale * (d - mean_g - unit * mean_gx)).astype(BF16)
        for w in range(windows):
            at = w * places + s * quarter
            grad[at:at + quarter] = d[w * quarter:(w + 1) * quarter]
    stores[3].start()

    @pl.loop(0, channels // TILE)
    def _(n):
        columns = aligned(n * TILE, TILE)
        d = dot(grad[...], wout[columns], NT).astype(BF16).astype(F32)
        d = d * inverse[:, columns]
        dmr[:, columns] = d.astype(BF16)
        dmm[:, columns] = (-d * mixture[:, columns].astype(F32)).astype(BF16)

    stores[4].start()
    stores[5].start()

    def turn(field, out):
        @pl.loop(0, channels // TILE)
        def _(n):
            rows = aligned(n * TILE, TILE)
            turned[rows] = field[:, rows].T

        for d in range(devices):
            out[d * block:(d + 1) * block] = turned[owner[d] * block:(owner[d] + 1) * block]

    turn(normed, normt)
    stores[2].start()
    mixt = wqkv.at[:, :count]
    turn(mixture, mixt)

    @pl.loop(0, channels // TILE)
    def _(n):
        columns = aligned(n * TILE, TILE)
        out_terms[:, columns] = dot(mixt[...], grad[:, columns]).astype(BF16)

    for store in stores:
        store.wait()


def backward_kernel(
    edge, proj_h, dmr_h, dmm_h, normt_h, pgrad_h, terms_h,
    proj, dmr, dmm, normt, pgrad, terms, in_sem, sem, out_sem,
):
    count, channels = dmr.shape
    places = 2 * WIN * WIN
    windows = count // places
    per_row = windows // 2
    masks = head_masks()
    factor = score_scale(channels)
    plain = (channels // HEADS) ** -0.5
    width = TILE
    steps = channels // width

    def loads(g):
        for i in range(5):
            src, dst = ((proj_h, proj), (dmr_h, dmr), (dmm_h, dmm))[max(i - 2, 0)]
            columns = aligned((i * channels if i < 3 else 0) + g * width, width)
            yield pltpu.make_async_copy(src.at[:, columns], dst.at[:, columns], in_sem.at[g, i])

    def stores(g):
        for i in range(3):
            columns = aligned(i * channels + g * width, width)
            yield pltpu.make_async_copy(pgrad.at[:, columns], pgrad_h.at[:, columns], out_sem.at[0, g, i])
            yield pltpu.make_async_copy(terms.at[:, columns], terms_h.at[:, columns], out_sem.at[1, g, i])

    for g in range(steps):
        for load in loads(g):
            load.start()
    turned_load = pltpu.make_async_copy(normt_h, normt, sem.at[0])
    turned_load.start()
    edge_bias = region_bias(places, edge[0] == 1)

    @pl.loop(0, steps)
    def _(g):
        for load in loads(g):
            load.wait()

        for half in range(width // LANES):
            at = [aligned(i * channels + g * width + half * LANES, LANES) for i in range(3)]
            for w in range(windows):
                rows = slice(w * places, (w + 1) * places)
                q, k, v = (proj[rows, at[i]] for i in range(3))
                dm, dd = dmr[rows, at[0]], dmm[rows, at[0]]
                keys = jnp.concatenate([k * m for m in masks], axis=0)
                scores = dot(keys, q, NT)
                values = jnp.concatenate(
                    [jnp.concatenate([v * m, m], axis=1) for m in masks], axis=0
                )
                slope = dot(values, jnp.concatenate([dm, dd], axis=1), NT)
                weights, slopes = [], []
                for h in range(4):
                    block = slice(h * places, (h + 1) * places)
                    part = scores[block] * factor
                    if w < per_row:
                        part = part + edge_bias
                    part = jnp.exp2(part - jnp.max(part, axis=0, keepdims=True))
                    weights.append(part.astype(BF16))
                    slopes.append((part * slope[block]).astype(BF16))
                dv = dot(
                    jnp.concatenate(weights, axis=1),
                    jnp.concatenate([dm * m for m in masks], axis=0),
                )
                dk = dot(
                    jnp.concatenate(slopes, axis=1),
                    jnp.concatenate([q * m for m in masks], axis=0),
                )
                dq = dot(jnp.concatenate(slopes, axis=0), keys, TN)
                pgrad[rows, at[0]] = (dq * plain).astype(BF16)
                pgrad[rows, at[1]] = (dk * plain).astype(BF16)
                pgrad[rows, at[2]] = dv.astype(BF16)

        @pl.when(g == 0)
        def _():
            turned_load.wait()

        for i in range(3):
            columns = aligned(i * channels + g * width, width)
            terms[:, columns] = dot(normt[...], pgrad[:, columns]).astype(BF16)
        for store in stores(g):
            store.start()

    for g in range(steps):
        for store in stores(g):
            store.wait()


def input_kernel(
    pgrad_h, wqkv_h, normed_h, rstd_h, grad_h, merged, pick_first, pick_last, pick_groups,
    full, side, below, corner, pgrad, wqkv, ngrad, normed, rstd, grad, sem,
):
    count, channels = ngrad.shape
    tiles = channels // TILE

    def rows_of(n):
        return pl.ds(n * TILE, TILE)

    loads = [pltpu.make_async_copy(pgrad_h, pgrad, sem.at[0])] + [
        pltpu.make_async_copy(wqkv_h.at[rows_of(n)], wqkv.at[rows_of(n)], sem.at[1 + n])
        for n in range(tiles)
    ]
    more = [
        pltpu.make_async_copy(src, dst, sem.at[1 + tiles + i])
        for i, (src, dst) in enumerate([(normed_h, normed), (rstd_h, rstd), (grad_h, grad)])
    ]
    for load in loads + more:
        load.start()
    loads[0].wait()
    for n in range(tiles):
        loads[1 + n].wait()
        ngrad[:, rows_of(n)] = dot(pgrad[...], wqkv[rows_of(n)], NT).astype(BF16)
    for load in more:
        load.wait()
    places = 2 * WIN * WIN

    @pl.loop(0, count // places)
    def _(w):
        rows = aligned(w * places, places)
        d = ngrad[rows].astype(F32)
        unit = normed[rows].astype(F32)
        mean_d = jnp.mean(d, axis=1, keepdims=True)
        mean_dx = jnp.mean(d * unit, axis=1, keepdims=True)
        part = rstd[rows, :1] * (d - mean_d - unit * mean_dx)
        full[rows] = (part.astype(BF16).astype(F32) + grad[rows].astype(F32)).astype(BF16)

    (n_side, g_side), (n_above, g_above), (n_corner, g_corner) = strip_rows(None, None)
    side_cut = 2 * SHIFT * SHIFT
    first = dot(pick_first[...], full[:count // 2]).astype(BF16)
    last = dot(pick_last[...], full[count // 2:]).astype(BF16)
    groups = dot(pick_groups[...], merged[...]).astype(BF16)
    side[:side_cut] = first[:side_cut]
    side[side_cut:n_side] = last
    below[:n_above] = first[side_cut:side_cut + n_above]
    corner[:n_corner] = first[side_cut + n_above:]
    side[n_side:] = groups[:g_side]
    below[n_above:] = groups[g_side:g_side + g_above]
    corner[n_corner:] = groups[g_side + g_above:]


def unpack_kernel(full, merged, side, below, corner, pick_top, pick_middle, pick_bottom,
                  pick_groups, tokens_out, merged_out):
    count = full.shape[0]
    half = count // 2
    (n_side, _), (n_above, _), (n_corner, _) = strip_rows(None, None)
    side_cut = 2 * SHIFT * SHIFT
    line = half // (2 * WIN)
    pieces = [
        (pick_top, [full[:half], side[:side_cut]]),
        (pick_middle, [full[half:], side[side_cut:n_side]]),
        (pick_bottom, [below[:n_above], corner[:n_corner]]),
    ]
    at = 0
    for pick, held in pieces:
        rows = pick.shape[0] // 2
        out = dot(pick[...], jnp.concatenate(held, axis=0)).astype(BF16)
        for level in range(2):
            start = level * half + at
            tokens_out[start:start + rows] = out[level * rows:(level + 1) * rows]
        at += rows
    held = [merged[...], side[n_side:], below[n_above:], corner[n_corner:]]
    merged_out[...] = dot(pick_groups[...], jnp.concatenate(held, axis=0)).astype(BF16)


def sent(block, sizes, lat_step, lon_step):
    n_lat, n_lon = sizes
    route = [
        (a * n_lon + b, (a + lat_step) % n_lat * n_lon + (b + lon_step) % n_lon)
        for a in range(n_lat) for b in range(n_lon)
    ]
    return lax.ppermute(block, ("lat", "lon"), route)


def sent_strips(strips, sizes, step):
    side, lines, corner = strips
    return [sent(side, sizes, 0, step), sent(lines, sizes, step, 0), sent(corner, sizes, step, step)]


def device_rows(channels, sizes):
    n_lat, n_lon = sizes
    place = np.arange(n_lat * n_lon)
    return place % n_lat * n_lon + place // n_lat


def summed(terms):
    part = lax.psum_scatter(terms, "lon", scatter_dimension=0, tiled=True)
    part = lax.psum_scatter(part, "lat", scatter_dimension=0, tiled=True)
    return part.astype(F32)


def shards(sizes, tokens, qkv_weight, out_weight, merge_weight, merged_grad):
    levels, lat_rows, lon_cols, channels = tokens.shape
    merged_width = merge_weight.shape[1]
    count = levels * lat_rows * lon_cols
    groups = count // 4
    strip_rows.extent = (lat_rows, lon_cols)
    vmem = pl.BlockSpec(memory_space=pltpu.VMEM)
    smem = pl.BlockSpec(memory_space=pltpu.SMEM)
    hbm = pl.BlockSpec(memory_space=pl.ANY)

    def shape(*extent, dtype=BF16):
        return jax.ShapeDtypeStruct(extent, dtype)

    def settings(weight):
        return dict(
            compiler_params=pltpu.CompilerParams(vmem_limit_bytes=60 * MIB),
            cost_estimate=pl.CostEstimate(
                flops=int(weight * 1e10), bytes_accessed=16 * MIB, transcendentals=0
            ),
        )

    g_rows, g_cols = lat_rows // 2, lon_cols // 2
    cells = window_cells(levels, lat_rows, lon_cols)
    grps = window_groups(levels, g_rows, g_cols)
    cs = Strips(levels, lat_rows, lon_cols, SHIFT, True)
    gs = Strips(levels, g_rows, g_cols, HALF, False)
    g_strips = [padded(gs.side), padded(gs.above), padded(gs.corner)]
    to = ((0, lon_cols), (lat_rows, 0), (lat_rows, lon_cols))
    g_to = ((0, g_cols), (g_rows, 0), (g_rows, g_cols))
    own_rows = range(SHIFT, SHIFT + lat_rows)
    own_cols = range(SHIFT, SHIFT + lon_cols)
    own = box(levels, own_rows, own_cols)
    g_own = turned_box(levels, range(HALF, HALF + g_rows), range(HALF, HALF + g_cols))
    half_cells = count // 2
    side_cut = levels * SHIFT * SHIFT
    sent_cells = sum((Strips.sent(s, *t) for s, t in zip((cs.side, cs.above, cs.corner), to)), [])
    sent_groups = sum((Strips.sent(s, *t) for s, t in zip(g_strips, g_to)), [])
    held_top = box(levels, range(SHIFT, 2 * SHIFT), own_cols) + cs.side[:side_cut] + cs.above + cs.corner
    held_low = box(levels, range(2 * SHIFT, lat_rows), own_cols) + cs.side[side_cut:]
    depth = max(len(held_top), len(held_low))
    depth += -depth % 16
    held_top += [None] * (depth - len(held_top))
    held_low += [None] * (depth - len(held_low))

    tokens_flat = tokens.reshape(count, channels)
    merged_grad_flat = merged_grad.transpose(0, 2, 1, 3).reshape(groups, merged_width)
    extents = [(n + g, channels) for n, g in strip_rows(None, None)]
    strips = pl.pallas_call(
        pack_kernel,
        out_shape=[shape(*e) for e in extents],
        in_specs=[vmem] * 4, out_specs=[vmem] * 3,
        name="pack_strips", **settings(1),
    )(tokens_flat, merged_grad_flat, picks(sent_cells, own), picks(sent_groups, g_own))
    strips = sent_strips(strips, sizes, 1)

    order = jnp.concatenate([picks(cells[:half_cells], held_top), picks(cells[half_cells:], held_low)])
    group = picks(grps, g_own + sum(g_strips, []))
    edge = (lax.axis_index("lat") == 0).astype(jnp.int32).reshape(1)
    owner = tuple(int(d) for d in device_rows(channels, sizes))

    wide = shape(count, channels)
    normed, normt, proj, dmr, dmm, grad, rstd, merged, out_terms = pl.pallas_call(
        functools.partial(forward_kernel, owner),
        out_shape=[
            wide, shape(channels, count), shape(count, 3 * channels), wide, wide, wide,
            shape(count, LANES, dtype=F32), shape(groups, merged_width),
            shape(channels, channels),
        ],
        in_specs=[smem] + [vmem] * 7 + [hbm] * 3,
        out_specs=[hbm] * 6 + [vmem] * 3,
        scratch_shapes=[
            pltpu.VMEM(qkv_weight.shape, BF16),
            pltpu.VMEM(out_weight.shape, BF16),
            pltpu.VMEM(merge_weight.shape, BF16),
            pltpu.VMEM((2, depth, channels), BF16),
            pltpu.VMEM((count, channels), BF16),
            pltpu.VMEM((count, channels), BF16),
            pltpu.VMEM((channels, count), BF16),
            pltpu.VMEM((count, 3 * channels), BF16),
            pltpu.VMEM((count, channels), BF16),
            pltpu.VMEM((count, channels), F32),
            pltpu.VMEM((4, groups, channels), BF16),
            pltpu.VMEM((groups, 4 * channels), BF16),
            pltpu.VMEM((groups, merged_width), BF16),
            pltpu.VMEM((count, channels), BF16),
            pltpu.VMEM((count, channels), BF16),
            pltpu.VMEM((count, channels), BF16),
            pltpu.VMEM((channels, count), BF16),
            pltpu.SemaphoreType.DMA((3,)),
            pltpu.SemaphoreType.DMA((6,)),
        ],
        name="block_forward", **settings(30),
    )(edge, tokens_flat, merged_grad_flat, *strips, order, group,
      qkv_weight, out_weight, merge_weight)

    out_weight_grad = summed(out_terms)

    steps = channels // TILE
    pgrad, terms = pl.pallas_call(
        backward_kernel,
        out_shape=[shape(count, 3 * channels), shape(channels, 3 * channels)],
        in_specs=[smem] + [hbm] * 4, out_specs=[hbm] * 2,
        scratch_shapes=[
            pltpu.VMEM((count, 3 * channels), BF16),
            pltpu.VMEM((count, channels), BF16),
            pltpu.VMEM((count, channels), BF16),
            pltpu.VMEM((channels, count), BF16),
            pltpu.VMEM((count, 3 * channels), BF16),
            pltpu.VMEM((channels, 3 * channels), BF16),
            pltpu.SemaphoreType.DMA((steps, 5)),
            pltpu.SemaphoreType.DMA((1,)),
            pltpu.SemaphoreType.DMA((2, steps, 3)),
        ],
        name="attention_backward", **settings(30),
    )(edge, proj, dmr, dmm, normt)
    qkv_weight_grad = summed(terms)

    first_picks = picks(cs.side[:side_cut] + cs.above + cs.corner, cells[:half_cells])
    last_picks = picks(cs.side[side_cut:], cells[half_cells:])
    full, *strips = pl.pallas_call(
        input_kernel,
        out_shape=[wide] + [shape(*e) for e in extents],
        in_specs=[hbm] * 5 + [vmem] * 4, out_specs=[vmem] * 4,
        scratch_shapes=[
            pltpu.VMEM((count, 3 * channels), BF16),
            pltpu.VMEM(qkv_weight.shape, BF16),
            pltpu.VMEM((count, channels), BF16),
            pltpu.VMEM((count, channels), BF16),
            pltpu.VMEM((count, LANES), F32),
            pltpu.VMEM((count, channels), BF16),
            pltpu.SemaphoreType.DMA((4 + steps,)),
        ],
        name="input_backward", **settings(12),
    )(pgrad, qkv_weight, normed, rstd, grad, merged,
      first_picks, last_picks, picks(sum(g_strips, []), grps))
    strips = sent_strips(strips, sizes, -1)

    got = [Strips.sent(s, *t) for s, t in zip((cs.side, cs.above, cs.corner), to)]
    g_got = sum((Strips.sent(s, *t) for s, t in zip(g_strips, g_to)), [])
    tokens_grad, merged = pl.pallas_call(
        unpack_kernel,
        out_shape=[wide, shape(groups, merged_width)],
        in_specs=[vmem] * 9, out_specs=[vmem] * 2,
        name="unpack_strips", **settings(2),
    )(
        full, merged, *strips,
        picks(box(levels, range(SHIFT, 2 * SHIFT), own_cols), cells[:half_cells] + got[0][:side_cut]),
        picks(box(levels, range(2 * SHIFT, lat_rows), own_cols), cells[half_cells:] + got[0][side_cut:]),
        picks(box(levels, range(lat_rows, lat_rows + SHIFT), own_cols), got[1] + got[2]),
        picks(g_own, grps + g_got),
    )
    merged = merged.reshape(levels, g_cols, g_rows, merged_width).transpose(0, 2, 1, 3)

    return merged, tokens_grad.reshape(tokens.shape), qkv_weight_grad, out_weight_grad


def solution(mesh):
    sizes = (mesh.shape["lat"], mesh.shape["lon"])
    in_specs = (P(None, "lat", "lon", None), P(), P(), P(), P(None, "lat", "lon", None))
    out_specs = (
        P(None, "lat", "lon", None),
        P(None, "lat", "lon", None),
        P(("lat", "lon"), None),
        P(("lat", "lon"), None),
    )
    return jax.shard_map(
        functools.partial(shards, sizes),
        mesh=mesh, in_specs=in_specs, out_specs=out_specs, check_vma=False,
    )
```

```python
import functools

import jax
import jax.numpy as jnp
import numpy as np
from jax import lax
from jax.experimental import pallas as pl
from jax.experimental.pallas import tpu as pltpu
from jax.sharding import PartitionSpec as P

HEADS = 32
WIN = 8
SHIFT = 4
LANES = 128
HALF = SHIFT // 2
TILE = 256
EPSILON = 1e-05
MIB = 1 << 20

NN = (((1,), (0,)), ((), ()))
NT = (((1,), (1,)), ((), ()))
TN = (((0,), (0,)), ((), ()))
BF16 = jnp.bfloat16
F32 = jnp.float32


def dot(a, b, dims=NN):
    return lax.dot_general(a, b, dims, preferred_element_type=F32)


def window_cells(levels, rows, columns):
    half = WIN // 2
    return [
        (level, wi * WIN + 2 * row + sub % 2, wj * WIN + 2 * column + sub // 2)
        for wi in range(rows // WIN) for wj in range(columns // WIN) for sub in range(4)
        for level in range(levels) for row in range(half) for column in range(half)
    ]


def window_groups(levels, rows, columns):
    half = WIN // 2
    return [
        (level, wi * half + row, wj * half + column)
        for wi in range(rows // half) for wj in range(columns // half)
        for level in range(levels) for row in range(half) for column in range(half)
    ]


def box(levels, rows, columns):
    return [(l, r, c) for l in range(levels) for r in rows for c in columns]


def turned_box(levels, rows, columns):
    return [(l, r, c) for l in range(levels) for c in columns for r in rows]


def padded(cells, step=16):
    return cells + [None] * (-len(cells) % step)


def picks(wanted, held):
    spot = {cell: i for i, cell in enumerate(held) if cell is not None}
    table = np.zeros((len(wanted), len(held)), np.float32)
    for i, cell in enumerate(wanted):
        if cell is not None:
            table[i, spot[cell]] = 1.0
    return jnp.asarray(table, BF16)


class Strips:
    def __init__(self, levels, rows, columns, width, cut):
        self.side = (box(levels, range(width, 2 * width), range(width))
                     + box(levels, range(2 * width, rows), range(width)))
        self.above = box(levels, range(width), range(width, columns))
        self.corner = box(levels, range(width), range(width))
        if not cut:
            self.side = box(levels, range(width, rows), range(width))

    @staticmethod
    def sent(cells, down, across):
        return [None if c is None else (c[0], c[1] + down, c[2] + across) for c in cells]


def head_masks():
    head = lax.broadcasted_iota(jnp.int32, (LANES, LANES), 1) // (LANES // 4)
    return [jnp.where(head == h, 1.0, 0.0).astype(BF16) for h in range(4)]


def region_bias(places, active):
    step = 2 * (WIN // 2)
    one = (lax.broadcasted_iota(jnp.int32, (places, places), 0) // step) % 2
    other = (lax.broadcasted_iota(jnp.int32, (places, places), 1) // step) % 2
    return jnp.where((one != other) & active, -1e30, 0.0)


def score_scale(channels):
    return float((channels // HEADS) ** -0.5 * np.log2(np.e))


def aligned(start, size, step=None):
    return pl.ds(pl.multiple_of(start, step or size), size)


def pack_kernel(tokens, merged_grad, pick_cells, pick_groups, side, above, corner):
    cells = dot(pick_cells[...], tokens[...]).astype(BF16)
    groups = dot(pick_groups[...], merged_grad[...]).astype(BF16)
    at, at_group = 0, 0
    for out, (count, extra) in zip((side, above, corner), strip_rows(pick_cells, pick_groups)):
        out[:count] = cells[at:at + count]
        out[count:] = groups[at_group:at_group + extra]
        at, at_group = at + count, at_group + extra


def strip_rows(pick_cells, pick_groups):
    levels = 2
    rows, columns = strip_rows.extent
    cells = [levels * (rows - SHIFT) * SHIFT, levels * SHIFT * (columns - SHIFT), levels * SHIFT * SHIFT]
    groups = [n // 4 + (-(n // 4)) % 16 for n in cells]
    return list(zip(cells, groups))


def forward_kernel(
    owner, edge, core, tokens, merged_grad, side, above, corner, order, group,
    wqkv_h, wout_h, wm_h,
    normed_h, normt_h, proj_h, dmr_h, dmm_h, grad_h, rstd, merged, out_mine, out_theirs,
    wqkv, wout, wm, source, xw, normed, normt, proj, mixture, inverse, subs, dsubs, cotangent,
    grad, dmr, dmm, turned, in_sem, out_sem,
):
    count, channels = xw.shape
    places = 2 * WIN * WIN
    windows = count // places
    per_row = windows // 2
    quarter = places // 4
    groups = count // 4
    devices = len(owner)
    block = channels // devices

    loads = [
        pltpu.make_async_copy(src, dst, in_sem.at[i])
        for i, (src, dst) in enumerate([(wqkv_h, wqkv), (wout_h, wout), (wm_h, wm)])
    ]
    for load in loads:
        load.start()
    stores = [
        pltpu.make_async_copy(src, dst, out_sem.at[i])
        for i, (src, dst) in enumerate(
            [(normed, normed_h), (proj, proj_h), (normt, normt_h),
             (grad, grad_h), (dmr, dmr_h), (dmm, dmm_h)]
        )
    ]

    (n_side, g_side), (n_above, g_above), (n_corner, g_corner) = strip_rows(None, None)
    half = count // 2
    line = half // (2 * WIN)
    cut = SHIFT * line
    side_cut = 2 * SHIFT * SHIFT
    blocks = [
        [tokens[:cut], tokens[half:half + cut], side[:side_cut], above[:n_above], corner[:n_corner]],
        [tokens[cut:cut + WIN * line], tokens[half + cut:half + cut + WIN * line], side[side_cut:n_side]],
    ]
    for wi in range(2):
        at = 0
        for piece in blocks[wi]:
            source[wi, at:at + piece.shape[0]] = piece
            at += piece.shape[0]
        if at < source.shape[1]:
            source[wi, at:] = jnp.zeros((source.shape[1] - at, channels), BF16)

    @pl.loop(0, windows)
    def _(w):
        rows = aligned(w * places, places)
        x = dot(order[rows], source[w // per_row])
        xw[rows] = x.astype(BF16)
        center = jnp.mean(x, axis=1, keepdims=True)
        moved = x - center
        scale = lax.rsqrt(jnp.mean(moved * moved, axis=1, keepdims=True) + EPSILON)
        rstd[rows] = jnp.broadcast_to(scale, (places, LANES))
        normed[rows] = (moved * scale).astype(BF16)

    stores[0].start()
    loads[0].wait()

    @pl.loop(0, wqkv.shape[1] // TILE)
    def _(n):
        columns = aligned(n * TILE, TILE)
        proj[:, columns] = dot(normed[...], wqkv[:, columns]).astype(BF16)

    stores[1].start()

    masks = head_masks()
    factor = score_scale(channels)

    edge_bias = region_bias(places, edge[0] == 1)
    held = jnp.concatenate(
        [merged_grad[...], side[n_side:], above[n_above:], corner[n_corner:]], axis=0
    )
    cotangent[...] = dot(group[...], held).astype(BF16)
    loads[2].wait()
    steps = channels // LANES
    per_step = 4 * channels // TILE // steps

    @pl.loop(0, steps)
    def _(g):
        lanes = aligned(g * LANES, LANES)
        key_lanes = aligned(channels + g * LANES, LANES)
        value_lanes = aligned(2 * channels + g * LANES, LANES)
        for w in range(windows):
            rows = slice(w * places, (w + 1) * places)
            q, k, v = proj[rows, lanes], proj[rows, key_lanes], proj[rows, value_lanes]
            scores = dot(q, jnp.concatenate([k * m for m in masks], axis=0), NT)
            parts = []
            for h in range(4):
                part = scores[:, h * places:(h + 1) * places] * factor
                if w < per_row:
                    part = part + edge_bias
                part = part - jnp.max(part, axis=1, keepdims=True)
                parts.append(jnp.exp2(part).astype(BF16))
            values = jnp.concatenate(
                [jnp.concatenate([v * m, m], axis=1) for m in masks], axis=0
            )
            summed = dot(jnp.concatenate(parts, axis=1), values)
            inv = 1.0 / summed[:, LANES:]
            inverse[rows, lanes] = inv
            mixture[rows, lanes] = (summed[:, :LANES] * inv).astype(BF16)
        for i in range(per_step):
            at = aligned((g * per_step + i) * TILE, TILE)
            dsubs[:, at] = dot(cotangent[...], wm[at], NT).astype(BF16)

    loads[1].wait()

    @pl.loop(0, channels // TILE)
    def _(n):
        columns = aligned(n * TILE, TILE)
        out = dot(mixture[...], wout[:, columns]) + xw[:, columns].astype(F32)
        out = out.astype(BF16)
        for w in range(windows):
            for s in range(4):
                at = w * places + s * quarter
                subs[s, w * quarter:(w + 1) * quarter, columns] = out[at:at + quarter]

    total = jnp.zeros((groups, 1), F32)
    for s in range(4):
        total += jnp.sum(subs[s].astype(F32), axis=1, keepdims=True)
    center = total / (4 * channels)
    total = jnp.zeros((groups, 1), F32)
    for s in range(4):
        moved = subs[s].astype(F32) - center
        total += jnp.sum(moved * moved, axis=1, keepdims=True)
    scale = lax.rsqrt(total / (4 * channels) + EPSILON)
    result = jnp.zeros((groups, wm.shape[1]), F32)
    for s in range(4):
        unit = ((subs[s].astype(F32) - center) * scale).astype(BF16)
        result += dot(unit, wm[s * channels:(s + 1) * channels])
    merged[...] = result.astype(BF16)

    mean_g = jnp.zeros((groups, 1), F32)
    mean_gx = jnp.zeros((groups, 1), F32)
    for s in range(4):
        d = dsubs[:, s * channels:(s + 1) * channels].astype(F32)
        mean_g += jnp.sum(d, axis=1, keepdims=True)
        mean_gx += jnp.sum(d * ((subs[s].astype(F32) - center) * scale), axis=1, keepdims=True)
    mean_g = mean_g / (4 * channels)
    mean_gx = mean_gx / (4 * channels)
    for s in range(4):
        unit = (subs[s].astype(F32) - center) * scale
        d = dsubs[:, s * channels:(s + 1) * channels].astype(F32)
        d = (scale * (d - mean_g - unit * mean_gx)).astype(BF16)
        for w in range(windows):
            at = w * places + s * quarter
            grad[at:at + quarter] = d[w * quarter:(w + 1) * quarter]
    stores[3].start()

    @pl.loop(0, channels // TILE)
    def _(n):
        columns = aligned(n * TILE, TILE)
        d = dot(grad[...], wout[columns], NT).astype(BF16).astype(F32)
        d = d * inverse[:, columns]
        dmr[:, columns] = d.astype(BF16)
        dmm[:, columns] = (-d * mixture[:, columns].astype(F32)).astype(BF16)

    stores[4].start()
    stores[5].start()

    def turn(field, out):
        @pl.loop(0, channels // TILE)
        def _(n):
            rows = aligned(n * TILE, TILE)
            turned[rows] = field[:, rows].T

        for d in range(devices):
            out[d * block:(d + 1) * block] = turned[owner[d] * block:(owner[d] + 1) * block]

    turn(normed, normt)
    stores[2].start()
    mixt = wqkv.at[:, :count]
    turn(mixture, mixt)
    own = aligned(core[0] * (channels // 2), channels // 2)
    other = aligned((1 - core[0]) * (channels // 2), channels // 2)

    @pl.loop(0, channels // TILE)
    def _(n):
        columns = aligned(n * TILE, TILE)
        out_mine[:, columns] = dot(mixt[own], grad[:, columns]).astype(BF16)
        out_theirs[:, columns] = dot(mixt[other], grad[:, columns]).astype(BF16)

    for store in stores:
        store.wait()


def backward_kernel(
    index, waits, *refs,
):
    (edge, core, proj_h, dmr_h, dmm_h, normt_h, pgrad_h, mine_h, theirs_h,
     held, normt, pgrad, mine, theirs, in_sem, sem, out_sem) = refs[waits:]
    _, count, width = held.shape
    channels = normt.shape[0]
    half = channels // 2
    places = 2 * WIN * WIN
    windows = count // places
    per_row = windows // 2
    masks = head_masks()
    factor = score_scale(channels)
    plain = (channels // HEADS) ** -0.5
    steps = width // TILE

    def loads(g):
        columns = aligned(g * TILE, TILE)
        for i in range(5):
            src = (proj_h, proj_h, proj_h, dmr_h, dmm_h)[i]
            start = (i * channels if i < 3 else 0) + index * width
            yield pltpu.make_async_copy(
                src.at[:, aligned(start + g * TILE, TILE)], held.at[i, :, columns], in_sem.at[g, i]
            )

    def stores(g):
        for i in range(3):
            columns = aligned(i * width + g * TILE, TILE)
            for j, (src, dst) in enumerate(((pgrad, pgrad_h), (mine, mine_h), (theirs, theirs_h))):
                yield pltpu.make_async_copy(src.at[:, columns], dst.at[:, columns], out_sem.at[g, i, j])

    for g in range(steps):
        for load in loads(g):
            load.start()
    turned_load = pltpu.make_async_copy(normt_h, normt, sem.at[0])
    turned_load.start()
    edge_bias = region_bias(places, edge[0] == 1)
    own = aligned(core[0] * half, half)
    other = aligned((1 - core[0]) * half, half)

    @pl.loop(0, steps)
    def _(g):
        for load in loads(g):
            load.wait()

        for part_of in range(TILE // LANES):
            lanes = aligned(g * TILE + part_of * LANES, LANES)
            for w in range(windows):
                rows = slice(w * places, (w + 1) * places)
                q, k, v, dm, dd = (held[i, rows, lanes] for i in range(5))
                keys = jnp.concatenate([k * m for m in masks], axis=0)
                scores = dot(keys, q, NT)
                values = jnp.concatenate(
                    [jnp.concatenate([v * m, m], axis=1) for m in masks], axis=0
                )
                slope = dot(values, jnp.concatenate([dm, dd], axis=1), NT)
                weights, slopes = [], []
                for h in range(4):
                    block = slice(h * places, (h + 1) * places)
                    part = scores[block] * factor
                    if w < per_row:
                        part = part + edge_bias
                    part = jnp.exp2(part - jnp.max(part, axis=0, keepdims=True))
                    weights.append(part.astype(BF16))
                    slopes.append((part * slope[block]).astype(BF16))
                dv = dot(
                    jnp.concatenate(weights, axis=1),
                    jnp.concatenate([dm * m for m in masks], axis=0),
                )
                dk = dot(
                    jnp.concatenate(slopes, axis=1),
                    jnp.concatenate([q * m for m in masks], axis=0),
                )
                dq = dot(jnp.concatenate(slopes, axis=0), keys, TN)
                at = g * TILE + part_of * LANES
                pgrad[rows, lanes] = (dq * plain).astype(BF16)
                pgrad[rows, aligned(width + at, LANES)] = (dk * plain).astype(BF16)
                pgrad[rows, aligned(2 * width + at, LANES)] = dv.astype(BF16)

        @pl.when(g == 0)
        def _():
            turned_load.wait()

        for i in range(3):
            columns = aligned(i * width + g * TILE, TILE)
            mine[:, columns] = dot(normt[own], pgrad[:, columns]).astype(BF16)
            theirs[:, columns] = dot(normt[other], pgrad[:, columns]).astype(BF16)
        for store in stores(g):
            store.start()

    for g in range(steps):
        for store in stores(g):
            store.wait()


def projection_loads(pgrads, wqkv_h, pgrad, wqkv, sem, start):
    width = pgrads[0].shape[1] // 3
    channels = pgrad.shape[1] // 3
    loads = [
        pltpu.make_async_copy(
            field.at[:, pl.ds(i * width, width)],
            pgrad.at[:, pl.ds(i * channels + c * width, width)], sem.at[c * 3 + i],
        )
        for c, field in enumerate(pgrads) for i in range(3)
    ]
    tiles = [
        pltpu.make_async_copy(
            wqkv_h.at[pl.ds(start + n * TILE, TILE)], wqkv.at[pl.ds(n * TILE, TILE)],
            sem.at[3 * len(pgrads) + n],
        )
        for n in range(wqkv.shape[0] // TILE)
    ]
    for load in loads + tiles:
        load.start()
    return loads, tiles


def input_first_kernel(pg0, pg1, wqkv_h, ngrad, pgrad, wqkv, sem):
    loads, tiles = projection_loads([pg0, pg1], wqkv_h, pgrad, wqkv, sem, 0)
    for load in loads:
        load.wait()
    for n, load in enumerate(tiles):
        load.wait()
        rows = pl.ds(n * TILE, TILE)
        ngrad[:, rows] = dot(pgrad[...], wqkv[rows], NT).astype(BF16)


def input_last_kernel(waits, *refs):
    (pg0, pg1, wqkv_h, nfirst_h, normed_h, rstd_h, grad_h, merged,
     pick_first, pick_last, pick_groups, full, side, below, corner,
     pgrad, wqkv, ngrad, normed, rstd, grad, sem, more_sem) = refs[waits:]
    count, channels = ngrad.shape
    half = channels // 2
    loads, tiles = projection_loads([pg0, pg1], wqkv_h, pgrad, wqkv, sem, half)
    more = [
        pltpu.make_async_copy(src, dst, more_sem.at[i])
        for i, (src, dst) in enumerate(
            [(nfirst_h, ngrad.at[:, pl.ds(0, half)]), (normed_h, normed), (rstd_h, rstd), (grad_h, grad)]
        )
    ]
    for load in more:
        load.start()
    for load in loads:
        load.wait()
    for n, load in enumerate(tiles):
        load.wait()
        ngrad[:, pl.ds(half + n * TILE, TILE)] = dot(
            pgrad[...], wqkv[pl.ds(n * TILE, TILE)], NT
        ).astype(BF16)
    for load in more:
        load.wait()
    places = 2 * WIN * WIN

    @pl.loop(0, count // places)
    def _(w):
        rows = aligned(w * places, places)
        d = ngrad[rows].astype(F32)
        unit = normed[rows].astype(F32)
        mean_d = jnp.mean(d, axis=1, keepdims=True)
        mean_dx = jnp.mean(d * unit, axis=1, keepdims=True)
        part = rstd[rows, :1] * (d - mean_d - unit * mean_dx)
        full[rows] = (part.astype(BF16).astype(F32) + grad[rows].astype(F32)).astype(BF16)

    (n_side, g_side), (n_above, g_above), (n_corner, g_corner) = strip_rows(None, None)
    side_cut = 2 * SHIFT * SHIFT
    first = dot(pick_first[...], full[:count // 2]).astype(BF16)
    last = dot(pick_last[...], full[count // 2:]).astype(BF16)
    groups = dot(pick_groups[...], merged[...]).astype(BF16)
    side[:side_cut] = first[:side_cut]
    side[side_cut:n_side] = last
    below[:n_above] = first[side_cut:side_cut + n_above]
    corner[:n_corner] = first[side_cut + n_above:]
    side[n_side:] = groups[:g_side]
    below[n_above:] = groups[g_side:g_side + g_above]
    corner[n_corner:] = groups[g_side + g_above:]


def unpack_kernel(full, merged, side, below, corner, pick_top, pick_middle, pick_bottom,
                  pick_groups, tokens_out, merged_out):
    count = full.shape[0]
    half = count // 2
    (n_side, _), (n_above, _), (n_corner, _) = strip_rows(None, None)
    side_cut = 2 * SHIFT * SHIFT
    line = half // (2 * WIN)
    pieces = [
        (pick_top, [full[:half], side[:side_cut]]),
        (pick_middle, [full[half:], side[side_cut:n_side]]),
        (pick_bottom, [below[:n_above], corner[:n_corner]]),
    ]
    at = 0
    for pick, held in pieces:
        rows = pick.shape[0] // 2
        out = dot(pick[...], jnp.concatenate(held, axis=0)).astype(BF16)
        for level in range(2):
            start = level * half + at
            tokens_out[start:start + rows] = out[level * rows:(level + 1) * rows]
        at += rows
    held = [merged[...], side[n_side:], below[n_above:], corner[n_corner:]]
    merged_out[...] = dot(pick_groups[...], jnp.concatenate(held, axis=0)).astype(BF16)


def sent(block, sizes, lat_step, lon_step):
    n_lat, n_lon = sizes
    route = [
        (a * n_lon + b, (a + lat_step) % n_lat * n_lon + (b + lon_step) % n_lon)
        for a in range(n_lat) for b in range(n_lon)
    ]
    return lax.ppermute(block, ("lat", "lon"), route)


def sent_strips(strips, sizes, step):
    side, lines, corner = strips
    return [sent(side, sizes, 0, step), sent(lines, sizes, step, 0), sent(corner, sizes, step, step)]


def device_rows(channels, sizes):
    n_lat, n_lon = sizes
    place = np.arange(n_lat * n_lon)
    chips = n_lon // 2
    return place % n_lat * n_lon + place // n_lat % chips * 2 + place // (n_lat * chips)


def core_step(theirs, sizes):
    n_lat, n_lon = sizes
    return lax.ppermute(theirs, ("lat", "lon"), [(i, i ^ 1) for i in range(n_lat * n_lon)])


def core_sum(mine, arrived):
    return (mine.astype(F32) + arrived.astype(F32)).astype(BF16)


def layer_step(total, sizes):
    cores = [list(range(c, sizes[1], 2)) for c in range(2)]
    return lax.all_to_all(total, "lon", 0, 0, axis_index_groups=cores, tiled=True)


def column_step(total, sizes):
    return lax.all_to_all(total, "lat", 0, 0, tiled=True)


def block_sum(blocks, count, dtype=BF16):
    blocks = blocks.reshape(count, blocks.shape[0] // count, blocks.shape[1]).astype(F32)
    return jnp.sum(blocks, axis=0).astype(dtype)


def shards(sizes, tokens, qkv_weight, out_weight, merge_weight, merged_grad):
    levels, lat_rows, lon_cols, channels = tokens.shape
    merged_width = merge_weight.shape[1]
    count = levels * lat_rows * lon_cols
    groups = count // 4
    half = channels // 2
    strip_rows.extent = (lat_rows, lon_cols)
    vmem = pl.BlockSpec(memory_space=pltpu.VMEM)
    smem = pl.BlockSpec(memory_space=pltpu.SMEM)
    hbm = pl.BlockSpec(memory_space=pl.ANY)
    pinned = pl.BlockSpec(memory_space=pltpu.HBM)

    def shape(*extent, dtype=BF16):
        return jax.ShapeDtypeStruct(extent, dtype)

    def settings(weight, limit=60):
        return dict(
            compiler_params=pltpu.CompilerParams(vmem_limit_bytes=limit * MIB),
            cost_estimate=pl.CostEstimate(
                flops=int(weight * 1e10), bytes_accessed=16 * MIB, transcendentals=0
            ),
        )

    g_rows, g_cols = lat_rows // 2, lon_cols // 2
    cells = window_cells(levels, lat_rows, lon_cols)
    grps = window_groups(levels, g_rows, g_cols)
    cs = Strips(levels, lat_rows, lon_cols, SHIFT, True)
    gs = Strips(levels, g_rows, g_cols, HALF, False)
    g_strips = [padded(gs.side), padded(gs.above), padded(gs.corner)]
    to = ((0, lon_cols), (lat_rows, 0), (lat_rows, lon_cols))
    g_to = ((0, g_cols), (g_rows, 0), (g_rows, g_cols))
    own_rows = range(SHIFT, SHIFT + lat_rows)
    own_cols = range(SHIFT, SHIFT + lon_cols)
    own = box(levels, own_rows, own_cols)
    g_own = turned_box(levels, range(HALF, HALF + g_rows), range(HALF, HALF + g_cols))
    half_cells = count // 2
    side_cut = levels * SHIFT * SHIFT
    sent_cells = sum((Strips.sent(s, *t) for s, t in zip((cs.side, cs.above, cs.corner), to)), [])
    sent_groups = sum((Strips.sent(s, *t) for s, t in zip(g_strips, g_to)), [])
    held_top = box(levels, range(SHIFT, 2 * SHIFT), own_cols) + cs.side[:side_cut] + cs.above + cs.corner
    held_low = box(levels, range(2 * SHIFT, lat_rows), own_cols) + cs.side[side_cut:]
    depth = max(len(held_top), len(held_low))
    depth += -depth % 16
    held_top += [None] * (depth - len(held_top))
    held_low += [None] * (depth - len(held_low))

    tokens_flat = tokens.reshape(count, channels)
    merged_grad_flat = merged_grad.transpose(0, 2, 1, 3).reshape(groups, merged_width)
    extents = [(n + g, channels) for n, g in strip_rows(None, None)]
    strips = pl.pallas_call(
        pack_kernel,
        out_shape=[shape(*e) for e in extents],
        in_specs=[vmem] * 4, out_specs=[vmem] * 3,
        name="pack_strips", **settings(1),
    )(tokens_flat, merged_grad_flat, picks(sent_cells, own), picks(sent_groups, g_own))
    strips = sent_strips(strips, sizes, 1)

    order = jnp.concatenate([picks(cells[:half_cells], held_top), picks(cells[half_cells:], held_low)])
    group = picks(grps, g_own + sum(g_strips, []))
    edge = (lax.axis_index("lat") == 0).astype(jnp.int32).reshape(1)
    core = (lax.axis_index("lon") % 2).astype(jnp.int32).reshape(1)
    owner = tuple(int(d) for d in device_rows(channels, sizes))

    wide = shape(count, channels)
    normed, normt, proj, dmr, dmm, grad, rstd, merged, out_mine, out_theirs = pl.pallas_call(
        functools.partial(forward_kernel, owner),
        out_shape=[
            wide, shape(channels, count), shape(count, 3 * channels), wide, wide, wide,
            shape(count, LANES, dtype=F32), shape(groups, merged_width),
            shape(half, channels), shape(half, channels),
        ],
        in_specs=[smem] * 2 + [vmem] * 7 + [hbm] * 3,
        out_specs=[hbm] * 6 + [vmem] * 4,
        scratch_shapes=[
            pltpu.VMEM(qkv_weight.shape, BF16),
            pltpu.VMEM(out_weight.shape, BF16),
            pltpu.VMEM(merge_weight.shape, BF16),
            pltpu.VMEM((2, depth, channels), BF16),
            pltpu.VMEM((count, channels), BF16),
            pltpu.VMEM((count, channels), BF16),
            pltpu.VMEM((channels, count), BF16),
            pltpu.VMEM((count, 3 * channels), BF16),
            pltpu.VMEM((count, channels), BF16),
            pltpu.VMEM((count, channels), F32),
            pltpu.VMEM((4, groups, channels), BF16),
            pltpu.VMEM((groups, 4 * channels), BF16),
            pltpu.VMEM((groups, merged_width), BF16),
            pltpu.VMEM((count, channels), BF16),
            pltpu.VMEM((count, channels), BF16),
            pltpu.VMEM((count, channels), BF16),
            pltpu.VMEM((channels, count), BF16),
            pltpu.SemaphoreType.DMA((3,)),
            pltpu.SemaphoreType.DMA((6,)),
        ],
        name="block_forward", **settings(30, 54),
    )(edge, core, tokens_flat, merged_grad_flat, *strips, order, group,
      qkv_weight, out_weight, merge_weight)

    halves = 2
    width = channels // halves
    steps = width // TILE

    def backward(index, after):
        return pl.pallas_call(
            functools.partial(backward_kernel, index, len(after)),
            out_shape=[shape(count, 3 * width), shape(half, 3 * width), shape(half, 3 * width)],
            in_specs=[hbm] * len(after) + [smem] * 2 + [pinned] * 4, out_specs=[hbm] * 3,
            scratch_shapes=[
                pltpu.VMEM((5, count, width), BF16),
                pltpu.VMEM((channels, count), BF16),
                pltpu.VMEM((count, 3 * width), BF16),
                pltpu.VMEM((half, 3 * width), BF16),
                pltpu.VMEM((half, 3 * width), BF16),
                pltpu.SemaphoreType.DMA((steps, 5)),
                pltpu.SemaphoreType.DMA((1,)),
                pltpu.SemaphoreType.DMA((steps, 3, 3)),
            ],
            name="attention_backward", **settings(15, 30),
        )(*after, edge, core, proj, dmr, dmm, normt)

    chips, layers = sizes[1] // 2, sizes[0]
    arrived = core_step(out_theirs, sizes)
    pg0, mine1, theirs1 = backward(0, [])
    total0 = core_sum(out_mine, arrived)
    blocks0 = layer_step(total0, sizes)
    arrived = core_step(theirs1, sizes)
    pg1, mine2, theirs2 = backward(1, [total0])
    total0 = block_sum(blocks0, chips)
    blocks0 = column_step(total0, sizes)
    total1 = core_sum(mine1, arrived)
    blocks1 = layer_step(total1, sizes)
    arrived = core_step(theirs2, sizes)

    in_scratch = [
        pltpu.VMEM((count, 3 * channels), BF16),
        pltpu.VMEM((half, 3 * channels), BF16),
    ]
    in_sems = pltpu.SemaphoreType.DMA((3 * halves + half // TILE,))
    nfirst = pl.pallas_call(
        input_first_kernel,
        out_shape=shape(count, half),
        in_specs=[hbm] * 3, out_specs=vmem,
        scratch_shapes=in_scratch + [in_sems],
        name="input_first", **settings(5, 30),
    )(pg0, pg1, qkv_weight)
    total2 = core_sum(mine2, arrived)
    blocks2 = layer_step(total2, sizes)
    after = [total1, total2]

    first_picks = picks(cs.side[:side_cut] + cs.above + cs.corner, cells[:half_cells])
    last_picks = picks(cs.side[side_cut:], cells[half_cells:])
    full, *strips = pl.pallas_call(
        functools.partial(input_last_kernel, len(after)),
        out_shape=[wide] + [shape(*e) for e in extents],
        in_specs=[hbm] * (len(after) + 7) + [vmem] * 4, out_specs=[vmem] * 4,
        scratch_shapes=in_scratch + [
            pltpu.VMEM((count, channels), BF16),
            pltpu.VMEM((count, channels), BF16),
            pltpu.VMEM((count, LANES), F32),
            pltpu.VMEM((count, channels), BF16),
            in_sems,
            pltpu.SemaphoreType.DMA((4,)),
        ],
        name="input_last", **settings(9, 36),
    )(*after, pg0, pg1, qkv_weight, nfirst, normed, rstd, grad, merged,
      first_picks, last_picks, picks(sum(g_strips, []), grps))
    strips = sent_strips(strips, sizes, -1)

    total1 = block_sum(blocks1, chips)
    blocks1 = column_step(total1, sizes)
    total2 = block_sum(blocks2, chips)
    blocks2 = column_step(total2, sizes)

    got = [Strips.sent(s, *t) for s, t in zip((cs.side, cs.above, cs.corner), to)]
    g_got = sum((Strips.sent(s, *t) for s, t in zip(g_strips, g_to)), [])
    tokens_grad, merged = pl.pallas_call(
        unpack_kernel,
        out_shape=[wide, shape(groups, merged_width)],
        in_specs=[vmem] * 9, out_specs=[vmem] * 2,
        name="unpack_strips", **settings(2),
    )(
        full, merged, *strips,
        picks(box(levels, range(SHIFT, 2 * SHIFT), own_cols), cells[:half_cells] + got[0][:side_cut]),
        picks(box(levels, range(2 * SHIFT, lat_rows), own_cols), cells[half_cells:] + got[0][side_cut:]),
        picks(box(levels, range(lat_rows, lat_rows + SHIFT), own_cols), got[1] + got[2]),
        picks(g_own, grps + g_got),
    )
    merged = merged.reshape(levels, g_cols, g_rows, merged_width).transpose(0, 2, 1, 3)

    out_weight_grad = block_sum(blocks0, layers, F32)
    parts = [block_sum(blocks1, layers, F32), block_sum(blocks2, layers, F32)]
    qkv_weight_grad = jnp.concatenate(
        [part[:, i * width:(i + 1) * width] for i in range(3) for part in parts], axis=1
    )
    return merged, tokens_grad.reshape(tokens.shape), qkv_weight_grad, out_weight_grad


def solution(mesh):
    sizes = (mesh.shape["lat"], mesh.shape["lon"])
    in_specs = (P(None, "lat", "lon", None), P(), P(), P(), P(None, "lat", "lon", None))
    out_specs = (
        P(None, "lat", "lon", None),
        P(None, "lat", "lon", None),
        P(("lat", "lon"), None),
        P(("lat", "lon"), None),
    )
    return jax.shard_map(
        functools.partial(shards, sizes),
        mesh=mesh, in_specs=in_specs, out_specs=out_specs, check_vma=False,
    )
```

```python
import functools

import jax
import jax.numpy as jnp
import numpy as np
from jax import lax
from jax.experimental import pallas as pl
from jax.experimental.pallas import tpu as pltpu
from jax.sharding import PartitionSpec as P

HEADS = 32
WIN = 8
SHIFT = 4
LANES = 128
HALF = SHIFT // 2
TILE = 256
EPSILON = 1e-05
MIB = 1 << 20

NN = (((1,), (0,)), ((), ()))
NT = (((1,), (1,)), ((), ()))
TN = (((0,), (0,)), ((), ()))
BF16 = jnp.bfloat16
F32 = jnp.float32


def dot(a, b, dims=NN):
    return lax.dot_general(a, b, dims, preferred_element_type=F32)


def window_cells(levels, rows, columns):
    half = WIN // 2
    return [
        (level, wi * WIN + 2 * row + sub % 2, wj * WIN + 2 * column + sub // 2)
        for wi in range(rows // WIN) for wj in range(columns // WIN) for sub in range(4)
        for level in range(levels) for row in range(half) for column in range(half)
    ]


def window_groups(levels, rows, columns):
    half = WIN // 2
    return [
        (level, wi * half + row, wj * half + column)
        for wi in range(rows // half) for wj in range(columns // half)
        for level in range(levels) for row in range(half) for column in range(half)
    ]


def box(levels, rows, columns):
    return [(l, r, c) for l in range(levels) for r in rows for c in columns]


def turned_box(levels, rows, columns):
    return [(l, r, c) for l in range(levels) for c in columns for r in rows]


def padded(cells, step=16):
    return cells + [None] * (-len(cells) % step)


def picks(wanted, held):
    spot = {cell: i for i, cell in enumerate(held) if cell is not None}
    table = np.zeros((len(wanted), len(held)), np.float32)
    for i, cell in enumerate(wanted):
        if cell is not None:
            table[i, spot[cell]] = 1.0
    return jnp.asarray(table, BF16)


class Strips:
    def __init__(self, levels, rows, columns, width, cut):
        self.side = (box(levels, range(width, 2 * width), range(width))
                     + box(levels, range(2 * width, rows), range(width)))
        self.above = box(levels, range(width), range(width, columns))
        self.corner = box(levels, range(width), range(width))
        if not cut:
            self.side = box(levels, range(width, rows), range(width))

    @staticmethod
    def sent(cells, down, across):
        return [None if c is None else (c[0], c[1] + down, c[2] + across) for c in cells]


def head_masks():
    head = lax.broadcasted_iota(jnp.int32, (LANES, LANES), 1) // (LANES // 4)
    return [jnp.where(head == h, 1.0, 0.0).astype(BF16) for h in range(4)]


def region_bias(places, active):
    step = 2 * (WIN // 2)
    one = (lax.broadcasted_iota(jnp.int32, (places, places), 0) // step) % 2
    other = (lax.broadcasted_iota(jnp.int32, (places, places), 1) // step) % 2
    return jnp.where((one != other) & active, -1e30, 0.0)


def score_scale(channels):
    return float((channels // HEADS) ** -0.5 * np.log2(np.e))


def aligned(start, size, step=None):
    return pl.ds(pl.multiple_of(start, step or size), size)


def pack_kernel(tokens, merged_grad, pick_cells, pick_groups, side, above, corner):
    cells = dot(pick_cells[...], tokens[...]).astype(BF16)
    groups = dot(pick_groups[...], merged_grad[...]).astype(BF16)
    at, at_group = 0, 0
    for out, (count, extra) in zip((side, above, corner), strip_rows(pick_cells, pick_groups)):
        out[:count] = cells[at:at + count]
        out[count:] = groups[at_group:at_group + extra]
        at, at_group = at + count, at_group + extra


def strip_rows(pick_cells, pick_groups):
    levels = 2
    rows, columns = strip_rows.extent
    cells = [levels * (rows - SHIFT) * SHIFT, levels * SHIFT * (columns - SHIFT), levels * SHIFT * SHIFT]
    groups = [n // 4 + (-(n // 4)) % 16 for n in cells]
    return list(zip(cells, groups))


def forward_kernel(
    edge, owner, tokens, merged_grad, side, above, corner, order, group, rowmap,
    wqkv_h, wout_h, wm_h,
    normed_h, normt_h, proj_h, dmr_h, dmm_h, grad_h, rstd, merged, out_mine, out_theirs,
    wqkv, wout, wm, source, xw, normed, normt, proj, mixture, inverse, subs, dsubs, cotangent,
    grad, dmr, dmm, turned, in_sem, out_sem,
):
    count, channels = xw.shape
    places = 2 * WIN * WIN
    windows = count // places
    per_row = windows // 2
    quarter = places // 4
    groups = count // 4
    devices = owner.shape[0]
    block = channels // devices

    loads = [
        pltpu.make_async_copy(src, dst, in_sem.at[i])
        for i, (src, dst) in enumerate([(wqkv_h, wqkv), (wout_h, wout), (wm_h, wm)])
    ]
    for load in loads:
        load.start()
    stores = [
        pltpu.make_async_copy(src, dst, out_sem.at[i])
        for i, (src, dst) in enumerate(
            [(normed, normed_h), (proj, proj_h), (normt, normt_h),
             (grad, grad_h), (dmr, dmr_h), (dmm, dmm_h)]
        )
    ]

    (n_side, g_side), (n_above, g_above), (n_corner, g_corner) = strip_rows(None, None)
    half = count // 2
    line = half // (2 * WIN)
    cut = SHIFT * line
    side_cut = 2 * SHIFT * SHIFT
    blocks = [
        [tokens[:cut], tokens[half:half + cut], side[:side_cut], above[:n_above], corner[:n_corner]],
        [tokens[cut:cut + WIN * line], tokens[half + cut:half + cut + WIN * line], side[side_cut:n_side]],
    ]
    for wi in range(2):
        at = 0
        for piece in blocks[wi]:
            source[wi, at:at + piece.shape[0]] = piece
            at += piece.shape[0]
        if at < source.shape[1]:
            source[wi, at:] = jnp.zeros((source.shape[1] - at, channels), BF16)

    @pl.loop(0, windows)
    def _(w):
        rows = aligned(w * places, places)
        x = dot(order[rows], source[w // per_row])
        xw[rows] = x.astype(BF16)
        center = jnp.mean(x, axis=1, keepdims=True)
        moved = x - center
        scale = lax.rsqrt(jnp.mean(moved * moved, axis=1, keepdims=True) + EPSILON)
        rstd[rows] = jnp.broadcast_to(scale, (places, LANES))
        normed[rows] = (moved * scale).astype(BF16)

    stores[0].start()
    loads[0].wait()

    @pl.loop(0, wqkv.shape[1] // TILE)
    def _(n):
        columns = aligned(n * TILE, TILE)
        proj[:, columns] = dot(normed[...], wqkv[:, columns]).astype(BF16)

    stores[1].start()

    masks = head_masks()
    factor = score_scale(channels)

    edge_bias = region_bias(places, edge[0] == 1)
    held = jnp.concatenate(
        [merged_grad[...], side[n_side:], above[n_above:], corner[n_corner:]], axis=0
    )
    cotangent[...] = dot(group[...], held).astype(BF16)
    loads[2].wait()
    steps = channels // LANES
    per_step = 4 * channels // TILE // steps

    @pl.loop(0, steps)
    def _(g):
        lanes = aligned(g * LANES, LANES)
        key_lanes = aligned(channels + g * LANES, LANES)
        value_lanes = aligned(2 * channels + g * LANES, LANES)
        for w in range(windows):
            rows = slice(w * places, (w + 1) * places)
            q, k, v = proj[rows, lanes], proj[rows, key_lanes], proj[rows, value_lanes]
            scores = dot(q, jnp.concatenate([k * m for m in masks], axis=0), NT)
            parts = []
            for h in range(4):
                part = scores[:, h * places:(h + 1) * places] * factor
                if w < per_row:
                    part = part + edge_bias
                part = part - jnp.max(part, axis=1, keepdims=True)
                parts.append(jnp.exp2(part).astype(BF16))
            values = jnp.concatenate(
                [jnp.concatenate([v * m, m], axis=1) for m in masks], axis=0
            )
            summed = dot(jnp.concatenate(parts, axis=1), values)
            inv = 1.0 / summed[:, LANES:]
            inverse[rows, lanes] = inv
            mixture[rows, lanes] = (summed[:, :LANES] * inv).astype(BF16)
        for i in range(per_step):
            at = aligned((g * per_step + i) * TILE, TILE)
            dsubs[:, at] = dot(cotangent[...], wm[at], NT).astype(BF16)

    loads[1].wait()

    @pl.loop(0, channels // TILE)
    def _(n):
        columns = aligned(n * TILE, TILE)
        out = dot(mixture[...], wout[:, columns]) + xw[:, columns].astype(F32)
        out = out.astype(BF16)
        for w in range(windows):
            for s in range(4):
                at = w * places + s * quarter
                subs[s, w * quarter:(w + 1) * quarter, columns] = out[at:at + quarter]

    total = jnp.zeros((groups, 1), F32)
    for s in range(4):
        total += jnp.sum(subs[s].astype(F32), axis=1, keepdims=True)
    center = total / (4 * channels)
    total = jnp.zeros((groups, 1), F32)
    for s in range(4):
        moved = subs[s].astype(F32) - center
        total += jnp.sum(moved * moved, axis=1, keepdims=True)
    scale = lax.rsqrt(total / (4 * channels) + EPSILON)
    result = jnp.zeros((groups, wm.shape[1]), F32)
    for s in range(4):
        unit = ((subs[s].astype(F32) - center) * scale).astype(BF16)
        result += dot(unit, wm[s * channels:(s + 1) * channels])
    merged[...] = result.astype(BF16)

    mean_g = jnp.zeros((groups, 1), F32)
    mean_gx = jnp.zeros((groups, 1), F32)
    for s in range(4):
        d = dsubs[:, s * channels:(s + 1) * channels].astype(F32)
        mean_g += jnp.sum(d, axis=1, keepdims=True)
        mean_gx += jnp.sum(d * ((subs[s].astype(F32) - center) * scale), axis=1, keepdims=True)
    mean_g = mean_g / (4 * channels)
    mean_gx = mean_gx / (4 * channels)
    for s in range(4):
        unit = (subs[s].astype(F32) - center) * scale
        d = dsubs[:, s * channels:(s + 1) * channels].astype(F32)
        d = (scale * (d - mean_g - unit * mean_gx)).astype(BF16)
        for w in range(windows):
            at = w * places + s * quarter
            grad[at:at + quarter] = d[w * quarter:(w + 1) * quarter]
    stores[3].start()

    @pl.loop(0, channels // TILE)
    def _(n):
        columns = aligned(n * TILE, TILE)
        d = dot(grad[...], wout[columns], NT).astype(BF16).astype(F32)
        d = d * inverse[:, columns]
        dmr[:, columns] = d.astype(BF16)
        dmm[:, columns] = (-d * mixture[:, columns].astype(F32)).astype(BF16)

    stores[4].start()
    stores[5].start()

    def turn(field, out):
        if block % 16:
            @pl.loop(0, channels // TILE)
            def _(n):
                rows = aligned(n * TILE, TILE)
                spot = lax.broadcasted_iota(jnp.int32, (TILE, channels), 1)
                pick = jnp.where(spot == rowmap[rows], 1.0, 0.0).astype(BF16)
                out[rows] = dot(pick, field[...], NT).astype(BF16)
        else:
            @pl.loop(0, channels // TILE)
            def _(n):
                rows = aligned(n * TILE, TILE)
                turned[rows] = field[:, rows].T

            for d in range(devices):
                out[d * block:(d + 1) * block] = turned[aligned(owner[d] * block, block)]

    turn(normed, normt)
    stores[2].start()
    mixt = wqkv.at[:, :count]
    turn(mixture, mixt)
    part = channels // 2

    @pl.loop(0, channels // TILE)
    def _(n):
        columns = aligned(n * TILE, TILE)
        out_mine[:, columns] = dot(mixt[:part], grad[:, columns]).astype(BF16)
        out_theirs[:, columns] = dot(mixt[part:], grad[:, columns]).astype(BF16)

    for store in stores:
        store.wait()


def backward_kernel(index, *refs):
    (edge, proj_h, dmr_h, dmm_h, normt_h, pgrad_h, mine_h, theirs_h,
     held, normt, pgrad, mine, theirs, in_sem, sem, out_sem) = refs
    _, count, width = held.shape
    channels = normt.shape[0]
    half = channels // 2
    places = 2 * WIN * WIN
    windows = count // places
    per_row = windows // 2
    masks = head_masks()
    factor = score_scale(channels)
    plain = (channels // HEADS) ** -0.5
    steps = width // TILE

    def loads(g):
        columns = aligned(g * TILE, TILE)
        for i in range(5):
            src = (proj_h, proj_h, proj_h, dmr_h, dmm_h)[i]
            start = (i * channels if i < 3 else 0) + index * width
            yield pltpu.make_async_copy(
                src.at[:, aligned(start + g * TILE, TILE)], held.at[i, :, columns], in_sem.at[g, i]
            )

    def stores(g):
        for i in range(3):
            columns = aligned(i * width + g * TILE, TILE)
            for j, (src, dst) in enumerate(((pgrad, pgrad_h), (mine, mine_h), (theirs, theirs_h))):
                yield pltpu.make_async_copy(src.at[:, columns], dst.at[:, columns], out_sem.at[g, i, j])

    for g in range(steps):
        for load in loads(g):
            load.start()
    turned_load = pltpu.make_async_copy(normt_h, normt, sem.at[0])
    turned_load.start()
    edge_bias = region_bias(places, edge[0] == 1)

    @pl.loop(0, steps)
    def _(g):
        for load in loads(g):
            load.wait()

        for part_of in range(TILE // LANES):
            lanes = aligned(g * TILE + part_of * LANES, LANES)
            for w in range(windows):
                rows = slice(w * places, (w + 1) * places)
                q, k, v, dm, dd = (held[i, rows, lanes] for i in range(5))
                keys = jnp.concatenate([k * m for m in masks], axis=0)
                scores = dot(keys, q, NT)
                values = jnp.concatenate(
                    [jnp.concatenate([v * m, m], axis=1) for m in masks], axis=0
                )
                slope = dot(values, jnp.concatenate([dm, dd], axis=1), NT)
                weights, slopes = [], []
                for h in range(4):
                    block = slice(h * places, (h + 1) * places)
                    part = scores[block] * factor
                    if w < per_row:
                        part = part + edge_bias
                    part = jnp.exp2(part - jnp.max(part, axis=0, keepdims=True))
                    weights.append(part.astype(BF16))
                    slopes.append((part * slope[block]).astype(BF16))
                dv = dot(
                    jnp.concatenate(weights, axis=1),
                    jnp.concatenate([dm * m for m in masks], axis=0),
                )
                dk = dot(
                    jnp.concatenate(slopes, axis=1),
                    jnp.concatenate([q * m for m in masks], axis=0),
                )
                dq = dot(jnp.concatenate(slopes, axis=0), keys, TN)
                at = g * TILE + part_of * LANES
                pgrad[rows, lanes] = (dq * plain).astype(BF16)
                pgrad[rows, aligned(width + at, LANES)] = (dk * plain).astype(BF16)
                pgrad[rows, aligned(2 * width + at, LANES)] = dv.astype(BF16)

        @pl.when(g == 0)
        def _():
            turned_load.wait()

        for i in range(3):
            columns = aligned(i * width + g * TILE, TILE)
            mine[:, columns] = dot(normt[:half], pgrad[:, columns]).astype(BF16)
            theirs[:, columns] = dot(normt[half:], pgrad[:, columns]).astype(BF16)
        for store in stores(g):
            store.start()

    for g in range(steps):
        for store in stores(g):
            store.wait()


def projection_loads(pgrads, wqkv_h, pgrad, wqkv, sem, start):
    width = pgrads[0].shape[1] // 3
    channels = pgrad.shape[1] // 3
    loads = [
        pltpu.make_async_copy(
            field.at[:, pl.ds(i * width, width)],
            pgrad.at[:, pl.ds(i * channels + c * width, width)], sem.at[c * 3 + i],
        )
        for c, field in enumerate(pgrads) for i in range(3)
    ]
    tiles = [
        pltpu.make_async_copy(
            wqkv_h.at[pl.ds(start + n * TILE, TILE)], wqkv.at[pl.ds(n * TILE, TILE)],
            sem.at[3 * len(pgrads) + n],
        )
        for n in range(wqkv.shape[0] // TILE)
    ]
    for load in loads + tiles:
        load.start()
    return loads, tiles


def input_first_kernel(pg0, pg1, wqkv_h, ngrad, pgrad, wqkv, sem):
    loads, tiles = projection_loads([pg0, pg1], wqkv_h, pgrad, wqkv, sem, 0)
    for load in loads:
        load.wait()
    for n, load in enumerate(tiles):
        load.wait()
        rows = pl.ds(n * TILE, TILE)
        ngrad[:, rows] = dot(pgrad[...], wqkv[rows], NT).astype(BF16)


def input_last_kernel(*refs):
    (pg0, pg1, wqkv_h, nfirst_h, normed_h, rstd_h, grad_h, merged,
     pick_first, pick_last, pick_groups, full, side, below, corner,
     pgrad, wqkv, ngrad, normed, rstd, grad, sem, more_sem) = refs
    count, channels = ngrad.shape
    half = channels // 2
    loads, tiles = projection_loads([pg0, pg1], wqkv_h, pgrad, wqkv, sem, half)
    more = [
        pltpu.make_async_copy(src, dst, more_sem.at[i])
        for i, (src, dst) in enumerate(
            [(nfirst_h, ngrad.at[:, pl.ds(0, half)]), (normed_h, normed), (rstd_h, rstd), (grad_h, grad)]
        )
    ]
    for load in more:
        load.start()
    for load in loads:
        load.wait()
    for n, load in enumerate(tiles):
        load.wait()
        ngrad[:, pl.ds(half + n * TILE, TILE)] = dot(
            pgrad[...], wqkv[pl.ds(n * TILE, TILE)], NT
        ).astype(BF16)
    for load in more:
        load.wait()
    places = 2 * WIN * WIN

    @pl.loop(0, count // places)
    def _(w):
        rows = aligned(w * places, places)
        d = ngrad[rows].astype(F32)
        unit = normed[rows].astype(F32)
        mean_d = jnp.mean(d, axis=1, keepdims=True)
        mean_dx = jnp.mean(d * unit, axis=1, keepdims=True)
        part = rstd[rows, :1] * (d - mean_d - unit * mean_dx)
        full[rows] = (part.astype(BF16).astype(F32) + grad[rows].astype(F32)).astype(BF16)

    (n_side, g_side), (n_above, g_above), (n_corner, g_corner) = strip_rows(None, None)
    side_cut = 2 * SHIFT * SHIFT
    first = dot(pick_first[...], full[:count // 2]).astype(BF16)
    last = dot(pick_last[...], full[count // 2:]).astype(BF16)
    groups = dot(pick_groups[...], merged[...]).astype(BF16)
    side[:side_cut] = first[:side_cut]
    side[side_cut:n_side] = last
    below[:n_above] = first[side_cut:side_cut + n_above]
    corner[:n_corner] = first[side_cut + n_above:]
    side[n_side:] = groups[:g_side]
    below[n_above:] = groups[g_side:g_side + g_above]
    corner[n_corner:] = groups[g_side + g_above:]


def unpack_kernel(full, merged, side, below, corner, pick_top, pick_middle, pick_bottom,
                  pick_groups, tokens_out, merged_out):
    count = full.shape[0]
    half = count // 2
    (n_side, _), (n_above, _), (n_corner, _) = strip_rows(None, None)
    side_cut = 2 * SHIFT * SHIFT
    line = half // (2 * WIN)
    pieces = [
        (pick_top, [full[:half], side[:side_cut]]),
        (pick_middle, [full[half:], side[side_cut:n_side]]),
        (pick_bottom, [below[:n_above], corner[:n_corner]]),
    ]
    at = 0
    for pick, held in pieces:
        rows = pick.shape[0] // 2
        out = dot(pick[...], jnp.concatenate(held, axis=0)).astype(BF16)
        for level in range(2):
            start = level * half + at
            tokens_out[start:start + rows] = out[level * rows:(level + 1) * rows]
        at += rows
    held = [merged[...], side[n_side:], below[n_above:], corner[n_corner:]]
    merged_out[...] = dot(pick_groups[...], jnp.concatenate(held, axis=0)).astype(BF16)


def sent(block, sizes, lat_step, lon_step):
    n_lat, n_lon = sizes
    route = [
        (a * n_lon + b, (a + lat_step) % n_lat * n_lon + (b + lon_step) % n_lon)
        for a in range(n_lat) for b in range(n_lon)
    ]
    return lax.ppermute(block, ("lat", "lon"), route)


def sent_strips(strips, sizes, step):
    side, lines, corner = strips
    return [sent(side, sizes, 0, step), sent(lines, sizes, step, 0), sent(corner, sizes, step, step)]


def bit_list(count):
    return [1 << i for i in range(count.bit_length() - 1)]


def device_rows(channels, sizes):
    n_lat, n_lon = sizes
    devices = n_lat * n_lon
    rows = channels // devices
    place = np.arange(devices)
    partner = np.zeros_like(place)
    for i, bit in enumerate(bit_list(devices)):
        partner |= np.where(place & (devices >> (i + 1)), bit, 0)
    me = (lax.axis_index("lat") * n_lon + lax.axis_index("lon")).astype(jnp.int32)
    owner = jnp.bitwise_xor(jnp.asarray(partner, jnp.int32), me)
    rowmap = owner[:, None] * rows + jnp.arange(rows, dtype=jnp.int32)[None, :]
    return owner, rowmap.reshape(channels, 1)


def exchange(block, sizes, bit):
    devices = sizes[0] * sizes[1]
    return lax.ppermute(block, ("lat", "lon"), [(i, i ^ bit) for i in range(devices)])


def added(a, b, zero, dtype=BF16):
    return (a.astype(F32) + b.astype(F32) + zero).astype(dtype)


class Sum:
    def __init__(self, mine, theirs, sizes):
        self.sizes, self.mine, self.theirs, self.zero = sizes, mine, theirs, 0.0
        self.bits = bit_list(sizes[0] * sizes[1])[1:]
        layer = bit_list(sizes[1])[1:]
        self.turns = [layer, layer[1:] + layer[:1]]
        self.column = [sizes[1] * b for b in bit_list(sizes[0])]

    def send_core(self):
        self.arrived = exchange(self.theirs, self.sizes, 1)

    def split(self, parts):
        self.kept, given = [], []
        for i, part in enumerate(parts):
            axis = self.bits_of[i].index(self.turns[i][0])
            self.kept.append(lax.index_in_dim(part, 0, axis, keepdims=False))
            given.append(lax.index_in_dim(part, 1, axis, keepdims=False))
        return given

    def send(self, given):
        self.arrived = []
        for i, block in enumerate(given):
            bit = self.turns[i][0]
            self.arrived.append(exchange(block, self.sizes, bit))
            self.turns[i] = self.turns[i][1:]
            self.bits_of[i] = [b for b in self.bits_of[i] if b != bit]

    def first(self):
        total = added(self.mine, self.arrived, self.zero)
        columns = total.shape[1] // 2
        rows = total.shape[0] >> len(self.bits)
        self.bits_of = [list(self.bits), list(self.bits)]
        return self.split([
            total[:, i * columns:(i + 1) * columns].reshape([2] * len(self.bits) + [rows, columns])
            for i in range(2)
        ])

    def next(self):
        parts = [added(k, a, self.zero) for k, a in zip(self.kept, self.arrived)]
        if not self.turns[0]:
            parts = [jnp.concatenate(parts, axis=-1)]
            self.turns, self.bits_of = [self.column], [self.bits_of[0]]
        return self.split(parts)

    def rest(self):
        while self.turns[0] or len(self.turns) > 1:
            self.send(self.next())
        return added(self.kept[0], self.arrived[0], self.zero, F32)


def tied_call(kernel, after, operands, in_specs, out_shape, out_specs, **rest):
    waits = len(after)
    reads = waits + len(operands)

    def body(*refs):
        refs[reads][...] = jnp.zeros_like(refs[reads])
        kernel(*refs[waits:reads], *refs[reads + 1:])

    zero, *out = pl.pallas_call(
        body,
        out_shape=[jax.ShapeDtypeStruct((8, LANES), F32)] + out_shape,
        in_specs=[pl.BlockSpec(memory_space=pl.ANY)] * waits + in_specs,
        out_specs=[pl.BlockSpec(memory_space=pltpu.VMEM)] + out_specs,
        **rest,
    )(*after, *operands)
    return zero[0, 0], out


def shards(sizes, tokens, qkv_weight, out_weight, merge_weight, merged_grad):
    levels, lat_rows, lon_cols, channels = tokens.shape
    merged_width = merge_weight.shape[1]
    count = levels * lat_rows * lon_cols
    groups = count // 4
    half = channels // 2
    strip_rows.extent = (lat_rows, lon_cols)
    vmem = pl.BlockSpec(memory_space=pltpu.VMEM)
    smem = pl.BlockSpec(memory_space=pltpu.SMEM)
    hbm = pl.BlockSpec(memory_space=pl.ANY)

    def shape(*extent, dtype=BF16):
        return jax.ShapeDtypeStruct(extent, dtype)

    def settings(weight, limit=60):
        return dict(
            compiler_params=pltpu.CompilerParams(vmem_limit_bytes=limit * MIB),
            cost_estimate=pl.CostEstimate(
                flops=int(weight * 1e10), bytes_accessed=16 * MIB, transcendentals=0
            ),
        )

    g_rows, g_cols = lat_rows // 2, lon_cols // 2
    cells = window_cells(levels, lat_rows, lon_cols)
    grps = window_groups(levels, g_rows, g_cols)
    cs = Strips(levels, lat_rows, lon_cols, SHIFT, True)
    gs = Strips(levels, g_rows, g_cols, HALF, False)
    g_strips = [padded(gs.side), padded(gs.above), padded(gs.corner)]
    to = ((0, lon_cols), (lat_rows, 0), (lat_rows, lon_cols))
    g_to = ((0, g_cols), (g_rows, 0), (g_rows, g_cols))
    own_rows = range(SHIFT, SHIFT + lat_rows)
    own_cols = range(SHIFT, SHIFT + lon_cols)
    own = box(levels, own_rows, own_cols)
    g_own = turned_box(levels, range(HALF, HALF + g_rows), range(HALF, HALF + g_cols))
    half_cells = count // 2
    side_cut = levels * SHIFT * SHIFT
    sent_cells = sum((Strips.sent(s, *t) for s, t in zip((cs.side, cs.above, cs.corner), to)), [])
    sent_groups = sum((Strips.sent(s, *t) for s, t in zip(g_strips, g_to)), [])
    held_top = box(levels, range(SHIFT, 2 * SHIFT), own_cols) + cs.side[:side_cut] + cs.above + cs.corner
    held_low = box(levels, range(2 * SHIFT, lat_rows), own_cols) + cs.side[side_cut:]
    depth = max(len(held_top), len(held_low))
    depth += -depth % 16
    held_top += [None] * (depth - len(held_top))
    held_low += [None] * (depth - len(held_low))

    tokens_flat = tokens.reshape(count, channels)
    merged_grad_flat = merged_grad.transpose(0, 2, 1, 3).reshape(groups, merged_width)
    extents = [(n + g, channels) for n, g in strip_rows(None, None)]
    strips = pl.pallas_call(
        pack_kernel,
        out_shape=[shape(*e) for e in extents],
        in_specs=[vmem] * 4, out_specs=[vmem] * 3,
        name="pack_strips", **settings(1),
    )(tokens_flat, merged_grad_flat, picks(sent_cells, own), picks(sent_groups, g_own))
    strips = sent_strips(strips, sizes, 1)

    order = jnp.concatenate([picks(cells[:half_cells], held_top), picks(cells[half_cells:], held_low)])
    group = picks(grps, g_own + sum(g_strips, []))
    edge = (lax.axis_index("lat") == 0).astype(jnp.int32).reshape(1)
    owner, rowmap = device_rows(channels, sizes)

    wide = shape(count, channels)
    normed, normt, proj, dmr, dmm, grad, rstd, merged, out_mine, out_theirs = pl.pallas_call(
        forward_kernel,
        out_shape=[
            wide, shape(channels, count), shape(count, 3 * channels), wide, wide, wide,
            shape(count, LANES, dtype=F32), shape(groups, merged_width),
            shape(half, channels), shape(half, channels),
        ],
        in_specs=[smem] * 2 + [vmem] * 8 + [hbm] * 3,
        out_specs=[hbm] * 6 + [vmem] * 4,
        scratch_shapes=[
            pltpu.VMEM(qkv_weight.shape, BF16),
            pltpu.VMEM(out_weight.shape, BF16),
            pltpu.VMEM(merge_weight.shape, BF16),
            pltpu.VMEM((2, depth, channels), BF16),
            pltpu.VMEM((count, channels), BF16),
            pltpu.VMEM((count, channels), BF16),
            pltpu.VMEM((channels, count), BF16),
            pltpu.VMEM((count, 3 * channels), BF16),
            pltpu.VMEM((count, channels), BF16),
            pltpu.VMEM((count, channels), F32),
            pltpu.VMEM((4, groups, channels), BF16),
            pltpu.VMEM((groups, 4 * channels), BF16),
            pltpu.VMEM((groups, merged_width), BF16),
            pltpu.VMEM((count, channels), BF16),
            pltpu.VMEM((count, channels), BF16),
            pltpu.VMEM((count, channels), BF16),
            pltpu.VMEM((channels, count), BF16),
            pltpu.SemaphoreType.DMA((3,)),
            pltpu.SemaphoreType.DMA((6,)),
        ],
        name="block_forward", **settings(30, 58),
    )(edge, owner, tokens_flat, merged_grad_flat, *strips, order, group, rowmap,
      qkv_weight, out_weight, merge_weight)

    halves = 2
    width = channels // halves
    steps = width // TILE

    def backward(index, after):
        return tied_call(
            functools.partial(backward_kernel, index), after,
            [edge, proj, dmr, dmm, normt], [smem] + [hbm] * 4,
            [shape(count, 3 * width), shape(half, 3 * width), shape(half, 3 * width)], [hbm] * 3,
            scratch_shapes=[
                pltpu.VMEM((5, count, width), BF16),
                pltpu.VMEM((channels, count), BF16),
                pltpu.VMEM((count, 3 * width), BF16),
                pltpu.VMEM((half, 3 * width), BF16),
                pltpu.VMEM((half, 3 * width), BF16),
                pltpu.SemaphoreType.DMA((steps, 5)),
                pltpu.SemaphoreType.DMA((1,)),
                pltpu.SemaphoreType.DMA((steps, 3, 3)),
            ],
            name="attention_backward", **settings(15, 48),
        )

    out_sum = Sum(out_mine, out_theirs, sizes)
    out_sum.send_core()
    out_sum.zero, (pg0, mine, theirs) = backward(0, [])
    given = out_sum.first()
    out_sum.send(given)
    first_sum = Sum(mine, theirs, sizes)
    first_sum.send_core()
    zero, (pg1, mine, theirs) = backward(1, given)
    first_sum.zero = out_sum.zero = zero
    after = out_sum.next()
    out_sum.send(after)
    given = first_sum.first()
    first_sum.send(given)
    last_sum = Sum(mine, theirs, sizes)
    last_sum.send_core()
    after = after + given

    in_scratch = [
        pltpu.VMEM((count, 3 * channels), BF16),
        pltpu.VMEM((half, 3 * channels), BF16),
    ]
    in_sems = pltpu.SemaphoreType.DMA((3 * halves + half // TILE,))
    zero, [nfirst] = tied_call(
        input_first_kernel, after,
        [pg0, pg1, qkv_weight], [hbm] * 3, [shape(count, half)], [vmem],
        scratch_shapes=in_scratch + [in_sems],
        name="input_first", **settings(5, 36),
    )
    last_sum.zero = out_sum.zero = zero
    given = last_sum.first()
    last_sum.send(given)
    after = out_sum.next()
    out_sum.send(after)
    after = after + given

    first_picks = picks(cs.side[:side_cut] + cs.above + cs.corner, cells[:half_cells])
    last_picks = picks(cs.side[side_cut:], cells[half_cells:])
    zero, [full, *strips] = tied_call(
        input_last_kernel, after,
        [pg0, pg1, qkv_weight, nfirst, normed, rstd, grad, merged,
         first_picks, last_picks, picks(sum(g_strips, []), grps)],
        [hbm] * 7 + [vmem] * 4, [wide] + [shape(*e) for e in extents], [vmem] * 4,
        scratch_shapes=in_scratch + [
            pltpu.VMEM((count, channels), BF16),
            pltpu.VMEM((count, channels), BF16),
            pltpu.VMEM((count, LANES), F32),
            pltpu.VMEM((count, channels), BF16),
            in_sems,
            pltpu.SemaphoreType.DMA((4,)),
        ],
        name="input_last", **settings(9, 36),
    )
    first_sum.zero = last_sum.zero = out_sum.zero = zero
    strips = sent_strips(strips, sizes, -1)

    first_part = first_sum.rest()
    last_part = last_sum.rest()
    out_weight_grad = out_sum.rest()

    got = [Strips.sent(s, *t) for s, t in zip((cs.side, cs.above, cs.corner), to)]
    g_got = sum((Strips.sent(s, *t) for s, t in zip(g_strips, g_to)), [])
    tokens_grad, merged = pl.pallas_call(
        unpack_kernel,
        out_shape=[wide, shape(groups, merged_width)],
        in_specs=[vmem] * 9, out_specs=[vmem] * 2,
        name="unpack_strips", **settings(2, 24),
    )(
        full, merged, *strips,
        picks(box(levels, range(SHIFT, 2 * SHIFT), own_cols), cells[:half_cells] + got[0][:side_cut]),
        picks(box(levels, range(2 * SHIFT, lat_rows), own_cols), cells[half_cells:] + got[0][side_cut:]),
        picks(box(levels, range(lat_rows, lat_rows + SHIFT), own_cols), got[1] + got[2]),
        picks(g_own, grps + g_got),
    )
    merged = merged.reshape(levels, g_cols, g_rows, merged_width).transpose(0, 2, 1, 3)

    qkv_weight_grad = jnp.concatenate(
        [part[:, i * width:(i + 1) * width] for i in range(3) for part in (first_part, last_part)],
        axis=1,
    )
    return merged, tokens_grad.reshape(tokens.shape), qkv_weight_grad, out_weight_grad


def solution(mesh):
    sizes = (mesh.shape["lat"], mesh.shape["lon"])
    in_specs = (P(None, "lat", "lon", None), P(), P(), P(), P(None, "lat", "lon", None))
    out_specs = (
        P(None, "lat", "lon", None),
        P(None, "lat", "lon", None),
        P(("lat", "lon"), None),
        P(("lat", "lon"), None),
    )
    return jax.shard_map(
        functools.partial(shards, sizes),
        mesh=mesh, in_specs=in_specs, out_specs=out_specs, check_vma=False,
    )
```

```python
import functools

import jax
import jax.numpy as jnp
import numpy as np
from jax import lax
from jax.experimental import pallas as pl
from jax.experimental.pallas import tpu as pltpu
from jax.sharding import PartitionSpec as P

HEADS = 32
WIN = 8
SHIFT = 4
LANES = 128
HALF = SHIFT // 2
TILE = 256
EPSILON = 1e-05
MIB = 1 << 20

NN = (((1,), (0,)), ((), ()))
NT = (((1,), (1,)), ((), ()))
TN = (((0,), (0,)), ((), ()))
BF16 = jnp.bfloat16
F32 = jnp.float32


def dot(a, b, dims=NN):
    return lax.dot_general(a, b, dims, preferred_element_type=F32)


def window_cells(levels, rows, columns):
    half = WIN // 2
    return [
        (level, wi * WIN + 2 * row + sub % 2, wj * WIN + 2 * column + sub // 2)
        for wi in range(rows // WIN) for wj in range(columns // WIN) for sub in range(4)
        for level in range(levels) for row in range(half) for column in range(half)
    ]


def window_groups(levels, rows, columns):
    half = WIN // 2
    return [
        (level, wi * half + row, wj * half + column)
        for wi in range(rows // half) for wj in range(columns // half)
        for level in range(levels) for row in range(half) for column in range(half)
    ]


def box(levels, rows, columns):
    return [(l, r, c) for l in range(levels) for r in rows for c in columns]


def turned_box(levels, rows, columns):
    return [(l, r, c) for l in range(levels) for c in columns for r in rows]


def padded(cells, step=16):
    return cells + [None] * (-len(cells) % step)


def picks(wanted, held):
    spot = {cell: i for i, cell in enumerate(held) if cell is not None}
    table = np.zeros((len(wanted), len(held)), np.float32)
    for i, cell in enumerate(wanted):
        if cell is not None:
            table[i, spot[cell]] = 1.0
    return jnp.asarray(table, BF16)


class Strips:
    def __init__(self, levels, rows, columns, width, cut):
        self.side = (box(levels, range(width, 2 * width), range(width))
                     + box(levels, range(2 * width, rows), range(width)))
        self.above = box(levels, range(width), range(width, columns))
        self.corner = box(levels, range(width), range(width))
        if not cut:
            self.side = box(levels, range(width, rows), range(width))

    @staticmethod
    def sent(cells, down, across):
        return [None if c is None else (c[0], c[1] + down, c[2] + across) for c in cells]


def head_masks():
    head = lax.broadcasted_iota(jnp.int32, (LANES, LANES), 1) // (LANES // 4)
    return [jnp.where(head == h, 1.0, 0.0).astype(BF16) for h in range(4)]


def region_bias(places, active):
    step = 2 * (WIN // 2)
    one = (lax.broadcasted_iota(jnp.int32, (places, places), 0) // step) % 2
    other = (lax.broadcasted_iota(jnp.int32, (places, places), 1) // step) % 2
    return jnp.where((one != other) & active, -1e30, 0.0)


def score_scale(channels):
    return float((channels // HEADS) ** -0.5 * np.log2(np.e))


def aligned(start, size, step=None):
    return pl.ds(pl.multiple_of(start, step or size), size)


def pack_kernel(tokens, merged_grad, pick_cells, pick_groups, side, above, corner):
    cells = dot(pick_cells[...], tokens[...]).astype(BF16)
    groups = dot(pick_groups[...], merged_grad[...]).astype(BF16)
    at, at_group = 0, 0
    for out, (count, extra) in zip((side, above, corner), strip_rows(pick_cells, pick_groups)):
        out[:count] = cells[at:at + count]
        out[count:] = groups[at_group:at_group + extra]
        at, at_group = at + count, at_group + extra


def strip_rows(pick_cells, pick_groups):
    levels = 2
    rows, columns = strip_rows.extent
    cells = [levels * (rows - SHIFT) * SHIFT, levels * SHIFT * (columns - SHIFT), levels * SHIFT * SHIFT]
    groups = [n // 4 + (-(n // 4)) % 16 for n in cells]
    return list(zip(cells, groups))


def forward_kernel(
    edge, owner, tokens, merged_grad, side, above, corner, order, group, rowmap,
    wqkv_h, wout_h, wm_h,
    normed_h, normt_h, proj_h, dmr_h, dmm_h, grad_h, rstd, merged, out_mine, out_theirs,
    wqkv, wout, wm, source, xw, normed, normt, proj, mixture, inverse, subs, dsubs, cotangent,
    grad, dmr, dmm, turned, in_sem, out_sem,
):
    count, channels = xw.shape
    places = 2 * WIN * WIN
    windows = count // places
    per_row = windows // 2
    quarter = places // 4
    groups = count // 4
    devices = owner.shape[0]
    block = channels // devices

    loads = [
        pltpu.make_async_copy(src, dst, in_sem.at[i])
        for i, (src, dst) in enumerate([(wqkv_h, wqkv), (wout_h, wout), (wm_h, wm)])
    ]
    for load in loads:
        load.start()
    stores = [
        pltpu.make_async_copy(src, dst, out_sem.at[i])
        for i, (src, dst) in enumerate(
            [(normed, normed_h), (proj, proj_h), (normt, normt_h),
             (grad, grad_h), (dmr, dmr_h), (dmm, dmm_h)]
        )
    ]

    (n_side, g_side), (n_above, g_above), (n_corner, g_corner) = strip_rows(None, None)
    half = count // 2
    line = half // (2 * WIN)
    cut = SHIFT * line
    side_cut = 2 * SHIFT * SHIFT
    blocks = [
        [tokens[:cut], tokens[half:half + cut], side[:side_cut], above[:n_above], corner[:n_corner]],
        [tokens[cut:cut + WIN * line], tokens[half + cut:half + cut + WIN * line], side[side_cut:n_side]],
    ]
    for wi in range(2):
        at = 0
        for piece in blocks[wi]:
            source[wi, at:at + piece.shape[0]] = piece
            at += piece.shape[0]
        if at < source.shape[1]:
            source[wi, at:] = jnp.zeros((source.shape[1] - at, channels), BF16)

    @pl.loop(0, windows)
    def _(w):
        rows = aligned(w * places, places)
        x = dot(order[rows], source[w // per_row])
        xw[rows] = x.astype(BF16)
        center = jnp.mean(x, axis=1, keepdims=True)
        moved = x - center
        scale = lax.rsqrt(jnp.mean(moved * moved, axis=1, keepdims=True) + EPSILON)
        rstd[rows] = jnp.broadcast_to(scale, (places, LANES))
        normed[rows] = (moved * scale).astype(BF16)

    stores[0].start()
    loads[0].wait()

    @pl.loop(0, wqkv.shape[1] // TILE)
    def _(n):
        columns = aligned(n * TILE, TILE)
        proj[:, columns] = dot(normed[...], wqkv[:, columns]).astype(BF16)

    stores[1].start()

    masks = head_masks()
    factor = score_scale(channels)

    edge_bias = region_bias(places, edge[0] == 1)
    held = jnp.concatenate(
        [merged_grad[...], side[n_side:], above[n_above:], corner[n_corner:]], axis=0
    )
    cotangent[...] = dot(group[...], held).astype(BF16)
    loads[2].wait()
    steps = channels // LANES
    per_step = 4 * channels // TILE // steps

    @pl.loop(0, steps)
    def _(g):
        lanes = aligned(g * LANES, LANES)
        key_lanes = aligned(channels + g * LANES, LANES)
        value_lanes = aligned(2 * channels + g * LANES, LANES)
        for w in range(windows):
            rows = slice(w * places, (w + 1) * places)
            q, k, v = proj[rows, lanes], proj[rows, key_lanes], proj[rows, value_lanes]
            scores = dot(q, jnp.concatenate([k * m for m in masks], axis=0), NT)
            parts = []
            for h in range(4):
                part = scores[:, h * places:(h + 1) * places] * factor
                if w < per_row:
                    part = part + edge_bias
                part = part - jnp.max(part, axis=1, keepdims=True)
                parts.append(jnp.exp2(part).astype(BF16))
            values = jnp.concatenate(
                [jnp.concatenate([v * m, m], axis=1) for m in masks], axis=0
            )
            summed = dot(jnp.concatenate(parts, axis=1), values)
            inv = 1.0 / summed[:, LANES:]
            inverse[rows, lanes] = inv
            mixture[rows, lanes] = (summed[:, :LANES] * inv).astype(BF16)
        for i in range(per_step):
            at = aligned((g * per_step + i) * TILE, TILE)
            dsubs[:, at] = dot(cotangent[...], wm[at], NT).astype(BF16)

    loads[1].wait()

    @pl.loop(0, channels // TILE)
    def _(n):
        columns = aligned(n * TILE, TILE)
        out = dot(mixture[...], wout[:, columns]) + xw[:, columns].astype(F32)
        out = out.astype(BF16)
        for w in range(windows):
            for s in range(4):
                at = w * places + s * quarter
                subs[s, w * quarter:(w + 1) * quarter, columns] = out[at:at + quarter]

    total = jnp.zeros((groups, 1), F32)
    for s in range(4):
        total += jnp.sum(subs[s].astype(F32), axis=1, keepdims=True)
    center = total / (4 * channels)
    total = jnp.zeros((groups, 1), F32)
    for s in range(4):
        moved = subs[s].astype(F32) - center
        total += jnp.sum(moved * moved, axis=1, keepdims=True)
    scale = lax.rsqrt(total / (4 * channels) + EPSILON)
    result = jnp.zeros((groups, wm.shape[1]), F32)
    for s in range(4):
        unit = ((subs[s].astype(F32) - center) * scale).astype(BF16)
        result += dot(unit, wm[s * channels:(s + 1) * channels])
    merged[...] = result.astype(BF16)

    mean_g = jnp.zeros((groups, 1), F32)
    mean_gx = jnp.zeros((groups, 1), F32)
    for s in range(4):
        d = dsubs[:, s * channels:(s + 1) * channels].astype(F32)
        mean_g += jnp.sum(d, axis=1, keepdims=True)
        mean_gx += jnp.sum(d * ((subs[s].astype(F32) - center) * scale), axis=1, keepdims=True)
    mean_g = mean_g / (4 * channels)
    mean_gx = mean_gx / (4 * channels)
    for s in range(4):
        unit = (subs[s].astype(F32) - center) * scale
        d = dsubs[:, s * channels:(s + 1) * channels].astype(F32)
        d = (scale * (d - mean_g - unit * mean_gx)).astype(BF16)
        for w in range(windows):
            at = w * places + s * quarter
            grad[at:at + quarter] = d[w * quarter:(w + 1) * quarter]
    stores[3].start()

    @pl.loop(0, channels // TILE)
    def _(n):
        columns = aligned(n * TILE, TILE)
        d = dot(grad[...], wout[columns], NT).astype(BF16).astype(F32)
        d = d * inverse[:, columns]
        dmr[:, columns] = d.astype(BF16)
        dmm[:, columns] = (-d * mixture[:, columns].astype(F32)).astype(BF16)

    stores[4].start()
    stores[5].start()

    def turn(field, out):
        if block % 16:
            @pl.loop(0, channels // TILE)
            def _(n):
                rows = aligned(n * TILE, TILE)
                spot = lax.broadcasted_iota(jnp.int32, (TILE, channels), 1)
                pick = jnp.where(spot == rowmap[rows], 1.0, 0.0).astype(BF16)
                out[rows] = dot(pick, field[...], NT).astype(BF16)
        else:
            @pl.loop(0, channels // TILE)
            def _(n):
                rows = aligned(n * TILE, TILE)
                turned[rows] = field[:, rows].T

            for d in range(devices):
                out[d * block:(d + 1) * block] = turned[aligned(owner[d] * block, block)]

    turn(normed, normt)
    stores[2].start()
    mixt = wqkv.at[:, :count]
    turn(mixture, mixt)
    part = channels // 2

    @pl.loop(0, channels // TILE)
    def _(n):
        columns = aligned(n * TILE, TILE)
        out_mine[:, columns] = dot(mixt[:part], grad[:, columns]).astype(BF16)
        out_theirs[:, columns] = dot(mixt[part:], grad[:, columns]).astype(BF16)

    for store in stores:
        store.wait()


def backward_kernel(index, *refs):
    (edge, proj_h, dmr_h, dmm_h, normt_h, pgrad_h, mine_h, theirs_h,
     held, normt, pgrad, mine, theirs, in_sem, sem, out_sem) = refs
    _, count, width = held.shape
    channels = normt.shape[0]
    half = channels // 2
    places = 2 * WIN * WIN
    windows = count // places
    per_row = windows // 2
    masks = head_masks()
    factor = score_scale(channels)
    plain = (channels // HEADS) ** -0.5
    steps = width // TILE

    def loads(g):
        columns = aligned(g * TILE, TILE)
        for i in range(5):
            src = (proj_h, proj_h, proj_h, dmr_h, dmm_h)[i]
            start = (i * channels if i < 3 else 0) + index * width
            yield pltpu.make_async_copy(
                src.at[:, aligned(start + g * TILE, TILE)], held.at[i, :, columns], in_sem.at[g, i]
            )

    def stores(g):
        for i in range(3):
            columns = aligned(i * width + g * TILE, TILE)
            for j, (src, dst) in enumerate(((pgrad, pgrad_h), (mine, mine_h), (theirs, theirs_h))):
                yield pltpu.make_async_copy(src.at[:, columns], dst.at[:, columns], out_sem.at[g, i, j])

    for g in range(steps):
        for load in loads(g):
            load.start()
    turned_load = pltpu.make_async_copy(normt_h, normt, sem.at[0])
    turned_load.start()
    edge_bias = region_bias(places, edge[0] == 1)

    @pl.loop(0, steps)
    def _(g):
        for load in loads(g):
            load.wait()

        for part_of in range(TILE // LANES):
            lanes = aligned(g * TILE + part_of * LANES, LANES)
            for w in range(windows):
                rows = slice(w * places, (w + 1) * places)
                q, k, v, dm, dd = (held[i, rows, lanes] for i in range(5))
                keys = jnp.concatenate([k * m for m in masks], axis=0)
                scores = dot(keys, q, NT)
                values = jnp.concatenate(
                    [jnp.concatenate([v * m, m], axis=1) for m in masks], axis=0
                )
                slope = dot(values, jnp.concatenate([dm, dd], axis=1), NT)
                weights, slopes = [], []
                for h in range(4):
                    block = slice(h * places, (h + 1) * places)
                    part = scores[block] * factor
                    if w < per_row:
                        part = part + edge_bias
                    part = jnp.exp2(part - jnp.max(part, axis=0, keepdims=True))
                    weights.append(part.astype(BF16))
                    slopes.append((part * slope[block]).astype(BF16))
                dv = dot(
                    jnp.concatenate(weights, axis=1),
                    jnp.concatenate([dm * m for m in masks], axis=0),
                )
                dk = dot(
                    jnp.concatenate(slopes, axis=1),
                    jnp.concatenate([q * m for m in masks], axis=0),
                )
                dq = dot(jnp.concatenate(slopes, axis=0), keys, TN)
                at = g * TILE + part_of * LANES
                pgrad[rows, lanes] = (dq * plain).astype(BF16)
                pgrad[rows, aligned(width + at, LANES)] = (dk * plain).astype(BF16)
                pgrad[rows, aligned(2 * width + at, LANES)] = dv.astype(BF16)

        @pl.when(g == 0)
        def _():
            turned_load.wait()

        for i in range(3):
            columns = aligned(i * width + g * TILE, TILE)
            mine[:, columns] = dot(normt[:half], pgrad[:, columns]).astype(BF16)
            theirs[:, columns] = dot(normt[half:], pgrad[:, columns]).astype(BF16)
        for store in stores(g):
            store.start()

    for g in range(steps):
        for store in stores(g):
            store.wait()


def projection_loads(pgrads, wqkv_h, pgrad, wqkv, sem, start):
    width = pgrads[0].shape[1] // 3
    channels = pgrad.shape[1] // 3
    loads = [
        pltpu.make_async_copy(
            field.at[:, pl.ds(i * width, width)],
            pgrad.at[:, pl.ds(i * channels + c * width, width)], sem.at[c * 3 + i],
        )
        for c, field in enumerate(pgrads) for i in range(3)
    ]
    tiles = [
        pltpu.make_async_copy(
            wqkv_h.at[pl.ds(start + n * TILE, TILE)], wqkv.at[pl.ds(n * TILE, TILE)],
            sem.at[3 * len(pgrads) + n],
        )
        for n in range(wqkv.shape[0] // TILE)
    ]
    for load in loads + tiles:
        load.start()
    return loads, tiles


def input_kernel(*refs):
    (pg0, pg1, wqkv_h, normed_h, rstd_h, grad_h, merged,
     pick_first, pick_last, pick_groups, full, side, below, corner,
     pgrad, wqkv, ngrad, normed, rstd, grad, sem, more_sem) = refs
    count, channels = ngrad.shape
    loads, tiles = projection_loads([pg0, pg1], wqkv_h, pgrad, wqkv, sem, 0)
    more = [
        pltpu.make_async_copy(src, dst, more_sem.at[i])
        for i, (src, dst) in enumerate([(normed_h, normed), (rstd_h, rstd), (grad_h, grad)])
    ]
    for load in more:
        load.start()
    for load in loads:
        load.wait()
    for n, load in enumerate(tiles):
        load.wait()
        ngrad[:, pl.ds(n * TILE, TILE)] = dot(
            pgrad[...], wqkv[pl.ds(n * TILE, TILE)], NT
        ).astype(BF16)
    for load in more:
        load.wait()
    places = 2 * WIN * WIN

    @pl.loop(0, count // places)
    def _(w):
        rows = aligned(w * places, places)
        d = ngrad[rows].astype(F32)
        unit = normed[rows].astype(F32)
        mean_d = jnp.mean(d, axis=1, keepdims=True)
        mean_dx = jnp.mean(d * unit, axis=1, keepdims=True)
        part = rstd[rows, :1] * (d - mean_d - unit * mean_dx)
        full[rows] = (part.astype(BF16).astype(F32) + grad[rows].astype(F32)).astype(BF16)

    (n_side, g_side), (n_above, g_above), (n_corner, g_corner) = strip_rows(None, None)
    side_cut = 2 * SHIFT * SHIFT
    first = dot(pick_first[...], full[:count // 2]).astype(BF16)
    last = dot(pick_last[...], full[count // 2:]).astype(BF16)
    groups = dot(pick_groups[...], merged[...]).astype(BF16)
    side[:side_cut] = first[:side_cut]
    side[side_cut:n_side] = last
    below[:n_above] = first[side_cut:side_cut + n_above]
    corner[:n_corner] = first[side_cut + n_above:]
    side[n_side:] = groups[:g_side]
    below[n_above:] = groups[g_side:g_side + g_above]
    corner[n_corner:] = groups[g_side + g_above:]


def unpack_kernel(full, merged, side, below, corner, pick_top, pick_middle, pick_bottom,
                  pick_groups, tokens_out, merged_out):
    count = full.shape[0]
    half = count // 2
    (n_side, _), (n_above, _), (n_corner, _) = strip_rows(None, None)
    side_cut = 2 * SHIFT * SHIFT
    line = half // (2 * WIN)
    pieces = [
        (pick_top, [full[:half], side[:side_cut]]),
        (pick_middle, [full[half:], side[side_cut:n_side]]),
        (pick_bottom, [below[:n_above], corner[:n_corner]]),
    ]
    at = 0
    for pick, held in pieces:
        rows = pick.shape[0] // 2
        out = dot(pick[...], jnp.concatenate(held, axis=0)).astype(BF16)
        for level in range(2):
            start = level * half + at
            tokens_out[start:start + rows] = out[level * rows:(level + 1) * rows]
        at += rows
    held = [merged[...], side[n_side:], below[n_above:], corner[n_corner:]]
    merged_out[...] = dot(pick_groups[...], jnp.concatenate(held, axis=0)).astype(BF16)


def sent(block, sizes, lat_step, lon_step):
    n_lat, n_lon = sizes
    route = [
        (a * n_lon + b, (a + lat_step) % n_lat * n_lon + (b + lon_step) % n_lon)
        for a in range(n_lat) for b in range(n_lon)
    ]
    return lax.ppermute(block, ("lat", "lon"), route)


def sent_strips(strips, sizes, step):
    side, lines, corner = strips
    return [sent(side, sizes, 0, step), sent(lines, sizes, step, 0), sent(corner, sizes, step, step)]


def device_rows(channels, sizes):
    n_lat, n_lon = sizes
    devices = n_lat * n_lon
    rows = channels // devices
    place = np.arange(devices)
    lon = 2 * (place // n_lat % (n_lon // 2)) + place // (devices // 2)
    lat = place % n_lat
    owner = (
        jnp.bitwise_xor(lax.axis_index("lat").astype(jnp.int32), jnp.asarray(lat, jnp.int32)) * n_lon
        + jnp.bitwise_xor(lax.axis_index("lon").astype(jnp.int32), jnp.asarray(lon, jnp.int32))
    )
    rowmap = owner[:, None] * rows + jnp.arange(rows, dtype=jnp.int32)[None, :]
    return owner, rowmap.reshape(channels, 1)


def exchange(block, sizes, lat_bits, lon_bits):
    n_lat, n_lon = sizes
    route = [
        (a * n_lon + b, (a ^ lat_bits) * n_lon + (b ^ lon_bits))
        for a in range(n_lat) for b in range(n_lon)
    ]
    return lax.ppermute(block, ("lat", "lon"), route)


def core_step(theirs, sizes):
    return exchange(theirs, sizes, 0, 1)


def layer_blocks(mine, arrived, sizes):
    blocks = sizes[1] // 2
    rows = mine.shape[0] // blocks
    total = [
        (mine[i * rows:(i + 1) * rows].astype(F32) + arrived[i * rows:(i + 1) * rows].astype(F32))
        for i in range(blocks)
    ]
    return [total[0]] + [t.astype(BF16) for t in total[1:]]


def layer_step(blocks, sizes):
    return [exchange(b, sizes, 0, 2 * i) for i, b in enumerate(blocks) if i]


def column_blocks(kept, arrived, sizes):
    total = kept
    for block in arrived:
        total = total + block.astype(F32)
    rows = total.shape[0] // sizes[0]
    blocks = [total[i * rows:(i + 1) * rows] for i in range(sizes[0])]
    return [blocks[0]] + [b.astype(BF16) for b in blocks[1:]]


def column_step(blocks, sizes):
    return [exchange(b, sizes, i, 0) for i, b in enumerate(blocks) if i]


def behind(values, marker):
    *values, _ = lax.optimization_barrier((*values, marker))
    return values


def finished(kept, arrived):
    for block in arrived:
        kept = kept + block.astype(F32)
    return kept


def tied_call(kernel, after, operands, in_specs, out_shape, out_specs, **rest):
    waits = len(after)

    def body(*refs):
        kernel(*refs[waits:])

    return pl.pallas_call(
        body, out_shape=out_shape,
        in_specs=[pl.BlockSpec(memory_space=pl.ANY)] * waits + in_specs, out_specs=out_specs, **rest,
    )(*after, *operands)


def shards(sizes, tokens, qkv_weight, out_weight, merge_weight, merged_grad):
    levels, lat_rows, lon_cols, channels = tokens.shape
    merged_width = merge_weight.shape[1]
    count = levels * lat_rows * lon_cols
    groups = count // 4
    half = channels // 2
    strip_rows.extent = (lat_rows, lon_cols)
    vmem = pl.BlockSpec(memory_space=pltpu.VMEM)
    smem = pl.BlockSpec(memory_space=pltpu.SMEM)
    hbm = pl.BlockSpec(memory_space=pl.ANY)

    def shape(*extent, dtype=BF16):
        return jax.ShapeDtypeStruct(extent, dtype)

    def settings(weight, limit=60):
        return dict(
            compiler_params=pltpu.CompilerParams(vmem_limit_bytes=limit * MIB),
            cost_estimate=pl.CostEstimate(
                flops=int(weight * 1e10), bytes_accessed=16 * MIB, transcendentals=0
            ),
        )

    g_rows, g_cols = lat_rows // 2, lon_cols // 2
    cells = window_cells(levels, lat_rows, lon_cols)
    grps = window_groups(levels, g_rows, g_cols)
    cs = Strips(levels, lat_rows, lon_cols, SHIFT, True)
    gs = Strips(levels, g_rows, g_cols, HALF, False)
    g_strips = [padded(gs.side), padded(gs.above), padded(gs.corner)]
    to = ((0, lon_cols), (lat_rows, 0), (lat_rows, lon_cols))
    g_to = ((0, g_cols), (g_rows, 0), (g_rows, g_cols))
    own_rows = range(SHIFT, SHIFT + lat_rows)
    own_cols = range(SHIFT, SHIFT + lon_cols)
    own = box(levels, own_rows, own_cols)
    g_own = turned_box(levels, range(HALF, HALF + g_rows), range(HALF, HALF + g_cols))
    half_cells = count // 2
    side_cut = levels * SHIFT * SHIFT
    sent_cells = sum((Strips.sent(s, *t) for s, t in zip((cs.side, cs.above, cs.corner), to)), [])
    sent_groups = sum((Strips.sent(s, *t) for s, t in zip(g_strips, g_to)), [])
    held_top = box(levels, range(SHIFT, 2 * SHIFT), own_cols) + cs.side[:side_cut] + cs.above + cs.corner
    held_low = box(levels, range(2 * SHIFT, lat_rows), own_cols) + cs.side[side_cut:]
    depth = max(len(held_top), len(held_low))
    depth += -depth % 16
    held_top += [None] * (depth - len(held_top))
    held_low += [None] * (depth - len(held_low))

    tokens_flat = tokens.reshape(count, channels)
    merged_grad_flat = merged_grad.transpose(0, 2, 1, 3).reshape(groups, merged_width)
    extents = [(n + g, channels) for n, g in strip_rows(None, None)]
    strips = pl.pallas_call(
        pack_kernel,
        out_shape=[shape(*e) for e in extents],
        in_specs=[vmem] * 4, out_specs=[vmem] * 3,
        name="pack_strips", **settings(1),
    )(tokens_flat, merged_grad_flat, picks(sent_cells, own), picks(sent_groups, g_own))
    strips = sent_strips(strips, sizes, 1)

    order = jnp.concatenate([picks(cells[:half_cells], held_top), picks(cells[half_cells:], held_low)])
    group = picks(grps, g_own + sum(g_strips, []))
    edge = (lax.axis_index("lat") == 0).astype(jnp.int32).reshape(1)
    owner, rowmap = device_rows(channels, sizes)

    wide = shape(count, channels)
    normed, normt, proj, dmr, dmm, grad, rstd, merged, out_mine, out_theirs = pl.pallas_call(
        forward_kernel,
        out_shape=[
            wide, shape(channels, count), shape(count, 3 * channels), wide, wide, wide,
            shape(count, LANES, dtype=F32), shape(groups, merged_width),
            shape(half, channels), shape(half, channels),
        ],
        in_specs=[smem] * 2 + [vmem] * 8 + [hbm] * 3,
        out_specs=[hbm] * 6 + [vmem] * 4,
        scratch_shapes=[
            pltpu.VMEM(qkv_weight.shape, BF16),
            pltpu.VMEM(out_weight.shape, BF16),
            pltpu.VMEM(merge_weight.shape, BF16),
            pltpu.VMEM((2, depth, channels), BF16),
            pltpu.VMEM((count, channels), BF16),
            pltpu.VMEM((count, channels), BF16),
            pltpu.VMEM((channels, count), BF16),
            pltpu.VMEM((count, 3 * channels), BF16),
            pltpu.VMEM((count, channels), BF16),
            pltpu.VMEM((count, channels), F32),
            pltpu.VMEM((4, groups, channels), BF16),
            pltpu.VMEM((groups, 4 * channels), BF16),
            pltpu.VMEM((groups, merged_width), BF16),
            pltpu.VMEM((count, channels), BF16),
            pltpu.VMEM((count, channels), BF16),
            pltpu.VMEM((count, channels), BF16),
            pltpu.VMEM((channels, count), BF16),
            pltpu.SemaphoreType.DMA((3,)),
            pltpu.SemaphoreType.DMA((6,)),
        ],
        name="block_forward", **settings(30, 58),
    )(edge, owner, tokens_flat, merged_grad_flat, *strips, order, group, rowmap,
      qkv_weight, out_weight, merge_weight)

    halves = 2
    width = channels // halves
    steps = width // TILE

    def backward(index, after):
        return tied_call(
            functools.partial(backward_kernel, index), after,
            [edge, proj, dmr, dmm, normt], [smem] + [hbm] * 4,
            [shape(count, 3 * width), shape(half, 3 * width), shape(half, 3 * width)], [hbm] * 3,
            scratch_shapes=[
                pltpu.VMEM((5, count, width), BF16),
                pltpu.VMEM((channels, count), BF16),
                pltpu.VMEM((count, 3 * width), BF16),
                pltpu.VMEM((half, 3 * width), BF16),
                pltpu.VMEM((half, 3 * width), BF16),
                pltpu.SemaphoreType.DMA((steps, 5)),
                pltpu.SemaphoreType.DMA((1,)),
                pltpu.SemaphoreType.DMA((steps, 3, 3)),
            ],
            name="attention_backward", **settings(15, 48),
        )

    arrived = core_step(out_theirs, sizes)
    pg0, mine1, theirs1 = backward(0, [])
    out_mine, arrived = behind([out_mine, arrived], pg0)
    layer0 = layer_blocks(out_mine, arrived, sizes)
    arrived0 = layer_step(layer0, sizes)
    arrived = core_step(theirs1, sizes)
    pg1, mine2, theirs2 = backward(1, layer0[1:])
    mine1, arrived, *arrived0 = behind([mine1, arrived] + arrived0, pg1)
    layer1 = layer_blocks(mine1, arrived, sizes)
    arrived1 = layer_step(layer1, sizes)
    arrived = core_step(theirs2, sizes)

    first_picks = picks(cs.side[:side_cut] + cs.above + cs.corner, cells[:half_cells])
    last_picks = picks(cs.side[side_cut:], cells[half_cells:])
    full, *strips = tied_call(
        input_kernel, layer1[1:],
        [pg0, pg1, qkv_weight, normed, rstd, grad, merged,
         first_picks, last_picks, picks(sum(g_strips, []), grps)],
        [hbm] * 6 + [vmem] * 4, [wide] + [shape(*e) for e in extents], [vmem] * 4,
        scratch_shapes=[
            pltpu.VMEM((count, 3 * channels), BF16),
            pltpu.VMEM(qkv_weight.shape, BF16),
            pltpu.VMEM((count, channels), BF16),
            pltpu.VMEM((count, channels), BF16),
            pltpu.VMEM((count, LANES), F32),
            pltpu.VMEM((count, channels), BF16),
            pltpu.SemaphoreType.DMA((3 * halves + channels // TILE,)),
            pltpu.SemaphoreType.DMA((3,)),
        ],
        name="input_backward", **settings(13, 40),
    )
    mine2, arrived = behind([mine2, arrived], full)
    layer2 = layer_blocks(mine2, arrived, sizes)
    arrived2 = layer_step(layer2, sizes)
    arrived1 = behind(arrived1, layer2[1])
    strips = sent_strips(strips, sizes, -1)

    kept = jnp.concatenate([layer0[0], layer1[0]], axis=1)
    joined = [jnp.concatenate(pair, axis=1) for pair in zip(arrived0, arrived1)]
    column1 = column_blocks(kept, joined, sizes)
    column2 = column_blocks(layer2[0], arrived2, sizes)
    part1 = finished(column1[0], column_step(column1, sizes))
    part2 = finished(column2[0], column_step(column2, sizes))
    out_weight_grad = part1[:, :channels]
    part1 = part1[:, channels:]

    got = [Strips.sent(s, *t) for s, t in zip((cs.side, cs.above, cs.corner), to)]
    g_got = sum((Strips.sent(s, *t) for s, t in zip(g_strips, g_to)), [])
    tokens_grad, merged = tied_call(
        unpack_kernel, layer2[1:] + column1[1:],
        [
            full, merged, *strips,
            picks(box(levels, range(SHIFT, 2 * SHIFT), own_cols), cells[:half_cells] + got[0][:side_cut]),
            picks(box(levels, range(2 * SHIFT, lat_rows), own_cols), cells[half_cells:] + got[0][side_cut:]),
            picks(box(levels, range(lat_rows, lat_rows + SHIFT), own_cols), got[1] + got[2]),
            picks(g_own, grps + g_got),
        ],
        [vmem] * 9, [wide, shape(groups, merged_width)], [vmem] * 2,
        name="unpack_strips", **settings(2, 24),
    )
    merged = merged.reshape(levels, g_cols, g_rows, merged_width).transpose(0, 2, 1, 3)

    qkv_weight_grad = jnp.concatenate(
        [part[:, i * width:(i + 1) * width] for i in range(3) for part in (part1, part2)],
        axis=1,
    )
    return merged, tokens_grad.reshape(tokens.shape), qkv_weight_grad, out_weight_grad


def solution(mesh):
    sizes = (mesh.shape["lat"], mesh.shape["lon"])
    in_specs = (P(None, "lat", "lon", None), P(), P(), P(), P(None, "lat", "lon", None))
    out_specs = (
        P(None, "lat", "lon", None),
        P(None, "lat", "lon", None),
        P(("lat", "lon"), None),
        P(("lat", "lon"), None),
    )
    return jax.shard_map(
        functools.partial(shards, sizes),
        mesh=mesh, in_specs=in_specs, out_specs=out_specs, check_vma=False,
    )
```

```python
import functools

import jax
import jax.numpy as jnp
import numpy as np
from jax import lax
from jax.experimental import pallas as pl
from jax.experimental.pallas import tpu as pltpu
from jax.sharding import PartitionSpec as P

HEADS = 32
WIN = 8
SHIFT = 4
LANES = 128
HALF = SHIFT // 2
TILE = 256
EPSILON = 1e-05
MIB = 1 << 20

NN = (((1,), (0,)), ((), ()))
NT = (((1,), (1,)), ((), ()))
TN = (((0,), (0,)), ((), ()))
BF16 = jnp.bfloat16
F32 = jnp.float32


def dot(a, b, dims=NN):
    return lax.dot_general(a, b, dims, preferred_element_type=F32)


def window_cells(levels, rows, columns):
    half = WIN // 2
    return [
        (level, wi * WIN + 2 * row + sub % 2, wj * WIN + 2 * column + sub // 2)
        for wi in range(rows // WIN) for wj in range(columns // WIN) for sub in range(4)
        for level in range(levels) for row in range(half) for column in range(half)
    ]


def window_groups(levels, rows, columns):
    half = WIN // 2
    return [
        (level, wi * half + row, wj * half + column)
        for wi in range(rows // half) for wj in range(columns // half)
        for level in range(levels) for row in range(half) for column in range(half)
    ]


def box(levels, rows, columns):
    return [(l, r, c) for l in range(levels) for r in rows for c in columns]


def turned_box(levels, rows, columns):
    return [(l, r, c) for l in range(levels) for c in columns for r in rows]


def padded(cells, step=16):
    return cells + [None] * (-len(cells) % step)


def picks(wanted, held):
    spot = {cell: i for i, cell in enumerate(held) if cell is not None}
    table = np.zeros((len(wanted), len(held)), np.float32)
    for i, cell in enumerate(wanted):
        if cell is not None:
            table[i, spot[cell]] = 1.0
    return jnp.asarray(table, BF16)


class Strips:
    def __init__(self, levels, rows, columns, width, cut):
        self.side = (box(levels, range(width, 2 * width), range(width))
                     + box(levels, range(2 * width, rows), range(width)))
        self.above = box(levels, range(width), range(width, columns))
        self.corner = box(levels, range(width), range(width))
        if not cut:
            self.side = box(levels, range(width, rows), range(width))

    @staticmethod
    def sent(cells, down, across):
        return [None if c is None else (c[0], c[1] + down, c[2] + across) for c in cells]


def head_masks():
    head = lax.broadcasted_iota(jnp.int32, (LANES, LANES), 1) // (LANES // 4)
    return [jnp.where(head == h, 1.0, 0.0).astype(BF16) for h in range(4)]


def region_bias(places, active):
    step = 2 * (WIN // 2)
    one = (lax.broadcasted_iota(jnp.int32, (places, places), 0) // step) % 2
    other = (lax.broadcasted_iota(jnp.int32, (places, places), 1) // step) % 2
    return jnp.where((one != other) & active, -1e30, 0.0)


def score_scale(channels):
    return float((channels // HEADS) ** -0.5 * np.log2(np.e))


def aligned(start, size, step=None):
    return pl.ds(pl.multiple_of(start, step or size), size)


def pack_kernel(tokens, merged_grad, pick_cells, pick_groups, side, above, corner):
    cells = dot(pick_cells[...], tokens[...]).astype(BF16)
    groups = dot(pick_groups[...], merged_grad[...]).astype(BF16)
    at, at_group = 0, 0
    for out, (count, extra) in zip((side, above, corner), strip_rows(pick_cells, pick_groups)):
        out[:count] = cells[at:at + count]
        out[count:] = groups[at_group:at_group + extra]
        at, at_group = at + count, at_group + extra


def strip_rows(pick_cells, pick_groups):
    levels = 2
    rows, columns = strip_rows.extent
    cells = [levels * (rows - SHIFT) * SHIFT, levels * SHIFT * (columns - SHIFT), levels * SHIFT * SHIFT]
    groups = [n // 4 + (-(n // 4)) % 16 for n in cells]
    return list(zip(cells, groups))


def normalized_window(x, rows, xw, normed, rstd):
    xw[rows] = x.astype(BF16)
    center = jnp.mean(x, axis=1, keepdims=True)
    moved = x - center
    scale = lax.rsqrt(jnp.mean(moved * moved, axis=1, keepdims=True) + EPSILON)
    rstd[rows] = jnp.broadcast_to(scale, (x.shape[0], LANES))
    normed[rows] = (moved * scale).astype(BF16)


def attended(proj, rows, lanes, masks, factor, bias, mixture, inverse):
    places = masks[0].shape[0]
    q, k, v = (proj[rows, at] for at in lanes)
    scores = dot(q, jnp.concatenate([k * m for m in masks], axis=0), NT)
    parts = []
    for h in range(4):
        part = scores[:, h * places:(h + 1) * places] * factor
        if bias is not None:
            part = part + bias
        part = part - jnp.max(part, axis=1, keepdims=True)
        parts.append(jnp.exp2(part).astype(BF16))
    values = jnp.concatenate([jnp.concatenate([v * m, m], axis=1) for m in masks], axis=0)
    summed = dot(jnp.concatenate(parts, axis=1), values)
    inv = 1.0 / summed[:, LANES:]
    inverse[rows, lanes[0]] = inv
    mixture[rows, lanes[0]] = (summed[:, :LANES] * inv).astype(BF16)


def inner_kernel(
    tokens, order, wqkv_h, xw, normed, rstd, mixture, inverse, proj, wqkv, in_sem,
):
    count, channels = xw.shape
    places = 2 * WIN * WIN
    tiles = wqkv.shape[1] // TILE

    def load(n):
        columns = aligned(n * TILE, TILE)
        return pltpu.make_async_copy(wqkv_h.at[:, columns], wqkv.at[:, columns], in_sem.at[n])

    for n in range(tiles):
        load(n).start()
    half = tokens.shape[0] // 2
    line = half // (2 * WIN)
    cut = SHIFT * line
    source = jnp.concatenate(
        [tokens[cut:cut + WIN * line], tokens[half + cut:half + cut + WIN * line]], axis=0
    )
    for w in range(count // places):
        rows = slice(w * places, (w + 1) * places)
        normalized_window(dot(order[rows, :source.shape[0]], source), rows, xw, normed, rstd)

    @pl.loop(0, tiles)
    def _(n):
        load(n).wait()
        columns = aligned(n * TILE, TILE)
        proj[:, columns] = dot(normed[...], wqkv[:, columns]).astype(BF16)

    masks = head_masks()
    factor = score_scale(channels)

    @pl.loop(0, channels // LANES // 2)
    def _(g):
        for i in range(2):
            lanes = [aligned(j * channels + (2 * g + i) * LANES, LANES) for j in range(3)]
            for w in range(count // places):
                rows = slice(w * places, (w + 1) * places)
                attended(proj, rows, lanes, masks, factor, None, mixture, inverse)


def forward_kernel(
    edge, owner, tokens, merged_grad, side, above, corner, order, group, rowmap,
    wqkv_h, wout_h, wm_h, xw_h, normed_in, rstd_h, mixture_h, inverse_h, proj_in,
    normed_h, normt_h, proj_h, dmr_h, dmm_h, grad_h, rstd, merged, out_mine, out_theirs,
    wqkv, wout, wm, source, xw, normed, normt, proj, mixture, inverse, subs, dsubs, cotangent,
    grad, dmr, dmm, turned, in_sem, out_sem,
):
    count, channels = xw.shape
    places = 2 * WIN * WIN
    windows = count // places
    per_row = windows // 2
    quarter = places // 4
    groups = count // 4
    devices = owner.shape[0]
    block = channels // devices

    loads = [
        pltpu.make_async_copy(src, dst, in_sem.at[i])
        for i, (src, dst) in enumerate([(wqkv_h, wqkv), (wout_h, wout), (wm_h, wm)])
    ]
    outer = count - xw_h.shape[0]
    ready = [
        pltpu.make_async_copy(src, dst.at[pl.ds(outer, count - outer)], in_sem.at[3 + i])
        for i, (src, dst) in enumerate(
            [(xw_h, xw), (normed_in, normed), (rstd_h, rstd), (mixture_h, mixture),
             (inverse_h, inverse), (proj_in, proj)]
        )
    ]
    for load in loads + ready:
        load.start()
    stores = [
        pltpu.make_async_copy(src, dst, out_sem.at[i])
        for i, (src, dst) in enumerate(
            [(normed, normed_h), (proj, proj_h), (normt, normt_h),
             (grad, grad_h), (dmr, dmr_h), (dmm, dmm_h)]
        )
    ]

    (n_side, g_side), (n_above, g_above), (n_corner, g_corner) = strip_rows(None, None)
    half = count // 2
    line = half // (2 * WIN)
    cut = SHIFT * line
    side_cut = 2 * SHIFT * SHIFT
    blocks = [
        [tokens[:cut], tokens[half:half + cut], side[:side_cut], above[:n_above], corner[:n_corner]],
        [tokens[cut:cut + WIN * line], tokens[half + cut:half + cut + WIN * line], side[side_cut:n_side]],
    ]
    for wi in range(2):
        at = 0
        for piece in blocks[wi]:
            source[wi, at:at + piece.shape[0]] = piece
            at += piece.shape[0]
        if at < source.shape[1]:
            source[wi, at:] = jnp.zeros((source.shape[1] - at, channels), BF16)

    @pl.loop(0, outer // places)
    def _(w):
        rows = aligned(w * places, places)
        normalized_window(dot(order[rows], source[w // per_row]), rows, xw, normed, rstd)

    loads[0].wait()
    outer_rows = slice(0, outer)

    @pl.loop(0, wqkv.shape[1] // TILE)
    def _(n):
        columns = aligned(n * TILE, TILE)
        proj[outer_rows, columns] = dot(normed[outer_rows], wqkv[:, columns]).astype(BF16)

    for load in ready:
        load.wait()
    stores[0].start()
    stores[1].start()

    masks = head_masks()
    factor = score_scale(channels)

    edge_bias = region_bias(places, edge[0] == 1)
    held = jnp.concatenate(
        [merged_grad[...], side[n_side:], above[n_above:], corner[n_corner:]], axis=0
    )
    cotangent[...] = dot(group[...], held).astype(BF16)
    loads[2].wait()
    steps = channels // LANES
    per_step = 4 * channels // TILE // steps

    @pl.loop(0, steps)
    def _(g):
        lanes = [aligned(i * channels + g * LANES, LANES) for i in range(3)]
        for w in range(outer // places):
            rows = slice(w * places, (w + 1) * places)
            bias = edge_bias if w < per_row else None
            attended(proj, rows, lanes, masks, factor, bias, mixture, inverse)
        for i in range(per_step):
            at = aligned((g * per_step + i) * TILE, TILE)
            dsubs[:, at] = dot(cotangent[...], wm[at], NT).astype(BF16)

    loads[1].wait()

    @pl.loop(0, channels // TILE)
    def _(n):
        columns = aligned(n * TILE, TILE)
        out = dot(mixture[...], wout[:, columns]) + xw[:, columns].astype(F32)
        out = out.astype(BF16)
        for w in range(windows):
            for s in range(4):
                at = w * places + s * quarter
                subs[s, w * quarter:(w + 1) * quarter, columns] = out[at:at + quarter]

    total = jnp.zeros((groups, 1), F32)
    for s in range(4):
        total += jnp.sum(subs[s].astype(F32), axis=1, keepdims=True)
    center = total / (4 * channels)
    total = jnp.zeros((groups, 1), F32)
    for s in range(4):
        moved = subs[s].astype(F32) - center
        total += jnp.sum(moved * moved, axis=1, keepdims=True)
    scale = lax.rsqrt(total / (4 * channels) + EPSILON)
    result = jnp.zeros((groups, wm.shape[1]), F32)
    for s in range(4):
        unit = ((subs[s].astype(F32) - center) * scale).astype(BF16)
        result += dot(unit, wm[s * channels:(s + 1) * channels])
    merged[...] = result.astype(BF16)

    mean_g = jnp.zeros((groups, 1), F32)
    mean_gx = jnp.zeros((groups, 1), F32)
    for s in range(4):
        d = dsubs[:, s * channels:(s + 1) * channels].astype(F32)
        mean_g += jnp.sum(d, axis=1, keepdims=True)
        mean_gx += jnp.sum(d * ((subs[s].astype(F32) - center) * scale), axis=1, keepdims=True)
    mean_g = mean_g / (4 * channels)
    mean_gx = mean_gx / (4 * channels)
    for s in range(4):
        unit = (subs[s].astype(F32) - center) * scale
        d = dsubs[:, s * channels:(s + 1) * channels].astype(F32)
        d = (scale * (d - mean_g - unit * mean_gx)).astype(BF16)
        for w in range(windows):
            at = w * places + s * quarter
            grad[at:at + quarter] = d[w * quarter:(w + 1) * quarter]
    stores[3].start()

    @pl.loop(0, channels // TILE)
    def _(n):
        columns = aligned(n * TILE, TILE)
        d = dot(grad[...], wout[columns], NT).astype(BF16).astype(F32)
        d = d * inverse[:, columns]
        dmr[:, columns] = d.astype(BF16)
        dmm[:, columns] = (-d * mixture[:, columns].astype(F32)).astype(BF16)

    stores[4].start()
    stores[5].start()

    def turn(field, out):
        if block % 16:
            @pl.loop(0, channels // TILE)
            def _(n):
                rows = aligned(n * TILE, TILE)
                spot = lax.broadcasted_iota(jnp.int32, (TILE, channels), 1)
                pick = jnp.where(spot == rowmap[rows], 1.0, 0.0).astype(BF16)
                out[rows] = dot(pick, field[...], NT).astype(BF16)
        else:
            @pl.loop(0, channels // TILE)
            def _(n):
                rows = aligned(n * TILE, TILE)
                turned[rows] = field[:, rows].T

            for d in range(devices):
                out[d * block:(d + 1) * block] = turned[aligned(owner[d] * block, block)]

    turn(normed, normt)
    stores[2].start()
    mixt = wqkv.at[:, :count]
    turn(mixture, mixt)
    part = channels // 2

    @pl.loop(0, channels // TILE)
    def _(n):
        columns = aligned(n * TILE, TILE)
        out_mine[:, columns] = dot(mixt[:part], grad[:, columns]).astype(BF16)
        out_theirs[:, columns] = dot(mixt[part:], grad[:, columns]).astype(BF16)

    for store in stores:
        store.wait()


def backward_kernel(index, *refs):
    (edge, proj_h, dmr_h, dmm_h, normt_h, pgrad_h, mine_h, theirs_h,
     held, normt, pgrad, mine, theirs, in_sem, sem, out_sem) = refs
    _, count, width = held.shape
    channels = normt.shape[0]
    half = channels // 2
    places = 2 * WIN * WIN
    windows = count // places
    per_row = windows // 2
    masks = head_masks()
    factor = score_scale(channels)
    plain = (channels // HEADS) ** -0.5
    steps = width // TILE

    def loads(g):
        columns = aligned(g * TILE, TILE)
        for i in range(5):
            src = (proj_h, proj_h, proj_h, dmr_h, dmm_h)[i]
            start = (i * channels if i < 3 else 0) + index * width
            yield pltpu.make_async_copy(
                src.at[:, aligned(start + g * TILE, TILE)], held.at[i, :, columns], in_sem.at[g, i]
            )

    def stores(g):
        for i in range(3):
            columns = aligned(i * width + g * TILE, TILE)
            for j, (src, dst) in enumerate(((pgrad, pgrad_h), (mine, mine_h), (theirs, theirs_h))):
                yield pltpu.make_async_copy(src.at[:, columns], dst.at[:, columns], out_sem.at[g, i, j])

    for g in range(steps):
        for load in loads(g):
            load.start()
    turned_load = pltpu.make_async_copy(normt_h, normt, sem.at[0])
    turned_load.start()
    edge_bias = region_bias(places, edge[0] == 1)

    @pl.loop(0, steps)
    def _(g):
        for load in loads(g):
            load.wait()

        for part_of in range(TILE // LANES):
            lanes = aligned(g * TILE + part_of * LANES, LANES)
            for w in range(windows):
                rows = slice(w * places, (w + 1) * places)
                q, k, v, dm, dd = (held[i, rows, lanes] for i in range(5))
                keys = jnp.concatenate([k * m for m in masks], axis=0)
                scores = dot(keys, q, NT)
                values = jnp.concatenate(
                    [jnp.concatenate([v * m, m], axis=1) for m in masks], axis=0
                )
                slope = dot(values, jnp.concatenate([dm, dd], axis=1), NT)
                weights, slopes = [], []
                for h in range(4):
                    block = slice(h * places, (h + 1) * places)
                    part = scores[block] * factor
                    if w < per_row:
                        part = part + edge_bias
                    part = jnp.exp2(part - jnp.max(part, axis=0, keepdims=True))
                    weights.append(part.astype(BF16))
                    slopes.append((part * slope[block]).astype(BF16))
                dv = dot(
                    jnp.concatenate(weights, axis=1),
                    jnp.concatenate([dm * m for m in masks], axis=0),
                )
                dk = dot(
                    jnp.concatenate(slopes, axis=1),
                    jnp.concatenate([q * m for m in masks], axis=0),
                )
                dq = dot(jnp.concatenate(slopes, axis=0), keys, TN)
                at = g * TILE + part_of * LANES
                pgrad[rows, lanes] = (dq * plain).astype(BF16)
                pgrad[rows, aligned(width + at, LANES)] = (dk * plain).astype(BF16)
                pgrad[rows, aligned(2 * width + at, LANES)] = dv.astype(BF16)

        @pl.when(g == 0)
        def _():
            turned_load.wait()

        for i in range(3):
            columns = aligned(i * width + g * TILE, TILE)
            mine[:, columns] = dot(normt[:half], pgrad[:, columns]).astype(BF16)
            theirs[:, columns] = dot(normt[half:], pgrad[:, columns]).astype(BF16)
        for store in stores(g):
            store.start()

    for g in range(steps):
        for store in stores(g):
            store.wait()


def projection_loads(pgrads, wqkv_h, pgrad, wqkv, sem, start):
    width = pgrads[0].shape[1] // 3
    channels = pgrad.shape[1] // 3
    loads = [
        pltpu.make_async_copy(
            field.at[:, pl.ds(i * width, width)],
            pgrad.at[:, pl.ds(i * channels + c * width, width)], sem.at[c * 3 + i],
        )
        for c, field in enumerate(pgrads) for i in range(3)
    ]
    tiles = [
        pltpu.make_async_copy(
            wqkv_h.at[pl.ds(start + n * TILE, TILE)], wqkv.at[pl.ds(n * TILE, TILE)],
            sem.at[3 * len(pgrads) + n],
        )
        for n in range(wqkv.shape[0] // TILE)
    ]
    for load in loads + tiles:
        load.start()
    return loads, tiles


def input_kernel(*refs):
    (pg0, pg1, wqkv_h, normed_h, rstd_h, grad_h, merged,
     pick_first, pick_last, pick_groups, full, side, below, corner,
     pgrad, wqkv, ngrad, normed, rstd, grad, sem, more_sem) = refs
    count, channels = ngrad.shape
    loads, tiles = projection_loads([pg0, pg1], wqkv_h, pgrad, wqkv, sem, 0)
    more = [
        pltpu.make_async_copy(src, dst, more_sem.at[i])
        for i, (src, dst) in enumerate([(normed_h, normed), (rstd_h, rstd), (grad_h, grad)])
    ]
    for load in more:
        load.start()
    for load in loads:
        load.wait()
    for n, load in enumerate(tiles):
        load.wait()
        ngrad[:, pl.ds(n * TILE, TILE)] = dot(
            pgrad[...], wqkv[pl.ds(n * TILE, TILE)], NT
        ).astype(BF16)
    for load in more:
        load.wait()
    places = 2 * WIN * WIN

    @pl.loop(0, count // places)
    def _(w):
        rows = aligned(w * places, places)
        d = ngrad[rows].astype(F32)
        unit = normed[rows].astype(F32)
        mean_d = jnp.mean(d, axis=1, keepdims=True)
        mean_dx = jnp.mean(d * unit, axis=1, keepdims=True)
        part = rstd[rows, :1] * (d - mean_d - unit * mean_dx)
        full[rows] = (part.astype(BF16).astype(F32) + grad[rows].astype(F32)).astype(BF16)

    (n_side, g_side), (n_above, g_above), (n_corner, g_corner) = strip_rows(None, None)
    side_cut = 2 * SHIFT * SHIFT
    first = dot(pick_first[...], full[:count // 2]).astype(BF16)
    last = dot(pick_last[...], full[count // 2:]).astype(BF16)
    groups = dot(pick_groups[...], merged[...]).astype(BF16)
    side[:side_cut] = first[:side_cut]
    side[side_cut:n_side] = last
    below[:n_above] = first[side_cut:side_cut + n_above]
    corner[:n_corner] = first[side_cut + n_above:]
    side[n_side:] = groups[:g_side]
    below[n_above:] = groups[g_side:g_side + g_above]
    corner[n_corner:] = groups[g_side + g_above:]


def unpack_kernel(full, merged, side, below, corner, pick_top, pick_middle, pick_bottom,
                  pick_groups, tokens_out, merged_out):
    count = full.shape[0]
    half = count // 2
    (n_side, _), (n_above, _), (n_corner, _) = strip_rows(None, None)
    side_cut = 2 * SHIFT * SHIFT
    line = half // (2 * WIN)
    pieces = [
        (pick_top, [full[:half], side[:side_cut]]),
        (pick_middle, [full[half:], side[side_cut:n_side]]),
        (pick_bottom, [below[:n_above], corner[:n_corner]]),
    ]
    at = 0
    for pick, held in pieces:
        rows = pick.shape[0] // 2
        out = dot(pick[...], jnp.concatenate(held, axis=0)).astype(BF16)
        for level in range(2):
            start = level * half + at
            tokens_out[start:start + rows] = out[level * rows:(level + 1) * rows]
        at += rows
    held = [merged[...], side[n_side:], below[n_above:], corner[n_corner:]]
    merged_out[...] = dot(pick_groups[...], jnp.concatenate(held, axis=0)).astype(BF16)


def sent(block, sizes, lat_step, lon_step):
    n_lat, n_lon = sizes
    route = [
        (a * n_lon + b, (a + lat_step) % n_lat * n_lon + (b + lon_step) % n_lon)
        for a in range(n_lat) for b in range(n_lon)
    ]
    return lax.ppermute(block, ("lat", "lon"), route)


def sent_strips(strips, sizes, step):
    side, lines, corner = strips
    return [sent(side, sizes, 0, step), sent(lines, sizes, step, 0), sent(corner, sizes, step, step)]


def device_rows(channels, sizes):
    n_lat, n_lon = sizes
    devices = n_lat * n_lon
    rows = channels // devices
    place = np.arange(devices)
    lon = 2 * (place // n_lat % (n_lon // 2)) + place // (devices // 2)
    lat = place % n_lat
    owner = (
        jnp.bitwise_xor(lax.axis_index("lat").astype(jnp.int32), jnp.asarray(lat, jnp.int32)) * n_lon
        + jnp.bitwise_xor(lax.axis_index("lon").astype(jnp.int32), jnp.asarray(lon, jnp.int32))
    )
    rowmap = owner[:, None] * rows + jnp.arange(rows, dtype=jnp.int32)[None, :]
    return owner, rowmap.reshape(channels, 1)


def exchange(block, sizes, lat_bits, lon_bits):
    n_lat, n_lon = sizes
    route = [
        (a * n_lon + b, (a ^ lat_bits) * n_lon + (b ^ lon_bits))
        for a in range(n_lat) for b in range(n_lon)
    ]
    return lax.ppermute(block, ("lat", "lon"), route)


def core_step(theirs, sizes):
    return exchange(theirs, sizes, 0, 1)


def layer_blocks(mine, arrived, sizes):
    blocks = sizes[1] // 2
    rows = mine.shape[0] // blocks
    total = [
        (mine[i * rows:(i + 1) * rows].astype(F32) + arrived[i * rows:(i + 1) * rows].astype(F32))
        for i in range(blocks)
    ]
    return [total[0]] + [t.astype(BF16) for t in total[1:]]


def layer_step(blocks, sizes):
    return [exchange(b, sizes, 0, 2 * i) for i, b in enumerate(blocks) if i]


def column_blocks(kept, arrived, sizes):
    total = kept
    for block in arrived:
        total = total + block.astype(F32)
    rows = total.shape[0] // sizes[0]
    blocks = [total[i * rows:(i + 1) * rows] for i in range(sizes[0])]
    return [blocks[0]] + [b.astype(BF16) for b in blocks[1:]]


def column_step(blocks, sizes):
    return [exchange(b, sizes, i, 0) for i, b in enumerate(blocks) if i]


def pinned(value):
    return pltpu.with_memory_space_constraint(value, pltpu.HBM)


def behind(values, marker):
    *values, _ = lax.optimization_barrier((*values, marker))
    return values


def finished(kept, arrived):
    for block in arrived:
        kept = kept + block.astype(F32)
    return kept


def tied_call(kernel, after, operands, in_specs, out_shape, out_specs, **rest):
    waits = len(after)

    def body(*refs):
        kernel(*refs[waits:])

    return pl.pallas_call(
        body, out_shape=out_shape,
        in_specs=[pl.BlockSpec(memory_space=pl.ANY)] * waits + in_specs, out_specs=out_specs, **rest,
    )(*after, *operands)


def shards(sizes, tokens, qkv_weight, out_weight, merge_weight, merged_grad):
    levels, lat_rows, lon_cols, channels = tokens.shape
    merged_width = merge_weight.shape[1]
    count = levels * lat_rows * lon_cols
    groups = count // 4
    half = channels // 2
    strip_rows.extent = (lat_rows, lon_cols)
    vmem = pl.BlockSpec(memory_space=pltpu.VMEM)
    smem = pl.BlockSpec(memory_space=pltpu.SMEM)
    hbm = pl.BlockSpec(memory_space=pl.ANY)

    def shape(*extent, dtype=BF16):
        return jax.ShapeDtypeStruct(extent, dtype)

    def settings(weight, limit=60):
        return dict(
            compiler_params=pltpu.CompilerParams(vmem_limit_bytes=limit * MIB),
            cost_estimate=pl.CostEstimate(
                flops=int(weight * 1e10), bytes_accessed=16 * MIB, transcendentals=0
            ),
        )

    g_rows, g_cols = lat_rows // 2, lon_cols // 2
    cells = window_cells(levels, lat_rows, lon_cols)
    grps = window_groups(levels, g_rows, g_cols)
    cs = Strips(levels, lat_rows, lon_cols, SHIFT, True)
    gs = Strips(levels, g_rows, g_cols, HALF, False)
    g_strips = [padded(gs.side), padded(gs.above), padded(gs.corner)]
    to = ((0, lon_cols), (lat_rows, 0), (lat_rows, lon_cols))
    g_to = ((0, g_cols), (g_rows, 0), (g_rows, g_cols))
    own_rows = range(SHIFT, SHIFT + lat_rows)
    own_cols = range(SHIFT, SHIFT + lon_cols)
    own = box(levels, own_rows, own_cols)
    g_own = turned_box(levels, range(HALF, HALF + g_rows), range(HALF, HALF + g_cols))
    half_cells = count // 2
    side_cut = levels * SHIFT * SHIFT
    sent_cells = sum((Strips.sent(s, *t) for s, t in zip((cs.side, cs.above, cs.corner), to)), [])
    sent_groups = sum((Strips.sent(s, *t) for s, t in zip(g_strips, g_to)), [])
    held_top = box(levels, range(SHIFT, 2 * SHIFT), own_cols) + cs.side[:side_cut] + cs.above + cs.corner
    held_low = box(levels, range(2 * SHIFT, lat_rows), own_cols) + cs.side[side_cut:]
    depth = max(len(held_top), len(held_low))
    depth += -depth % 16
    held_top += [None] * (depth - len(held_top))
    held_low += [None] * (depth - len(held_low))

    tokens_flat = tokens.reshape(count, channels)
    merged_grad_flat = merged_grad.transpose(0, 2, 1, 3).reshape(groups, merged_width)
    extents = [(n + g, channels) for n, g in strip_rows(None, None)]
    packed = pl.pallas_call(
        pack_kernel,
        out_shape=[shape(*e) for e in extents],
        in_specs=[vmem] * 4, out_specs=[vmem] * 3,
        name="pack_strips", **settings(1, 24),
    )(pinned(tokens_flat), pinned(merged_grad_flat), picks(sent_cells, own), picks(sent_groups, g_own))
    strips = sent_strips(packed, sizes, 1)

    order = jnp.concatenate([picks(cells[:half_cells], held_top), picks(cells[half_cells:], held_low)])
    group = picks(grps, g_own + sum(g_strips, []))
    edge = (lax.axis_index("lat") == 0).astype(jnp.int32).reshape(1)
    owner, rowmap = device_rows(channels, sizes)

    wide = shape(count, channels)
    inner = 2 * 2 * WIN * WIN
    ready = tied_call(
        inner_kernel, packed,
        [pinned(tokens_flat), order[count - inner:], pinned(qkv_weight)],
        [vmem] * 2 + [hbm],
        [shape(inner, channels), shape(inner, channels), shape(inner, LANES, dtype=F32),
         shape(inner, channels), shape(inner, channels, dtype=F32), shape(inner, 3 * channels)],
        [vmem] * 6,
        scratch_shapes=[
            pltpu.VMEM(qkv_weight.shape, BF16),
            pltpu.SemaphoreType.DMA((3 * channels // TILE,)),
        ],
        name="inner_windows", **settings(9, 36),
    )
    normed, normt, proj, dmr, dmm, grad, rstd, merged, out_mine, out_theirs = pl.pallas_call(
        forward_kernel,
        out_shape=[
            wide, shape(channels, count), shape(count, 3 * channels), wide, wide, wide,
            shape(count, LANES, dtype=F32), shape(groups, merged_width),
            shape(half, channels), shape(half, channels),
        ],
        in_specs=[smem] * 2 + [vmem] * 8 + [hbm] * 9,
        out_specs=[hbm] * 6 + [vmem] * 4,
        scratch_shapes=[
            pltpu.VMEM(qkv_weight.shape, BF16),
            pltpu.VMEM(out_weight.shape, BF16),
            pltpu.VMEM(merge_weight.shape, BF16),
            pltpu.VMEM((2, depth, channels), BF16),
            pltpu.VMEM((count, channels), BF16),
            pltpu.VMEM((count, channels), BF16),
            pltpu.VMEM((channels, count), BF16),
            pltpu.VMEM((count, 3 * channels), BF16),
            pltpu.VMEM((count, channels), BF16),
            pltpu.VMEM((count, channels), F32),
            pltpu.VMEM((4, groups, channels), BF16),
            pltpu.VMEM((groups, 4 * channels), BF16),
            pltpu.VMEM((groups, merged_width), BF16),
            pltpu.VMEM((count, channels), BF16),
            pltpu.VMEM((count, channels), BF16),
            pltpu.VMEM((count, channels), BF16),
            pltpu.VMEM((channels, count), BF16),
            pltpu.SemaphoreType.DMA((9,)),
            pltpu.SemaphoreType.DMA((6,)),
        ],
        name="block_forward", **settings(30, 58),
    )(edge, owner, tokens_flat, merged_grad_flat, *strips, order, group, rowmap,
      qkv_weight, out_weight, merge_weight, *ready)

    halves = 2
    width = channels // halves
    steps = width // TILE

    def backward(index, after):
        return tied_call(
            functools.partial(backward_kernel, index), after,
            [edge, pinned(proj), pinned(dmr), pinned(dmm), pinned(normt)], [smem] + [hbm] * 4,
            [shape(count, 3 * width), shape(half, 3 * width), shape(half, 3 * width)], [hbm] * 3,
            scratch_shapes=[
                pltpu.VMEM((5, count, width), BF16),
                pltpu.VMEM((channels, count), BF16),
                pltpu.VMEM((count, 3 * width), BF16),
                pltpu.VMEM((half, 3 * width), BF16),
                pltpu.VMEM((half, 3 * width), BF16),
                pltpu.SemaphoreType.DMA((steps, 5)),
                pltpu.SemaphoreType.DMA((1,)),
                pltpu.SemaphoreType.DMA((steps, 3, 3)),
            ],
            name="attention_backward", **settings(15, 32),
        )

    arrived = core_step(out_theirs, sizes)
    pg0, mine1, theirs1 = backward(0, [])
    out_mine, arrived = behind([out_mine, arrived], pg0)
    layer0 = layer_blocks(out_mine, arrived, sizes)
    arrived0 = layer_step(layer0, sizes)
    arrived = core_step(theirs1, sizes)
    pg1, mine2, theirs2 = backward(1, layer0[1:])
    mine1, arrived, *arrived0 = behind([mine1, arrived] + arrived0, pg1)
    layer1 = layer_blocks(mine1, arrived, sizes)
    arrived1 = layer_step(layer1, sizes)
    arrived = core_step(theirs2, sizes)

    first_picks = picks(cs.side[:side_cut] + cs.above + cs.corner, cells[:half_cells])
    last_picks = picks(cs.side[side_cut:], cells[half_cells:])
    full, *strips = tied_call(
        input_kernel, layer1[1:],
        [pg0, pg1, qkv_weight, pinned(normed), pinned(rstd), pinned(grad), merged,
         first_picks, last_picks, picks(sum(g_strips, []), grps)],
        [hbm] * 6 + [vmem] * 4, [wide] + [shape(*e) for e in extents], [vmem] * 4,
        scratch_shapes=[
            pltpu.VMEM((count, 3 * channels), BF16),
            pltpu.VMEM(qkv_weight.shape, BF16),
            pltpu.VMEM((count, channels), BF16),
            pltpu.VMEM((count, channels), BF16),
            pltpu.VMEM((count, LANES), F32),
            pltpu.VMEM((count, channels), BF16),
            pltpu.SemaphoreType.DMA((3 * halves + channels // TILE,)),
            pltpu.SemaphoreType.DMA((3,)),
        ],
        name="input_backward", **settings(13, 40),
    )
    mine2, arrived = behind([mine2, arrived], full)
    layer2 = layer_blocks(mine2, arrived, sizes)
    arrived2 = layer_step(layer2, sizes)
    strips = sent_strips(strips, sizes, -1)

    arrived1 = behind(arrived1, layer2[1])
    kept = jnp.concatenate([layer0[0], layer1[0]], axis=1)
    joined = [jnp.concatenate(pair, axis=1) for pair in zip(arrived0, arrived1)]
    column1 = column_blocks(kept, joined, sizes)
    got = [Strips.sent(s, *t) for s, t in zip((cs.side, cs.above, cs.corner), to)]
    g_got = sum((Strips.sent(s, *t) for s, t in zip(g_strips, g_to)), [])
    tokens_grad, merged = tied_call(
        unpack_kernel, layer2[1:] + column1[1:],
        [
            full, merged, *strips,
            picks(box(levels, range(SHIFT, 2 * SHIFT), own_cols), cells[:half_cells] + got[0][:side_cut]),
            picks(box(levels, range(2 * SHIFT, lat_rows), own_cols), cells[half_cells:] + got[0][side_cut:]),
            picks(box(levels, range(lat_rows, lat_rows + SHIFT), own_cols), got[1] + got[2]),
            picks(g_own, grps + g_got),
        ],
        [vmem] * 9, [wide, shape(groups, merged_width)], [vmem] * 2,
        name="unpack_strips", **settings(20, 24),
    )
    arrived2 = behind(arrived2, tokens_grad)
    column1[-1:] = behind(column1[-1:], tokens_grad)
    column2 = column_blocks(layer2[0], arrived2, sizes)
    part1 = finished(column1[0], column_step(column1, sizes))
    part2 = finished(column2[0], column_step(column2, sizes))
    out_weight_grad = part1[:, :channels]
    part1 = part1[:, channels:]

    merged = merged.reshape(levels, g_cols, g_rows, merged_width).transpose(0, 2, 1, 3)

    qkv_weight_grad = jnp.concatenate(
        [part[:, i * width:(i + 1) * width] for i in range(3) for part in (part1, part2)],
        axis=1,
    )
    return merged, tokens_grad.reshape(tokens.shape), qkv_weight_grad, out_weight_grad


def solution(mesh):
    sizes = (mesh.shape["lat"], mesh.shape["lon"])
    in_specs = (P(None, "lat", "lon", None), P(), P(), P(), P(None, "lat", "lon", None))
    out_specs = (
        P(None, "lat", "lon", None),
        P(None, "lat", "lon", None),
        P(("lat", "lon"), None),
        P(("lat", "lon"), None),
    )
    return jax.shard_map(
        functools.partial(shards, sizes),
        mesh=mesh, in_specs=in_specs, out_specs=out_specs, check_vma=False,
    )
```

```python
import functools

import jax
import jax.numpy as jnp
import numpy as np
from jax import lax
from jax.experimental import pallas as pl
from jax.experimental.pallas import tpu as pltpu
from jax.sharding import PartitionSpec as P

HEADS = 32
WIN = 8
SHIFT = 4
LANES = 128
HALF = SHIFT // 2
TILE = 256
EPSILON = 1e-05
MIB = 1 << 20

NN = (((1,), (0,)), ((), ()))
NT = (((1,), (1,)), ((), ()))
TN = (((0,), (0,)), ((), ()))
BF16 = jnp.bfloat16
F32 = jnp.float32


def dot(a, b, dims=NN):
    return lax.dot_general(a, b, dims, preferred_element_type=F32)


def window_cells(levels, rows, columns):
    half = WIN // 2
    return [
        (level, wi * WIN + 2 * row + sub % 2, wj * WIN + 2 * column + sub // 2)
        for wi in range(rows // WIN) for wj in range(columns // WIN) for sub in range(4)
        for level in range(levels) for row in range(half) for column in range(half)
    ]


def window_groups(levels, rows, columns):
    half = WIN // 2
    return [
        (level, wi * half + row, wj * half + column)
        for wi in range(rows // half) for wj in range(columns // half)
        for level in range(levels) for row in range(half) for column in range(half)
    ]


def box(levels, rows, columns):
    return [(l, r, c) for l in range(levels) for r in rows for c in columns]


def turned_box(levels, rows, columns):
    return [(l, r, c) for l in range(levels) for c in columns for r in rows]


def padded(cells, step=16):
    return cells + [None] * (-len(cells) % step)


def picks(wanted, held):
    spot = {cell: i for i, cell in enumerate(held) if cell is not None}
    table = np.zeros((len(wanted), len(held)), np.float32)
    for i, cell in enumerate(wanted):
        if cell is not None:
            table[i, spot[cell]] = 1.0
    return jnp.asarray(table, BF16)


class Strips:
    def __init__(self, levels, rows, columns, width, cut):
        self.side = (box(levels, range(width, 2 * width), range(width))
                     + box(levels, range(2 * width, rows), range(width)))
        self.above = box(levels, range(width), range(width, columns))
        self.corner = box(levels, range(width), range(width))
        if not cut:
            self.side = box(levels, range(width, rows), range(width))

    @staticmethod
    def sent(cells, down, across):
        return [None if c is None else (c[0], c[1] + down, c[2] + across) for c in cells]


def head_masks():
    head = lax.broadcasted_iota(jnp.int32, (LANES, LANES), 1) // (LANES // 4)
    return [jnp.where(head == h, 1.0, 0.0).astype(BF16) for h in range(4)]


def region_bias(places, active):
    step = 2 * (WIN // 2)
    one = (lax.broadcasted_iota(jnp.int32, (places, places), 0) // step) % 2
    other = (lax.broadcasted_iota(jnp.int32, (places, places), 1) // step) % 2
    return jnp.where((one != other) & active, -1e30, 0.0)


def score_scale(channels):
    return float((channels // HEADS) ** -0.5 * np.log2(np.e))


def aligned(start, size, step=None):
    return pl.ds(pl.multiple_of(start, step or size), size)


def pack_kernel(tokens, merged_grad, pick_cells, pick_groups, side, above, corner):
    cells = dot(pick_cells[...], tokens[...]).astype(BF16)
    groups = dot(pick_groups[...], merged_grad[...]).astype(BF16)
    at, at_group = 0, 0
    for out, (count, extra) in zip((side, above, corner), strip_rows(pick_cells, pick_groups)):
        out[:count] = cells[at:at + count]
        out[count:] = groups[at_group:at_group + extra]
        at, at_group = at + count, at_group + extra


def strip_rows(pick_cells, pick_groups):
    levels = 2
    rows, columns = strip_rows.extent
    cells = [levels * (rows - SHIFT) * SHIFT, levels * SHIFT * (columns - SHIFT), levels * SHIFT * SHIFT]
    groups = [n // 4 + (-(n // 4)) % 16 for n in cells]
    return list(zip(cells, groups))


def normalized_window(x, rows, xw, normed, rstd):
    xw[rows] = x.astype(BF16)
    center = jnp.mean(x, axis=1, keepdims=True)
    moved = x - center
    scale = lax.rsqrt(jnp.mean(moved * moved, axis=1, keepdims=True) + EPSILON)
    rstd[rows] = jnp.broadcast_to(scale, (x.shape[0], LANES))
    normed[rows] = (moved * scale).astype(BF16)


def attended(proj, rows, lanes, masks, factor, bias, mixture, inverse):
    places = masks[0].shape[0]
    q, k, v = (proj[rows, at] for at in lanes)
    scores = dot(q, jnp.concatenate([k * m for m in masks], axis=0), NT)
    parts = []
    for h in range(4):
        part = scores[:, h * places:(h + 1) * places] * factor
        if bias is not None:
            part = part + bias
        part = part - jnp.max(part, axis=1, keepdims=True)
        parts.append(jnp.exp2(part).astype(BF16))
    values = jnp.concatenate([jnp.concatenate([v * m, m], axis=1) for m in masks], axis=0)
    summed = dot(jnp.concatenate(parts, axis=1), values)
    inv = 1.0 / summed[:, LANES:]
    inverse[rows, lanes[0]] = inv
    mixture[rows, lanes[0]] = (summed[:, :LANES] * inv).astype(BF16)


def inner_kernel(
    tokens, order, wqkv_h, xw, normed, rstd, mixture, inverse, proj, wqkv, in_sem,
):
    count, channels = xw.shape
    places = 2 * WIN * WIN
    tiles = wqkv.shape[1] // TILE

    def load(n):
        columns = aligned(n * TILE, TILE)
        return pltpu.make_async_copy(wqkv_h.at[:, columns], wqkv.at[:, columns], in_sem.at[n])

    for n in range(tiles):
        load(n).start()
    half = tokens.shape[0] // 2
    line = half // (2 * WIN)
    cut = SHIFT * line
    source = jnp.concatenate(
        [tokens[cut:cut + WIN * line], tokens[half + cut:half + cut + WIN * line]], axis=0
    )
    x = dot(order[:, :source.shape[0]], source)
    for w in range(count // places):
        rows = slice(w * places, (w + 1) * places)
        normalized_window(x[rows], rows, xw, normed, rstd)

    @pl.loop(0, tiles)
    def _(n):
        load(n).wait()
        columns = aligned(n * TILE, TILE)
        proj[:, columns] = dot(normed[...], wqkv[:, columns]).astype(BF16)

    masks = head_masks()
    factor = score_scale(channels)

    @pl.loop(0, channels // LANES // 2)
    def _(g):
        for i in range(2):
            lanes = [aligned(j * channels + (2 * g + i) * LANES, LANES) for j in range(3)]
            for w in range(count // places):
                rows = slice(w * places, (w + 1) * places)
                attended(proj, rows, lanes, masks, factor, None, mixture, inverse)


def forward_kernel(
    edge, owner, tokens, merged_grad, side, above, corner, order, group, rowmap,
    wqkv_h, wout_h, wm_h, xw_h, normed_in, rstd_h, mixture_h, inverse_h, proj_in,
    normed_h, normt_h, proj_h, dmr_h, dmm_h, grad_h, rstd, merged, out_mine, out_theirs,
    wqkv, wout, wm, source, xw, normed, proj, mixture, inverse, subs, dsubs, cotangent,
    grad, dmr, dmm, in_sem, out_sem,
):
    count, channels = xw.shape
    places = 2 * WIN * WIN
    windows = count // places
    per_row = windows // 2
    quarter = places // 4
    groups = count // 4
    devices = owner.shape[0]
    block = channels // devices

    loads = [
        pltpu.make_async_copy(src, dst, in_sem.at[i])
        for i, (src, dst) in enumerate([(wqkv_h, wqkv), (wout_h, wout), (wm_h, wm)])
    ]
    outer = count - xw_h.shape[0]
    ready = [
        pltpu.make_async_copy(src, dst.at[pl.ds(outer, count - outer)], in_sem.at[3 + i])
        for i, (src, dst) in enumerate(
            [(xw_h, xw), (normed_in, normed), (rstd_h, rstd), (mixture_h, mixture),
             (inverse_h, inverse), (proj_in, proj)]
        )
    ]
    for load in loads + ready:
        load.start()
    stores = [
        pltpu.make_async_copy(src, dst, out_sem.at[i])
        for i, (src, dst) in enumerate(
            [(normed, normed_h), (proj, proj_h), (wqkv.at[:, pl.ds(count, count)], normt_h),
             (grad, grad_h), (dmr, dmr_h), (dmm, dmm_h)]
        )
    ]

    (n_side, g_side), (n_above, g_above), (n_corner, g_corner) = strip_rows(None, None)
    half = count // 2
    line = half // (2 * WIN)
    cut = SHIFT * line
    side_cut = 2 * SHIFT * SHIFT
    blocks = [
        [tokens[:cut], tokens[half:half + cut], side[:side_cut], above[:n_above], corner[:n_corner]],
        [tokens[cut:cut + WIN * line], tokens[half + cut:half + cut + WIN * line], side[side_cut:n_side]],
    ]
    for wi in range(2):
        at = 0
        for piece in blocks[wi]:
            source[wi, at:at + piece.shape[0]] = piece
            at += piece.shape[0]
        if at < source.shape[1]:
            source[wi, at:] = jnp.zeros((source.shape[1] - at, channels), BF16)

    for wi in range(2):
        first, last = wi * per_row, min((wi + 1) * per_row, outer // places)
        x = dot(order[first * places:last * places], source[wi])
        for w in range(first, last):
            rows = slice(w * places, (w + 1) * places)
            normalized_window(x[(w - first) * places:(w - first + 1) * places], rows, xw, normed, rstd)

    loads[0].wait()
    outer_rows = slice(0, outer)

    @pl.loop(0, wqkv.shape[1] // TILE)
    def _(n):
        columns = aligned(n * TILE, TILE)
        proj[outer_rows, columns] = dot(normed[outer_rows], wqkv[:, columns]).astype(BF16)

    for load in ready:
        load.wait()
    stores[0].start()
    stores[1].start()

    masks = head_masks()
    factor = score_scale(channels)

    edge_bias = region_bias(places, edge[0] == 1)
    held = jnp.concatenate(
        [merged_grad[...], side[n_side:], above[n_above:], corner[n_corner:]], axis=0
    )
    cotangent[...] = dot(group[...], held).astype(BF16)
    loads[2].wait()
    steps = channels // LANES
    per_step = 4 * channels // TILE // steps

    @pl.loop(0, steps)
    def _(g):
        lanes = [aligned(i * channels + g * LANES, LANES) for i in range(3)]
        for w in range(outer // places):
            rows = slice(w * places, (w + 1) * places)
            bias = edge_bias if w < per_row else None
            attended(proj, rows, lanes, masks, factor, bias, mixture, inverse)
        for i in range(per_step):
            at = aligned((g * per_step + i) * TILE, TILE)
            dsubs[:, at] = dot(cotangent[...], wm[at], NT).astype(BF16)

    loads[1].wait()

    @pl.loop(0, channels // TILE)
    def _(n):
        columns = aligned(n * TILE, TILE)
        out = dot(mixture[...], wout[:, columns]) + xw[:, columns].astype(F32)
        out = out.astype(BF16)
        for w in range(windows):
            for s in range(4):
                at = w * places + s * quarter
                subs[s, w * quarter:(w + 1) * quarter, columns] = out[at:at + quarter]

    total = jnp.zeros((groups, 1), F32)
    for s in range(4):
        total += jnp.sum(subs[s].astype(F32), axis=1, keepdims=True)
    center = total / (4 * channels)
    total = jnp.zeros((groups, 1), F32)
    for s in range(4):
        moved = subs[s].astype(F32) - center
        total += jnp.sum(moved * moved, axis=1, keepdims=True)
    scale = lax.rsqrt(total / (4 * channels) + EPSILON)
    result = jnp.zeros((groups, wm.shape[1]), F32)
    for s in range(4):
        unit = ((subs[s].astype(F32) - center) * scale).astype(BF16)
        result += dot(unit, wm[s * channels:(s + 1) * channels])
    merged[...] = result.astype(BF16)

    mean_g = jnp.zeros((groups, 1), F32)
    mean_gx = jnp.zeros((groups, 1), F32)
    for s in range(4):
        d = dsubs[:, s * channels:(s + 1) * channels].astype(F32)
        mean_g += jnp.sum(d, axis=1, keepdims=True)
        mean_gx += jnp.sum(d * ((subs[s].astype(F32) - center) * scale), axis=1, keepdims=True)
    mean_g = mean_g / (4 * channels)
    mean_gx = mean_gx / (4 * channels)
    for s in range(4):
        unit = (subs[s].astype(F32) - center) * scale
        d = dsubs[:, s * channels:(s + 1) * channels].astype(F32)
        d = (scale * (d - mean_g - unit * mean_gx)).astype(BF16)
        for w in range(windows):
            at = w * places + s * quarter
            grad[at:at + quarter] = d[w * quarter:(w + 1) * quarter]
    stores[3].start()

    @pl.loop(0, channels // TILE)
    def _(n):
        columns = aligned(n * TILE, TILE)
        d = dot(grad[...], wout[columns], NT).astype(BF16).astype(F32)
        d = d * inverse[:, columns]
        dmr[:, columns] = d.astype(BF16)
        dmm[:, columns] = (-d * mixture[:, columns].astype(F32)).astype(BF16)

    stores[4].start()
    stores[5].start()

    def turn(field, out):
        if block % 16:
            @pl.loop(0, channels // TILE)
            def _(n):
                rows = aligned(n * TILE, TILE)
                spot = lax.broadcasted_iota(jnp.int32, (TILE, channels), 1)
                pick = jnp.where(spot == rowmap[rows], 1.0, 0.0).astype(BF16)
                out[rows] = dot(pick, field[...], NT).astype(BF16)
        else:
            @pl.loop(0, channels // TILE)
            def _(n):
                rows = aligned(n * TILE, TILE)
                turned[rows] = field[:, rows].T

            for d in range(devices):
                out[d * block:(d + 1) * block] = turned[aligned(owner[d] * block, block)]

    turned, normt, mixt = (wqkv.at[:, pl.ds(i * count, count)] for i in range(3))
    turn(normed, normt)
    stores[2].start()
    turn(mixture, mixt)
    part = channels // 2

    @pl.loop(0, channels // TILE)
    def _(n):
        columns = aligned(n * TILE, TILE)
        out_mine[:, columns] = dot(mixt[:part], grad[:, columns]).astype(BF16)
        out_theirs[:, columns] = dot(mixt[part:], grad[:, columns]).astype(BF16)

    for store in stores:
        store.wait()


def backward_kernel(index, *refs):
    (edge, proj_h, dmr_h, dmm_h, normt_h, pgrad_h, mine_h, theirs_h,
     held, normt, pgrad, mine, theirs, in_sem, sem, out_sem) = refs
    _, count, width = held.shape
    channels = normt.shape[0]
    half = channels // 2
    places = 2 * WIN * WIN
    windows = count // places
    per_row = windows // 2
    masks = head_masks()
    factor = score_scale(channels)
    plain = (channels // HEADS) ** -0.5
    steps = width // TILE

    def loads(g):
        columns = aligned(g * TILE, TILE)
        for i in range(5):
            src = (proj_h, proj_h, proj_h, dmr_h, dmm_h)[i]
            start = (i * channels if i < 3 else 0) + index * width
            yield pltpu.make_async_copy(
                src.at[:, aligned(start + g * TILE, TILE)], held.at[i, :, columns], in_sem.at[g, i]
            )

    def stores(g):
        for i in range(3):
            columns = aligned(i * width + g * TILE, TILE)
            for j, (src, dst) in enumerate(((pgrad, pgrad_h), (mine, mine_h), (theirs, theirs_h))):
                yield pltpu.make_async_copy(src.at[:, columns], dst.at[:, columns], out_sem.at[g, i, j])

    for g in range(steps):
        for load in loads(g):
            load.start()
    turned_load = pltpu.make_async_copy(normt_h, normt, sem.at[0])
    turned_load.start()
    edge_bias = region_bias(places, edge[0] == 1)

    @pl.loop(0, steps)
    def _(g):
        for load in loads(g):
            load.wait()

        for part_of in range(TILE // LANES):
            lanes = aligned(g * TILE + part_of * LANES, LANES)
            for w in range(windows):
                rows = slice(w * places, (w + 1) * places)
                q, k, v, dm, dd = (held[i, rows, lanes] for i in range(5))
                keys = jnp.concatenate([k * m for m in masks], axis=0)
                scores = dot(keys, q, NT)
                values = jnp.concatenate(
                    [jnp.concatenate([v * m, m], axis=1) for m in masks], axis=0
                )
                slope = dot(values, jnp.concatenate([dm, dd], axis=1), NT)
                weights, slopes = [], []
                for h in range(4):
                    block = slice(h * places, (h + 1) * places)
                    part = scores[block] * factor
                    if w < per_row:
                        part = part + edge_bias
                    part = jnp.exp2(part - jnp.max(part, axis=0, keepdims=True))
                    weights.append(part.astype(BF16))
                    slopes.append((part * slope[block]).astype(BF16))
                dv = dot(
                    jnp.concatenate(weights, axis=1),
                    jnp.concatenate([dm * m for m in masks], axis=0),
                )
                dk = dot(
                    jnp.concatenate(slopes, axis=1),
                    jnp.concatenate([q * m for m in masks], axis=0),
                )
                dq = dot(jnp.concatenate(slopes, axis=0), keys, TN)
                at = g * TILE + part_of * LANES
                pgrad[rows, lanes] = (dq * plain).astype(BF16)
                pgrad[rows, aligned(width + at, LANES)] = (dk * plain).astype(BF16)
                pgrad[rows, aligned(2 * width + at, LANES)] = dv.astype(BF16)

        @pl.when(g == 0)
        def _():
            turned_load.wait()

        for i in range(3):
            columns = aligned(i * width + g * TILE, TILE)
            mine[:, columns] = dot(normt[:half], pgrad[:, columns]).astype(BF16)
            theirs[:, columns] = dot(normt[half:], pgrad[:, columns]).astype(BF16)
        for store in stores(g):
            store.start()

    for g in range(steps):
        for store in stores(g):
            store.wait()


def projection_loads(pgrads, wqkv_h, pgrad, wqkv, sem, start):
    width = pgrads[0].shape[1] // 3
    channels = pgrad.shape[1] // 3
    loads = [
        pltpu.make_async_copy(
            field.at[:, pl.ds(i * width, width)],
            pgrad.at[:, pl.ds(i * channels + c * width, width)], sem.at[c * 3 + i],
        )
        for c, field in enumerate(pgrads) for i in range(3)
    ]
    tiles = [
        pltpu.make_async_copy(
            wqkv_h.at[pl.ds(start + n * TILE, TILE)], wqkv.at[pl.ds(n * TILE, TILE)],
            sem.at[3 * len(pgrads) + n],
        )
        for n in range(wqkv.shape[0] // TILE)
    ]
    for load in loads + tiles:
        load.start()
    return loads, tiles


def input_kernel(*refs):
    (pg0, pg1, wqkv_h, normed_h, rstd_h, grad_h, merged,
     pick_first, pick_last, pick_groups, full, side, below, corner,
     pgrad, wqkv, ngrad, normed, rstd, grad, sem, more_sem) = refs
    count, channels = ngrad.shape
    loads, tiles = projection_loads([pg0, pg1], wqkv_h, pgrad, wqkv, sem, 0)
    more = [
        pltpu.make_async_copy(src, dst, more_sem.at[i])
        for i, (src, dst) in enumerate([(normed_h, normed), (rstd_h, rstd), (grad_h, grad)])
    ]
    for load in more:
        load.start()
    for load in loads:
        load.wait()
    for n, load in enumerate(tiles):
        load.wait()
        ngrad[:, pl.ds(n * TILE, TILE)] = dot(
            pgrad[...], wqkv[pl.ds(n * TILE, TILE)], NT
        ).astype(BF16)
    for load in more:
        load.wait()
    places = 2 * WIN * WIN

    @pl.loop(0, count // places)
    def _(w):
        rows = aligned(w * places, places)
        d = ngrad[rows].astype(F32)
        unit = normed[rows].astype(F32)
        mean_d = jnp.mean(d, axis=1, keepdims=True)
        mean_dx = jnp.mean(d * unit, axis=1, keepdims=True)
        part = rstd[rows, :1] * (d - mean_d - unit * mean_dx)
        full[rows] = (part.astype(BF16).astype(F32) + grad[rows].astype(F32)).astype(BF16)

    (n_side, g_side), (n_above, g_above), (n_corner, g_corner) = strip_rows(None, None)
    side_cut = 2 * SHIFT * SHIFT
    first = dot(pick_first[...], full[:count // 2]).astype(BF16)
    last = dot(pick_last[...], full[count // 2:]).astype(BF16)
    groups = dot(pick_groups[...], merged[...]).astype(BF16)
    side[:side_cut] = first[:side_cut]
    side[side_cut:n_side] = last
    below[:n_above] = first[side_cut:side_cut + n_above]
    corner[:n_corner] = first[side_cut + n_above:]
    side[n_side:] = groups[:g_side]
    below[n_above:] = groups[g_side:g_side + g_above]
    corner[n_corner:] = groups[g_side + g_above:]


def unpack_kernel(full, merged, side, below, corner, pick_top, pick_middle, pick_bottom,
                  pick_groups, tokens_out, merged_out):
    count = full.shape[0]
    half = count // 2
    (n_side, _), (n_above, _), (n_corner, _) = strip_rows(None, None)
    side_cut = 2 * SHIFT * SHIFT
    line = half // (2 * WIN)
    pieces = [
        (pick_top, [full[:half], side[:side_cut]]),
        (pick_middle, [full[half:], side[side_cut:n_side]]),
        (pick_bottom, [below[:n_above], corner[:n_corner]]),
    ]
    at = 0
    for pick, held in pieces:
        rows = pick.shape[0] // 2
        out = dot(pick[...], jnp.concatenate(held, axis=0)).astype(BF16)
        for level in range(2):
            start = level * half + at
            tokens_out[start:start + rows] = out[level * rows:(level + 1) * rows]
        at += rows
    held = [merged[...], side[n_side:], below[n_above:], corner[n_corner:]]
    merged_out[...] = dot(pick_groups[...], jnp.concatenate(held, axis=0)).astype(BF16)


def sent(block, sizes, lat_step, lon_step):
    n_lat, n_lon = sizes
    route = [
        (a * n_lon + b, (a + lat_step) % n_lat * n_lon + (b + lon_step) % n_lon)
        for a in range(n_lat) for b in range(n_lon)
    ]
    return lax.ppermute(block, ("lat", "lon"), route)


def sent_strips(strips, sizes, step):
    side, lines, corner = strips
    return [sent(side, sizes, 0, step), sent(lines, sizes, step, 0), sent(corner, sizes, step, step)]


def device_rows(channels, sizes):
    n_lat, n_lon = sizes
    devices = n_lat * n_lon
    rows = channels // devices
    place = np.arange(devices)
    lon = 2 * (place // n_lat % (n_lon // 2)) + place // (devices // 2)
    lat = place % n_lat
    owner = (
        jnp.bitwise_xor(lax.axis_index("lat").astype(jnp.int32), jnp.asarray(lat, jnp.int32)) * n_lon
        + jnp.bitwise_xor(lax.axis_index("lon").astype(jnp.int32), jnp.asarray(lon, jnp.int32))
    )
    rowmap = owner[:, None] * rows + jnp.arange(rows, dtype=jnp.int32)[None, :]
    return owner, rowmap.reshape(channels, 1)


def exchange(block, sizes, lat_bits, lon_bits):
    n_lat, n_lon = sizes
    route = [
        (a * n_lon + b, (a ^ lat_bits) * n_lon + (b ^ lon_bits))
        for a in range(n_lat) for b in range(n_lon)
    ]
    return lax.ppermute(block, ("lat", "lon"), route)


def core_step(theirs, sizes):
    return exchange(theirs, sizes, 0, 1)


def layer_blocks(mine, arrived, sizes):
    blocks = sizes[1] // 2
    rows = mine.shape[0] // blocks
    total = [
        (mine[i * rows:(i + 1) * rows].astype(F32) + arrived[i * rows:(i + 1) * rows].astype(F32))
        for i in range(blocks)
    ]
    return [total[0]] + [t.astype(BF16) for t in total[1:]]


def layer_step(blocks, sizes):
    return [exchange(b, sizes, 0, 2 * i) for i, b in enumerate(blocks) if i]


def column_blocks(kept, arrived, sizes):
    total = kept
    for block in arrived:
        total = total + block.astype(F32)
    rows = total.shape[0] // sizes[0]
    blocks = [total[i * rows:(i + 1) * rows] for i in range(sizes[0])]
    return [blocks[0]] + [b.astype(BF16) for b in blocks[1:]]


def column_step(blocks, sizes):
    return [exchange(b, sizes, i, 0) for i, b in enumerate(blocks) if i]


def pinned(value):
    return pltpu.with_memory_space_constraint(value, pltpu.HBM)


def behind(values, marker):
    *values, _ = lax.optimization_barrier((*values, marker))
    return values


def column_halves(total, sizes, bit):
    blocks = sizes[0] // (2 * bit)
    pairs = total.reshape(blocks, 2, total.shape[0] // (2 * blocks), total.shape[1])
    kept, given = pairs[:, 0], pairs[:, 1]
    return [x.reshape(-1, total.shape[1]) for x in (kept, given.astype(BF16))]


def finished(kept, arrived):
    for block in arrived:
        kept = kept + block.astype(F32)
    return kept


def tied_call(kernel, after, operands, in_specs, out_shape, out_specs, **rest):
    waits = len(after)

    def body(*refs):
        kernel(*refs[waits:])

    return pl.pallas_call(
        body, out_shape=out_shape,
        in_specs=[pl.BlockSpec(memory_space=pl.ANY)] * waits + in_specs, out_specs=out_specs, **rest,
    )(*after, *operands)


def shards(sizes, tokens, qkv_weight, out_weight, merge_weight, merged_grad):
    levels, lat_rows, lon_cols, channels = tokens.shape
    merged_width = merge_weight.shape[1]
    count = levels * lat_rows * lon_cols
    groups = count // 4
    half = channels // 2
    strip_rows.extent = (lat_rows, lon_cols)
    vmem = pl.BlockSpec(memory_space=pltpu.VMEM)
    smem = pl.BlockSpec(memory_space=pltpu.SMEM)
    hbm = pl.BlockSpec(memory_space=pl.ANY)

    def shape(*extent, dtype=BF16):
        return jax.ShapeDtypeStruct(extent, dtype)

    def settings(weight, limit=60):
        return dict(
            compiler_params=pltpu.CompilerParams(vmem_limit_bytes=limit * MIB),
            cost_estimate=pl.CostEstimate(
                flops=int(weight * 1e10), bytes_accessed=16 * MIB, transcendentals=0
            ),
        )

    g_rows, g_cols = lat_rows // 2, lon_cols // 2
    cells = window_cells(levels, lat_rows, lon_cols)
    grps = window_groups(levels, g_rows, g_cols)
    cs = Strips(levels, lat_rows, lon_cols, SHIFT, True)
    gs = Strips(levels, g_rows, g_cols, HALF, False)
    g_strips = [padded(gs.side), padded(gs.above), padded(gs.corner)]
    to = ((0, lon_cols), (lat_rows, 0), (lat_rows, lon_cols))
    g_to = ((0, g_cols), (g_rows, 0), (g_rows, g_cols))
    own_rows = range(SHIFT, SHIFT + lat_rows)
    own_cols = range(SHIFT, SHIFT + lon_cols)
    own = box(levels, own_rows, own_cols)
    g_own = turned_box(levels, range(HALF, HALF + g_rows), range(HALF, HALF + g_cols))
    half_cells = count // 2
    side_cut = levels * SHIFT * SHIFT
    sent_cells = sum((Strips.sent(s, *t) for s, t in zip((cs.side, cs.above, cs.corner), to)), [])
    sent_groups = sum((Strips.sent(s, *t) for s, t in zip(g_strips, g_to)), [])
    held_top = box(levels, range(SHIFT, 2 * SHIFT), own_cols) + cs.side[:side_cut] + cs.above + cs.corner
    held_low = box(levels, range(2 * SHIFT, lat_rows), own_cols) + cs.side[side_cut:]
    depth = max(len(held_top), len(held_low))
    depth += -depth % 16
    held_top += [None] * (depth - len(held_top))
    held_low += [None] * (depth - len(held_low))

    tokens_flat = tokens.reshape(count, channels)
    merged_grad_flat = merged_grad.transpose(0, 2, 1, 3).reshape(groups, merged_width)
    extents = [(n + g, channels) for n, g in strip_rows(None, None)]
    packed = pl.pallas_call(
        pack_kernel,
        out_shape=[shape(*e) for e in extents],
        in_specs=[vmem] * 4, out_specs=[vmem] * 3,
        name="pack_strips", **settings(1),
    )(pinned(tokens_flat), pinned(merged_grad_flat), picks(sent_cells, own), picks(sent_groups, g_own))
    strips = sent_strips(packed, sizes, 1)

    order = jnp.concatenate([picks(cells[:half_cells], held_top), picks(cells[half_cells:], held_low)])
    group = picks(grps, g_own + sum(g_strips, []))
    edge = (lax.axis_index("lat") == 0).astype(jnp.int32).reshape(1)
    owner, rowmap = device_rows(channels, sizes)
    if channels // (sizes[0] * sizes[1]) % 16 == 0:
        rowmap = jnp.zeros((8, 1), jnp.int32)

    wide = shape(count, channels)
    inner = 2 * 2 * WIN * WIN
    ready = tied_call(
        inner_kernel, packed,
        [pinned(tokens_flat), order[count - inner:], pinned(qkv_weight)],
        [vmem] * 2 + [hbm],
        [shape(inner, channels), shape(inner, channels), shape(inner, LANES, dtype=F32),
         shape(inner, channels), shape(inner, channels, dtype=F32), shape(inner, 3 * channels)],
        [vmem] * 6,
        scratch_shapes=[
            pltpu.VMEM(qkv_weight.shape, BF16),
            pltpu.SemaphoreType.DMA((3 * channels // TILE,)),
        ],
        name="inner_windows", **settings(9),
    )
    normed, normt, proj, dmr, dmm, grad, rstd, merged, out_mine, out_theirs = pl.pallas_call(
        forward_kernel,
        out_shape=[
            wide, shape(channels, count), shape(count, 3 * channels), wide, wide, wide,
            shape(count, LANES, dtype=F32), shape(groups, merged_width),
            shape(half, channels), shape(half, channels),
        ],
        in_specs=[smem] * 2 + [vmem] * 8 + [hbm] * 9,
        out_specs=[hbm] * 6 + [vmem] * 4,
        scratch_shapes=[
            pltpu.VMEM(qkv_weight.shape, BF16),
            pltpu.VMEM(out_weight.shape, BF16),
            pltpu.VMEM(merge_weight.shape, BF16),
            pltpu.VMEM((2, depth, channels), BF16),
            pltpu.VMEM((count, channels), BF16),
            pltpu.VMEM((count, channels), BF16),
            pltpu.VMEM((count, 3 * channels), BF16),
            pltpu.VMEM((count, channels), BF16),
            pltpu.VMEM((count, channels), F32),
            pltpu.VMEM((4, groups, channels), BF16),
            pltpu.VMEM((groups, 4 * channels), BF16),
            pltpu.VMEM((groups, merged_width), BF16),
            pltpu.VMEM((count, channels), BF16),
            pltpu.VMEM((count, channels), BF16),
            pltpu.VMEM((count, channels), BF16),
            pltpu.SemaphoreType.DMA((9,)),
            pltpu.SemaphoreType.DMA((6,)),
        ],
        name="block_forward", **settings(30, 55),
    )(edge, owner, tokens_flat, merged_grad_flat, *strips, order, group, rowmap,
      qkv_weight, out_weight, merge_weight, *ready)

    halves = 2
    width = channels // halves
    steps = width // TILE

    def backward(index, after):
        return tied_call(
            functools.partial(backward_kernel, index), after,
            [edge, pinned(proj), pinned(dmr), pinned(dmm), pinned(normt)], [smem] + [hbm] * 4,
            [shape(count, 3 * width), shape(half, 3 * width), shape(half, 3 * width)], [hbm] * 3,
            scratch_shapes=[
                pltpu.VMEM((5, count, width), BF16),
                pltpu.VMEM((channels, count), BF16),
                pltpu.VMEM((count, 3 * width), BF16),
                pltpu.VMEM((half, 3 * width), BF16),
                pltpu.VMEM((half, 3 * width), BF16),
                pltpu.SemaphoreType.DMA((steps, 5)),
                pltpu.SemaphoreType.DMA((1,)),
                pltpu.SemaphoreType.DMA((steps, 3, 3)),
            ],
            name="attention_backward", **settings(15, 32),
        )

    arrived = core_step(out_theirs, sizes)
    pg0, mine1, theirs1 = backward(0, [])
    out_mine, arrived = behind([out_mine, arrived], pg0)
    layer0 = layer_blocks(out_mine, arrived, sizes)
    arrived0 = layer_step(layer0, sizes)
    arrived = core_step(theirs1, sizes)
    pg1, mine2, theirs2 = backward(1, layer0[1:])
    mine1, arrived, *arrived0 = behind([mine1, arrived] + arrived0, pg1)
    layer1 = layer_blocks(mine1, arrived, sizes)
    arrived1 = layer_step(layer1, sizes)
    theirs2, = behind([theirs2], arrived0)
    arrived = core_step(theirs2, sizes)
    layer2 = layer_blocks(mine2, arrived, sizes)
    arrived2 = layer_step(layer2, sizes)

    first_picks = picks(cs.side[:side_cut] + cs.above + cs.corner, cells[:half_cells])
    last_picks = picks(cs.side[side_cut:], cells[half_cells:])
    full, *strips = tied_call(
        input_kernel, layer1[1:] + layer2[1:],
        [pg0, pg1, qkv_weight, pinned(normed), pinned(rstd), pinned(grad), merged,
         first_picks, last_picks, picks(sum(g_strips, []), grps)],
        [hbm] * 6 + [vmem] * 4, [wide] + [shape(*e) for e in extents], [vmem] * 4,
        scratch_shapes=[
            pltpu.VMEM((count, 3 * channels), BF16),
            pltpu.VMEM(qkv_weight.shape, BF16),
            pltpu.VMEM((count, channels), BF16),
            pltpu.VMEM((count, channels), BF16),
            pltpu.VMEM((count, LANES), F32),
            pltpu.VMEM((count, channels), BF16),
            pltpu.SemaphoreType.DMA((3 * halves + channels // TILE,)),
            pltpu.SemaphoreType.DMA((3,)),
        ],
        name="input_backward", **settings(13, 40),
    )
    arrived1 = behind(arrived1, full)
    strips = sent_strips(behind(strips, arrived1), sizes, -1)

    total1 = jnp.concatenate([layer0[0], layer1[0]], axis=1)
    for pair in zip(arrived0, arrived1):
        total1 = total1 + jnp.concatenate(pair, axis=1).astype(F32)
    kept1, given1 = column_halves(total1, sizes, 1)
    got1 = exchange(given1, sizes, 1, 0)

    part1 = kept1 + got1.astype(F32)
    bit = 2
    while bit < sizes[0]:
        kept1, given1 = column_halves(part1, sizes, bit)
        part1 = kept1 + exchange(given1, sizes, bit, 0).astype(F32)
        bit *= 2
    column2 = column_blocks(layer2[0], arrived2, sizes)
    got2 = column_step(column2, sizes)

    got = [Strips.sent(s, *t) for s, t in zip((cs.side, cs.above, cs.corner), to)]
    g_got = sum((Strips.sent(s, *t) for s, t in zip(g_strips, g_to)), [])
    tokens_grad, merged = tied_call(
        unpack_kernel, column2[1:] + [given1],
        [
            full, merged, *strips,
            picks(box(levels, range(SHIFT, 2 * SHIFT), own_cols), cells[:half_cells] + got[0][:side_cut]),
            picks(box(levels, range(2 * SHIFT, lat_rows), own_cols), cells[half_cells:] + got[0][side_cut:]),
            picks(box(levels, range(lat_rows, lat_rows + SHIFT), own_cols), got[1] + got[2]),
            picks(g_own, grps + g_got),
        ],
        [vmem] * 9, [wide, shape(groups, merged_width)], [vmem] * 2,
        name="unpack_strips", **settings(20, 24),
    )
    part2 = finished(column2[0], behind(got2, tokens_grad))
    out_weight_grad = part1[:, :channels]
    part1 = part1[:, channels:]

    merged = merged.reshape(levels, g_cols, g_rows, merged_width).transpose(0, 2, 1, 3)

    qkv_weight_grad = jnp.concatenate(
        [part[:, i * width:(i + 1) * width] for i in range(3) for part in (part1, part2)],
        axis=1,
    )
    return merged, tokens_grad.reshape(tokens.shape), qkv_weight_grad, out_weight_grad


def solution(mesh):
    sizes = (mesh.shape["lat"], mesh.shape["lon"])
    in_specs = (P(None, "lat", "lon", None), P(), P(), P(), P(None, "lat", "lon", None))
    out_specs = (
        P(None, "lat", "lon", None),
        P(None, "lat", "lon", None),
        P(("lat", "lon"), None),
        P(("lat", "lon"), None),
    )
    return jax.shard_map(
        functools.partial(shards, sizes),
        mesh=mesh, in_specs=in_specs, out_specs=out_specs, check_vma=False,
    )
```

```python
import functools

import jax
import jax.numpy as jnp
import numpy as np
from jax import lax
from jax.experimental import pallas as pl
from jax.experimental.pallas import tpu as pltpu
from jax.sharding import PartitionSpec as P

HEADS = 32
WIN = 8
SHIFT = 4
LANES = 128
HALF = SHIFT // 2
TILE = 256
EPSILON = 1e-05
MIB = 1 << 20

NN = (((1,), (0,)), ((), ()))
NT = (((1,), (1,)), ((), ()))
TN = (((0,), (0,)), ((), ()))
BF16 = jnp.bfloat16
F32 = jnp.float32


def dot(a, b, dims=NN):
    return lax.dot_general(a, b, dims, preferred_element_type=F32)


def window_cells(levels, rows, columns):
    half = WIN // 2
    return [
        (level, wi * WIN + 2 * row + sub % 2, wj * WIN + 2 * column + sub // 2)
        for wi in range(rows // WIN) for wj in range(columns // WIN) for sub in range(4)
        for level in range(levels) for row in range(half) for column in range(half)
    ]


def window_groups(levels, rows, columns):
    half = WIN // 2
    return [
        (level, wi * half + row, wj * half + column)
        for wi in range(rows // half) for wj in range(columns // half)
        for level in range(levels) for row in range(half) for column in range(half)
    ]


def box(levels, rows, columns):
    return [(l, r, c) for l in range(levels) for r in rows for c in columns]


def turned_box(levels, rows, columns):
    return [(l, r, c) for l in range(levels) for c in columns for r in rows]


def padded(cells, step=16):
    return cells + [None] * (-len(cells) % step)


def picks(wanted, held):
    spot = {cell: i for i, cell in enumerate(held) if cell is not None}
    table = np.zeros((len(wanted), len(held)), np.float32)
    for i, cell in enumerate(wanted):
        if cell is not None:
            table[i, spot[cell]] = 1.0
    return jnp.asarray(table, BF16)


class Strips:
    def __init__(self, levels, rows, columns, width, cut):
        self.side = (box(levels, range(width, 2 * width), range(width))
                     + box(levels, range(2 * width, rows), range(width)))
        self.above = box(levels, range(width), range(width, columns))
        self.corner = box(levels, range(width), range(width))
        if not cut:
            self.side = box(levels, range(width, rows), range(width))

    @staticmethod
    def sent(cells, down, across):
        return [None if c is None else (c[0], c[1] + down, c[2] + across) for c in cells]


def head_masks():
    head = lax.broadcasted_iota(jnp.int32, (LANES, LANES), 1) // (LANES // 4)
    return [jnp.where(head == h, 1.0, 0.0).astype(BF16) for h in range(4)]


def region_bias(places, active):
    step = 2 * (WIN // 2)
    one = (lax.broadcasted_iota(jnp.int32, (places, places), 0) // step) % 2
    other = (lax.broadcasted_iota(jnp.int32, (places, places), 1) // step) % 2
    return jnp.where((one != other) & active, -1e30, 0.0)


def score_scale(channels):
    return float((channels // HEADS) ** -0.5 * np.log2(np.e))


def aligned(start, size, step=None):
    return pl.ds(pl.multiple_of(start, step or size), size)


def pack_kernel(tokens, merged_grad, pick_cells, pick_groups, side, above, corner):
    cells = dot(pick_cells[...], tokens[...]).astype(BF16)
    groups = dot(pick_groups[...], merged_grad[...]).astype(BF16)
    at, at_group = 0, 0
    for out, (count, extra) in zip((side, above, corner), strip_rows(pick_cells, pick_groups)):
        out[:count] = cells[at:at + count]
        out[count:] = groups[at_group:at_group + extra]
        at, at_group = at + count, at_group + extra


def strip_rows(pick_cells, pick_groups):
    levels = 2
    rows, columns = strip_rows.extent
    cells = [levels * (rows - SHIFT) * SHIFT, levels * SHIFT * (columns - SHIFT), levels * SHIFT * SHIFT]
    groups = [n // 4 + (-(n // 4)) % 16 for n in cells]
    return list(zip(cells, groups))


def by_rows(count, step, body):
    @pl.loop(0, count // step)
    def _(i):
        body(aligned(i * step, step))


def normalize_rows(count, raw, xw, normed, rstd):
    def block(rows):
        x = raw[rows]
        xw[rows] = x.astype(BF16)
        center = jnp.mean(x, axis=1, keepdims=True)
        moved = x - center
        scale = lax.rsqrt(jnp.mean(moved * moved, axis=1, keepdims=True) + EPSILON)
        rstd[rows] = jnp.broadcast_to(scale, (x.shape[0], LANES))
        normed[rows] = (moved * scale).astype(BF16)

    by_rows(count, 32, block)


def attended(proj, rows, lanes, masks, factor, bias, mixture, inverse):
    places = masks[0].shape[0]
    q, k, v = (proj[rows, at] for at in lanes)
    scores = dot(q, jnp.concatenate([k * m for m in masks], axis=0), NT)
    parts = []
    for h in range(4):
        part = scores[:, h * places:(h + 1) * places] * factor
        if bias is not None:
            part = part + bias
        part = part - jnp.max(part, axis=1, keepdims=True)
        parts.append(jnp.exp2(part).astype(BF16))
    values = jnp.concatenate([jnp.concatenate([v * m, m], axis=1) for m in masks], axis=0)
    summed = dot(jnp.concatenate(parts, axis=1), values)
    inv = 1.0 / summed[:, LANES:]
    inverse[rows, lanes[0]] = inv
    mixture[rows, lanes[0]] = (summed[:, :LANES] * inv).astype(BF16)


def inner_kernel(
    tokens, order, wqkv_h, xw, normed, rstd, mixture, inverse, proj, wqkv, raw, in_sem,
):
    count, channels = xw.shape
    places = 2 * WIN * WIN
    tiles = wqkv.shape[1] // TILE

    def load(n):
        columns = aligned(n * TILE, TILE)
        return pltpu.make_async_copy(wqkv_h.at[:, columns], wqkv.at[:, columns], in_sem.at[n])

    for n in range(tiles):
        load(n).start()
    half = tokens.shape[0] // 2
    line = half // (2 * WIN)
    cut = SHIFT * line
    source = jnp.concatenate(
        [tokens[cut:cut + WIN * line], tokens[half + cut:half + cut + WIN * line]], axis=0
    )
    raw[...] = dot(order[:, :source.shape[0]], source)
    normalize_rows(count, raw, xw, normed, rstd)

    @pl.loop(0, tiles)
    def _(n):
        load(n).wait()
        columns = aligned(n * TILE, TILE)
        proj[:, columns] = dot(normed[...], wqkv[:, columns]).astype(BF16)

    masks = head_masks()
    factor = score_scale(channels)

    @pl.loop(0, channels // LANES // 2)
    def _(g):
        for i in range(2):
            lanes = [aligned(j * channels + (2 * g + i) * LANES, LANES) for j in range(3)]
            for w in range(count // places):
                rows = slice(w * places, (w + 1) * places)
                attended(proj, rows, lanes, masks, factor, None, mixture, inverse)


def forward_kernel(
    edge, owner, tokens, merged_grad, side, above, corner, order, group, rowmap,
    wqkv_h, wout_h, wm_h, xw_h, normed_in, rstd_h, mixture_h, inverse_h, proj_in,
    normed_h, normt_h, proj_h, dmr_h, dmm_h, grad_h, rstd, merged, out_mine, out_theirs,
    wqkv, wout, wm, source, xw, normed, proj, mixture, inverse, subs, dsubs, cotangent,
    grad, dmr, dmm, in_sem, out_sem,
):
    count, channels = xw.shape
    places = 2 * WIN * WIN
    windows = count // places
    per_row = windows // 2
    quarter = places // 4
    groups = count // 4
    devices = owner.shape[0]
    block = channels // devices

    loads = [
        pltpu.make_async_copy(src, dst, in_sem.at[i])
        for i, (src, dst) in enumerate([(wqkv_h, wqkv), (wout_h, wout), (wm_h, wm)])
    ]
    outer = count - xw_h.shape[0]
    ready = [
        pltpu.make_async_copy(src, dst.at[pl.ds(outer, count - outer)], in_sem.at[3 + i])
        for i, (src, dst) in enumerate(
            [(xw_h, xw), (normed_in, normed), (rstd_h, rstd), (mixture_h, mixture),
             (inverse_h, inverse), (proj_in, proj)]
        )
    ]
    for load in loads + ready:
        load.start()
    stores = [
        pltpu.make_async_copy(src, dst, out_sem.at[i])
        for i, (src, dst) in enumerate(
            [(normed, normed_h), (proj, proj_h), (wqkv.at[:, pl.ds(count, count)], normt_h),
             (grad, grad_h), (dmr, dmr_h), (dmm, dmm_h)]
        )
    ]

    (n_side, g_side), (n_above, g_above), (n_corner, g_corner) = strip_rows(None, None)
    half = count // 2
    line = half // (2 * WIN)
    cut = SHIFT * line
    side_cut = 2 * SHIFT * SHIFT
    blocks = [
        [tokens[:cut], tokens[half:half + cut], side[:side_cut], above[:n_above], corner[:n_corner]],
        [tokens[cut:cut + WIN * line], tokens[half + cut:half + cut + WIN * line], side[side_cut:n_side]],
    ]
    for wi in range(2):
        at = 0
        for piece in blocks[wi]:
            source[wi, at:at + piece.shape[0]] = piece
            at += piece.shape[0]
        if at < source.shape[1]:
            source[wi, at:] = jnp.zeros((source.shape[1] - at, channels), BF16)

    for wi in range(2):
        first, last = wi * per_row, min((wi + 1) * per_row, outer // places)
        inverse[first * places:last * places] = dot(
            order[first * places:last * places], source[wi]
        )
    normalize_rows(outer, inverse, xw, normed, rstd)

    loads[0].wait()
    outer_rows = slice(0, outer)

    @pl.loop(0, wqkv.shape[1] // TILE)
    def _(n):
        columns = aligned(n * TILE, TILE)
        proj[outer_rows, columns] = dot(normed[outer_rows], wqkv[:, columns]).astype(BF16)

    for load in ready:
        load.wait()
    stores[0].start()
    stores[1].start()

    masks = head_masks()
    factor = score_scale(channels)

    edge_bias = region_bias(places, edge[0] == 1)
    held = jnp.concatenate(
        [merged_grad[...], side[n_side:], above[n_above:], corner[n_corner:]], axis=0
    )
    cotangent[...] = dot(group[...], held).astype(BF16)
    loads[2].wait()
    steps = channels // LANES
    per_step = 4 * channels // TILE // steps

    @pl.loop(0, steps)
    def _(g):
        lanes = [aligned(i * channels + g * LANES, LANES) for i in range(3)]
        for w in range(outer // places):
            rows = slice(w * places, (w + 1) * places)
            bias = edge_bias if w < per_row else None
            attended(proj, rows, lanes, masks, factor, bias, mixture, inverse)
        for i in range(per_step):
            at = aligned((g * per_step + i) * TILE, TILE)
            dsubs[:, at] = dot(cotangent[...], wm[at], NT).astype(BF16)

    loads[1].wait()

    @pl.loop(0, channels // TILE)
    def _(n):
        columns = aligned(n * TILE, TILE)
        out = dot(mixture[...], wout[:, columns]) + xw[:, columns].astype(F32)
        out = out.astype(BF16)
        for w in range(windows):
            for s in range(4):
                at = w * places + s * quarter
                spot = aligned(s * channels + n * TILE, TILE)
                subs[w * quarter:(w + 1) * quarter, spot] = out[at:at + quarter]

    depth = 4 * channels

    def merging(rows):
        values = [subs[rows, s * channels:(s + 1) * channels].astype(F32) for s in range(4)]
        center = sum(jnp.sum(v, axis=1, keepdims=True) for v in values) / depth
        values = [v - center for v in values]
        spread = sum(jnp.sum(v * v, axis=1, keepdims=True) for v in values) / depth
        scale = lax.rsqrt(spread + EPSILON)
        values = [v * scale for v in values]
        for s in range(4):
            subs[rows, s * channels:(s + 1) * channels] = values[s].astype(BF16)
        slopes = [dsubs[rows, s * channels:(s + 1) * channels].astype(F32) for s in range(4)]
        mean_g = sum(jnp.sum(d, axis=1, keepdims=True) for d in slopes) / depth
        mean_gx = sum(jnp.sum(d * v, axis=1, keepdims=True) for d, v in zip(slopes, values)) / depth
        for s in range(4):
            d = scale * (slopes[s] - mean_g - values[s] * mean_gx)
            dsubs[rows, s * channels:(s + 1) * channels] = d.astype(BF16)

    by_rows(groups, 16, merging)
    for w in range(windows):
        for s in range(4):
            at = w * places + s * quarter
            grad[at:at + quarter] = dsubs[
                w * quarter:(w + 1) * quarter, s * channels:(s + 1) * channels
            ]
    stores[3].start()

    @pl.loop(0, channels // TILE)
    def _(n):
        columns = aligned(n * TILE, TILE)
        dmr[:, columns] = dot(grad[...], wout[columns], NT).astype(BF16)

    @pl.loop(0, wm.shape[1] // TILE)
    def _(n):
        columns = aligned(n * TILE, TILE)
        merged[:, columns] = dot(subs[...], wm[:, columns]).astype(BF16)

    def scaled(rows):
        d = dmr[rows].astype(F32) * inverse[rows]
        dmr[rows] = d.astype(BF16)
        dmm[rows] = (-d * mixture[rows].astype(F32)).astype(BF16)

    by_rows(count, 32, scaled)
    stores[4].start()
    stores[5].start()

    def turn(field, out):
        if block % 16:
            @pl.loop(0, channels // TILE)
            def _(n):
                rows = aligned(n * TILE, TILE)
                spot = lax.broadcasted_iota(jnp.int32, (TILE, channels), 1)
                pick = jnp.where(spot == rowmap[rows], 1.0, 0.0).astype(BF16)
                out[rows] = dot(pick, field[...], NT).astype(BF16)
        else:
            @pl.loop(0, channels // TILE)
            def _(n):
                rows = aligned(n * TILE, TILE)
                turned[rows] = field[:, rows].T

            for d in range(devices):
                out[d * block:(d + 1) * block] = turned[aligned(owner[d] * block, block)]

    turned, normt, mixt = (wqkv.at[:, pl.ds(i * count, count)] for i in range(3))
    turn(normed, normt)
    stores[2].start()
    turn(mixture, mixt)
    part = channels // 2

    @pl.loop(0, channels // TILE)
    def _(n):
        columns = aligned(n * TILE, TILE)
        out_mine[:, columns] = dot(mixt[:part], grad[:, columns]).astype(BF16)
        out_theirs[:, columns] = dot(mixt[part:], grad[:, columns]).astype(BF16)

    for store in stores:
        store.wait()


def backward_kernel(index, *refs):
    (edge, proj_h, dmr_h, dmm_h, normt_h, pgrad_h, mine_h, theirs_h,
     held, normt, pgrad, mine, theirs, in_sem, sem, out_sem) = refs
    _, count, width = held.shape
    channels = normt.shape[0]
    half = channels // 2
    places = 2 * WIN * WIN
    windows = count // places
    per_row = windows // 2
    masks = head_masks()
    factor = score_scale(channels)
    plain = (channels // HEADS) ** -0.5
    steps = width // TILE

    def loads(g):
        columns = aligned(g * TILE, TILE)
        for i in range(5):
            src = (proj_h, proj_h, proj_h, dmr_h, dmm_h)[i]
            start = (i * channels if i < 3 else 0) + index * width
            yield pltpu.make_async_copy(
                src.at[:, aligned(start + g * TILE, TILE)], held.at[i, :, columns], in_sem.at[g, i]
            )

    def stores(g):
        for i in range(3):
            columns = aligned(i * width + g * TILE, TILE)
            for j, (src, dst) in enumerate(((pgrad, pgrad_h), (mine, mine_h), (theirs, theirs_h))):
                yield pltpu.make_async_copy(src.at[:, columns], dst.at[:, columns], out_sem.at[g, i, j])

    for g in range(steps):
        for load in loads(g):
            load.start()
    turned_load = pltpu.make_async_copy(normt_h, normt, sem.at[0])
    turned_load.start()
    edge_bias = region_bias(places, edge[0] == 1)

    @pl.loop(0, steps)
    def _(g):
        for load in loads(g):
            load.wait()

        for part_of in range(TILE // LANES):
            lanes = aligned(g * TILE + part_of * LANES, LANES)
            for w in range(windows):
                rows = slice(w * places, (w + 1) * places)
                q, k, v, dm, dd = (held[i, rows, lanes] for i in range(5))
                keys = jnp.concatenate([k * m for m in masks], axis=0)
                scores = dot(keys, q, NT)
                values = jnp.concatenate(
                    [jnp.concatenate([v * m, m], axis=1) for m in masks], axis=0
                )
                slope = dot(values, jnp.concatenate([dm, dd], axis=1), NT)
                weights, slopes = [], []
                for h in range(4):
                    block = slice(h * places, (h + 1) * places)
                    part = scores[block] * factor
                    if w < per_row:
                        part = part + edge_bias
                    part = jnp.exp2(part - jnp.max(part, axis=0, keepdims=True))
                    weights.append(part.astype(BF16))
                    slopes.append((part * slope[block]).astype(BF16))
                dv = dot(
                    jnp.concatenate(weights, axis=1),
                    jnp.concatenate([dm * m for m in masks], axis=0),
                )
                dk = dot(
                    jnp.concatenate(slopes, axis=1),
                    jnp.concatenate([q * m for m in masks], axis=0),
                )
                dq = dot(jnp.concatenate(slopes, axis=0), keys, TN)
                at = g * TILE + part_of * LANES
                pgrad[rows, lanes] = (dq * plain).astype(BF16)
                pgrad[rows, aligned(width + at, LANES)] = (dk * plain).astype(BF16)
                pgrad[rows, aligned(2 * width + at, LANES)] = dv.astype(BF16)

        @pl.when(g == 0)
        def _():
            turned_load.wait()

        for i in range(3):
            columns = aligned(i * width + g * TILE, TILE)
            mine[:, columns] = dot(normt[:half], pgrad[:, columns]).astype(BF16)
            theirs[:, columns] = dot(normt[half:], pgrad[:, columns]).astype(BF16)
        for store in stores(g):
            store.start()

    for g in range(steps):
        for store in stores(g):
            store.wait()


def projection_loads(pgrads, wqkv_h, pgrad, wqkv, sem, start):
    width = pgrads[0].shape[1] // 3
    channels = pgrad.shape[1] // 3
    loads = [
        pltpu.make_async_copy(
            field.at[:, pl.ds(i * width, width)],
            pgrad.at[:, pl.ds(i * channels + c * width, width)], sem.at[c * 3 + i],
        )
        for c, field in enumerate(pgrads) for i in range(3)
    ]
    tiles = [
        pltpu.make_async_copy(
            wqkv_h.at[pl.ds(start + n * TILE, TILE)], wqkv.at[pl.ds(n * TILE, TILE)],
            sem.at[3 * len(pgrads) + n],
        )
        for n in range(wqkv.shape[0] // TILE)
    ]
    for load in loads + tiles:
        load.start()
    return loads, tiles


def input_kernel(*refs):
    (pg0, pg1, wqkv_h, normed_h, rstd_h, grad_h, merged,
     pick_first, pick_last, pick_groups, full, side, below, corner,
     pgrad, wqkv, ngrad, normed, rstd, grad, sem, more_sem) = refs
    count, channels = ngrad.shape
    loads, tiles = projection_loads([pg0, pg1], wqkv_h, pgrad, wqkv, sem, 0)
    more = [
        pltpu.make_async_copy(src, dst, more_sem.at[i])
        for i, (src, dst) in enumerate([(normed_h, normed), (rstd_h, rstd), (grad_h, grad)])
    ]
    for load in more:
        load.start()
    for load in loads:
        load.wait()
    for n, load in enumerate(tiles):
        load.wait()
        ngrad[:, pl.ds(n * TILE, TILE)] = dot(
            pgrad[...], wqkv[pl.ds(n * TILE, TILE)], NT
        ).astype(BF16)
    for load in more:
        load.wait()
    places = 2 * WIN * WIN

    def block(rows):
        d = ngrad[rows].astype(F32)
        unit = normed[rows].astype(F32)
        mean_d = jnp.mean(d, axis=1, keepdims=True)
        mean_dx = jnp.mean(d * unit, axis=1, keepdims=True)
        part = rstd[rows, :1] * (d - mean_d - unit * mean_dx)
        full[rows] = (part.astype(BF16).astype(F32) + grad[rows].astype(F32)).astype(BF16)

    by_rows(count, 32, block)

    (n_side, g_side), (n_above, g_above), (n_corner, g_corner) = strip_rows(None, None)
    side_cut = 2 * SHIFT * SHIFT
    first = dot(pick_first[...], full[:count // 2]).astype(BF16)
    last = dot(pick_last[...], full[count // 2:]).astype(BF16)
    groups = dot(pick_groups[...], merged[...]).astype(BF16)
    side[:side_cut] = first[:side_cut]
    side[side_cut:n_side] = last
    below[:n_above] = first[side_cut:side_cut + n_above]
    corner[:n_corner] = first[side_cut + n_above:]
    side[n_side:] = groups[:g_side]
    below[n_above:] = groups[g_side:g_side + g_above]
    corner[n_corner:] = groups[g_side + g_above:]


def unpack_kernel(full, merged, side, below, corner, pick_top, pick_middle, pick_bottom,
                  pick_groups, tokens_out, merged_out):
    count = full.shape[0]
    half = count // 2
    (n_side, _), (n_above, _), (n_corner, _) = strip_rows(None, None)
    side_cut = 2 * SHIFT * SHIFT
    line = half // (2 * WIN)
    pieces = [
        (pick_top, [full[:half], side[:side_cut]]),
        (pick_middle, [full[half:], side[side_cut:n_side]]),
        (pick_bottom, [below[:n_above], corner[:n_corner]]),
    ]
    at = 0
    for pick, held in pieces:
        rows = pick.shape[0] // 2
        out = dot(pick[...], jnp.concatenate(held, axis=0)).astype(BF16)
        for level in range(2):
            start = level * half + at
            tokens_out[start:start + rows] = out[level * rows:(level + 1) * rows]
        at += rows
    held = [merged[...], side[n_side:], below[n_above:], corner[n_corner:]]
    merged_out[...] = dot(pick_groups[...], jnp.concatenate(held, axis=0)).astype(BF16)


def sent(block, sizes, lat_step, lon_step):
    n_lat, n_lon = sizes
    route = [
        (a * n_lon + b, (a + lat_step) % n_lat * n_lon + (b + lon_step) % n_lon)
        for a in range(n_lat) for b in range(n_lon)
    ]
    return lax.ppermute(block, ("lat", "lon"), route)


def sent_strips(strips, sizes, step):
    side, lines, corner = strips
    return [sent(side, sizes, 0, step), sent(lines, sizes, step, 0), sent(corner, sizes, step, step)]


def device_rows(channels, sizes):
    n_lat, n_lon = sizes
    devices = n_lat * n_lon
    rows = channels // devices
    place = np.arange(devices)
    lon = 2 * (place // n_lat % (n_lon // 2)) + place // (devices // 2)
    lat = place % n_lat
    owner = (
        jnp.bitwise_xor(lax.axis_index("lat").astype(jnp.int32), jnp.asarray(lat, jnp.int32)) * n_lon
        + jnp.bitwise_xor(lax.axis_index("lon").astype(jnp.int32), jnp.asarray(lon, jnp.int32))
    )
    rowmap = owner[:, None] * rows + jnp.arange(rows, dtype=jnp.int32)[None, :]
    return owner, rowmap.reshape(channels, 1)


def exchange(block, sizes, lat_bits, lon_bits):
    n_lat, n_lon = sizes
    route = [
        (a * n_lon + b, (a ^ lat_bits) * n_lon + (b ^ lon_bits))
        for a in range(n_lat) for b in range(n_lon)
    ]
    return lax.ppermute(block, ("lat", "lon"), route)


def core_step(theirs, sizes):
    return exchange(theirs, sizes, 0, 1)


def layer_blocks(mine, arrived, sizes):
    blocks = sizes[1] // 2
    rows = mine.shape[0] // blocks
    total = [
        (mine[i * rows:(i + 1) * rows].astype(F32) + arrived[i * rows:(i + 1) * rows].astype(F32))
        for i in range(blocks)
    ]
    return [total[0]] + [t.astype(BF16) for t in total[1:]]


def layer_step(blocks, sizes):
    return [exchange(b, sizes, 0, 2 * i) for i, b in enumerate(blocks) if i]


def column_blocks(kept, arrived, sizes):
    total = kept
    for block in arrived:
        total = total + block.astype(F32)
    rows = total.shape[0] // sizes[0]
    blocks = [total[i * rows:(i + 1) * rows] for i in range(sizes[0])]
    return [blocks[0]] + [b.astype(BF16) for b in blocks[1:]]


def column_step(blocks, sizes):
    return [exchange(b, sizes, i, 0) for i, b in enumerate(blocks) if i]


def pinned(value):
    return pltpu.with_memory_space_constraint(value, pltpu.HBM)


def behind(values, marker):
    *values, _ = lax.optimization_barrier((*values, marker))
    return values


def column_halves(total, sizes, bit):
    blocks = sizes[0] // (2 * bit)
    pairs = total.reshape(blocks, 2, total.shape[0] // (2 * blocks), total.shape[1])
    kept, given = pairs[:, 0], pairs[:, 1]
    return [x.reshape(-1, total.shape[1]) for x in (kept, given.astype(BF16))]


def finished(kept, arrived):
    for block in arrived:
        kept = kept + block.astype(F32)
    return kept


def tied_call(kernel, after, operands, in_specs, out_shape, out_specs, **rest):
    waits = len(after)

    def body(*refs):
        kernel(*refs[waits:])

    return pl.pallas_call(
        body, out_shape=out_shape,
        in_specs=[pl.BlockSpec(memory_space=pl.ANY)] * waits + in_specs, out_specs=out_specs, **rest,
    )(*after, *operands)


def shards(sizes, tokens, qkv_weight, out_weight, merge_weight, merged_grad):
    levels, lat_rows, lon_cols, channels = tokens.shape
    merged_width = merge_weight.shape[1]
    count = levels * lat_rows * lon_cols
    groups = count // 4
    half = channels // 2
    strip_rows.extent = (lat_rows, lon_cols)
    vmem = pl.BlockSpec(memory_space=pltpu.VMEM)
    smem = pl.BlockSpec(memory_space=pltpu.SMEM)
    hbm = pl.BlockSpec(memory_space=pl.ANY)

    def shape(*extent, dtype=BF16):
        return jax.ShapeDtypeStruct(extent, dtype)

    def settings(weight, limit=60):
        return dict(
            compiler_params=pltpu.CompilerParams(vmem_limit_bytes=limit * MIB),
            cost_estimate=pl.CostEstimate(
                flops=int(weight * 1e10), bytes_accessed=16 * MIB, transcendentals=0
            ),
        )

    g_rows, g_cols = lat_rows // 2, lon_cols // 2
    cells = window_cells(levels, lat_rows, lon_cols)
    grps = window_groups(levels, g_rows, g_cols)
    cs = Strips(levels, lat_rows, lon_cols, SHIFT, True)
    gs = Strips(levels, g_rows, g_cols, HALF, False)
    g_strips = [padded(gs.side), padded(gs.above), padded(gs.corner)]
    to = ((0, lon_cols), (lat_rows, 0), (lat_rows, lon_cols))
    g_to = ((0, g_cols), (g_rows, 0), (g_rows, g_cols))
    own_rows = range(SHIFT, SHIFT + lat_rows)
    own_cols = range(SHIFT, SHIFT + lon_cols)
    own = box(levels, own_rows, own_cols)
    g_own = turned_box(levels, range(HALF, HALF + g_rows), range(HALF, HALF + g_cols))
    half_cells = count // 2
    side_cut = levels * SHIFT * SHIFT
    sent_cells = sum((Strips.sent(s, *t) for s, t in zip((cs.side, cs.above, cs.corner), to)), [])
    sent_groups = sum((Strips.sent(s, *t) for s, t in zip(g_strips, g_to)), [])
    held_top = box(levels, range(SHIFT, 2 * SHIFT), own_cols) + cs.side[:side_cut] + cs.above + cs.corner
    held_low = box(levels, range(2 * SHIFT, lat_rows), own_cols) + cs.side[side_cut:]
    depth = max(len(held_top), len(held_low))
    depth += -depth % 16
    held_top += [None] * (depth - len(held_top))
    held_low += [None] * (depth - len(held_low))

    tokens_flat = tokens.reshape(count, channels)
    merged_grad_flat = merged_grad.transpose(0, 2, 1, 3).reshape(groups, merged_width)
    extents = [(n + g, channels) for n, g in strip_rows(None, None)]
    packed = pl.pallas_call(
        pack_kernel,
        out_shape=[shape(*e) for e in extents],
        in_specs=[vmem] * 4, out_specs=[vmem] * 3,
        name="pack_strips", **settings(1),
    )(pinned(tokens_flat), pinned(merged_grad_flat), picks(sent_cells, own), picks(sent_groups, g_own))
    strips = sent_strips(packed, sizes, 1)

    order = jnp.concatenate([picks(cells[:half_cells], held_top), picks(cells[half_cells:], held_low)])
    group = picks(grps, g_own + sum(g_strips, []))
    edge = (lax.axis_index("lat") == 0).astype(jnp.int32).reshape(1)
    owner, rowmap = device_rows(channels, sizes)
    if channels // (sizes[0] * sizes[1]) % 16 == 0:
        rowmap = jnp.zeros((8, 1), jnp.int32)

    wide = shape(count, channels)
    inner = 2 * 2 * WIN * WIN
    ready = tied_call(
        inner_kernel, packed,
        [pinned(tokens_flat), order[count - inner:], pinned(qkv_weight)],
        [vmem] * 2 + [hbm],
        [shape(inner, channels), shape(inner, channels), shape(inner, LANES, dtype=F32),
         shape(inner, channels), shape(inner, channels, dtype=F32), shape(inner, 3 * channels)],
        [vmem] * 6,
        scratch_shapes=[
            pltpu.VMEM(qkv_weight.shape, BF16),
            pltpu.VMEM((inner, channels), F32),
            pltpu.SemaphoreType.DMA((3 * channels // TILE,)),
        ],
        name="inner_windows", **settings(9),
    )
    normed, normt, proj, dmr, dmm, grad, rstd, merged, out_mine, out_theirs = pl.pallas_call(
        forward_kernel,
        out_shape=[
            wide, shape(channels, count), shape(count, 3 * channels), wide, wide, wide,
            shape(count, LANES, dtype=F32), shape(groups, merged_width),
            shape(half, channels), shape(half, channels),
        ],
        in_specs=[smem] * 2 + [vmem] * 8 + [hbm] * 9,
        out_specs=[hbm] * 6 + [vmem] * 4,
        scratch_shapes=[
            pltpu.VMEM(qkv_weight.shape, BF16),
            pltpu.VMEM(out_weight.shape, BF16),
            pltpu.VMEM(merge_weight.shape, BF16),
            pltpu.VMEM((2, depth, channels), BF16),
            pltpu.VMEM((count, channels), BF16),
            pltpu.VMEM((count, channels), BF16),
            pltpu.VMEM((count, 3 * channels), BF16),
            pltpu.VMEM((count, channels), BF16),
            pltpu.VMEM((count, channels), F32),
            pltpu.VMEM((groups, 4 * channels), BF16),
            pltpu.VMEM((groups, 4 * channels), BF16),
            pltpu.VMEM((groups, merged_width), BF16),
            pltpu.VMEM((count, channels), BF16),
            pltpu.VMEM((count, channels), BF16),
            pltpu.VMEM((count, channels), BF16),
            pltpu.SemaphoreType.DMA((9,)),
            pltpu.SemaphoreType.DMA((6,)),
        ],
        name="block_forward", **settings(30, 55),
    )(edge, owner, tokens_flat, merged_grad_flat, *strips, order, group, rowmap,
      qkv_weight, out_weight, merge_weight, *ready)

    halves = 2
    width = channels // halves
    steps = width // TILE

    def backward(index, after):
        return tied_call(
            functools.partial(backward_kernel, index), after,
            [edge, pinned(proj), pinned(dmr), pinned(dmm), pinned(normt)], [smem] + [hbm] * 4,
            [shape(count, 3 * width), shape(half, 3 * width), shape(half, 3 * width)], [hbm] * 3,
            scratch_shapes=[
                pltpu.VMEM((5, count, width), BF16),
                pltpu.VMEM((channels, count), BF16),
                pltpu.VMEM((count, 3 * width), BF16),
                pltpu.VMEM((half, 3 * width), BF16),
                pltpu.VMEM((half, 3 * width), BF16),
                pltpu.SemaphoreType.DMA((steps, 5)),
                pltpu.SemaphoreType.DMA((1,)),
                pltpu.SemaphoreType.DMA((steps, 3, 3)),
            ],
            name="attention_backward", **settings(15, 32),
        )

    arrived = core_step(out_theirs, sizes)
    pg0, mine1, theirs1 = backward(0, [])
    out_mine, arrived = behind([out_mine, arrived], pg0)
    layer0 = layer_blocks(out_mine, arrived, sizes)
    arrived0 = layer_step(layer0, sizes)
    arrived = core_step(theirs1, sizes)
    pg1, mine2, theirs2 = backward(1, layer0[1:])
    mine1, arrived, *arrived0 = behind([mine1, arrived] + arrived0, pg1)
    layer1 = layer_blocks(mine1, arrived, sizes)
    arrived1 = layer_step(layer1, sizes)
    theirs2, = behind([theirs2], arrived0)
    arrived = core_step(theirs2, sizes)
    layer2 = layer_blocks(mine2, arrived, sizes)
    arrived2 = layer_step(layer2, sizes)

    first_picks = picks(cs.side[:side_cut] + cs.above + cs.corner, cells[:half_cells])
    last_picks = picks(cs.side[side_cut:], cells[half_cells:])
    full, *strips = tied_call(
        input_kernel, layer1[1:] + layer2[1:],
        [pg0, pg1, qkv_weight, pinned(normed), pinned(rstd), pinned(grad), merged,
         first_picks, last_picks, picks(sum(g_strips, []), grps)],
        [hbm] * 6 + [vmem] * 4, [wide] + [shape(*e) for e in extents], [vmem] * 4,
        scratch_shapes=[
            pltpu.VMEM((count, 3 * channels), BF16),
            pltpu.VMEM(qkv_weight.shape, BF16),
            pltpu.VMEM((count, channels), BF16),
            pltpu.VMEM((count, channels), BF16),
            pltpu.VMEM((count, LANES), F32),
            pltpu.VMEM((count, channels), BF16),
            pltpu.SemaphoreType.DMA((3 * halves + channels // TILE,)),
            pltpu.SemaphoreType.DMA((3,)),
        ],
        name="input_backward", **settings(13, 40),
    )
    arrived1 = behind(arrived1, full)
    early = [arrived2[0], arrived2[2]]
    strips = sent_strips(behind(strips, (arrived1, early)), sizes, -1)
    arrived1 = behind(arrived1, early)

    total1 = jnp.concatenate([layer0[0], layer1[0]], axis=1)
    for pair in zip(arrived0, arrived1):
        total1 = total1 + jnp.concatenate(pair, axis=1).astype(F32)
    kept1, given1 = column_halves(total1, sizes, 1)
    got1 = exchange(given1, sizes, 1, 0)

    part1 = kept1 + got1.astype(F32)
    column2 = column_blocks(layer2[0], arrived2, sizes)
    bit = 2
    while 2 * bit < sizes[0]:
        kept1, given1 = column_halves(part1, sizes, bit)
        part1 = kept1 + exchange(given1, sizes, bit, 0).astype(F32)
        bit *= 2
    kept1, last1 = column_halves(part1, sizes, bit)
    last_columns = last1.shape[1]
    column2[bit] = jnp.concatenate([last1, column2[bit]], axis=1)
    got2 = column_step(column2, sizes)

    got = [Strips.sent(s, *t) for s, t in zip((cs.side, cs.above, cs.corner), to)]
    g_got = sum((Strips.sent(s, *t) for s, t in zip(g_strips, g_to)), [])
    tokens_grad, merged = tied_call(
        unpack_kernel, column2[1:] + [given1],
        [
            full, merged, *strips,
            picks(box(levels, range(SHIFT, 2 * SHIFT), own_cols), cells[:half_cells] + got[0][:side_cut]),
            picks(box(levels, range(2 * SHIFT, lat_rows), own_cols), cells[half_cells:] + got[0][side_cut:]),
            picks(box(levels, range(lat_rows, lat_rows + SHIFT), own_cols), got[1] + got[2]),
            picks(g_own, grps + g_got),
        ],
        [vmem] * 9, [wide, shape(groups, merged_width)], [vmem] * 2,
        name="unpack_strips", **settings(20, 24),
    )
    got2 = behind(got2, tokens_grad)
    part1 = kept1 + got2[bit - 1][:, :last_columns].astype(F32)
    got2[bit - 1] = got2[bit - 1][:, last_columns:]
    part2 = finished(column2[0], got2)
    out_weight_grad = part1[:, :channels]
    part1 = part1[:, channels:]

    merged = merged.reshape(levels, g_cols, g_rows, merged_width).transpose(0, 2, 1, 3)

    qkv_weight_grad = jnp.concatenate(
        [part[:, i * width:(i + 1) * width] for i in range(3) for part in (part1, part2)],
        axis=1,
    )
    return merged, tokens_grad.reshape(tokens.shape), qkv_weight_grad, out_weight_grad


def solution(mesh):
    sizes = (mesh.shape["lat"], mesh.shape["lon"])
    in_specs = (P(None, "lat", "lon", None), P(), P(), P(), P(None, "lat", "lon", None))
    out_specs = (
        P(None, "lat", "lon", None),
        P(None, "lat", "lon", None),
        P(("lat", "lon"), None),
        P(("lat", "lon"), None),
    )
    return jax.shard_map(
        functools.partial(shards, sizes),
        mesh=mesh, in_specs=in_specs, out_specs=out_specs, check_vma=False,
    )
```

```python
import functools

import jax
import jax.numpy as jnp
import numpy as np
from jax import lax
from jax.experimental import pallas as pl
from jax.experimental.pallas import tpu as pltpu
from jax.sharding import PartitionSpec as P

HEADS = 32
WIN = 8
SHIFT = 4
LANES = 128
HALF = SHIFT // 2
TILE = 256
WIDE = 512
EPSILON = 1e-05
MIB = 1 << 20

NN = (((1,), (0,)), ((), ()))
NT = (((1,), (1,)), ((), ()))
TN = (((0,), (0,)), ((), ()))
BF16 = jnp.bfloat16
F32 = jnp.float32


def dot(a, b, dims=NN):
    return lax.dot_general(a, b, dims, preferred_element_type=F32)


def window_cells(levels, rows, columns):
    half = WIN // 2
    return [
        (level, wi * WIN + 2 * row + sub % 2, wj * WIN + 2 * column + sub // 2)
        for wi in range(rows // WIN) for wj in range(columns // WIN) for sub in range(4)
        for level in range(levels) for row in range(half) for column in range(half)
    ]


def window_groups(levels, rows, columns):
    half = WIN // 2
    return [
        (level, wi * half + row, wj * half + column)
        for wi in range(rows // half) for wj in range(columns // half)
        for level in range(levels) for row in range(half) for column in range(half)
    ]


def box(levels, rows, columns):
    return [(l, r, c) for l in range(levels) for r in rows for c in columns]


def turned_box(levels, rows, columns):
    return [(l, r, c) for l in range(levels) for c in columns for r in rows]


def padded(cells, step=16):
    return cells + [None] * (-len(cells) % step)


def picks(wanted, held):
    spot = {cell: i for i, cell in enumerate(held) if cell is not None}
    table = np.zeros((len(wanted), len(held)), np.float32)
    for i, cell in enumerate(wanted):
        if cell is not None:
            table[i, spot[cell]] = 1.0
    return jnp.asarray(table, BF16)


class Strips:
    def __init__(self, levels, rows, columns, width, cut):
        self.side = (box(levels, range(width, 2 * width), range(width))
                     + box(levels, range(2 * width, rows), range(width)))
        self.above = box(levels, range(width), range(width, columns))
        self.corner = box(levels, range(width), range(width))
        if not cut:
            self.side = box(levels, range(width, rows), range(width))

    @staticmethod
    def sent(cells, down, across):
        return [None if c is None else (c[0], c[1] + down, c[2] + across) for c in cells]


def head_masks():
    head = lax.broadcasted_iota(jnp.int32, (LANES, LANES), 1) // (LANES // 4)
    return [jnp.where(head == h, 1.0, 0.0).astype(BF16) for h in range(4)]


def region_bias(places, active):
    step = 2 * (WIN // 2)
    one = (lax.broadcasted_iota(jnp.int32, (places, places), 0) // step) % 2
    other = (lax.broadcasted_iota(jnp.int32, (places, places), 1) // step) % 2
    return jnp.where((one != other) & active, -1e30, 0.0)


def score_scale(channels):
    return float((channels // HEADS) ** -0.5 * np.log2(np.e))


def aligned(start, size, step=None):
    return pl.ds(pl.multiple_of(start, step or size), size)


def pack_kernel(tokens, merged_grad, pick_cells, pick_groups, side, above, corner):
    cells = dot(pick_cells[...], tokens[...]).astype(BF16)
    groups = dot(pick_groups[...], merged_grad[...]).astype(BF16)
    at, at_group = 0, 0
    for out, (count, extra) in zip((side, above, corner), strip_rows(pick_cells, pick_groups)):
        out[:count] = cells[at:at + count]
        out[count:] = groups[at_group:at_group + extra]
        at, at_group = at + count, at_group + extra


def strip_rows(pick_cells, pick_groups):
    levels = 2
    rows, columns = strip_rows.extent
    cells = [levels * (rows - SHIFT) * SHIFT, levels * SHIFT * (columns - SHIFT), levels * SHIFT * SHIFT]
    groups = [n // 4 + (-(n // 4)) % 16 for n in cells]
    return list(zip(cells, groups))


def normalized_window(x, rows, xw, normed, rstd):
    xw[rows] = x.astype(BF16)
    center = jnp.mean(x, axis=1, keepdims=True)
    moved = x - center
    scale = lax.rsqrt(jnp.mean(moved * moved, axis=1, keepdims=True) + EPSILON)
    rstd[rows] = jnp.broadcast_to(scale, (x.shape[0], LANES))
    normed[rows] = (moved * scale).astype(BF16)


def attended(proj, rows, lanes, masks, factor, bias, mixture, inverse):
    places = masks[0].shape[0]
    q, k, v = (proj[rows, at] for at in lanes)
    scores = dot(q, jnp.concatenate([k * m for m in masks], axis=0), NT)
    parts = []
    for h in range(4):
        part = scores[:, h * places:(h + 1) * places] * factor
        if bias is not None:
            part = part + bias
        part = part - jnp.max(part, axis=1, keepdims=True)
        parts.append(jnp.exp2(part).astype(BF16))
    values = jnp.concatenate([jnp.concatenate([v * m, m], axis=1) for m in masks], axis=0)
    summed = dot(jnp.concatenate(parts, axis=1), values)
    inv = 1.0 / summed[:, LANES:]
    inverse[rows, lanes[0]] = inv
    mixture[rows, lanes[0]] = (summed[:, :LANES] * inv).astype(BF16)


def inner_kernel(
    tokens, order, wqkv_h, xw, normed, rstd, mixture, inverse, proj, wqkv, in_sem,
):
    count, channels = xw.shape
    places = 2 * WIN * WIN
    tiles = wqkv.shape[1] // WIDE

    def load(n):
        columns = aligned(n * WIDE, WIDE)
        return pltpu.make_async_copy(wqkv_h.at[:, columns], wqkv.at[:, columns], in_sem.at[n])

    for n in range(tiles):
        load(n).start()
    half = tokens.shape[0] // 2
    line = half // (2 * WIN)
    cut = SHIFT * line
    source = jnp.concatenate(
        [tokens[cut:cut + WIN * line], tokens[half + cut:half + cut + WIN * line]], axis=0
    )
    x = dot(order[:, :source.shape[0]], source)
    for w in range(count // places):
        rows = slice(w * places, (w + 1) * places)
        normalized_window(x[rows], rows, xw, normed, rstd)

    @pl.loop(0, tiles)
    def _(n):
        load(n).wait()
        columns = aligned(n * WIDE, WIDE)
        proj[:, columns] = dot(normed[...], wqkv[:, columns]).astype(BF16)

    masks = head_masks()
    factor = score_scale(channels)

    @pl.loop(0, channels // LANES // 2)
    def _(g):
        for i in range(2):
            lanes = [aligned(j * channels + (2 * g + i) * LANES, LANES) for j in range(3)]
            for w in range(count // places):
                rows = slice(w * places, (w + 1) * places)
                attended(proj, rows, lanes, masks, factor, None, mixture, inverse)


def forward_kernel(
    edge, owner, tokens, merged_grad, side, above, corner, order, group, rowmap,
    wqkv_h, wout_h, wm_h, xw_h, normed_in, rstd_h, mixture_h, inverse_h, proj_in,
    normed_h, normt_h, proj_h, dmr_h, dmm_h, grad_h, rstd, merged, out_mine, out_theirs,
    wqkv, wout, wm, source, xw, normed, proj, mixture, inverse, subs, dsubs, cotangent,
    grad, dmr, dmm, in_sem, out_sem,
):
    count, channels = xw.shape
    places = 2 * WIN * WIN
    windows = count // places
    per_row = windows // 2
    quarter = places // 4
    groups = count // 4
    devices = owner.shape[0]
    block = channels // devices

    loads = [
        pltpu.make_async_copy(src, dst, in_sem.at[i])
        for i, (src, dst) in enumerate([(wqkv_h, wqkv), (wout_h, wout), (wm_h, wm)])
    ]
    outer = count - xw_h.shape[0]
    ready = [
        pltpu.make_async_copy(src, dst.at[pl.ds(outer, count - outer)], in_sem.at[3 + i])
        for i, (src, dst) in enumerate(
            [(xw_h, xw), (normed_in, normed), (rstd_h, rstd), (mixture_h, mixture),
             (inverse_h, inverse), (proj_in, proj)]
        )
    ]
    for load in loads + ready:
        load.start()
    stores = [
        pltpu.make_async_copy(src, dst, out_sem.at[i])
        for i, (src, dst) in enumerate(
            [(normed, normed_h), (proj, proj_h), (wqkv.at[:, pl.ds(count, count)], normt_h),
             (grad, grad_h), (dmr, dmr_h), (dmm, dmm_h)]
        )
    ]

    (n_side, g_side), (n_above, g_above), (n_corner, g_corner) = strip_rows(None, None)
    half = count // 2
    line = half // (2 * WIN)
    cut = SHIFT * line
    side_cut = 2 * SHIFT * SHIFT
    blocks = [
        [tokens[:cut], tokens[half:half + cut], side[:side_cut], above[:n_above], corner[:n_corner]],
        [tokens[cut:cut + WIN * line], tokens[half + cut:half + cut + WIN * line], side[side_cut:n_side]],
    ]
    for wi in range(2):
        at = 0
        for piece in blocks[wi]:
            source[wi, at:at + piece.shape[0]] = piece
            at += piece.shape[0]
        if at < source.shape[1]:
            source[wi, at:] = jnp.zeros((source.shape[1] - at, channels), BF16)

    for wi in range(2):
        first, last = wi * per_row, min((wi + 1) * per_row, outer // places)
        x = dot(order[first * places:last * places], source[wi])
        for w in range(first, last):
            rows = slice(w * places, (w + 1) * places)
            normalized_window(x[(w - first) * places:(w - first + 1) * places], rows, xw, normed, rstd)

    loads[0].wait()
    outer_rows = slice(0, outer)

    @pl.loop(0, wqkv.shape[1] // WIDE)
    def _(n):
        columns = aligned(n * WIDE, WIDE)
        proj[outer_rows, columns] = dot(normed[outer_rows], wqkv[:, columns]).astype(BF16)

    for load in ready:
        load.wait()
    stores[0].start()
    stores[1].start()

    masks = head_masks()
    factor = score_scale(channels)

    edge_bias = region_bias(places, edge[0] == 1)
    held = jnp.concatenate(
        [merged_grad[...], side[n_side:], above[n_above:], corner[n_corner:]], axis=0
    )
    cotangent[...] = dot(group[...], held).astype(BF16)
    loads[2].wait()
    steps = channels // LANES
    per_step = 4 * channels // TILE // steps

    @pl.loop(0, steps)
    def _(g):
        lanes = [aligned(i * channels + g * LANES, LANES) for i in range(3)]
        for w in range(outer // places):
            rows = slice(w * places, (w + 1) * places)
            bias = edge_bias if w < per_row else None
            attended(proj, rows, lanes, masks, factor, bias, mixture, inverse)
        for i in range(per_step):
            at = aligned((g * per_step + i) * TILE, TILE)
            dsubs[:, at] = dot(cotangent[...], wm[at], NT).astype(BF16)

    loads[1].wait()

    @pl.loop(0, channels // WIDE)
    def _(n):
        columns = aligned(n * WIDE, WIDE)
        out = dot(mixture[...], wout[:, columns]) + xw[:, columns].astype(F32)
        out = out.astype(BF16)
        for w in range(windows):
            for s in range(4):
                at = w * places + s * quarter
                subs[s, w * quarter:(w + 1) * quarter, columns] = out[at:at + quarter]

    total = jnp.zeros((groups, 1), F32)
    for s in range(4):
        total += jnp.sum(subs[s].astype(F32), axis=1, keepdims=True)
    center = total / (4 * channels)
    total = jnp.zeros((groups, 1), F32)
    for s in range(4):
        moved = subs[s].astype(F32) - center
        total += jnp.sum(moved * moved, axis=1, keepdims=True)
    scale = lax.rsqrt(total / (4 * channels) + EPSILON)
    result = jnp.zeros((groups, wm.shape[1]), F32)
    for s in range(4):
        unit = ((subs[s].astype(F32) - center) * scale).astype(BF16)
        result += dot(unit, wm[s * channels:(s + 1) * channels])
    merged[...] = result.astype(BF16)

    mean_g = jnp.zeros((groups, 1), F32)
    mean_gx = jnp.zeros((groups, 1), F32)
    for s in range(4):
        d = dsubs[:, s * channels:(s + 1) * channels].astype(F32)
        mean_g += jnp.sum(d, axis=1, keepdims=True)
        mean_gx += jnp.sum(d * ((subs[s].astype(F32) - center) * scale), axis=1, keepdims=True)
    mean_g = mean_g / (4 * channels)
    mean_gx = mean_gx / (4 * channels)
    for s in range(4):
        unit = (subs[s].astype(F32) - center) * scale
        d = dsubs[:, s * channels:(s + 1) * channels].astype(F32)
        d = (scale * (d - mean_g - unit * mean_gx)).astype(BF16)
        for w in range(windows):
            at = w * places + s * quarter
            grad[at:at + quarter] = d[w * quarter:(w + 1) * quarter]
    stores[3].start()

    @pl.loop(0, channels // WIDE)
    def _(n):
        columns = aligned(n * WIDE, WIDE)
        d = dot(grad[...], wout[columns], NT).astype(BF16).astype(F32)
        d = d * inverse[:, columns]
        dmr[:, columns] = d.astype(BF16)
        dmm[:, columns] = (-d * mixture[:, columns].astype(F32)).astype(BF16)

    stores[4].start()
    stores[5].start()

    def turn(field, out):
        if block % 16:
            @pl.loop(0, channels // TILE)
            def _(n):
                rows = aligned(n * TILE, TILE)
                spot = lax.broadcasted_iota(jnp.int32, (TILE, channels), 1)
                pick = jnp.where(spot == rowmap[rows], 1.0, 0.0).astype(BF16)
                out[rows] = dot(pick, field[...], NT).astype(BF16)
        else:
            @pl.loop(0, channels // WIDE)
            def _(n):
                rows = aligned(n * WIDE, WIDE)
                turned[rows] = field[:, rows].T

            for d in range(devices):
                out[d * block:(d + 1) * block] = turned[aligned(owner[d] * block, block)]

    turned, normt, mixt = (wqkv.at[:, pl.ds(i * count, count)] for i in range(3))
    turn(normed, normt)
    stores[2].start()
    turn(mixture, mixt)
    part = channels // 2

    @pl.loop(0, channels // WIDE)
    def _(n):
        columns = aligned(n * WIDE, WIDE)
        terms = dot(mixt[...], grad[:, columns]).astype(BF16)
        out_mine[:, columns] = terms[:part]
        out_theirs[:, columns] = terms[part:]

    for store in stores:
        store.wait()


def backward_kernel(index, *refs):
    (edge, proj_h, dmr_h, dmm_h, normt_h, pgrad_h, mine_h, theirs_h,
     held, normt, pgrad, mine, theirs, in_sem, sem, out_sem) = refs
    _, count, width = held.shape
    channels = normt.shape[0]
    half = channels // 2
    places = 2 * WIN * WIN
    windows = count // places
    per_row = windows // 2
    masks = head_masks()
    factor = score_scale(channels)
    plain = (channels // HEADS) ** -0.5
    steps = width // TILE

    def loads(g):
        columns = aligned(g * TILE, TILE)
        for i in range(5):
            src = (proj_h, proj_h, proj_h, dmr_h, dmm_h)[i]
            start = (i * channels if i < 3 else 0) + index * width
            yield pltpu.make_async_copy(
                src.at[:, aligned(start + g * TILE, TILE)], held.at[i, :, columns], in_sem.at[g, i]
            )

    def stores(g):
        for i in range(3):
            columns = aligned(i * width + g * TILE, TILE)
            for j, (src, dst) in enumerate(((pgrad, pgrad_h), (mine, mine_h), (theirs, theirs_h))):
                yield pltpu.make_async_copy(src.at[:, columns], dst.at[:, columns], out_sem.at[g, i, j])

    for g in range(steps):
        for load in loads(g):
            load.start()
    turned_load = pltpu.make_async_copy(normt_h, normt, sem.at[0])
    turned_load.start()
    edge_bias = region_bias(places, edge[0] == 1)

    @pl.loop(0, steps)
    def _(g):
        for load in loads(g):
            load.wait()

        for part_of in range(TILE // LANES):
            lanes = aligned(g * TILE + part_of * LANES, LANES)
            for w in range(windows):
                rows = slice(w * places, (w + 1) * places)
                q, k, v, dm, dd = (held[i, rows, lanes] for i in range(5))
                keys = jnp.concatenate([k * m for m in masks], axis=0)
                scores = dot(keys, q, NT)
                values = jnp.concatenate(
                    [jnp.concatenate([v * m, m], axis=1) for m in masks], axis=0
                )
                slope = dot(values, jnp.concatenate([dm, dd], axis=1), NT)
                weights, slopes = [], []
                for h in range(4):
                    block = slice(h * places, (h + 1) * places)
                    part = scores[block] * factor
                    if w < per_row:
                        part = part + edge_bias
                    part = jnp.exp2(part - jnp.max(part, axis=0, keepdims=True))
                    weights.append(part.astype(BF16))
                    slopes.append((part * slope[block]).astype(BF16))
                dv = dot(
                    jnp.concatenate(weights, axis=1),
                    jnp.concatenate([dm * m for m in masks], axis=0),
                )
                dk = dot(
                    jnp.concatenate(slopes, axis=1),
                    jnp.concatenate([q * m for m in masks], axis=0),
                )
                dq = dot(jnp.concatenate(slopes, axis=0), keys, TN)
                at = g * TILE + part_of * LANES
                pgrad[rows, lanes] = (dq * plain).astype(BF16)
                pgrad[rows, aligned(width + at, LANES)] = (dk * plain).astype(BF16)
                pgrad[rows, aligned(2 * width + at, LANES)] = dv.astype(BF16)

        @pl.when(g == 0)
        def _():
            turned_load.wait()

        for i in range(3):
            columns = aligned(i * width + g * TILE, TILE)
            terms = dot(normt[...], pgrad[:, columns]).astype(BF16)
            mine[:, columns] = terms[:half]
            theirs[:, columns] = terms[half:]
        for store in stores(g):
            store.start()

    for g in range(steps):
        for store in stores(g):
            store.wait()


def projection_loads(pgrads, wqkv_h, pgrad, wqkv, sem, start):
    width = pgrads[0].shape[1] // 3
    channels = pgrad.shape[1] // 3
    loads = [
        pltpu.make_async_copy(
            field.at[:, pl.ds(i * width, width)],
            pgrad.at[:, pl.ds(i * channels + c * width, width)], sem.at[c * 3 + i],
        )
        for c, field in enumerate(pgrads) for i in range(3)
    ]
    tiles = [
        pltpu.make_async_copy(
            wqkv_h.at[pl.ds(start + n * TILE, TILE)], wqkv.at[pl.ds(n * TILE, TILE)],
            sem.at[3 * len(pgrads) + n],
        )
        for n in range(wqkv.shape[0] // TILE)
    ]
    for load in loads + tiles:
        load.start()
    return loads, tiles


def input_kernel(*refs):
    (pg0, pg1, wqkv_h, normed_h, rstd_h, grad_h, merged,
     pick_first, pick_last, pick_groups, full, side, below, corner,
     pgrad, wqkv, ngrad, normed, rstd, grad, sem, more_sem) = refs
    count, channels = ngrad.shape
    loads, tiles = projection_loads([pg0, pg1], wqkv_h, pgrad, wqkv, sem, 0)
    more = [
        pltpu.make_async_copy(src, dst, more_sem.at[i])
        for i, (src, dst) in enumerate([(normed_h, normed), (rstd_h, rstd), (grad_h, grad)])
    ]
    for load in more:
        load.start()
    for load in loads:
        load.wait()
    for load in tiles:
        load.wait()

    @pl.loop(0, channels // WIDE)
    def _(n):
        rows = aligned(n * WIDE, WIDE)
        ngrad[:, rows] = dot(pgrad[...], wqkv[rows], NT).astype(BF16)

    for load in more:
        load.wait()
    places = 2 * WIN * WIN

    @pl.loop(0, count // places)
    def _(w):
        rows = aligned(w * places, places)
        d = ngrad[rows].astype(F32)
        unit = normed[rows].astype(F32)
        mean_d = jnp.mean(d, axis=1, keepdims=True)
        mean_dx = jnp.mean(d * unit, axis=1, keepdims=True)
        part = rstd[rows, :1] * (d - mean_d - unit * mean_dx)
        full[rows] = (part.astype(BF16).astype(F32) + grad[rows].astype(F32)).astype(BF16)

    (n_side, g_side), (n_above, g_above), (n_corner, g_corner) = strip_rows(None, None)
    side_cut = 2 * SHIFT * SHIFT
    first = dot(pick_first[...], full[:count // 2]).astype(BF16)
    last = dot(pick_last[...], full[count // 2:]).astype(BF16)
    groups = dot(pick_groups[...], merged[...]).astype(BF16)
    side[:side_cut] = first[:side_cut]
    side[side_cut:n_side] = last
    below[:n_above] = first[side_cut:side_cut + n_above]
    corner[:n_corner] = first[side_cut + n_above:]
    side[n_side:] = groups[:g_side]
    below[n_above:] = groups[g_side:g_side + g_above]
    corner[n_corner:] = groups[g_side + g_above:]


def end_kernel(bit, kept1, kept2, *refs):
    arrived, (qkv, out) = refs[:-2], refs[-2:]
    channels = out.shape[1]
    columns = kept1.shape[1]
    first = kept1[...] + arrived[bit - 1][:, :columns].astype(F32)
    last = kept2[...]
    for i, block in enumerate(arrived):
        last += (block[:, columns:] if i == bit - 1 else block[...]).astype(F32)
    out[...] = first[:, :channels]
    width = channels // 2
    for i in range(3):
        at = i * channels
        qkv[:, at:at + width] = first[:, channels + i * width:channels + (i + 1) * width]
        qkv[:, at + width:at + channels] = last[:, i * width:(i + 1) * width]


def unpack_kernel(full, merged, side, below, corner, pick_top, pick_middle, pick_bottom,
                  pick_groups, tokens_out, merged_out):
    count = full.shape[0]
    half = count // 2
    (n_side, _), (n_above, _), (n_corner, _) = strip_rows(None, None)
    side_cut = 2 * SHIFT * SHIFT
    line = half // (2 * WIN)
    pieces = [
        (pick_top, [full[:half], side[:side_cut]]),
        (pick_middle, [full[half:], side[side_cut:n_side]]),
        (pick_bottom, [below[:n_above], corner[:n_corner]]),
    ]
    at = 0
    for pick, held in pieces:
        rows = pick.shape[0] // 2
        out = dot(pick[...], jnp.concatenate(held, axis=0)).astype(BF16)
        for level in range(2):
            start = level * half + at
            tokens_out[start:start + rows] = out[level * rows:(level + 1) * rows]
        at += rows
    held = [merged[...], side[n_side:], below[n_above:], corner[n_corner:]]
    merged_out[...] = dot(pick_groups[...], jnp.concatenate(held, axis=0)).astype(BF16)


def sent(block, sizes, lat_step, lon_step):
    n_lat, n_lon = sizes
    route = [
        (a * n_lon + b, (a + lat_step) % n_lat * n_lon + (b + lon_step) % n_lon)
        for a in range(n_lat) for b in range(n_lon)
    ]
    return lax.ppermute(block, ("lat", "lon"), route)


def sent_strips(strips, sizes, step):
    side, lines, corner = strips
    return [sent(side, sizes, 0, step), sent(lines, sizes, step, 0), sent(corner, sizes, step, step)]


def device_rows(channels, sizes):
    n_lat, n_lon = sizes
    devices = n_lat * n_lon
    rows = channels // devices
    place = np.arange(devices)
    lon = 2 * (place // n_lat % (n_lon // 2)) + place // (devices // 2)
    lat = place % n_lat
    owner = (
        jnp.bitwise_xor(lax.axis_index("lat").astype(jnp.int32), jnp.asarray(lat, jnp.int32)) * n_lon
        + jnp.bitwise_xor(lax.axis_index("lon").astype(jnp.int32), jnp.asarray(lon, jnp.int32))
    )
    rowmap = owner[:, None] * rows + jnp.arange(rows, dtype=jnp.int32)[None, :]
    return owner, rowmap.reshape(channels, 1)


def exchange(block, sizes, lat_bits, lon_bits):
    n_lat, n_lon = sizes
    route = [
        (a * n_lon + b, (a ^ lat_bits) * n_lon + (b ^ lon_bits))
        for a in range(n_lat) for b in range(n_lon)
    ]
    return lax.ppermute(block, ("lat", "lon"), route)


def core_step(theirs, sizes):
    return exchange(theirs, sizes, 0, 1)


def layer_blocks(mine, arrived, sizes):
    blocks = sizes[1] // 2
    rows = mine.shape[0] // blocks
    total = [
        (mine[i * rows:(i + 1) * rows].astype(F32) + arrived[i * rows:(i + 1) * rows].astype(F32))
        for i in range(blocks)
    ]
    return [total[0]] + [t.astype(BF16) for t in total[1:]]


def layer_step(blocks, sizes):
    return [exchange(b, sizes, 0, 2 * i) for i, b in enumerate(blocks) if i]


def column_blocks(kept, arrived, sizes):
    total = kept
    for block in arrived:
        total = total + block.astype(F32)
    rows = total.shape[0] // sizes[0]
    blocks = [total[i * rows:(i + 1) * rows] for i in range(sizes[0])]
    return [blocks[0]] + [b.astype(BF16) for b in blocks[1:]]


def column_step(blocks, sizes):
    return [exchange(b, sizes, i, 0) for i, b in enumerate(blocks) if i]


def pinned(value):
    return pltpu.with_memory_space_constraint(value, pltpu.HBM)


def behind(values, marker):
    *values, _ = lax.optimization_barrier((*values, marker))
    return values


def column_halves(total, sizes, bit):
    blocks = sizes[0] // (2 * bit)
    pairs = total.reshape(blocks, 2, total.shape[0] // (2 * blocks), total.shape[1])
    kept, given = pairs[:, 0], pairs[:, 1]
    return [x.reshape(-1, total.shape[1]) for x in (kept, given.astype(BF16))]


def finished(kept, arrived):
    for block in arrived:
        kept = kept + block.astype(F32)
    return kept


def tied_call(kernel, after, operands, in_specs, out_shape, out_specs, **rest):
    waits = len(after)

    def body(*refs):
        kernel(*refs[waits:])

    return pl.pallas_call(
        body, out_shape=out_shape,
        in_specs=[pl.BlockSpec(memory_space=pl.ANY)] * waits + in_specs, out_specs=out_specs, **rest,
    )(*after, *operands)


def shards(sizes, tokens, qkv_weight, out_weight, merge_weight, merged_grad):
    levels, lat_rows, lon_cols, channels = tokens.shape
    merged_width = merge_weight.shape[1]
    count = levels * lat_rows * lon_cols
    groups = count // 4
    half = channels // 2
    strip_rows.extent = (lat_rows, lon_cols)
    vmem = pl.BlockSpec(memory_space=pltpu.VMEM)
    smem = pl.BlockSpec(memory_space=pltpu.SMEM)
    hbm = pl.BlockSpec(memory_space=pl.ANY)

    def shape(*extent, dtype=BF16):
        return jax.ShapeDtypeStruct(extent, dtype)

    def settings(weight, limit=60):
        return dict(
            compiler_params=pltpu.CompilerParams(vmem_limit_bytes=limit * MIB),
            cost_estimate=pl.CostEstimate(
                flops=int(weight * 1e10), bytes_accessed=16 * MIB, transcendentals=0
            ),
        )

    g_rows, g_cols = lat_rows // 2, lon_cols // 2
    cells = window_cells(levels, lat_rows, lon_cols)
    grps = window_groups(levels, g_rows, g_cols)
    cs = Strips(levels, lat_rows, lon_cols, SHIFT, True)
    gs = Strips(levels, g_rows, g_cols, HALF, False)
    g_strips = [padded(gs.side), padded(gs.above), padded(gs.corner)]
    to = ((0, lon_cols), (lat_rows, 0), (lat_rows, lon_cols))
    g_to = ((0, g_cols), (g_rows, 0), (g_rows, g_cols))
    own_rows = range(SHIFT, SHIFT + lat_rows)
    own_cols = range(SHIFT, SHIFT + lon_cols)
    own = box(levels, own_rows, own_cols)
    g_own = turned_box(levels, range(HALF, HALF + g_rows), range(HALF, HALF + g_cols))
    half_cells = count // 2
    side_cut = levels * SHIFT * SHIFT
    sent_cells = sum((Strips.sent(s, *t) for s, t in zip((cs.side, cs.above, cs.corner), to)), [])
    sent_groups = sum((Strips.sent(s, *t) for s, t in zip(g_strips, g_to)), [])
    held_top = box(levels, range(SHIFT, 2 * SHIFT), own_cols) + cs.side[:side_cut] + cs.above + cs.corner
    held_low = box(levels, range(2 * SHIFT, lat_rows), own_cols) + cs.side[side_cut:]
    depth = max(len(held_top), len(held_low))
    depth += -depth % 16
    held_top += [None] * (depth - len(held_top))
    held_low += [None] * (depth - len(held_low))

    tokens_flat = tokens.reshape(count, channels)
    merged_grad_flat = merged_grad.transpose(0, 2, 1, 3).reshape(groups, merged_width)
    extents = [(n + g, channels) for n, g in strip_rows(None, None)]
    packed = pl.pallas_call(
        pack_kernel,
        out_shape=[shape(*e) for e in extents],
        in_specs=[vmem] * 4, out_specs=[vmem] * 3,
        name="pack_strips", **settings(1),
    )(pinned(tokens_flat), pinned(merged_grad_flat), picks(sent_cells, own), picks(sent_groups, g_own))
    strips = sent_strips(packed, sizes, 1)

    order = jnp.concatenate([picks(cells[:half_cells], held_top), picks(cells[half_cells:], held_low)])
    group = picks(grps, g_own + sum(g_strips, []))
    edge = (lax.axis_index("lat") == 0).astype(jnp.int32).reshape(1)
    owner, rowmap = device_rows(channels, sizes)
    if channels // (sizes[0] * sizes[1]) % 16 == 0:
        rowmap = jnp.zeros((8, 1), jnp.int32)

    wide = shape(count, channels)
    inner = 2 * 2 * WIN * WIN
    ready = tied_call(
        inner_kernel, packed,
        [pinned(tokens_flat), order[count - inner:], pinned(qkv_weight)],
        [vmem] * 2 + [hbm],
        [shape(inner, channels), shape(inner, channels), shape(inner, LANES, dtype=F32),
         shape(inner, channels), shape(inner, channels, dtype=F32), shape(inner, 3 * channels)],
        [vmem] * 6,
        scratch_shapes=[
            pltpu.VMEM(qkv_weight.shape, BF16),
            pltpu.SemaphoreType.DMA((3 * channels // TILE,)),
        ],
        name="inner_windows", **settings(9),
    )
    normed, normt, proj, dmr, dmm, grad, rstd, merged, out_mine, out_theirs = pl.pallas_call(
        forward_kernel,
        out_shape=[
            wide, shape(channels, count), shape(count, 3 * channels), wide, wide, wide,
            shape(count, LANES, dtype=F32), shape(groups, merged_width),
            shape(half, channels), shape(half, channels),
        ],
        in_specs=[smem] * 2 + [vmem] * 8 + [hbm] * 9,
        out_specs=[hbm] * 6 + [vmem] * 4,
        scratch_shapes=[
            pltpu.VMEM(qkv_weight.shape, BF16),
            pltpu.VMEM(out_weight.shape, BF16),
            pltpu.VMEM(merge_weight.shape, BF16),
            pltpu.VMEM((2, depth, channels), BF16),
            pltpu.VMEM((count, channels), BF16),
            pltpu.VMEM((count, channels), BF16),
            pltpu.VMEM((count, 3 * channels), BF16),
            pltpu.VMEM((count, channels), BF16),
            pltpu.VMEM((count, channels), F32),
            pltpu.VMEM((4, groups, channels), BF16),
            pltpu.VMEM((groups, 4 * channels), BF16),
            pltpu.VMEM((groups, merged_width), BF16),
            pltpu.VMEM((count, channels), BF16),
            pltpu.VMEM((count, channels), BF16),
            pltpu.VMEM((count, channels), BF16),
            pltpu.SemaphoreType.DMA((9,)),
            pltpu.SemaphoreType.DMA((6,)),
        ],
        name="block_forward", **settings(30, 55),
    )(edge, owner, tokens_flat, merged_grad_flat, *strips, order, group, rowmap,
      qkv_weight, out_weight, merge_weight, *ready)

    halves = 2
    width = channels // halves
    steps = width // TILE

    def backward(index, after):
        return tied_call(
            functools.partial(backward_kernel, index), after,
            [edge, pinned(proj), pinned(dmr), pinned(dmm), pinned(normt)], [smem] + [hbm] * 4,
            [shape(count, 3 * width), shape(half, 3 * width), shape(half, 3 * width)], [hbm] * 3,
            scratch_shapes=[
                pltpu.VMEM((5, count, width), BF16),
                pltpu.VMEM((channels, count), BF16),
                pltpu.VMEM((count, 3 * width), BF16),
                pltpu.VMEM((half, 3 * width), BF16),
                pltpu.VMEM((half, 3 * width), BF16),
                pltpu.SemaphoreType.DMA((steps, 5)),
                pltpu.SemaphoreType.DMA((1,)),
                pltpu.SemaphoreType.DMA((steps, 3, 3)),
            ],
            name="attention_backward", **settings(15, 32),
        )

    arrived = core_step(out_theirs, sizes)
    pg0, mine1, theirs1 = backward(0, [])
    out_mine, arrived = behind([out_mine, arrived], pg0)
    layer0 = layer_blocks(out_mine, arrived, sizes)
    arrived0 = layer_step(layer0, sizes)
    arrived = core_step(theirs1, sizes)
    pg1, mine2, theirs2 = backward(1, layer0[1:])
    mine1, arrived, *arrived0 = behind([mine1, arrived] + arrived0, pg1)
    layer1 = layer_blocks(mine1, arrived, sizes)
    arrived1 = layer_step(layer1, sizes)
    theirs2, = behind([theirs2], arrived0)
    arrived = core_step(theirs2, sizes)
    layer2 = layer_blocks(mine2, arrived, sizes)
    arrived2 = layer_step(layer2, sizes)

    first_picks = picks(cs.side[:side_cut] + cs.above + cs.corner, cells[:half_cells])
    last_picks = picks(cs.side[side_cut:], cells[half_cells:])
    full, *strips = tied_call(
        input_kernel, layer1[1:] + layer2[1:],
        [pg0, pg1, qkv_weight, pinned(normed), pinned(rstd), pinned(grad), merged,
         first_picks, last_picks, picks(sum(g_strips, []), grps)],
        [hbm] * 6 + [vmem] * 4, [wide] + [shape(*e) for e in extents], [vmem] * 4,
        scratch_shapes=[
            pltpu.VMEM((count, 3 * channels), BF16),
            pltpu.VMEM(qkv_weight.shape, BF16),
            pltpu.VMEM((count, channels), BF16),
            pltpu.VMEM((count, channels), BF16),
            pltpu.VMEM((count, LANES), F32),
            pltpu.VMEM((count, channels), BF16),
            pltpu.SemaphoreType.DMA((3 * halves + channels // TILE,)),
            pltpu.SemaphoreType.DMA((3,)),
        ],
        name="input_backward", **settings(13, 40),
    )
    arrived1 = behind(arrived1, full)
    strips = sent_strips(behind(strips, arrived1), sizes, -1)

    total1 = jnp.concatenate([layer0[0], layer1[0]], axis=1)
    for pair in zip(arrived0, arrived1):
        total1 = total1 + jnp.concatenate(pair, axis=1).astype(F32)
    kept1, given1 = column_halves(total1, sizes, 1)
    got1 = exchange(given1, sizes, 1, 0)

    part1 = kept1 + got1.astype(F32)
    column2 = column_blocks(layer2[0], arrived2, sizes)
    bit = 2
    while 2 * bit < sizes[0]:
        kept1, given1 = column_halves(part1, sizes, bit)
        part1 = kept1 + exchange(given1, sizes, bit, 0).astype(F32)
        bit *= 2
    kept1, last1 = column_halves(part1, sizes, bit)
    column2[bit] = jnp.concatenate([last1, column2[bit]], axis=1)
    got2 = column_step(column2, sizes)

    got = [Strips.sent(s, *t) for s, t in zip((cs.side, cs.above, cs.corner), to)]
    g_got = sum((Strips.sent(s, *t) for s, t in zip(g_strips, g_to)), [])
    tokens_grad, merged = tied_call(
        unpack_kernel, column2[1:] + [given1],
        [
            full, merged, *strips,
            picks(box(levels, range(SHIFT, 2 * SHIFT), own_cols), cells[:half_cells] + got[0][:side_cut]),
            picks(box(levels, range(2 * SHIFT, lat_rows), own_cols), cells[half_cells:] + got[0][side_cut:]),
            picks(box(levels, range(lat_rows, lat_rows + SHIFT), own_cols), got[1] + got[2]),
            picks(g_own, grps + g_got),
        ],
        [vmem] * 9, [wide, shape(groups, merged_width)], [vmem] * 2,
        name="unpack_strips", **settings(20, 24),
    )
    got2 = behind(got2, tokens_grad)
    qkv_weight_grad, out_weight_grad = pl.pallas_call(
        functools.partial(end_kernel, bit),
        out_shape=[
            shape(kept1.shape[0], 3 * channels, dtype=F32), shape(kept1.shape[0], channels, dtype=F32),
        ],
        in_specs=[vmem] * (2 + len(got2)), out_specs=[vmem] * 2,
        name="end_sums", **settings(1, 16),
    )(kept1, column2[0], *got2)
    merged = merged.reshape(levels, g_cols, g_rows, merged_width).transpose(0, 2, 1, 3)
    return merged, tokens_grad.reshape(tokens.shape), qkv_weight_grad, out_weight_grad


def solution(mesh):
    sizes = (mesh.shape["lat"], mesh.shape["lon"])
    in_specs = (P(None, "lat", "lon", None), P(), P(), P(), P(None, "lat", "lon", None))
    out_specs = (
        P(None, "lat", "lon", None),
        P(None, "lat", "lon", None),
        P(("lat", "lon"), None),
        P(("lat", "lon"), None),
    )
    return jax.shard_map(
        functools.partial(shards, sizes),
        mesh=mesh, in_specs=in_specs, out_specs=out_specs, check_vma=False,
    )
```

```python
import functools

import jax
import jax.numpy as jnp
import numpy as np
from jax import lax
from jax.experimental import pallas as pl
from jax.experimental.pallas import tpu as pltpu
from jax.sharding import PartitionSpec as P

HEADS = 32
WIN = 8
SHIFT = 4
LANES = 128
HALF = SHIFT // 2
TILE = 256
WIDE = 512
EPSILON = 1e-05
MIB = 1 << 20

NN = (((1,), (0,)), ((), ()))
NT = (((1,), (1,)), ((), ()))
TN = (((0,), (0,)), ((), ()))
BF16 = jnp.bfloat16
F32 = jnp.float32


def dot(a, b, dims=NN):
    return lax.dot_general(a, b, dims, preferred_element_type=F32)


def window_cells(levels, rows, columns):
    half = WIN // 2
    return [
        (level, wi * WIN + 2 * row + sub % 2, wj * WIN + 2 * column + sub // 2)
        for wi in range(rows // WIN) for wj in range(columns // WIN) for sub in range(4)
        for level in range(levels) for row in range(half) for column in range(half)
    ]


def window_groups(levels, rows, columns):
    half = WIN // 2
    return [
        (level, wi * half + row, wj * half + column)
        for wi in range(rows // half) for wj in range(columns // half)
        for level in range(levels) for row in range(half) for column in range(half)
    ]


def box(levels, rows, columns):
    return [(l, r, c) for l in range(levels) for r in rows for c in columns]


def turned_box(levels, rows, columns):
    return [(l, r, c) for l in range(levels) for c in columns for r in rows]


def padded(cells, step=16):
    return cells + [None] * (-len(cells) % step)


def picks(wanted, held):
    spot = {cell: i for i, cell in enumerate(held) if cell is not None}
    table = np.zeros((len(wanted), len(held)), np.float32)
    for i, cell in enumerate(wanted):
        if cell is not None:
            table[i, spot[cell]] = 1.0
    return jnp.asarray(table, BF16)


class Strips:
    def __init__(self, levels, rows, columns, width, cut):
        self.side = (box(levels, range(width, 2 * width), range(width))
                     + box(levels, range(2 * width, rows), range(width)))
        self.above = box(levels, range(width), range(width, columns))
        self.corner = box(levels, range(width), range(width))
        if not cut:
            self.side = box(levels, range(width, rows), range(width))

    @staticmethod
    def sent(cells, down, across):
        return [None if c is None else (c[0], c[1] + down, c[2] + across) for c in cells]


def head_masks():
    head = lax.broadcasted_iota(jnp.int32, (LANES, LANES), 1) // (LANES // 4)
    return [jnp.where(head == h, 1.0, 0.0).astype(BF16) for h in range(4)]


def region_bias(places, active):
    step = 2 * (WIN // 2)
    one = (lax.broadcasted_iota(jnp.int32, (places, places), 0) // step) % 2
    other = (lax.broadcasted_iota(jnp.int32, (places, places), 1) // step) % 2
    return jnp.where((one != other) & active, -1e30, 0.0)


def score_scale(channels):
    return float((channels // HEADS) ** -0.5 * np.log2(np.e))


def aligned(start, size, step=None):
    return pl.ds(pl.multiple_of(start, step or size), size)


def pack_kernel(tokens, merged_grad, pick_cells, pick_groups, side, above, corner):
    cells = dot(pick_cells[...], tokens[...]).astype(BF16)
    groups = dot(pick_groups[...], merged_grad[...]).astype(BF16)
    at, at_group = 0, 0
    for out, (count, extra) in zip((side, above, corner), strip_rows(pick_cells, pick_groups)):
        out[:count] = cells[at:at + count]
        out[count:] = groups[at_group:at_group + extra]
        at, at_group = at + count, at_group + extra


def strip_rows(pick_cells, pick_groups):
    levels = 2
    rows, columns = strip_rows.extent
    cells = [levels * (rows - SHIFT) * SHIFT, levels * SHIFT * (columns - SHIFT), levels * SHIFT * SHIFT]
    groups = [n // 4 + (-(n // 4)) % 16 for n in cells]
    return list(zip(cells, groups))


def normalized_window(x, rows, xw, normed, rstd):
    xw[rows] = x.astype(BF16)
    center = jnp.mean(x, axis=1, keepdims=True)
    moved = x - center
    scale = lax.rsqrt(jnp.mean(moved * moved, axis=1, keepdims=True) + EPSILON)
    rstd[rows] = jnp.broadcast_to(scale, (x.shape[0], LANES))
    normed[rows] = (moved * scale).astype(BF16)


def attended(proj, rows, lanes, masks, factor, bias, mixture, inverse):
    places = masks[0].shape[0]
    q, k, v = (proj[rows, at] for at in lanes)
    scores = dot(q, jnp.concatenate([k * m for m in masks], axis=0), NT)
    parts = []
    for h in range(4):
        part = scores[:, h * places:(h + 1) * places] * factor
        if bias is not None:
            part = part + bias
        part = part - jnp.max(part, axis=1, keepdims=True)
        parts.append(jnp.exp2(part).astype(BF16))
    values = jnp.concatenate([jnp.concatenate([v * m, m], axis=1) for m in masks], axis=0)
    summed = dot(jnp.concatenate(parts, axis=1), values)
    inv = 1.0 / summed[:, LANES:]
    inverse[rows, lanes[0]] = inv
    mixture[rows, lanes[0]] = (summed[:, :LANES] * inv).astype(BF16)


def inner_kernel(
    tokens, order, wqkv_h, xw, normed, rstd, mixture, inverse, proj, wqkv, in_sem,
):
    count, channels = xw.shape
    places = 2 * WIN * WIN
    tiles = wqkv.shape[1] // WIDE

    def load(n):
        columns = aligned(n * WIDE, WIDE)
        return pltpu.make_async_copy(wqkv_h.at[:, columns], wqkv.at[:, columns], in_sem.at[n])

    for n in range(tiles):
        load(n).start()
    half = tokens.shape[0] // 2
    line = half // (2 * WIN)
    cut = SHIFT * line
    source = jnp.concatenate(
        [tokens[cut:cut + WIN * line], tokens[half + cut:half + cut + WIN * line]], axis=0
    )
    x = dot(order[:, :source.shape[0]], source)
    for w in range(count // places):
        rows = slice(w * places, (w + 1) * places)
        normalized_window(x[rows], rows, xw, normed, rstd)

    @pl.loop(0, tiles)
    def _(n):
        load(n).wait()
        columns = aligned(n * WIDE, WIDE)
        proj[:, columns] = dot(normed[...], wqkv[:, columns]).astype(BF16)

    masks = head_masks()
    factor = score_scale(channels)

    @pl.loop(0, channels // LANES // 2)
    def _(g):
        for i in range(2):
            lanes = [aligned(j * channels + (2 * g + i) * LANES, LANES) for j in range(3)]
            for w in range(count // places):
                rows = slice(w * places, (w + 1) * places)
                attended(proj, rows, lanes, masks, factor, None, mixture, inverse)


def forward_kernel(
    edge, owner, tokens, merged_grad, side, above, corner, order, group, rowmap,
    wqkv_h, wout_h, wm_h, xw_h, normed_in, rstd_h, mixture_h, inverse_h, proj_in,
    normed_h, normt_h, proj_h, dmr_h, dmm_h, grad_h, rstd, merged, out_mine, out_theirs,
    wqkv, wout, wm, source, xw, normed, proj, mixture, inverse, subs, dsubs, cotangent,
    grad, dmr, dmm, in_sem, out_sem,
):
    count, channels = xw.shape
    places = 2 * WIN * WIN
    windows = count // places
    per_row = windows // 2
    quarter = places // 4
    groups = count // 4
    devices = owner.shape[0]
    block = channels // devices

    loads = [
        pltpu.make_async_copy(src, dst, in_sem.at[i])
        for i, (src, dst) in enumerate([(wqkv_h, wqkv), (wout_h, wout), (wm_h, wm)])
    ]
    outer = count - xw_h.shape[0]
    ready = [
        pltpu.make_async_copy(src, dst.at[pl.ds(outer, count - outer)], in_sem.at[3 + i])
        for i, (src, dst) in enumerate(
            [(xw_h, xw), (normed_in, normed), (rstd_h, rstd), (mixture_h, mixture),
             (inverse_h, inverse), (proj_in, proj)]
        )
    ]
    for load in loads + ready:
        load.start()
    stores = [
        pltpu.make_async_copy(src, dst, out_sem.at[i])
        for i, (src, dst) in enumerate(
            [(normed, normed_h), (proj, proj_h), (wqkv.at[:, pl.ds(count, count)], normt_h),
             (grad, grad_h), (dmr, dmr_h), (dmm, dmm_h)]
        )
    ]

    (n_side, g_side), (n_above, g_above), (n_corner, g_corner) = strip_rows(None, None)
    half = count // 2
    line = half // (2 * WIN)
    cut = SHIFT * line
    side_cut = 2 * SHIFT * SHIFT
    blocks = [
        [tokens[:cut], tokens[half:half + cut], side[:side_cut], above[:n_above], corner[:n_corner]],
        [tokens[cut:cut + WIN * line], tokens[half + cut:half + cut + WIN * line], side[side_cut:n_side]],
    ]
    for wi in range(2):
        at = 0
        for piece in blocks[wi]:
            source[wi, at:at + piece.shape[0]] = piece
            at += piece.shape[0]
        if at < source.shape[1]:
            source[wi, at:] = jnp.zeros((source.shape[1] - at, channels), BF16)

    for wi in range(2):
        first, last = wi * per_row, min((wi + 1) * per_row, outer // places)
        x = dot(order[first * places:last * places], source[wi])
        for w in range(first, last):
            rows = slice(w * places, (w + 1) * places)
            normalized_window(x[(w - first) * places:(w - first + 1) * places], rows, xw, normed, rstd)

    loads[0].wait()
    outer_rows = slice(0, outer)

    @pl.loop(0, wqkv.shape[1] // WIDE)
    def _(n):
        columns = aligned(n * WIDE, WIDE)
        proj[outer_rows, columns] = dot(normed[outer_rows], wqkv[:, columns]).astype(BF16)

    for load in ready:
        load.wait()
    stores[0].start()
    stores[1].start()

    masks = head_masks()
    factor = score_scale(channels)

    edge_bias = region_bias(places, edge[0] == 1)
    held = jnp.concatenate(
        [merged_grad[...], side[n_side:], above[n_above:], corner[n_corner:]], axis=0
    )
    cotangent[...] = dot(group[...], held).astype(BF16)
    loads[2].wait()
    steps = channels // LANES
    per_step = 4 * channels // TILE // steps

    @pl.loop(0, steps)
    def _(g):
        lanes = [aligned(i * channels + g * LANES, LANES) for i in range(3)]
        for w in range(outer // places):
            rows = slice(w * places, (w + 1) * places)
            bias = edge_bias if w < per_row else None
            attended(proj, rows, lanes, masks, factor, bias, mixture, inverse)
        for i in range(per_step):
            at = aligned((g * per_step + i) * TILE, TILE)
            dsubs[:, at] = dot(cotangent[...], wm[at], NT).astype(BF16)

    loads[1].wait()

    @pl.loop(0, channels // WIDE)
    def _(n):
        columns = aligned(n * WIDE, WIDE)
        out = dot(mixture[...], wout[:, columns]) + xw[:, columns].astype(F32)
        out = out.astype(BF16)
        for w in range(windows):
            for s in range(4):
                at = w * places + s * quarter
                subs[s, w * quarter:(w + 1) * quarter, columns] = out[at:at + quarter]

    total = jnp.zeros((groups, 1), F32)
    for s in range(4):
        total += jnp.sum(subs[s].astype(F32), axis=1, keepdims=True)
    center = total / (4 * channels)
    total = jnp.zeros((groups, 1), F32)
    for s in range(4):
        moved = subs[s].astype(F32) - center
        total += jnp.sum(moved * moved, axis=1, keepdims=True)
    scale = lax.rsqrt(total / (4 * channels) + EPSILON)
    result = jnp.zeros((groups, wm.shape[1]), F32)
    for s in range(4):
        unit = ((subs[s].astype(F32) - center) * scale).astype(BF16)
        result += dot(unit, wm[s * channels:(s + 1) * channels])
    merged[...] = result.astype(BF16)

    mean_g = jnp.zeros((groups, 1), F32)
    mean_gx = jnp.zeros((groups, 1), F32)
    for s in range(4):
        d = dsubs[:, s * channels:(s + 1) * channels].astype(F32)
        mean_g += jnp.sum(d, axis=1, keepdims=True)
        mean_gx += jnp.sum(d * ((subs[s].astype(F32) - center) * scale), axis=1, keepdims=True)
    mean_g = mean_g / (4 * channels)
    mean_gx = mean_gx / (4 * channels)
    for s in range(4):
        unit = (subs[s].astype(F32) - center) * scale
        d = dsubs[:, s * channels:(s + 1) * channels].astype(F32)
        d = (scale * (d - mean_g - unit * mean_gx)).astype(BF16)
        for w in range(windows):
            at = w * places + s * quarter
            grad[at:at + quarter] = d[w * quarter:(w + 1) * quarter]
    stores[3].start()

    @pl.loop(0, channels // WIDE)
    def _(n):
        columns = aligned(n * WIDE, WIDE)
        d = dot(grad[...], wout[columns], NT).astype(BF16).astype(F32)
        d = d * inverse[:, columns]
        dmr[:, columns] = d.astype(BF16)
        dmm[:, columns] = (-d * mixture[:, columns].astype(F32)).astype(BF16)

    stores[4].start()
    stores[5].start()

    def turn(field, out):
        if block % 16:
            @pl.loop(0, channels // TILE)
            def _(n):
                rows = aligned(n * TILE, TILE)
                spot = lax.broadcasted_iota(jnp.int32, (TILE, channels), 1)
                pick = jnp.where(spot == rowmap[rows], 1.0, 0.0).astype(BF16)
                out[rows] = dot(pick, field[...], NT).astype(BF16)
        else:
            @pl.loop(0, channels // WIDE)
            def _(n):
                rows = aligned(n * WIDE, WIDE)
                turned[rows] = field[:, rows].T

            for d in range(devices):
                out[d * block:(d + 1) * block] = turned[aligned(owner[d] * block, block)]

    turned, normt, mixt = (wqkv.at[:, pl.ds(i * count, count)] for i in range(3))
    turn(normed, normt)
    stores[2].start()
    turn(mixture, mixt)
    part = channels // 2

    @pl.loop(0, channels // WIDE)
    def _(n):
        columns = aligned(n * WIDE, WIDE)
        terms = dot(mixt[...], grad[:, columns]).astype(BF16)
        out_mine[:, columns] = terms[:part]
        out_theirs[:, columns] = terms[part:]

    for store in stores:
        store.wait()


def backward_kernel(index, *refs):
    (edge, proj_h, dmr_h, dmm_h, normt_h, pgrad_h, mine_h, theirs_h,
     held, normt, pgrad, mine, theirs, in_sem, sem, out_sem) = refs
    _, count, width = held.shape
    channels = normt.shape[0]
    half = channels // 2
    places = 2 * WIN * WIN
    windows = count // places
    per_row = windows // 2
    masks = head_masks()
    factor = score_scale(channels)
    plain = (channels // HEADS) ** -0.5
    steps = width // TILE

    def loads(g):
        columns = aligned(g * TILE, TILE)
        for i in range(5):
            src = (proj_h, proj_h, proj_h, dmr_h, dmm_h)[i]
            start = (i * channels if i < 3 else 0) + index * width
            yield pltpu.make_async_copy(
                src.at[:, aligned(start + g * TILE, TILE)], held.at[i, :, columns], in_sem.at[g, i]
            )

    def stores(g):
        for i in range(3):
            columns = aligned(i * width + g * TILE, TILE)
            for j, (src, dst) in enumerate(((pgrad, pgrad_h), (mine, mine_h), (theirs, theirs_h))):
                yield pltpu.make_async_copy(src.at[:, columns], dst.at[:, columns], out_sem.at[g, i, j])

    for g in range(steps):
        for load in loads(g):
            load.start()
    turned_load = pltpu.make_async_copy(normt_h, normt, sem.at[0])
    turned_load.start()
    edge_bias = region_bias(places, edge[0] == 1)

    @pl.loop(0, steps)
    def _(g):
        for load in loads(g):
            load.wait()

        for part_of in range(TILE // LANES):
            lanes = aligned(g * TILE + part_of * LANES, LANES)
            for w in range(windows):
                rows = slice(w * places, (w + 1) * places)
                q, k, v, dm, dd = (held[i, rows, lanes] for i in range(5))
                keys = jnp.concatenate([k * m for m in masks], axis=0)
                scores = dot(keys, q, NT)
                values = jnp.concatenate(
                    [jnp.concatenate([v * m, m], axis=1) for m in masks], axis=0
                )
                slope = dot(values, jnp.concatenate([dm, dd], axis=1), NT)
                weights, slopes = [], []
                for h in range(4):
                    block = slice(h * places, (h + 1) * places)
                    part = scores[block] * factor
                    if w < per_row:
                        part = part + edge_bias
                    part = jnp.exp2(part - jnp.max(part, axis=0, keepdims=True))
                    weights.append(part.astype(BF16))
                    slopes.append((part * slope[block]).astype(BF16))
                dv = dot(
                    jnp.concatenate(weights, axis=1),
                    jnp.concatenate([dm * m for m in masks], axis=0),
                )
                dk = dot(
                    jnp.concatenate(slopes, axis=1),
                    jnp.concatenate([q * m for m in masks], axis=0),
                )
                dq = dot(jnp.concatenate(slopes, axis=0), keys, TN)
                at = g * TILE + part_of * LANES
                pgrad[rows, lanes] = (dq * plain).astype(BF16)
                pgrad[rows, aligned(width + at, LANES)] = (dk * plain).astype(BF16)
                pgrad[rows, aligned(2 * width + at, LANES)] = dv.astype(BF16)

        @pl.when(g == 0)
        def _():
            turned_load.wait()

        for i in range(3):
            columns = aligned(i * width + g * TILE, TILE)
            terms = dot(normt[...], pgrad[:, columns]).astype(BF16)
            mine[:, columns] = terms[:half]
            theirs[:, columns] = terms[half:]
        for store in stores(g):
            store.start()

    for g in range(steps):
        for store in stores(g):
            store.wait()


def projection_loads(pgrads, wqkv_h, pgrad, wqkv, sem, start):
    width = pgrads[0].shape[1] // 3
    channels = pgrad.shape[1] // 3
    loads = [
        pltpu.make_async_copy(
            field.at[:, pl.ds(i * width, width)],
            pgrad.at[:, pl.ds(i * channels + c * width, width)], sem.at[c * 3 + i],
        )
        for c, field in enumerate(pgrads) for i in range(3)
    ]
    tiles = [
        pltpu.make_async_copy(
            wqkv_h.at[pl.ds(start + n * TILE, TILE)], wqkv.at[pl.ds(n * TILE, TILE)],
            sem.at[3 * len(pgrads) + n],
        )
        for n in range(wqkv.shape[0] // TILE)
    ]
    for load in loads + tiles:
        load.start()
    return loads, tiles


def input_kernel(*refs):
    (pg0, pg1, wqkv_h, normed_h, rstd_h, grad_h, merged,
     pick_first, pick_last, pick_groups, full, side, below, corner,
     pgrad, wqkv, ngrad, normed, rstd, grad, sem, more_sem) = refs
    count, channels = ngrad.shape
    loads, tiles = projection_loads([pg0, pg1], wqkv_h, pgrad, wqkv, sem, 0)
    more = [
        pltpu.make_async_copy(src, dst, more_sem.at[i])
        for i, (src, dst) in enumerate([(normed_h, normed), (rstd_h, rstd), (grad_h, grad)])
    ]
    for load in more:
        load.start()
    for load in loads:
        load.wait()
    for load in tiles:
        load.wait()

    @pl.loop(0, channels // WIDE)
    def _(n):
        rows = aligned(n * WIDE, WIDE)
        ngrad[:, rows] = dot(pgrad[...], wqkv[rows], NT).astype(BF16)

    for load in more:
        load.wait()
    places = 2 * WIN * WIN

    @pl.loop(0, count // places)
    def _(w):
        rows = aligned(w * places, places)
        d = ngrad[rows].astype(F32)
        unit = normed[rows].astype(F32)
        mean_d = jnp.mean(d, axis=1, keepdims=True)
        mean_dx = jnp.mean(d * unit, axis=1, keepdims=True)
        part = rstd[rows, :1] * (d - mean_d - unit * mean_dx)
        full[rows] = (part.astype(BF16).astype(F32) + grad[rows].astype(F32)).astype(BF16)

    (n_side, g_side), (n_above, g_above), (n_corner, g_corner) = strip_rows(None, None)
    side_cut = 2 * SHIFT * SHIFT
    first = dot(pick_first[...], full[:count // 2]).astype(BF16)
    last = dot(pick_last[...], full[count // 2:]).astype(BF16)
    groups = dot(pick_groups[...], merged[...]).astype(BF16)
    side[:side_cut] = first[:side_cut]
    side[side_cut:n_side] = last
    below[:n_above] = first[side_cut:side_cut + n_above]
    corner[:n_corner] = first[side_cut + n_above:]
    side[n_side:] = groups[:g_side]
    below[n_above:] = groups[g_side:g_side + g_above]
    corner[n_corner:] = groups[g_side + g_above:]


def end_kernel(bit, kept1, kept2, *refs):
    arrived, (qkv, out) = refs[:-2], refs[-2:]
    channels = out.shape[1]
    columns = kept1.shape[1]
    first = kept1[...] + arrived[bit - 1][:, :columns].astype(F32)
    last = kept2[...]
    for i, block in enumerate(arrived):
        last += (block[:, columns:] if i == bit - 1 else block[...]).astype(F32)
    out[...] = first[:, :channels]
    width = channels // 2
    for i in range(3):
        at = i * channels
        qkv[:, at:at + width] = first[:, channels + i * width:channels + (i + 1) * width]
        qkv[:, at + width:at + channels] = last[:, i * width:(i + 1) * width]


def unpack_kernel(full, merged, side, below, corner, pick_top, pick_middle, pick_bottom,
                  pick_groups, tokens_out, merged_out):
    count = full.shape[0]
    half = count // 2
    (n_side, _), (n_above, _), (n_corner, _) = strip_rows(None, None)
    side_cut = 2 * SHIFT * SHIFT
    line = half // (2 * WIN)
    pieces = [
        (pick_top, [full[:half], side[:side_cut]]),
        (pick_middle, [full[half:], side[side_cut:n_side]]),
        (pick_bottom, [below[:n_above], corner[:n_corner]]),
    ]
    at = 0
    for pick, held in pieces:
        rows = pick.shape[0] // 2
        out = dot(pick[...], jnp.concatenate(held, axis=0)).astype(BF16)
        for level in range(2):
            start = level * half + at
            tokens_out[start:start + rows] = out[level * rows:(level + 1) * rows]
        at += rows
    held = [merged[...], side[n_side:], below[n_above:], corner[n_corner:]]
    merged_out[...] = dot(pick_groups[...], jnp.concatenate(held, axis=0)).astype(BF16)


def sent(block, sizes, lat_step, lon_step):
    n_lat, n_lon = sizes
    route = [
        (a * n_lon + b, (a + lat_step) % n_lat * n_lon + (b + lon_step) % n_lon)
        for a in range(n_lat) for b in range(n_lon)
    ]
    return lax.ppermute(block, ("lat", "lon"), route)


def sent_strips(strips, sizes, step):
    side, lines, corner = strips
    return [sent(side, sizes, 0, step), sent(lines, sizes, step, 0), sent(corner, sizes, step, step)]


def device_rows(channels, sizes):
    n_lat, n_lon = sizes
    devices = n_lat * n_lon
    rows = channels // devices
    place = np.arange(devices)
    lon = 2 * (place // n_lat % (n_lon // 2)) + place // (devices // 2)
    lat = place % n_lat
    owner = (
        jnp.bitwise_xor(lax.axis_index("lat").astype(jnp.int32), jnp.asarray(lat, jnp.int32)) * n_lon
        + jnp.bitwise_xor(lax.axis_index("lon").astype(jnp.int32), jnp.asarray(lon, jnp.int32))
    )
    rowmap = owner[:, None] * rows + jnp.arange(rows, dtype=jnp.int32)[None, :]
    return owner, rowmap.reshape(channels, 1)


def exchange(block, sizes, lat_bits, lon_bits):
    n_lat, n_lon = sizes
    route = [
        (a * n_lon + b, (a ^ lat_bits) * n_lon + (b ^ lon_bits))
        for a in range(n_lat) for b in range(n_lon)
    ]
    return lax.ppermute(block, ("lat", "lon"), route)


def core_step(theirs, sizes):
    return exchange(theirs, sizes, 0, 1)


def core_sum(mine, arrived):
    return (mine.astype(F32) + arrived.astype(F32)).astype(BF16)


class Layer:
    def __init__(self, total, sizes):
        self.sizes = sizes
        chips = sizes[1] // 2
        bits = [1 << i for i in range(chips.bit_length() - 1)]
        self.orders = [list(bits), bits[1:] + bits[:1]]
        self.bits = [bits[::-1], bits[::-1]]
        columns = total.shape[1] // 2
        rows = total.shape[0] // chips
        self.parts = [
            total[:, i * columns:(i + 1) * columns].reshape([2] * len(bits) + [rows, columns])
            for i in range(2)
        ]

    def give(self):
        self.kept, given = [], []
        for i, part in enumerate(self.parts):
            axis = self.bits[i].index(self.orders[i][0])
            self.kept.append(lax.index_in_dim(part, 0, axis, keepdims=False))
            given.append(lax.index_in_dim(part, 1, axis, keepdims=False))
        return given

    def send(self, given):
        arrived = []
        for i, block in enumerate(given):
            bit = self.orders[i].pop(0)
            self.bits[i] = [b for b in self.bits[i] if b != bit]
            arrived.append(exchange(block, self.sizes, 0, 2 * bit))
        return arrived

    def add(self, arrived):
        self.parts = [core_sum(k, a) for k, a in zip(self.kept, arrived)]

    def finish(self):
        while self.orders[0]:
            self.add(self.send(self.give()))
        return jnp.concatenate(self.parts, axis=-1).astype(F32)


def column_blocks(kept, arrived, sizes):
    total = kept
    for block in arrived:
        total = total + block.astype(F32)
    rows = total.shape[0] // sizes[0]
    blocks = [total[i * rows:(i + 1) * rows] for i in range(sizes[0])]
    return [blocks[0]] + [b.astype(BF16) for b in blocks[1:]]


def column_step(blocks, sizes):
    return [exchange(b, sizes, i, 0) for i, b in enumerate(blocks) if i]


def pinned(value):
    return pltpu.with_memory_space_constraint(value, pltpu.HBM)


def behind(values, marker):
    *values, _ = lax.optimization_barrier((*values, marker))
    return values


def column_halves(total, sizes, bit):
    blocks = sizes[0] // (2 * bit)
    pairs = total.reshape(blocks, 2, total.shape[0] // (2 * blocks), total.shape[1])
    kept, given = pairs[:, 0], pairs[:, 1]
    return [x.reshape(-1, total.shape[1]) for x in (kept, given.astype(BF16))]


def finished(kept, arrived):
    for block in arrived:
        kept = kept + block.astype(F32)
    return kept


def tied_call(kernel, after, operands, in_specs, out_shape, out_specs, **rest):
    waits = len(after)

    def body(*refs):
        kernel(*refs[waits:])

    return pl.pallas_call(
        body, out_shape=out_shape,
        in_specs=[pl.BlockSpec(memory_space=pl.ANY)] * waits + in_specs, out_specs=out_specs, **rest,
    )(*after, *operands)


def shards(sizes, tokens, qkv_weight, out_weight, merge_weight, merged_grad):
    levels, lat_rows, lon_cols, channels = tokens.shape
    merged_width = merge_weight.shape[1]
    count = levels * lat_rows * lon_cols
    groups = count // 4
    half = channels // 2
    strip_rows.extent = (lat_rows, lon_cols)
    vmem = pl.BlockSpec(memory_space=pltpu.VMEM)
    smem = pl.BlockSpec(memory_space=pltpu.SMEM)
    hbm = pl.BlockSpec(memory_space=pl.ANY)

    def shape(*extent, dtype=BF16):
        return jax.ShapeDtypeStruct(extent, dtype)

    def settings(weight, limit=60):
        return dict(
            compiler_params=pltpu.CompilerParams(vmem_limit_bytes=limit * MIB),
            cost_estimate=pl.CostEstimate(
                flops=int(weight * 1e10), bytes_accessed=16 * MIB, transcendentals=0
            ),
        )

    g_rows, g_cols = lat_rows // 2, lon_cols // 2
    cells = window_cells(levels, lat_rows, lon_cols)
    grps = window_groups(levels, g_rows, g_cols)
    cs = Strips(levels, lat_rows, lon_cols, SHIFT, True)
    gs = Strips(levels, g_rows, g_cols, HALF, False)
    g_strips = [padded(gs.side), padded(gs.above), padded(gs.corner)]
    to = ((0, lon_cols), (lat_rows, 0), (lat_rows, lon_cols))
    g_to = ((0, g_cols), (g_rows, 0), (g_rows, g_cols))
    own_rows = range(SHIFT, SHIFT + lat_rows)
    own_cols = range(SHIFT, SHIFT + lon_cols)
    own = box(levels, own_rows, own_cols)
    g_own = turned_box(levels, range(HALF, HALF + g_rows), range(HALF, HALF + g_cols))
    half_cells = count // 2
    side_cut = levels * SHIFT * SHIFT
    sent_cells = sum((Strips.sent(s, *t) for s, t in zip((cs.side, cs.above, cs.corner), to)), [])
    sent_groups = sum((Strips.sent(s, *t) for s, t in zip(g_strips, g_to)), [])
    held_top = box(levels, range(SHIFT, 2 * SHIFT), own_cols) + cs.side[:side_cut] + cs.above + cs.corner
    held_low = box(levels, range(2 * SHIFT, lat_rows), own_cols) + cs.side[side_cut:]
    depth = max(len(held_top), len(held_low))
    depth += -depth % 16
    held_top += [None] * (depth - len(held_top))
    held_low += [None] * (depth - len(held_low))

    tokens_flat = tokens.reshape(count, channels)
    merged_grad_flat = merged_grad.transpose(0, 2, 1, 3).reshape(groups, merged_width)
    extents = [(n + g, channels) for n, g in strip_rows(None, None)]
    packed = pl.pallas_call(
        pack_kernel,
        out_shape=[shape(*e) for e in extents],
        in_specs=[vmem] * 4, out_specs=[vmem] * 3,
        name="pack_strips", **settings(1),
    )(pinned(tokens_flat), pinned(merged_grad_flat), picks(sent_cells, own), picks(sent_groups, g_own))
    strips = sent_strips(packed, sizes, 1)

    order = jnp.concatenate([picks(cells[:half_cells], held_top), picks(cells[half_cells:], held_low)])
    group = picks(grps, g_own + sum(g_strips, []))
    edge = (lax.axis_index("lat") == 0).astype(jnp.int32).reshape(1)
    owner, rowmap = device_rows(channels, sizes)
    if channels // (sizes[0] * sizes[1]) % 16 == 0:
        rowmap = jnp.zeros((8, 1), jnp.int32)

    wide = shape(count, channels)
    inner = 2 * 2 * WIN * WIN
    ready = tied_call(
        inner_kernel, packed,
        [pinned(tokens_flat), order[count - inner:], pinned(qkv_weight)],
        [vmem] * 2 + [hbm],
        [shape(inner, channels), shape(inner, channels), shape(inner, LANES, dtype=F32),
         shape(inner, channels), shape(inner, channels, dtype=F32), shape(inner, 3 * channels)],
        [vmem] * 6,
        scratch_shapes=[
            pltpu.VMEM(qkv_weight.shape, BF16),
            pltpu.SemaphoreType.DMA((3 * channels // TILE,)),
        ],
        name="inner_windows", **settings(9),
    )
    normed, normt, proj, dmr, dmm, grad, rstd, merged, out_mine, out_theirs = pl.pallas_call(
        forward_kernel,
        out_shape=[
            wide, shape(channels, count), shape(count, 3 * channels), wide, wide, wide,
            shape(count, LANES, dtype=F32), shape(groups, merged_width),
            shape(half, channels), shape(half, channels),
        ],
        in_specs=[smem] * 2 + [vmem] * 8 + [hbm] * 9,
        out_specs=[hbm] * 6 + [vmem] * 4,
        scratch_shapes=[
            pltpu.VMEM(qkv_weight.shape, BF16),
            pltpu.VMEM(out_weight.shape, BF16),
            pltpu.VMEM(merge_weight.shape, BF16),
            pltpu.VMEM((2, depth, channels), BF16),
            pltpu.VMEM((count, channels), BF16),
            pltpu.VMEM((count, channels), BF16),
            pltpu.VMEM((count, 3 * channels), BF16),
            pltpu.VMEM((count, channels), BF16),
            pltpu.VMEM((count, channels), F32),
            pltpu.VMEM((4, groups, channels), BF16),
            pltpu.VMEM((groups, 4 * channels), BF16),
            pltpu.VMEM((groups, merged_width), BF16),
            pltpu.VMEM((count, channels), BF16),
            pltpu.VMEM((count, channels), BF16),
            pltpu.VMEM((count, channels), BF16),
            pltpu.SemaphoreType.DMA((9,)),
            pltpu.SemaphoreType.DMA((6,)),
        ],
        name="block_forward", **settings(30, 55),
    )(edge, owner, tokens_flat, merged_grad_flat, *strips, order, group, rowmap,
      qkv_weight, out_weight, merge_weight, *ready)

    halves = 2
    width = channels // halves
    steps = width // TILE

    def backward(index, after):
        return tied_call(
            functools.partial(backward_kernel, index), after,
            [edge, pinned(proj), pinned(dmr), pinned(dmm), pinned(normt)], [smem] + [hbm] * 4,
            [shape(count, 3 * width), shape(half, 3 * width), shape(half, 3 * width)], [hbm] * 3,
            scratch_shapes=[
                pltpu.VMEM((5, count, width), BF16),
                pltpu.VMEM((channels, count), BF16),
                pltpu.VMEM((count, 3 * width), BF16),
                pltpu.VMEM((half, 3 * width), BF16),
                pltpu.VMEM((half, 3 * width), BF16),
                pltpu.SemaphoreType.DMA((steps, 5)),
                pltpu.SemaphoreType.DMA((1,)),
                pltpu.SemaphoreType.DMA((steps, 3, 3)),
            ],
            name="attention_backward", **settings(15, 32),
        )

    arrived = core_step(out_theirs, sizes)
    pg0, mine1, theirs1 = backward(0, [])
    out_mine, arrived = behind([out_mine, arrived], pg0)
    theirs1, = behind([theirs1], arrived)
    total = core_sum(out_mine, arrived)
    total1 = core_sum(mine1, core_step(theirs1, sizes))
    layer1 = Layer(jnp.concatenate([total, total1], axis=1), sizes)
    given = layer1.give()
    arrived1 = layer1.send(given)
    pg1, mine2, theirs2 = backward(1, given)
    arrived1 = behind(arrived1, pg1)
    theirs2, = behind([theirs2], arrived1)
    arrived = core_step(theirs2, sizes)
    layer1.add(arrived1)
    given1 = layer1.give()
    arrived1 = layer1.send(given1)
    layer2 = Layer(core_sum(mine2, arrived), sizes)
    given2 = layer2.give()
    arrived2 = layer2.send(given2)

    first_picks = picks(cs.side[:side_cut] + cs.above + cs.corner, cells[:half_cells])
    last_picks = picks(cs.side[side_cut:], cells[half_cells:])
    full, *strips = tied_call(
        input_kernel, given1 + given2,
        [pg0, pg1, qkv_weight, pinned(normed), pinned(rstd), pinned(grad), merged,
         first_picks, last_picks, picks(sum(g_strips, []), grps)],
        [hbm] * 6 + [vmem] * 4, [wide] + [shape(*e) for e in extents], [vmem] * 4,
        scratch_shapes=[
            pltpu.VMEM((count, 3 * channels), BF16),
            pltpu.VMEM(qkv_weight.shape, BF16),
            pltpu.VMEM((count, channels), BF16),
            pltpu.VMEM((count, channels), BF16),
            pltpu.VMEM((count, LANES), F32),
            pltpu.VMEM((count, channels), BF16),
            pltpu.SemaphoreType.DMA((3 * halves + channels // TILE,)),
            pltpu.SemaphoreType.DMA((3,)),
        ],
        name="input_backward", **settings(13, 40),
    )
    arrived1 = behind(arrived1, full)
    arrived2 = behind(arrived2, full)
    arrived1 = behind(arrived1, arrived2)
    strips = sent_strips(behind(strips, (arrived1, arrived2)), sizes, -1)
    layer2.add(arrived2)
    total2 = layer2.finish()
    layer1.add(arrived1)
    total1 = layer1.finish()
    kept1, given1 = column_halves(total1, sizes, 1)
    got1 = exchange(given1, sizes, 1, 0)

    part1 = kept1 + got1.astype(F32)
    column2 = column_blocks(total2, [], sizes)
    bit = 2
    while 2 * bit < sizes[0]:
        kept1, given1 = column_halves(part1, sizes, bit)
        part1 = kept1 + exchange(given1, sizes, bit, 0).astype(F32)
        bit *= 2
    kept1, last1 = column_halves(part1, sizes, bit)
    column2[bit] = jnp.concatenate([last1, column2[bit]], axis=1)
    got2 = column_step(column2, sizes)

    got = [Strips.sent(s, *t) for s, t in zip((cs.side, cs.above, cs.corner), to)]
    g_got = sum((Strips.sent(s, *t) for s, t in zip(g_strips, g_to)), [])
    tokens_grad, merged = tied_call(
        unpack_kernel, column2[1:] + [given1],
        [
            full, merged, *strips,
            picks(box(levels, range(SHIFT, 2 * SHIFT), own_cols), cells[:half_cells] + got[0][:side_cut]),
            picks(box(levels, range(2 * SHIFT, lat_rows), own_cols), cells[half_cells:] + got[0][side_cut:]),
            picks(box(levels, range(lat_rows, lat_rows + SHIFT), own_cols), got[1] + got[2]),
            picks(g_own, grps + g_got),
        ],
        [vmem] * 9, [wide, shape(groups, merged_width)], [vmem] * 2,
        name="unpack_strips", **settings(20, 24),
    )
    got2 = behind(got2, tokens_grad)
    qkv_weight_grad, out_weight_grad = pl.pallas_call(
        functools.partial(end_kernel, bit),
        out_shape=[
            shape(kept1.shape[0], 3 * channels, dtype=F32), shape(kept1.shape[0], channels, dtype=F32),
        ],
        in_specs=[vmem] * (2 + len(got2)), out_specs=[vmem] * 2,
        name="end_sums", **settings(1, 16),
    )(kept1, column2[0], *got2)
    merged = merged.reshape(levels, g_cols, g_rows, merged_width).transpose(0, 2, 1, 3)
    return merged, tokens_grad.reshape(tokens.shape), qkv_weight_grad, out_weight_grad


def solution(mesh):
    sizes = (mesh.shape["lat"], mesh.shape["lon"])
    in_specs = (P(None, "lat", "lon", None), P(), P(), P(), P(None, "lat", "lon", None))
    out_specs = (
        P(None, "lat", "lon", None),
        P(None, "lat", "lon", None),
        P(("lat", "lon"), None),
        P(("lat", "lon"), None),
    )
    return jax.shard_map(
        functools.partial(shards, sizes),
        mesh=mesh, in_specs=in_specs, out_specs=out_specs, check_vma=False,
    )
```

```python
import functools

import jax
import jax.numpy as jnp
import numpy as np
from jax import lax
from jax.experimental import pallas as pl
from jax.experimental.pallas import tpu as pltpu
from jax.sharding import PartitionSpec as P

HEADS = 32
WIN = 8
SHIFT = 4
LANES = 128
HALF = SHIFT // 2
TILE = 256
WIDE = 512
BROAD = 1024
EPSILON = 1e-05
MIB = 1 << 20

NN = (((1,), (0,)), ((), ()))
NT = (((1,), (1,)), ((), ()))
TN = (((0,), (0,)), ((), ()))
BF16 = jnp.bfloat16
F32 = jnp.float32


def dot(a, b, dims=NN):
    return lax.dot_general(a, b, dims, preferred_element_type=F32)


def window_cells(levels, rows, columns):
    half = WIN // 2
    return [
        (level, wi * WIN + 2 * row + sub % 2, wj * WIN + 2 * column + sub // 2)
        for wi in range(rows // WIN) for wj in range(columns // WIN) for sub in range(4)
        for level in range(levels) for row in range(half) for column in range(half)
    ]


def window_groups(levels, rows, columns):
    half = WIN // 2
    return [
        (level, wi * half + row, wj * half + column)
        for wi in range(rows // half) for wj in range(columns // half)
        for level in range(levels) for row in range(half) for column in range(half)
    ]


def box(levels, rows, columns):
    return [(l, r, c) for l in range(levels) for r in rows for c in columns]


def turned_box(levels, rows, columns):
    return [(l, r, c) for l in range(levels) for c in columns for r in rows]


def padded(cells, step=16):
    return cells + [None] * (-len(cells) % step)


def picks(wanted, held):
    spot = {cell: i for i, cell in enumerate(held) if cell is not None}
    table = np.zeros((len(wanted), len(held)), np.float32)
    for i, cell in enumerate(wanted):
        if cell is not None:
            table[i, spot[cell]] = 1.0
    return jnp.asarray(table, BF16)


class Strips:
    def __init__(self, levels, rows, columns, width, cut):
        self.side = (box(levels, range(width, 2 * width), range(width))
                     + box(levels, range(2 * width, rows), range(width)))
        self.above = box(levels, range(width), range(width, columns))
        self.corner = box(levels, range(width), range(width))
        if not cut:
            self.side = box(levels, range(width, rows), range(width))

    @staticmethod
    def sent(cells, down, across):
        return [None if c is None else (c[0], c[1] + down, c[2] + across) for c in cells]


def head_masks():
    head = lax.broadcasted_iota(jnp.int32, (LANES, LANES), 1) // (LANES // 4)
    return [jnp.where(head == h, 1.0, 0.0).astype(BF16) for h in range(4)]


def region_bias(places, active):
    step = 2 * (WIN // 2)
    one = (lax.broadcasted_iota(jnp.int32, (places, places), 0) // step) % 2
    other = (lax.broadcasted_iota(jnp.int32, (places, places), 1) // step) % 2
    return jnp.where((one != other) & active, -1e30, 0.0)


def score_scale(channels):
    return float((channels // HEADS) ** -0.5 * np.log2(np.e))


def aligned(start, size, step=None):
    return pl.ds(pl.multiple_of(start, step or size), size)


def pack_kernel(tokens, merged_grad, pick_cells, pick_groups, side, above, corner):
    cells = dot(pick_cells[...], tokens[...]).astype(BF16)
    groups = dot(pick_groups[...], merged_grad[...]).astype(BF16)
    at, at_group = 0, 0
    for out, (count, extra) in zip((side, above, corner), strip_rows(pick_cells, pick_groups)):
        out[:count] = cells[at:at + count]
        out[count:] = groups[at_group:at_group + extra]
        at, at_group = at + count, at_group + extra


def strip_rows(pick_cells, pick_groups):
    levels = 2
    rows, columns = strip_rows.extent
    cells = [levels * (rows - SHIFT) * SHIFT, levels * SHIFT * (columns - SHIFT), levels * SHIFT * SHIFT]
    groups = [n // 4 + (-(n // 4)) % 16 for n in cells]
    return list(zip(cells, groups))


def normalized_window(x, rows, xw, normed, rstd):
    xw[rows] = x.astype(BF16)
    center = jnp.mean(x, axis=1, keepdims=True)
    moved = x - center
    scale = lax.rsqrt(jnp.mean(moved * moved, axis=1, keepdims=True) + EPSILON)
    rstd[rows] = jnp.broadcast_to(scale, (x.shape[0], LANES))
    normed[rows] = (moved * scale).astype(BF16)


def attended(proj, rows, lanes, masks, factor, bias, mixture, inverse):
    places = masks[0].shape[0]
    q, k, v = (proj[rows, at] for at in lanes)
    scores = dot(q, jnp.concatenate([k * m for m in masks], axis=0), NT)
    parts = []
    for h in range(4):
        part = scores[:, h * places:(h + 1) * places] * factor
        if bias is not None:
            part = part + bias
        part = part - jnp.max(part, axis=1, keepdims=True)
        parts.append(jnp.exp2(part).astype(BF16))
    values = jnp.concatenate([jnp.concatenate([v * m, m], axis=1) for m in masks], axis=0)
    summed = dot(jnp.concatenate(parts, axis=1), values)
    inv = 1.0 / summed[:, LANES:]
    inverse[rows, lanes[0]] = inv
    mixture[rows, lanes[0]] = (summed[:, :LANES] * inv).astype(BF16)


def inner_kernel(
    tokens, order, wqkv_h, xw, normed, rstd, mixture, inverse, proj, wqkv, in_sem,
):
    count, channels = xw.shape
    places = 2 * WIN * WIN
    tiles = wqkv.shape[1] // BROAD

    def load(n):
        columns = aligned(n * BROAD, BROAD)
        return pltpu.make_async_copy(wqkv_h.at[:, columns], wqkv.at[:, columns], in_sem.at[n])

    for n in range(tiles):
        load(n).start()
    half = tokens.shape[0] // 2
    line = half // (2 * WIN)
    cut = SHIFT * line
    source = jnp.concatenate(
        [tokens[cut:cut + WIN * line], tokens[half + cut:half + cut + WIN * line]], axis=0
    )
    x = dot(order[:, :source.shape[0]], source)
    for w in range(count // places):
        rows = slice(w * places, (w + 1) * places)
        normalized_window(x[rows], rows, xw, normed, rstd)

    @pl.loop(0, tiles)
    def _(n):
        load(n).wait()
        columns = aligned(n * BROAD, BROAD)
        proj[:, columns] = dot(normed[...], wqkv[:, columns]).astype(BF16)

    masks = head_masks()
    factor = score_scale(channels)

    @pl.loop(0, channels // LANES // 2)
    def _(g):
        for i in range(2):
            lanes = [aligned(j * channels + (2 * g + i) * LANES, LANES) for j in range(3)]
            for w in range(count // places):
                rows = slice(w * places, (w + 1) * places)
                attended(proj, rows, lanes, masks, factor, None, mixture, inverse)


def forward_kernel(
    edge, owner, tokens, merged_grad, side, above, corner, order, group, rowmap,
    wqkv_h, wout_h, wm_h, xw_h, normed_in, rstd_h, mixture_h, inverse_h, proj_in,
    normed_h, normt_h, proj_h, dmr_h, dmm_h, grad_h, rstd, merged, out_mine, out_theirs,
    wqkv, wout, wm, source, xw, normed, proj, mixture, inverse, subs, dsubs, cotangent,
    grad, dmr, dmm, in_sem, out_sem,
):
    count, channels = xw.shape
    places = 2 * WIN * WIN
    windows = count // places
    per_row = windows // 2
    quarter = places // 4
    groups = count // 4
    devices = owner.shape[0]
    block = channels // devices

    loads = [
        pltpu.make_async_copy(src, dst, in_sem.at[i])
        for i, (src, dst) in enumerate([(wqkv_h, wqkv), (wout_h, wout), (wm_h, wm)])
    ]
    outer = count - xw_h.shape[0]
    ready = [
        pltpu.make_async_copy(src, dst.at[pl.ds(outer, count - outer)], in_sem.at[3 + i])
        for i, (src, dst) in enumerate(
            [(xw_h, xw), (normed_in, normed), (rstd_h, rstd), (mixture_h, mixture),
             (inverse_h, inverse), (proj_in, proj)]
        )
    ]
    for load in loads + ready:
        load.start()
    stores = [
        pltpu.make_async_copy(src, dst, out_sem.at[i])
        for i, (src, dst) in enumerate(
            [(normed, normed_h), (proj, proj_h), (wqkv.at[:, pl.ds(count, count)], normt_h),
             (grad, grad_h), (dmr, dmr_h), (dmm, dmm_h)]
        )
    ]

    (n_side, g_side), (n_above, g_above), (n_corner, g_corner) = strip_rows(None, None)
    half = count // 2
    line = half // (2 * WIN)
    cut = SHIFT * line
    side_cut = 2 * SHIFT * SHIFT
    blocks = [
        [tokens[:cut], tokens[half:half + cut], side[:side_cut], above[:n_above], corner[:n_corner]],
        [tokens[cut:cut + WIN * line], tokens[half + cut:half + cut + WIN * line], side[side_cut:n_side]],
    ]
    for wi in range(2):
        at = 0
        for piece in blocks[wi]:
            source[wi, at:at + piece.shape[0]] = piece
            at += piece.shape[0]
        if at < source.shape[1]:
            source[wi, at:] = jnp.zeros((source.shape[1] - at, channels), BF16)

    for wi in range(2):
        first, last = wi * per_row, min((wi + 1) * per_row, outer // places)
        x = dot(order[first * places:last * places], source[wi])
        for w in range(first, last):
            rows = slice(w * places, (w + 1) * places)
            normalized_window(x[(w - first) * places:(w - first + 1) * places], rows, xw, normed, rstd)

    loads[0].wait()
    outer_rows = slice(0, outer)

    @pl.loop(0, wqkv.shape[1] // BROAD)
    def _(n):
        columns = aligned(n * BROAD, BROAD)
        proj[outer_rows, columns] = dot(normed[outer_rows], wqkv[:, columns]).astype(BF16)

    for load in ready:
        load.wait()
    stores[0].start()
    stores[1].start()

    masks = head_masks()
    factor = score_scale(channels)

    edge_bias = region_bias(places, edge[0] == 1)
    held = jnp.concatenate(
        [merged_grad[...], side[n_side:], above[n_above:], corner[n_corner:]], axis=0
    )
    cotangent[...] = dot(group[...], held).astype(BF16)
    loads[2].wait()
    steps = channels // LANES
    per_step = 4 * channels // TILE // steps

    @pl.loop(0, steps)
    def _(g):
        lanes = [aligned(i * channels + g * LANES, LANES) for i in range(3)]
        for w in range(outer // places):
            rows = slice(w * places, (w + 1) * places)
            bias = edge_bias if w < per_row else None
            attended(proj, rows, lanes, masks, factor, bias, mixture, inverse)
        for i in range(per_step):
            at = aligned((g * per_step + i) * TILE, TILE)
            dsubs[:, at] = dot(cotangent[...], wm[at], NT).astype(BF16)

    loads[1].wait()

    @pl.loop(0, channels // WIDE)
    def _(n):
        columns = aligned(n * WIDE, WIDE)
        out = dot(mixture[...], wout[:, columns]) + xw[:, columns].astype(F32)
        out = out.astype(BF16)
        for w in range(windows):
            for s in range(4):
                at = w * places + s * quarter
                subs[s, w * quarter:(w + 1) * quarter, columns] = out[at:at + quarter]

    total = jnp.zeros((groups, 1), F32)
    for s in range(4):
        total += jnp.sum(subs[s].astype(F32), axis=1, keepdims=True)
    center = total / (4 * channels)
    total = jnp.zeros((groups, 1), F32)
    for s in range(4):
        moved = subs[s].astype(F32) - center
        total += jnp.sum(moved * moved, axis=1, keepdims=True)
    scale = lax.rsqrt(total / (4 * channels) + EPSILON)
    result = jnp.zeros((groups, wm.shape[1]), F32)
    for s in range(4):
        unit = ((subs[s].astype(F32) - center) * scale).astype(BF16)
        result += dot(unit, wm[s * channels:(s + 1) * channels])
    merged[...] = result.astype(BF16)

    mean_g = jnp.zeros((groups, 1), F32)
    mean_gx = jnp.zeros((groups, 1), F32)
    for s in range(4):
        d = dsubs[:, s * channels:(s + 1) * channels].astype(F32)
        mean_g += jnp.sum(d, axis=1, keepdims=True)
        mean_gx += jnp.sum(d * ((subs[s].astype(F32) - center) * scale), axis=1, keepdims=True)
    mean_g = mean_g / (4 * channels)
    mean_gx = mean_gx / (4 * channels)
    for s in range(4):
        unit = (subs[s].astype(F32) - center) * scale
        d = dsubs[:, s * channels:(s + 1) * channels].astype(F32)
        d = (scale * (d - mean_g - unit * mean_gx)).astype(BF16)
        for w in range(windows):
            at = w * places + s * quarter
            grad[at:at + quarter] = d[w * quarter:(w + 1) * quarter]
    stores[3].start()

    @pl.loop(0, channels // WIDE)
    def _(n):
        columns = aligned(n * WIDE, WIDE)
        d = dot(grad[...], wout[columns], NT).astype(BF16).astype(F32)
        d = d * inverse[:, columns]
        dmr[:, columns] = d.astype(BF16)
        dmm[:, columns] = (-d * mixture[:, columns].astype(F32)).astype(BF16)

    stores[4].start()
    stores[5].start()

    def turn(field, out):
        if block % 16:
            @pl.loop(0, channels // TILE)
            def _(n):
                rows = aligned(n * TILE, TILE)
                spot = lax.broadcasted_iota(jnp.int32, (TILE, channels), 1)
                pick = jnp.where(spot == rowmap[rows], 1.0, 0.0).astype(BF16)
                out[rows] = dot(pick, field[...], NT).astype(BF16)
        else:
            @pl.loop(0, channels // WIDE)
            def _(n):
                rows = aligned(n * WIDE, WIDE)
                turned[rows] = field[:, rows].T

            for d in range(devices):
                out[d * block:(d + 1) * block] = turned[aligned(owner[d] * block, block)]

    turned, normt, mixt = (wqkv.at[:, pl.ds(i * count, count)] for i in range(3))
    turn(normed, normt)
    stores[2].start()
    turn(mixture, mixt)
    part = channels // 2

    @pl.loop(0, channels // WIDE)
    def _(n):
        columns = aligned(n * WIDE, WIDE)
        terms = dot(mixt[...], grad[:, columns]).astype(BF16)
        out_mine[:, columns] = terms[:part]
        out_theirs[:, columns] = terms[part:]

    for store in stores:
        store.wait()


def backward_kernel(index, *refs):
    (edge, proj_h, dmr_h, dmm_h, normt_h, pgrad_h, mine_h, theirs_h,
     held, normt, pgrad, mine, theirs, in_sem, sem, out_sem) = refs
    _, count, width = held.shape
    channels = normt.shape[0]
    half = channels // 2
    places = 2 * WIN * WIN
    windows = count // places
    per_row = windows // 2
    masks = head_masks()
    factor = score_scale(channels)
    plain = (channels // HEADS) ** -0.5
    steps = width // TILE

    def loads(g):
        columns = aligned(g * TILE, TILE)
        for i in range(5):
            src = (proj_h, proj_h, proj_h, dmr_h, dmm_h)[i]
            start = (i * channels if i < 3 else 0) + index * width
            yield pltpu.make_async_copy(
                src.at[:, aligned(start + g * TILE, TILE)], held.at[i, :, columns], in_sem.at[g, i]
            )

    def stores(g):
        for i in range(3):
            columns = aligned(i * width + g * TILE, TILE)
            for j, (src, dst) in enumerate(((pgrad, pgrad_h), (mine, mine_h), (theirs, theirs_h))):
                yield pltpu.make_async_copy(src.at[:, columns], dst.at[:, columns], out_sem.at[g, i, j])

    for g in range(steps):
        for load in loads(g):
            load.start()
    turned_load = pltpu.make_async_copy(normt_h, normt, sem.at[0])
    turned_load.start()
    edge_bias = region_bias(places, edge[0] == 1)

    @pl.loop(0, steps)
    def _(g):
        for load in loads(g):
            load.wait()

        for part_of in range(TILE // LANES):
            lanes = aligned(g * TILE + part_of * LANES, LANES)
            for w in range(windows):
                rows = slice(w * places, (w + 1) * places)
                q, k, v, dm, dd = (held[i, rows, lanes] for i in range(5))
                keys = jnp.concatenate([k * m for m in masks], axis=0)
                scores = dot(keys, q, NT)
                values = jnp.concatenate(
                    [jnp.concatenate([v * m, m], axis=1) for m in masks], axis=0
                )
                slope = dot(values, jnp.concatenate([dm, dd], axis=1), NT)
                weights, slopes = [], []
                for h in range(4):
                    block = slice(h * places, (h + 1) * places)
                    part = scores[block] * factor
                    if w < per_row:
                        part = part + edge_bias
                    part = jnp.exp2(part - jnp.max(part, axis=0, keepdims=True))
                    weights.append(part.astype(BF16))
                    slopes.append((part * slope[block]).astype(BF16))
                dv = dot(
                    jnp.concatenate(weights, axis=1),
                    jnp.concatenate([dm * m for m in masks], axis=0),
                )
                dk = dot(
                    jnp.concatenate(slopes, axis=1),
                    jnp.concatenate([q * m for m in masks], axis=0),
                )
                dq = dot(jnp.concatenate(slopes, axis=0), keys, TN)
                at = g * TILE + part_of * LANES
                pgrad[rows, lanes] = (dq * plain).astype(BF16)
                pgrad[rows, aligned(width + at, LANES)] = (dk * plain).astype(BF16)
                pgrad[rows, aligned(2 * width + at, LANES)] = dv.astype(BF16)

        @pl.when(g == 0)
        def _():
            turned_load.wait()

        for i in range(3):
            columns = aligned(i * width + g * TILE, TILE)
            terms = dot(normt[...], pgrad[:, columns]).astype(BF16)
            mine[:, columns] = terms[:half]
            theirs[:, columns] = terms[half:]
        for store in stores(g):
            store.start()

    for g in range(steps):
        for store in stores(g):
            store.wait()


def projection_loads(pgrads, wqkv_h, pgrad, wqkv, sem, start):
    width = pgrads[0].shape[1] // 3
    channels = pgrad.shape[1] // 3
    loads = [
        pltpu.make_async_copy(
            field.at[:, pl.ds(i * width, width)],
            pgrad.at[:, pl.ds(i * channels + c * width, width)], sem.at[c * 3 + i],
        )
        for c, field in enumerate(pgrads) for i in range(3)
    ]
    tiles = [
        pltpu.make_async_copy(
            wqkv_h.at[pl.ds(start + n * TILE, TILE)], wqkv.at[pl.ds(n * TILE, TILE)],
            sem.at[3 * len(pgrads) + n],
        )
        for n in range(wqkv.shape[0] // TILE)
    ]
    for load in loads + tiles:
        load.start()
    return loads, tiles


def product_kernel(pg0, pg1, wqkv_h, ngrad, pgrad, wqkv, sem):
    channels = ngrad.shape[1]
    loads, tiles = projection_loads([pg0, pg1], wqkv_h, pgrad, wqkv, sem, 0)
    for load in loads + tiles:
        load.wait()

    @pl.loop(0, channels // BROAD)
    def _(n):
        rows = aligned(n * BROAD, BROAD)
        ngrad[:, rows] = dot(pgrad[...], wqkv[rows], NT).astype(BF16)


def input_kernel(
    ngrad, normed, rstd, grad, merged, pick_first, pick_last, pick_groups, full, side, below, corner,
):
    count, channels = ngrad.shape
    places = 2 * WIN * WIN

    @pl.loop(0, count // places)
    def _(w):
        rows = aligned(w * places, places)
        d = ngrad[rows].astype(F32)
        unit = normed[rows].astype(F32)
        mean_d = jnp.mean(d, axis=1, keepdims=True)
        mean_dx = jnp.mean(d * unit, axis=1, keepdims=True)
        part = rstd[rows, :1] * (d - mean_d - unit * mean_dx)
        full[rows] = (part.astype(BF16).astype(F32) + grad[rows].astype(F32)).astype(BF16)

    (n_side, g_side), (n_above, g_above), (n_corner, g_corner) = strip_rows(None, None)
    side_cut = 2 * SHIFT * SHIFT
    first = dot(pick_first[...], full[:count // 2]).astype(BF16)
    last = dot(pick_last[...], full[count // 2:]).astype(BF16)
    groups = dot(pick_groups[...], merged[...]).astype(BF16)
    side[:side_cut] = first[:side_cut]
    side[side_cut:n_side] = last
    below[:n_above] = first[side_cut:side_cut + n_above]
    corner[:n_corner] = first[side_cut + n_above:]
    side[n_side:] = groups[:g_side]
    below[n_above:] = groups[g_side:g_side + g_above]
    corner[n_corner:] = groups[g_side + g_above:]


def end_kernel(bit, kept1, kept2, *refs):
    arrived, (qkv, out) = refs[:-2], refs[-2:]
    channels = out.shape[1]
    columns = kept1.shape[1]
    first = kept1[...] + arrived[bit - 1][:, :columns].astype(F32)
    last = kept2[...]
    for i, block in enumerate(arrived):
        last += (block[:, columns:] if i == bit - 1 else block[...]).astype(F32)
    out[...] = first[:, :channels]
    width = channels // 2
    for i in range(3):
        at = i * channels
        qkv[:, at:at + width] = first[:, channels + i * width:channels + (i + 1) * width]
        qkv[:, at + width:at + channels] = last[:, i * width:(i + 1) * width]


def unpack_kernel(full, merged, side, below, corner, pick_top, pick_middle, pick_bottom,
                  pick_groups, tokens_out, merged_out):
    count = full.shape[0]
    half = count // 2
    (n_side, _), (n_above, _), (n_corner, _) = strip_rows(None, None)
    side_cut = 2 * SHIFT * SHIFT
    line = half // (2 * WIN)
    pieces = [
        (pick_top, [full[:half], side[:side_cut]]),
        (pick_middle, [full[half:], side[side_cut:n_side]]),
        (pick_bottom, [below[:n_above], corner[:n_corner]]),
    ]
    at = 0
    for pick, held in pieces:
        rows = pick.shape[0] // 2
        out = dot(pick[...], jnp.concatenate(held, axis=0)).astype(BF16)
        for level in range(2):
            start = level * half + at
            tokens_out[start:start + rows] = out[level * rows:(level + 1) * rows]
        at += rows
    held = [merged[...], side[n_side:], below[n_above:], corner[n_corner:]]
    merged_out[...] = dot(pick_groups[...], jnp.concatenate(held, axis=0)).astype(BF16)


def sent(block, sizes, lat_step, lon_step):
    n_lat, n_lon = sizes
    route = [
        (a * n_lon + b, (a + lat_step) % n_lat * n_lon + (b + lon_step) % n_lon)
        for a in range(n_lat) for b in range(n_lon)
    ]
    return lax.ppermute(block, ("lat", "lon"), route)


def sent_strips(strips, sizes, step):
    side, lines, corner = strips
    return [sent(side, sizes, 0, step), sent(lines, sizes, step, 0), sent(corner, sizes, step, step)]


def device_rows(channels, sizes):
    n_lat, n_lon = sizes
    devices = n_lat * n_lon
    rows = channels // devices
    place = np.arange(devices)
    lon = 2 * (place // n_lat % (n_lon // 2)) + place // (devices // 2)
    lat = place % n_lat
    owner = (
        jnp.bitwise_xor(lax.axis_index("lat").astype(jnp.int32), jnp.asarray(lat, jnp.int32)) * n_lon
        + jnp.bitwise_xor(lax.axis_index("lon").astype(jnp.int32), jnp.asarray(lon, jnp.int32))
    )
    rowmap = owner[:, None] * rows + jnp.arange(rows, dtype=jnp.int32)[None, :]
    return owner, rowmap.reshape(channels, 1)


def exchange(block, sizes, lat_bits, lon_bits):
    n_lat, n_lon = sizes
    route = [
        (a * n_lon + b, (a ^ lat_bits) * n_lon + (b ^ lon_bits))
        for a in range(n_lat) for b in range(n_lon)
    ]
    return lax.ppermute(block, ("lat", "lon"), route)


def core_step(theirs, sizes):
    return exchange(theirs, sizes, 0, 1)


def core_sum(mine, arrived):
    return (mine.astype(F32) + arrived.astype(F32)).astype(BF16)


class Layer:
    def __init__(self, total, sizes):
        self.sizes = sizes
        chips = sizes[1] // 2
        bits = [1 << i for i in range(chips.bit_length() - 1)]
        self.orders = [list(bits), bits[1:] + bits[:1]]
        self.bits = [bits[::-1], bits[::-1]]
        columns = total.shape[1] // 2
        rows = total.shape[0] // chips
        self.parts = [
            total[:, i * columns:(i + 1) * columns].reshape([2] * len(bits) + [rows, columns])
            for i in range(2)
        ]

    def give(self):
        self.kept, given = [], []
        for i, part in enumerate(self.parts):
            axis = self.bits[i].index(self.orders[i][0])
            self.kept.append(lax.index_in_dim(part, 0, axis, keepdims=False))
            given.append(lax.index_in_dim(part, 1, axis, keepdims=False))
        return given

    def send(self, given):
        arrived = []
        for i, block in enumerate(given):
            bit = self.orders[i].pop(0)
            self.bits[i] = [b for b in self.bits[i] if b != bit]
            arrived.append(exchange(block, self.sizes, 0, 2 * bit))
        return arrived

    def add(self, arrived):
        self.parts = [core_sum(k, a) for k, a in zip(self.kept, arrived)]

    def finish(self):
        while self.orders[0]:
            self.add(self.send(self.give()))
        return jnp.concatenate(self.parts, axis=-1).astype(F32)


def column_blocks(kept, arrived, sizes):
    total = kept
    for block in arrived:
        total = total + block.astype(F32)
    rows = total.shape[0] // sizes[0]
    blocks = [total[i * rows:(i + 1) * rows] for i in range(sizes[0])]
    return [blocks[0]] + [b.astype(BF16) for b in blocks[1:]]


def column_step(blocks, sizes):
    return [exchange(b, sizes, i, 0) for i, b in enumerate(blocks) if i]


def pinned(value):
    return pltpu.with_memory_space_constraint(value, pltpu.HBM)


def behind(values, marker):
    *values, _ = lax.optimization_barrier((*values, marker))
    return values


def column_halves(total, sizes, bit):
    blocks = sizes[0] // (2 * bit)
    pairs = total.reshape(blocks, 2, total.shape[0] // (2 * blocks), total.shape[1])
    kept, given = pairs[:, 0], pairs[:, 1]
    return [x.reshape(-1, total.shape[1]) for x in (kept, given.astype(BF16))]


def finished(kept, arrived):
    for block in arrived:
        kept = kept + block.astype(F32)
    return kept


def tied_call(kernel, after, operands, in_specs, out_shape, out_specs, **rest):
    waits = len(after)

    def body(*refs):
        kernel(*refs[waits:])

    return pl.pallas_call(
        body, out_shape=out_shape,
        in_specs=[pl.BlockSpec(memory_space=pl.ANY)] * waits + in_specs, out_specs=out_specs, **rest,
    )(*after, *operands)


def shards(sizes, tokens, qkv_weight, out_weight, merge_weight, merged_grad):
    levels, lat_rows, lon_cols, channels = tokens.shape
    merged_width = merge_weight.shape[1]
    count = levels * lat_rows * lon_cols
    groups = count // 4
    half = channels // 2
    strip_rows.extent = (lat_rows, lon_cols)
    vmem = pl.BlockSpec(memory_space=pltpu.VMEM)
    smem = pl.BlockSpec(memory_space=pltpu.SMEM)
    hbm = pl.BlockSpec(memory_space=pl.ANY)

    def shape(*extent, dtype=BF16):
        return jax.ShapeDtypeStruct(extent, dtype)

    def settings(weight, limit=60):
        return dict(
            compiler_params=pltpu.CompilerParams(vmem_limit_bytes=limit * MIB),
            cost_estimate=pl.CostEstimate(
                flops=int(weight * 1e10), bytes_accessed=16 * MIB, transcendentals=0
            ),
        )

    g_rows, g_cols = lat_rows // 2, lon_cols // 2
    cells = window_cells(levels, lat_rows, lon_cols)
    grps = window_groups(levels, g_rows, g_cols)
    cs = Strips(levels, lat_rows, lon_cols, SHIFT, True)
    gs = Strips(levels, g_rows, g_cols, HALF, False)
    g_strips = [padded(gs.side), padded(gs.above), padded(gs.corner)]
    to = ((0, lon_cols), (lat_rows, 0), (lat_rows, lon_cols))
    g_to = ((0, g_cols), (g_rows, 0), (g_rows, g_cols))
    own_rows = range(SHIFT, SHIFT + lat_rows)
    own_cols = range(SHIFT, SHIFT + lon_cols)
    own = box(levels, own_rows, own_cols)
    g_own = turned_box(levels, range(HALF, HALF + g_rows), range(HALF, HALF + g_cols))
    half_cells = count // 2
    side_cut = levels * SHIFT * SHIFT
    sent_cells = sum((Strips.sent(s, *t) for s, t in zip((cs.side, cs.above, cs.corner), to)), [])
    sent_groups = sum((Strips.sent(s, *t) for s, t in zip(g_strips, g_to)), [])
    held_top = box(levels, range(SHIFT, 2 * SHIFT), own_cols) + cs.side[:side_cut] + cs.above + cs.corner
    held_low = box(levels, range(2 * SHIFT, lat_rows), own_cols) + cs.side[side_cut:]
    depth = max(len(held_top), len(held_low))
    depth += -depth % 16
    held_top += [None] * (depth - len(held_top))
    held_low += [None] * (depth - len(held_low))

    tokens_flat = tokens.reshape(count, channels)
    merged_grad_flat = merged_grad.transpose(0, 2, 1, 3).reshape(groups, merged_width)
    extents = [(n + g, channels) for n, g in strip_rows(None, None)]
    packed = pl.pallas_call(
        pack_kernel,
        out_shape=[shape(*e) for e in extents],
        in_specs=[vmem] * 4, out_specs=[vmem] * 3,
        name="pack_strips", **settings(1),
    )(pinned(tokens_flat), pinned(merged_grad_flat), picks(sent_cells, own), picks(sent_groups, g_own))
    strips = sent_strips(packed, sizes, 1)

    order = jnp.concatenate([picks(cells[:half_cells], held_top), picks(cells[half_cells:], held_low)])
    group = picks(grps, g_own + sum(g_strips, []))
    edge = (lax.axis_index("lat") == 0).astype(jnp.int32).reshape(1)
    owner, rowmap = device_rows(channels, sizes)
    if channels // (sizes[0] * sizes[1]) % 16 == 0:
        rowmap = jnp.zeros((8, 1), jnp.int32)

    wide = shape(count, channels)
    inner = 2 * 2 * WIN * WIN
    ready = tied_call(
        inner_kernel, packed,
        [pinned(tokens_flat), order[count - inner:], pinned(qkv_weight)],
        [vmem] * 2 + [hbm],
        [shape(inner, channels), shape(inner, channels), shape(inner, LANES, dtype=F32),
         shape(inner, channels), shape(inner, channels, dtype=F32), shape(inner, 3 * channels)],
        [vmem] * 6,
        scratch_shapes=[
            pltpu.VMEM(qkv_weight.shape, BF16),
            pltpu.SemaphoreType.DMA((3 * channels // TILE,)),
        ],
        name="inner_windows", **settings(9),
    )
    normed, normt, proj, dmr, dmm, grad, rstd, merged, out_mine, out_theirs = pl.pallas_call(
        forward_kernel,
        out_shape=[
            wide, shape(channels, count), shape(count, 3 * channels), wide, wide, wide,
            shape(count, LANES, dtype=F32), shape(groups, merged_width),
            shape(half, channels), shape(half, channels),
        ],
        in_specs=[smem] * 2 + [vmem] * 8 + [hbm] * 9,
        out_specs=[hbm] * 6 + [vmem] * 4,
        scratch_shapes=[
            pltpu.VMEM(qkv_weight.shape, BF16),
            pltpu.VMEM(out_weight.shape, BF16),
            pltpu.VMEM(merge_weight.shape, BF16),
            pltpu.VMEM((2, depth, channels), BF16),
            pltpu.VMEM((count, channels), BF16),
            pltpu.VMEM((count, channels), BF16),
            pltpu.VMEM((count, 3 * channels), BF16),
            pltpu.VMEM((count, channels), BF16),
            pltpu.VMEM((count, channels), F32),
            pltpu.VMEM((4, groups, channels), BF16),
            pltpu.VMEM((groups, 4 * channels), BF16),
            pltpu.VMEM((groups, merged_width), BF16),
            pltpu.VMEM((count, channels), BF16),
            pltpu.VMEM((count, channels), BF16),
            pltpu.VMEM((count, channels), BF16),
            pltpu.SemaphoreType.DMA((9,)),
            pltpu.SemaphoreType.DMA((6,)),
        ],
        name="block_forward", **settings(30, 55),
    )(edge, owner, tokens_flat, merged_grad_flat, *strips, order, group, rowmap,
      qkv_weight, out_weight, merge_weight, *ready)

    halves = 2
    width = channels // halves
    steps = width // TILE

    def backward(index, after):
        return tied_call(
            functools.partial(backward_kernel, index), after,
            [edge, pinned(proj), pinned(dmr), pinned(dmm), pinned(normt)], [smem] + [hbm] * 4,
            [shape(count, 3 * width), shape(half, 3 * width), shape(half, 3 * width)], [hbm] * 3,
            scratch_shapes=[
                pltpu.VMEM((5, count, width), BF16),
                pltpu.VMEM((channels, count), BF16),
                pltpu.VMEM((count, 3 * width), BF16),
                pltpu.VMEM((half, 3 * width), BF16),
                pltpu.VMEM((half, 3 * width), BF16),
                pltpu.SemaphoreType.DMA((steps, 5)),
                pltpu.SemaphoreType.DMA((1,)),
                pltpu.SemaphoreType.DMA((steps, 3, 3)),
            ],
            name="attention_backward", **settings(15, 32),
        )

    arrived = core_step(out_theirs, sizes)
    pg0, mine1, theirs1 = backward(0, [])
    out_mine, arrived = behind([out_mine, arrived], pg0)
    theirs1, = behind([theirs1], arrived)
    total = core_sum(out_mine, arrived)
    total1 = core_sum(mine1, core_step(theirs1, sizes))
    layer1 = Layer(jnp.concatenate([total, total1], axis=1), sizes)
    given = layer1.give()
    arrived1 = layer1.send(given)
    pg1, mine2, theirs2 = backward(1, given)
    arrived1 = behind(arrived1, pg1)
    theirs2, = behind([theirs2], arrived1)
    arrived = core_step(theirs2, sizes)
    layer1.add(arrived1)
    given1 = layer1.give()
    arrived1 = layer1.send(given1)
    layer2 = Layer(core_sum(mine2, arrived), sizes)
    given2 = layer2.give()
    arrived2 = layer2.send(given2)

    first_picks = picks(cs.side[:side_cut] + cs.above + cs.corner, cells[:half_cells])
    last_picks = picks(cs.side[side_cut:], cells[half_cells:])
    [ngrad] = tied_call(
        product_kernel, given1 + given2,
        [pg0, pg1, qkv_weight], [hbm] * 3, [wide], [vmem],
        scratch_shapes=[
            pltpu.VMEM((count, 3 * channels), BF16),
            pltpu.VMEM(qkv_weight.shape, BF16),
            pltpu.SemaphoreType.DMA((3 * halves + channels // TILE,)),
        ],
        name="input_product", **settings(8, 36),
    )
    arrived1 = behind(arrived1, ngrad)
    layer1.add(arrived1)
    total1 = layer1.finish()
    kept1, given1 = column_halves(total1, sizes, 1)
    got1 = exchange(given1, sizes, 1, 0)
    full, *strips = tied_call(
        input_kernel, [given1],
        [ngrad, normed, rstd, grad, merged,
         first_picks, last_picks, picks(sum(g_strips, []), grps)],
        [vmem] * 8, [wide] + [shape(*e) for e in extents], [vmem] * 4,
        name="input_backward", **settings(5, 30),
    )
    got1, *arrived2 = behind([got1] + arrived2, full)
    strips = sent_strips(behind(strips, (got1, arrived2)), sizes, -1)
    layer2.add(arrived2)
    total2 = layer2.finish()

    part1 = kept1 + got1.astype(F32)
    column2 = column_blocks(total2, [], sizes)
    bit = 2
    while 2 * bit < sizes[0]:
        kept1, given1 = column_halves(part1, sizes, bit)
        part1 = kept1 + exchange(given1, sizes, bit, 0).astype(F32)
        bit *= 2
    kept1, last1 = column_halves(part1, sizes, bit)
    column2[bit] = jnp.concatenate([last1, column2[bit]], axis=1)
    got2 = column_step(column2, sizes)

    got = [Strips.sent(s, *t) for s, t in zip((cs.side, cs.above, cs.corner), to)]
    g_got = sum((Strips.sent(s, *t) for s, t in zip(g_strips, g_to)), [])
    tokens_grad, merged = tied_call(
        unpack_kernel, column2[1:] + [given1],
        [
            full, merged, *strips,
            picks(box(levels, range(SHIFT, 2 * SHIFT), own_cols), cells[:half_cells] + got[0][:side_cut]),
            picks(box(levels, range(2 * SHIFT, lat_rows), own_cols), cells[half_cells:] + got[0][side_cut:]),
            picks(box(levels, range(lat_rows, lat_rows + SHIFT), own_cols), got[1] + got[2]),
            picks(g_own, grps + g_got),
        ],
        [vmem] * 9, [wide, shape(groups, merged_width)], [vmem] * 2,
        name="unpack_strips", **settings(20, 24),
    )
    got2 = behind(got2, tokens_grad)
    qkv_weight_grad, out_weight_grad = pl.pallas_call(
        functools.partial(end_kernel, bit),
        out_shape=[
            shape(kept1.shape[0], 3 * channels, dtype=F32), shape(kept1.shape[0], channels, dtype=F32),
        ],
        in_specs=[vmem] * (2 + len(got2)), out_specs=[vmem] * 2,
        name="end_sums", **settings(1, 16),
    )(kept1, column2[0], *got2)
    merged = merged.reshape(levels, g_cols, g_rows, merged_width).transpose(0, 2, 1, 3)
    return merged, tokens_grad.reshape(tokens.shape), qkv_weight_grad, out_weight_grad


def solution(mesh):
    sizes = (mesh.shape["lat"], mesh.shape["lon"])
    in_specs = (P(None, "lat", "lon", None), P(), P(), P(), P(None, "lat", "lon", None))
    out_specs = (
        P(None, "lat", "lon", None),
        P(None, "lat", "lon", None),
        P(("lat", "lon"), None),
        P(("lat", "lon"), None),
    )
    return jax.shard_map(
        functools.partial(shards, sizes),
        mesh=mesh, in_specs=in_specs, out_specs=out_specs, check_vma=False,
    )
```

```python
import functools

import jax
import jax.numpy as jnp
import numpy as np
from jax import lax
from jax.experimental import pallas as pl
from jax.experimental.pallas import tpu as pltpu
from jax.sharding import PartitionSpec as P

HEADS = 32
WIN = 8
SHIFT = 4
LANES = 128
HALF = SHIFT // 2
TILE = 256
WIDE = 512
BROAD = 1024
EPSILON = 1e-05
MIB = 1 << 20

NN = (((1,), (0,)), ((), ()))
NT = (((1,), (1,)), ((), ()))
TN = (((0,), (0,)), ((), ()))
BF16 = jnp.bfloat16
F32 = jnp.float32


def dot(a, b, dims=NN):
    return lax.dot_general(a, b, dims, preferred_element_type=F32)


def window_cells(levels, rows, columns):
    half = WIN // 2
    return [
        (level, wi * WIN + 2 * row + sub % 2, wj * WIN + 2 * column + sub // 2)
        for wi in range(rows // WIN) for wj in range(columns // WIN) for sub in range(4)
        for level in range(levels) for row in range(half) for column in range(half)
    ]


def window_groups(levels, rows, columns):
    half = WIN // 2
    return [
        (level, wi * half + row, wj * half + column)
        for wi in range(rows // half) for wj in range(columns // half)
        for level in range(levels) for row in range(half) for column in range(half)
    ]


def box(levels, rows, columns):
    return [(l, r, c) for l in range(levels) for r in rows for c in columns]


def turned_box(levels, rows, columns):
    return [(l, r, c) for l in range(levels) for c in columns for r in rows]


def padded(cells, step=16):
    return cells + [None] * (-len(cells) % step)


def picks(wanted, held):
    spot = {cell: i for i, cell in enumerate(held) if cell is not None}
    table = np.zeros((len(wanted), len(held)), np.float32)
    for i, cell in enumerate(wanted):
        if cell is not None:
            table[i, spot[cell]] = 1.0
    return jnp.asarray(table, BF16)


class Strips:
    def __init__(self, levels, rows, columns, width, cut):
        self.side = (box(levels, range(width, 2 * width), range(width))
                     + box(levels, range(2 * width, rows), range(width)))
        self.above = box(levels, range(width), range(width, columns))
        self.corner = box(levels, range(width), range(width))
        if not cut:
            self.side = box(levels, range(width, rows), range(width))

    @staticmethod
    def sent(cells, down, across):
        return [None if c is None else (c[0], c[1] + down, c[2] + across) for c in cells]


def head_masks():
    head = lax.broadcasted_iota(jnp.int32, (LANES, LANES), 1) // (LANES // 4)
    return [jnp.where(head == h, 1.0, 0.0).astype(BF16) for h in range(4)]


def region_bias(places, active):
    step = 2 * (WIN // 2)
    one = (lax.broadcasted_iota(jnp.int32, (places, places), 0) // step) % 2
    other = (lax.broadcasted_iota(jnp.int32, (places, places), 1) // step) % 2
    return jnp.where((one != other) & active, -1e30, 0.0)


def score_scale(channels):
    return float((channels // HEADS) ** -0.5 * np.log2(np.e))


def aligned(start, size, step=None):
    return pl.ds(pl.multiple_of(start, step or size), size)


def pack_kernel(tokens, merged_grad, pick_cells, pick_groups, side, above, corner):
    cells = dot(pick_cells[...], tokens[...]).astype(BF16)
    groups = dot(pick_groups[...], merged_grad[...]).astype(BF16)
    at, at_group = 0, 0
    for out, (count, extra) in zip((side, above, corner), strip_rows(pick_cells, pick_groups)):
        out[:count] = cells[at:at + count]
        out[count:] = groups[at_group:at_group + extra]
        at, at_group = at + count, at_group + extra


def strip_rows(pick_cells, pick_groups):
    levels = 2
    rows, columns = strip_rows.extent
    cells = [levels * (rows - SHIFT) * SHIFT, levels * SHIFT * (columns - SHIFT), levels * SHIFT * SHIFT]
    groups = [n // 4 + (-(n // 4)) % 16 for n in cells]
    return list(zip(cells, groups))


def normalized_window(x, rows, xw, normed, rstd):
    xw[rows] = x.astype(BF16)
    center = jnp.mean(x, axis=1, keepdims=True)
    moved = x - center
    scale = lax.rsqrt(jnp.mean(moved * moved, axis=1, keepdims=True) + EPSILON)
    rstd[rows] = jnp.broadcast_to(scale, (x.shape[0], LANES))
    normed[rows] = (moved * scale).astype(BF16)


def attended(proj, rows, lanes, masks, factor, bias, mixture, inverse):
    places = masks[0].shape[0]
    q, k, v = (proj[rows, at] for at in lanes)
    scores = dot(q, jnp.concatenate([k * m for m in masks], axis=0), NT)
    parts = []
    for h in range(4):
        part = scores[:, h * places:(h + 1) * places] * factor
        if bias is not None:
            part = part + bias
        part = part - jnp.max(part, axis=1, keepdims=True)
        parts.append(jnp.exp2(part).astype(BF16))
    values = jnp.concatenate([jnp.concatenate([v * m, m], axis=1) for m in masks], axis=0)
    summed = dot(jnp.concatenate(parts, axis=1), values)
    inv = 1.0 / summed[:, LANES:]
    inverse[rows, lanes[0]] = inv
    mixture[rows, lanes[0]] = (summed[:, :LANES] * inv).astype(BF16)


def inner_kernel(
    tokens, order, wqkv_h, xw, normed, rstd, mixture, inverse, proj, wqkv, in_sem,
):
    count, channels = xw.shape
    places = 2 * WIN * WIN
    tiles = wqkv.shape[1] // BROAD

    def load(n):
        columns = aligned(n * BROAD, BROAD)
        return pltpu.make_async_copy(wqkv_h.at[:, columns], wqkv.at[:, columns], in_sem.at[n])

    for n in range(tiles):
        load(n).start()
    half = tokens.shape[0] // 2
    line = half // (2 * WIN)
    cut = SHIFT * line
    source = jnp.concatenate(
        [tokens[cut:cut + WIN * line], tokens[half + cut:half + cut + WIN * line]], axis=0
    )
    x = dot(order[:, :source.shape[0]], source)
    for w in range(count // places):
        rows = slice(w * places, (w + 1) * places)
        normalized_window(x[rows], rows, xw, normed, rstd)

    @pl.loop(0, tiles)
    def _(n):
        load(n).wait()
        columns = aligned(n * BROAD, BROAD)
        proj[:, columns] = dot(normed[...], wqkv[:, columns]).astype(BF16)

    masks = head_masks()
    factor = score_scale(channels)

    @pl.loop(0, channels // LANES // 2)
    def _(g):
        for i in range(2):
            lanes = [aligned(j * channels + (2 * g + i) * LANES, LANES) for j in range(3)]
            for w in range(count // places):
                rows = slice(w * places, (w + 1) * places)
                attended(proj, rows, lanes, masks, factor, None, mixture, inverse)


def forward_kernel(
    edge, owner, tokens, merged_grad, side, above, corner, order, group, rowmap,
    wqkv_h, wout_h, wm_h, xw_h, normed_in, rstd_h, mixture_h, inverse_h, proj_in,
    normed_h, normt_h, proj_h, dmr_h, dmm_h, grad_h, rstd, merged, out_mine, out_theirs,
    wqkv, wout, wm, source, xw, normed, proj, mixture, inverse, subs, dsubs, cotangent,
    grad, dmr, dmm, in_sem, out_sem,
):
    count, channels = xw.shape
    places = 2 * WIN * WIN
    windows = count // places
    per_row = windows // 2
    quarter = places // 4
    groups = count // 4
    devices = owner.shape[0]
    block = channels // devices

    loads = [
        pltpu.make_async_copy(src, dst, in_sem.at[i])
        for i, (src, dst) in enumerate([(wqkv_h, wqkv), (wout_h, wout), (wm_h, wm)])
    ]
    outer = count - xw_h.shape[0]
    ready = [
        pltpu.make_async_copy(src, dst.at[pl.ds(outer, count - outer)], in_sem.at[3 + i])
        for i, (src, dst) in enumerate(
            [(xw_h, xw), (normed_in, normed), (rstd_h, rstd), (mixture_h, mixture),
             (inverse_h, inverse), (proj_in, proj)]
        )
    ]
    for load in loads + ready:
        load.start()
    stores = [
        pltpu.make_async_copy(src, dst, out_sem.at[i])
        for i, (src, dst) in enumerate(
            [(normed, normed_h), (proj, proj_h), (wqkv.at[:, pl.ds(count, count)], normt_h),
             (grad, grad_h), (dmr, dmr_h), (dmm, dmm_h)]
        )
    ]

    (n_side, g_side), (n_above, g_above), (n_corner, g_corner) = strip_rows(None, None)
    half = count // 2
    line = half // (2 * WIN)
    cut = SHIFT * line
    side_cut = 2 * SHIFT * SHIFT
    blocks = [
        [tokens[:cut], tokens[half:half + cut], side[:side_cut], above[:n_above], corner[:n_corner]],
        [tokens[cut:cut + WIN * line], tokens[half + cut:half + cut + WIN * line], side[side_cut:n_side]],
    ]
    for wi in range(2):
        at = 0
        for piece in blocks[wi]:
            source[wi, at:at + piece.shape[0]] = piece
            at += piece.shape[0]
        if at < source.shape[1]:
            source[wi, at:] = jnp.zeros((source.shape[1] - at, channels), BF16)

    for wi in range(2):
        first, last = wi * per_row, min((wi + 1) * per_row, outer // places)
        x = dot(order[first * places:last * places], source[wi])
        for w in range(first, last):
            rows = slice(w * places, (w + 1) * places)
            normalized_window(x[(w - first) * places:(w - first + 1) * places], rows, xw, normed, rstd)

    loads[0].wait()
    outer_rows = slice(0, outer)

    @pl.loop(0, wqkv.shape[1] // BROAD)
    def _(n):
        columns = aligned(n * BROAD, BROAD)
        proj[outer_rows, columns] = dot(normed[outer_rows], wqkv[:, columns]).astype(BF16)

    for load in ready:
        load.wait()
    stores[0].start()
    stores[1].start()

    masks = head_masks()
    factor = score_scale(channels)

    edge_bias = region_bias(places, edge[0] == 1)
    held = jnp.concatenate(
        [merged_grad[...], side[n_side:], above[n_above:], corner[n_corner:]], axis=0
    )
    cotangent[...] = dot(group[...], held).astype(BF16)
    loads[2].wait()
    steps = channels // LANES
    per_step = 4 * channels // TILE // steps

    @pl.loop(0, steps)
    def _(g):
        lanes = [aligned(i * channels + g * LANES, LANES) for i in range(3)]
        for w in range(outer // places):
            rows = slice(w * places, (w + 1) * places)
            bias = edge_bias if w < per_row else None
            attended(proj, rows, lanes, masks, factor, bias, mixture, inverse)
        for i in range(per_step):
            at = aligned((g * per_step + i) * TILE, TILE)
            dsubs[:, at] = dot(cotangent[...], wm[at], NT).astype(BF16)

    loads[1].wait()

    @pl.loop(0, channels // WIDE)
    def _(n):
        columns = aligned(n * WIDE, WIDE)
        out = dot(mixture[...], wout[:, columns]) + xw[:, columns].astype(F32)
        out = out.astype(BF16)
        for w in range(windows):
            for s in range(4):
                at = w * places + s * quarter
                subs[s, w * quarter:(w + 1) * quarter, columns] = out[at:at + quarter]

    total = jnp.zeros((groups, 1), F32)
    for s in range(4):
        total += jnp.sum(subs[s].astype(F32), axis=1, keepdims=True)
    center = total / (4 * channels)
    total = jnp.zeros((groups, 1), F32)
    for s in range(4):
        moved = subs[s].astype(F32) - center
        total += jnp.sum(moved * moved, axis=1, keepdims=True)
    scale = lax.rsqrt(total / (4 * channels) + EPSILON)
    result = jnp.zeros((groups, wm.shape[1]), F32)
    for s in range(4):
        unit = ((subs[s].astype(F32) - center) * scale).astype(BF16)
        result += dot(unit, wm[s * channels:(s + 1) * channels])
    merged[...] = result.astype(BF16)

    mean_g = jnp.zeros((groups, 1), F32)
    mean_gx = jnp.zeros((groups, 1), F32)
    for s in range(4):
        d = dsubs[:, s * channels:(s + 1) * channels].astype(F32)
        mean_g += jnp.sum(d, axis=1, keepdims=True)
        mean_gx += jnp.sum(d * ((subs[s].astype(F32) - center) * scale), axis=1, keepdims=True)
    mean_g = mean_g / (4 * channels)
    mean_gx = mean_gx / (4 * channels)
    for s in range(4):
        unit = (subs[s].astype(F32) - center) * scale
        d = dsubs[:, s * channels:(s + 1) * channels].astype(F32)
        d = (scale * (d - mean_g - unit * mean_gx)).astype(BF16)
        for w in range(windows):
            at = w * places + s * quarter
            grad[at:at + quarter] = d[w * quarter:(w + 1) * quarter]
    stores[3].start()

    @pl.loop(0, channels // WIDE)
    def _(n):
        columns = aligned(n * WIDE, WIDE)
        d = dot(grad[...], wout[columns], NT).astype(BF16).astype(F32)
        d = d * inverse[:, columns]
        dmr[:, columns] = d.astype(BF16)
        dmm[:, columns] = (-d * mixture[:, columns].astype(F32)).astype(BF16)

    stores[4].start()
    stores[5].start()

    def turn(field, out):
        if block % 16:
            @pl.loop(0, channels // TILE)
            def _(n):
                rows = aligned(n * TILE, TILE)
                spot = lax.broadcasted_iota(jnp.int32, (TILE, channels), 1)
                pick = jnp.where(spot == rowmap[rows], 1.0, 0.0).astype(BF16)
                out[rows] = dot(pick, field[...], NT).astype(BF16)
        else:
            @pl.loop(0, channels // WIDE)
            def _(n):
                rows = aligned(n * WIDE, WIDE)
                turned[rows] = field[:, rows].T

            for d in range(devices):
                out[d * block:(d + 1) * block] = turned[aligned(owner[d] * block, block)]

    turned, normt, mixt = (wqkv.at[:, pl.ds(i * count, count)] for i in range(3))
    turn(normed, normt)
    stores[2].start()
    turn(mixture, mixt)
    part = channels // 2

    @pl.loop(0, channels // WIDE)
    def _(n):
        columns = aligned(n * WIDE, WIDE)
        terms = dot(mixt[...], grad[:, columns]).astype(BF16)
        out_mine[:, columns] = terms[:part]
        out_theirs[:, columns] = terms[part:]

    for store in stores:
        store.wait()


def backward_kernel(index, *refs):
    (edge, proj_h, dmr_h, dmm_h, normt_h, pgrad_h, mine_h, theirs_h,
     held, normt, pgrad, mine, theirs, in_sem, sem, out_sem) = refs
    _, count, width = held.shape
    channels = normt.shape[0]
    half = channels // 2
    places = 2 * WIN * WIN
    windows = count // places
    per_row = windows // 2
    masks = head_masks()
    factor = score_scale(channels)
    plain = (channels // HEADS) ** -0.5
    steps = width // TILE

    def loads(g):
        columns = aligned(g * TILE, TILE)
        for i in range(5):
            src = (proj_h, proj_h, proj_h, dmr_h, dmm_h)[i]
            start = (i * channels if i < 3 else 0) + index * width
            yield pltpu.make_async_copy(
                src.at[:, aligned(start + g * TILE, TILE)], held.at[i, :, columns], in_sem.at[g, i]
            )

    def stores(g):
        for i in range(3):
            columns = aligned(i * width + g * TILE, TILE)
            for j, (src, dst) in enumerate(((pgrad, pgrad_h), (mine, mine_h), (theirs, theirs_h))):
                yield pltpu.make_async_copy(src.at[:, columns], dst.at[:, columns], out_sem.at[g, i, j])

    for g in range(steps):
        for load in loads(g):
            load.start()
    turned_load = pltpu.make_async_copy(normt_h, normt, sem.at[0])
    turned_load.start()
    edge_bias = region_bias(places, edge[0] == 1)

    @pl.loop(0, steps)
    def _(g):
        for load in loads(g):
            load.wait()

        for part_of in range(TILE // LANES):
            lanes = aligned(g * TILE + part_of * LANES, LANES)
            for w in range(windows):
                rows = slice(w * places, (w + 1) * places)
                q, k, v, dm, dd = (held[i, rows, lanes] for i in range(5))
                keys = jnp.concatenate([k * m for m in masks], axis=0)
                scores = dot(keys, q, NT)
                values = jnp.concatenate(
                    [jnp.concatenate([v * m, m], axis=1) for m in masks], axis=0
                )
                slope = dot(values, jnp.concatenate([dm, dd], axis=1), NT)
                weights, slopes = [], []
                for h in range(4):
                    block = slice(h * places, (h + 1) * places)
                    part = scores[block] * factor
                    if w < per_row:
                        part = part + edge_bias
                    part = jnp.exp2(part - jnp.max(part, axis=0, keepdims=True))
                    weights.append(part.astype(BF16))
                    slopes.append((part * slope[block]).astype(BF16))
                dv = dot(
                    jnp.concatenate(weights, axis=1),
                    jnp.concatenate([dm * m for m in masks], axis=0),
                )
                dk = dot(
                    jnp.concatenate(slopes, axis=1),
                    jnp.concatenate([q * m for m in masks], axis=0),
                )
                dq = dot(jnp.concatenate(slopes, axis=0), keys, TN)
                at = g * TILE + part_of * LANES
                pgrad[rows, lanes] = (dq * plain).astype(BF16)
                pgrad[rows, aligned(width + at, LANES)] = (dk * plain).astype(BF16)
                pgrad[rows, aligned(2 * width + at, LANES)] = dv.astype(BF16)

        @pl.when(g == 0)
        def _():
            turned_load.wait()

        for i in range(3):
            columns = aligned(i * width + g * TILE, TILE)
            terms = dot(normt[...], pgrad[:, columns]).astype(BF16)
            mine[:, columns] = terms[:half]
            theirs[:, columns] = terms[half:]
        for store in stores(g):
            store.start()

    for g in range(steps):
        for store in stores(g):
            store.wait()


def projection_loads(pgrads, wqkv_h, pgrad, wqkv, sem, start):
    width = pgrads[0].shape[1] // 3
    channels = pgrad.shape[1] // 3
    loads = [
        pltpu.make_async_copy(
            field.at[:, pl.ds(i * width, width)],
            pgrad.at[:, pl.ds(i * channels + c * width, width)], sem.at[c * 3 + i],
        )
        for c, field in enumerate(pgrads) for i in range(3)
    ]
    tiles = [
        pltpu.make_async_copy(
            wqkv_h.at[pl.ds(start + n * TILE, TILE)], wqkv.at[pl.ds(n * TILE, TILE)],
            sem.at[3 * len(pgrads) + n],
        )
        for n in range(wqkv.shape[0] // TILE)
    ]
    for load in loads + tiles:
        load.start()
    return loads, tiles


def product_kernel(pg0, pg1, wqkv_h, ngrad, pgrad, wqkv, sem):
    channels = ngrad.shape[1]
    loads, tiles = projection_loads([pg0, pg1], wqkv_h, pgrad, wqkv, sem, 0)
    for load in loads + tiles:
        load.wait()

    @pl.loop(0, channels // BROAD)
    def _(n):
        rows = aligned(n * BROAD, BROAD)
        ngrad[:, rows] = dot(pgrad[...], wqkv[rows], NT).astype(BF16)


def input_kernel(
    ngrad, normed, rstd, grad, merged, pick_first, pick_last, pick_groups, full, side, below, corner,
):
    count, channels = ngrad.shape
    places = 2 * WIN * WIN

    @pl.loop(0, count // places)
    def _(w):
        rows = aligned(w * places, places)
        d = ngrad[rows].astype(F32)
        unit = normed[rows].astype(F32)
        mean_d = jnp.mean(d, axis=1, keepdims=True)
        mean_dx = jnp.mean(d * unit, axis=1, keepdims=True)
        part = rstd[rows, :1] * (d - mean_d - unit * mean_dx)
        full[rows] = (part.astype(BF16).astype(F32) + grad[rows].astype(F32)).astype(BF16)

    (n_side, g_side), (n_above, g_above), (n_corner, g_corner) = strip_rows(None, None)
    side_cut = 2 * SHIFT * SHIFT
    first = dot(pick_first[...], full[:count // 2]).astype(BF16)
    last = dot(pick_last[...], full[count // 2:]).astype(BF16)
    groups = dot(pick_groups[...], merged[...]).astype(BF16)
    side[:side_cut] = first[:side_cut]
    side[side_cut:n_side] = last
    below[:n_above] = first[side_cut:side_cut + n_above]
    corner[:n_corner] = first[side_cut + n_above:]
    side[n_side:] = groups[:g_side]
    below[n_above:] = groups[g_side:g_side + g_above]
    corner[n_corner:] = groups[g_side + g_above:]


def end_kernel(bit, kept1, kept2, *refs):
    arrived, (qkv, out) = refs[:-2], refs[-2:]
    channels = out.shape[1]
    columns = kept1.shape[1]
    first = kept1[...] + arrived[bit - 1][:, :columns].astype(F32)
    last = kept2[...]
    for i, block in enumerate(arrived):
        last += (block[:, columns:] if i == bit - 1 else block[...]).astype(F32)
    out[...] = first[:, :channels]
    width = channels // 2
    for i in range(3):
        at = i * channels
        qkv[:, at:at + width] = first[:, channels + i * width:channels + (i + 1) * width]
        qkv[:, at + width:at + channels] = last[:, i * width:(i + 1) * width]


def unpack_kernel(full, merged, side, below, corner, pick_top, pick_middle, pick_bottom,
                  pick_groups, tokens_out, merged_out):
    count = full.shape[0]
    half = count // 2
    (n_side, _), (n_above, _), (n_corner, _) = strip_rows(None, None)
    side_cut = 2 * SHIFT * SHIFT
    line = half // (2 * WIN)
    pieces = [
        (pick_top, [full[:half], side[:side_cut]]),
        (pick_middle, [full[half:], side[side_cut:n_side]]),
        (pick_bottom, [below[:n_above], corner[:n_corner]]),
    ]
    at = 0
    for pick, held in pieces:
        rows = pick.shape[0] // 2
        out = dot(pick[...], jnp.concatenate(held, axis=0)).astype(BF16)
        for level in range(2):
            start = level * half + at
            tokens_out[start:start + rows] = out[level * rows:(level + 1) * rows]
        at += rows
    held = [merged[...], side[n_side:], below[n_above:], corner[n_corner:]]
    merged_out[...] = dot(pick_groups[...], jnp.concatenate(held, axis=0)).astype(BF16)


def sent(block, sizes, lat_step, lon_step):
    n_lat, n_lon = sizes
    route = [
        (a * n_lon + b, (a + lat_step) % n_lat * n_lon + (b + lon_step) % n_lon)
        for a in range(n_lat) for b in range(n_lon)
    ]
    return lax.ppermute(block, ("lat", "lon"), route)


def sent_strips(strips, sizes, step):
    side, lines, corner = strips
    return [sent(side, sizes, 0, step), sent(lines, sizes, step, 0), sent(corner, sizes, step, step)]


def device_rows(channels, sizes):
    n_lat, n_lon = sizes
    devices = n_lat * n_lon
    rows = channels // devices
    place = np.arange(devices)
    lon = 2 * (place // n_lat % (n_lon // 2)) + place // (devices // 2)
    lat = place % n_lat
    owner = (
        jnp.bitwise_xor(lax.axis_index("lat").astype(jnp.int32), jnp.asarray(lat, jnp.int32)) * n_lon
        + jnp.bitwise_xor(lax.axis_index("lon").astype(jnp.int32), jnp.asarray(lon, jnp.int32))
    )
    rowmap = owner[:, None] * rows + jnp.arange(rows, dtype=jnp.int32)[None, :]
    return owner, rowmap.reshape(channels, 1)


def exchange(block, sizes, lat_bits, lon_bits):
    n_lat, n_lon = sizes
    route = [
        (a * n_lon + b, (a ^ lat_bits) * n_lon + (b ^ lon_bits))
        for a in range(n_lat) for b in range(n_lon)
    ]
    return lax.ppermute(block, ("lat", "lon"), route)


def core_step(theirs, sizes):
    return exchange(theirs, sizes, 0, 1)


def core_sum(mine, arrived):
    return (mine.astype(F32) + arrived.astype(F32)).astype(BF16)


class Layer:
    def __init__(self, total, sizes):
        self.sizes = sizes
        chips = sizes[1] // 2
        bits = [1 << i for i in range(chips.bit_length() - 1)]
        self.orders = [list(bits), bits[1:] + bits[:1]]
        self.bits = [bits[::-1], bits[::-1]]
        columns = total.shape[1] // 2
        rows = total.shape[0] // chips
        self.parts = [
            total[:, i * columns:(i + 1) * columns].reshape([2] * len(bits) + [rows, columns])
            for i in range(2)
        ]

    def give(self):
        self.kept, given = [], []
        for i, part in enumerate(self.parts):
            axis = self.bits[i].index(self.orders[i][0])
            self.kept.append(lax.index_in_dim(part, 0, axis, keepdims=False))
            given.append(lax.index_in_dim(part, 1, axis, keepdims=False))
        return given

    def send(self, given):
        arrived = []
        for i, block in enumerate(given):
            bit = self.orders[i].pop(0)
            self.bits[i] = [b for b in self.bits[i] if b != bit]
            arrived.append(exchange(block, self.sizes, 0, 2 * bit))
        return arrived

    def add(self, arrived):
        self.parts = [core_sum(k, a) for k, a in zip(self.kept, arrived)]

    def finish(self):
        while self.orders[0]:
            self.add(self.send(self.give()))
        return jnp.concatenate(self.parts, axis=-1).astype(F32)


def column_blocks(kept, arrived, sizes):
    total = kept
    for block in arrived:
        total = total + block.astype(F32)
    rows = total.shape[0] // sizes[0]
    blocks = [total[i * rows:(i + 1) * rows] for i in range(sizes[0])]
    return [blocks[0]] + [b.astype(BF16) for b in blocks[1:]]


def column_step(blocks, sizes):
    return [exchange(b, sizes, i, 0) for i, b in enumerate(blocks) if i]


def pinned(value):
    return pltpu.with_memory_space_constraint(value, pltpu.HBM)


def behind(values, marker):
    *values, _ = lax.optimization_barrier((*values, marker))
    return values


def column_halves(total, sizes, bit):
    blocks = sizes[0] // (2 * bit)
    pairs = total.reshape(blocks, 2, total.shape[0] // (2 * blocks), total.shape[1])
    kept, given = pairs[:, 0], pairs[:, 1]
    return [x.reshape(-1, total.shape[1]) for x in (kept, given.astype(BF16))]


def finished(kept, arrived):
    for block in arrived:
        kept = kept + block.astype(F32)
    return kept


def tied_call(kernel, after, operands, in_specs, out_shape, out_specs, **rest):
    waits = len(after)

    def body(*refs):
        kernel(*refs[waits:])

    return pl.pallas_call(
        body, out_shape=out_shape,
        in_specs=[pl.BlockSpec(memory_space=pl.ANY)] * waits + in_specs, out_specs=out_specs, **rest,
    )(*after, *operands)


def shards(sizes, tokens, qkv_weight, out_weight, merge_weight, merged_grad):
    levels, lat_rows, lon_cols, channels = tokens.shape
    merged_width = merge_weight.shape[1]
    count = levels * lat_rows * lon_cols
    groups = count // 4
    half = channels // 2
    strip_rows.extent = (lat_rows, lon_cols)
    vmem = pl.BlockSpec(memory_space=pltpu.VMEM)
    smem = pl.BlockSpec(memory_space=pltpu.SMEM)
    hbm = pl.BlockSpec(memory_space=pl.ANY)

    def shape(*extent, dtype=BF16):
        return jax.ShapeDtypeStruct(extent, dtype)

    def settings(weight, limit=60):
        return dict(
            compiler_params=pltpu.CompilerParams(vmem_limit_bytes=limit * MIB),
            cost_estimate=pl.CostEstimate(
                flops=int(weight * 1e10), bytes_accessed=16 * MIB, transcendentals=0
            ),
        )

    g_rows, g_cols = lat_rows // 2, lon_cols // 2
    cells = window_cells(levels, lat_rows, lon_cols)
    grps = window_groups(levels, g_rows, g_cols)
    cs = Strips(levels, lat_rows, lon_cols, SHIFT, True)
    gs = Strips(levels, g_rows, g_cols, HALF, False)
    g_strips = [padded(gs.side), padded(gs.above), padded(gs.corner)]
    to = ((0, lon_cols), (lat_rows, 0), (lat_rows, lon_cols))
    g_to = ((0, g_cols), (g_rows, 0), (g_rows, g_cols))
    own_rows = range(SHIFT, SHIFT + lat_rows)
    own_cols = range(SHIFT, SHIFT + lon_cols)
    own = box(levels, own_rows, own_cols)
    g_own = turned_box(levels, range(HALF, HALF + g_rows), range(HALF, HALF + g_cols))
    half_cells = count // 2
    side_cut = levels * SHIFT * SHIFT
    sent_cells = sum((Strips.sent(s, *t) for s, t in zip((cs.side, cs.above, cs.corner), to)), [])
    sent_groups = sum((Strips.sent(s, *t) for s, t in zip(g_strips, g_to)), [])
    held_top = box(levels, range(SHIFT, 2 * SHIFT), own_cols) + cs.side[:side_cut] + cs.above + cs.corner
    held_low = box(levels, range(2 * SHIFT, lat_rows), own_cols) + cs.side[side_cut:]
    depth = max(len(held_top), len(held_low))
    depth += -depth % 16
    held_top += [None] * (depth - len(held_top))
    held_low += [None] * (depth - len(held_low))

    tokens_flat = tokens.reshape(count, channels)
    merged_grad_flat = merged_grad.transpose(0, 2, 1, 3).reshape(groups, merged_width)
    extents = [(n + g, channels) for n, g in strip_rows(None, None)]
    packed = pl.pallas_call(
        pack_kernel,
        out_shape=[shape(*e) for e in extents],
        in_specs=[vmem] * 4, out_specs=[vmem] * 3,
        name="pack_strips", **settings(1),
    )(pinned(tokens_flat), pinned(merged_grad_flat), picks(sent_cells, own), picks(sent_groups, g_own))
    strips = sent_strips(packed, sizes, 1)

    order = jnp.concatenate([picks(cells[:half_cells], held_top), picks(cells[half_cells:], held_low)])
    group = picks(grps, g_own + sum(g_strips, []))
    edge = (lax.axis_index("lat") == 0).astype(jnp.int32).reshape(1)
    owner, rowmap = device_rows(channels, sizes)
    if channels // (sizes[0] * sizes[1]) % 16 == 0:
        rowmap = jnp.asarray(np.zeros((8, LANES), np.int32))

    wide = shape(count, channels)
    inner = 2 * 2 * WIN * WIN
    ready = tied_call(
        inner_kernel, packed,
        [pinned(tokens_flat), order[count - inner:], pinned(qkv_weight)],
        [vmem] * 2 + [hbm],
        [shape(inner, channels), shape(inner, channels), shape(inner, LANES, dtype=F32),
         shape(inner, channels), shape(inner, channels, dtype=F32), shape(inner, 3 * channels)],
        [vmem] * 6,
        scratch_shapes=[
            pltpu.VMEM(qkv_weight.shape, BF16),
            pltpu.SemaphoreType.DMA((3 * channels // TILE,)),
        ],
        name="inner_windows", **settings(9),
    )
    normed, normt, proj, dmr, dmm, grad, rstd, merged, out_mine, out_theirs = pl.pallas_call(
        forward_kernel,
        out_shape=[
            wide, shape(channels, count), shape(count, 3 * channels), wide, wide, wide,
            shape(count, LANES, dtype=F32), shape(groups, merged_width),
            shape(half, channels), shape(half, channels),
        ],
        in_specs=[smem] * 2 + [vmem] * 8 + [hbm] * 9,
        out_specs=[hbm] * 6 + [vmem] * 4,
        scratch_shapes=[
            pltpu.VMEM(qkv_weight.shape, BF16),
            pltpu.VMEM(out_weight.shape, BF16),
            pltpu.VMEM(merge_weight.shape, BF16),
            pltpu.VMEM((2, depth, channels), BF16),
            pltpu.VMEM((count, channels), BF16),
            pltpu.VMEM((count, channels), BF16),
            pltpu.VMEM((count, 3 * channels), BF16),
            pltpu.VMEM((count, channels), BF16),
            pltpu.VMEM((count, channels), F32),
            pltpu.VMEM((4, groups, channels), BF16),
            pltpu.VMEM((groups, 4 * channels), BF16),
            pltpu.VMEM((groups, merged_width), BF16),
            pltpu.VMEM((count, channels), BF16),
            pltpu.VMEM((count, channels), BF16),
            pltpu.VMEM((count, channels), BF16),
            pltpu.SemaphoreType.DMA((9,)),
            pltpu.SemaphoreType.DMA((6,)),
        ],
        name="block_forward", **settings(30, 55),
    )(edge, owner, tokens_flat, merged_grad_flat, *strips, order, group, rowmap,
      qkv_weight, out_weight, merge_weight, *ready)

    halves = 2
    width = channels // halves
    steps = width // TILE

    def backward(index, after):
        return tied_call(
            functools.partial(backward_kernel, index), after,
            [edge, pinned(proj), pinned(dmr), pinned(dmm), pinned(normt)], [smem] + [hbm] * 4,
            [shape(count, 3 * width), shape(half, 3 * width), shape(half, 3 * width)], [hbm] * 3,
            scratch_shapes=[
                pltpu.VMEM((5, count, width), BF16),
                pltpu.VMEM((channels, count), BF16),
                pltpu.VMEM((count, 3 * width), BF16),
                pltpu.VMEM((half, 3 * width), BF16),
                pltpu.VMEM((half, 3 * width), BF16),
                pltpu.SemaphoreType.DMA((steps, 5)),
                pltpu.SemaphoreType.DMA((1,)),
                pltpu.SemaphoreType.DMA((steps, 3, 3)),
            ],
            name="attention_backward", **settings(15, 32),
        )

    arrived = core_step(out_theirs, sizes)
    pg0, mine1, theirs1 = backward(0, [])
    out_mine, arrived = behind([out_mine, arrived], pg0)
    theirs1, = behind([theirs1], arrived)
    total = core_sum(out_mine, arrived)
    total1 = core_sum(mine1, core_step(theirs1, sizes))
    layer1 = Layer(jnp.concatenate([total, total1], axis=1), sizes)
    given = layer1.give()
    arrived1 = layer1.send(given)
    pg1, mine2, theirs2 = backward(1, given)
    arrived1 = behind(arrived1, pg1)
    theirs2, = behind([theirs2], arrived1)
    arrived = core_step(theirs2, sizes)
    layer1.add(arrived1)
    given1 = layer1.give()
    arrived1 = layer1.send(given1)
    layer2 = Layer(core_sum(mine2, arrived), sizes)
    given2 = layer2.give()
    arrived2 = layer2.send(given2)

    first_picks = picks(cs.side[:side_cut] + cs.above + cs.corner, cells[:half_cells])
    last_picks = picks(cs.side[side_cut:], cells[half_cells:])
    [ngrad] = tied_call(
        product_kernel, given1 + given2,
        [pg0, pg1, qkv_weight], [hbm] * 3, [wide], [vmem],
        scratch_shapes=[
            pltpu.VMEM((count, 3 * channels), BF16),
            pltpu.VMEM(qkv_weight.shape, BF16),
            pltpu.SemaphoreType.DMA((3 * halves + channels // TILE,)),
        ],
        name="input_product", **settings(8, 36),
    )
    arrived1 = behind(arrived1, ngrad)
    layer1.add(arrived1)
    total1 = layer1.finish()
    kept1, given1 = column_halves(total1, sizes, 1)
    got1 = exchange(given1, sizes, 1, 0)
    full, *strips = tied_call(
        input_kernel, [given1],
        [ngrad, normed, rstd, grad, merged,
         first_picks, last_picks, picks(sum(g_strips, []), grps)],
        [vmem] * 8, [wide] + [shape(*e) for e in extents], [vmem] * 4,
        name="input_backward", **settings(5, 30),
    )
    got1, *arrived2 = behind([got1] + arrived2, full)
    strips = sent_strips(strips, sizes, -1)
    layer2.add(arrived2)
    total2 = layer2.finish()

    part1 = kept1 + got1.astype(F32)
    column2 = column_blocks(total2, [], sizes)
    bit = 2
    while 2 * bit < sizes[0]:
        kept1, given1 = column_halves(part1, sizes, bit)
        part1 = kept1 + exchange(given1, sizes, bit, 0).astype(F32)
        bit *= 2
    kept1, last1 = column_halves(part1, sizes, bit)
    column2[bit] = jnp.concatenate([last1, column2[bit]], axis=1)
    got2 = column_step(column2, sizes)

    got = [Strips.sent(s, *t) for s, t in zip((cs.side, cs.above, cs.corner), to)]
    g_got = sum((Strips.sent(s, *t) for s, t in zip(g_strips, g_to)), [])
    tokens_grad, merged = tied_call(
        unpack_kernel, column2[1:] + [given1],
        [
            full, merged, *strips,
            picks(box(levels, range(SHIFT, 2 * SHIFT), own_cols), cells[:half_cells] + got[0][:side_cut]),
            picks(box(levels, range(2 * SHIFT, lat_rows), own_cols), cells[half_cells:] + got[0][side_cut:]),
            picks(box(levels, range(lat_rows, lat_rows + SHIFT), own_cols), got[1] + got[2]),
            picks(g_own, grps + g_got),
        ],
        [vmem] * 9, [wide, shape(groups, merged_width)], [vmem] * 2,
        name="unpack_strips", **settings(20, 24),
    )
    got2 = behind(got2, tokens_grad)
    qkv_weight_grad, out_weight_grad = pl.pallas_call(
        functools.partial(end_kernel, bit),
        out_shape=[
            shape(kept1.shape[0], 3 * channels, dtype=F32), shape(kept1.shape[0], channels, dtype=F32),
        ],
        in_specs=[vmem] * (2 + len(got2)), out_specs=[vmem] * 2,
        name="end_sums", **settings(1, 16),
    )(kept1, column2[0], *got2)
    merged = merged.reshape(levels, g_cols, g_rows, merged_width).transpose(0, 2, 1, 3)
    return merged, tokens_grad.reshape(tokens.shape), qkv_weight_grad, out_weight_grad


def solution(mesh):
    sizes = (mesh.shape["lat"], mesh.shape["lon"])
    in_specs = (P(None, "lat", "lon", None), P(), P(), P(), P(None, "lat", "lon", None))
    out_specs = (
        P(None, "lat", "lon", None),
        P(None, "lat", "lon", None),
        P(("lat", "lon"), None),
        P(("lat", "lon"), None),
    )
    return jax.shard_map(
        functools.partial(shards, sizes),
        mesh=mesh, in_specs=in_specs, out_specs=out_specs, check_vma=False,
    )
```
